32 devices in a mesh: groups: 2 (over x), blk: 16 (over z, y, core).
Axes of the slice: x: 2, y: 2, z: 4, core: 2. Of those that a mesh axis runs over, the one named last changes fastest.
Arguments:
- moe_input: bfloat16 [4096, 2048], P(('groups', 'blk')), parts along dimension 0, may hold values from -6 to 6
- moe_grad: bfloat16 [4096, 2048], P(('groups', 'blk')), parts along dimension 0, may hold values from -6 to 6
- routes: int32 [4096, 2], P(('groups', 'blk')), parts along dimension 0, may hold values from 0 to 7, all different within a row; in each aligned block of 128 rows (0 to 127, 128 to 255, ...) at most 48 rows name the same one
- route_weight: float32 [4096, 2], P(('groups', 'blk')), parts along dimension 0, may hold values from 0.1 to 1
- w_gate: bfloat16 [2048, 6144], P(None, 'blk'), may hold values from -0.125 to 0.125
- w_up: bfloat16 [2048, 6144], P(None, 'blk'), may hold values from -0.125 to 0.125
- w_down: bfloat16 [6144, 2048], P('blk'), may hold values from -0.21875 to 0.21875
- w_out: bfloat16 [2048, 4096], P('blk'), may hold values from -0.125 to 0.125
- queries: bfloat16 [4096, 4096], P(('groups', 'blk')), parts along dimension 0, may hold values from -200 to 200
- key_heads: bfloat16 [4096, 256], P(('groups', 'blk')), parts along dimension 0, may hold values from -6 to 6
- value_heads: bfloat16 [4096, 256], P(('groups', 'blk')), parts along dimension 0, may hold values from -6 to 6
- segments: int32 [4096], P(('groups', 'blk')), parts along dimension 0, may hold values from 0 to 15, never falling along the last dimension, each value on 1 to 384 neighbouring positions
Outputs:
- moe_input_grad: bfloat16 [4096, 2048], P(('groups', 'blk')), parts along dimension 0
- query_grad: bfloat16 [4096, 4096], P(('groups', 'blk')), parts along dimension 0
- key_grad: float32 [4096, 256], P(('groups', 'blk')), parts along dimension 0
- value_grad: float32 [4096, 256], P(('groups', 'blk')), parts along dimension 0
The draws below stay inside these ranges and needn't reach their ends.
There are 2 independent parts, one for each index of `groups`. The reference program is written for one: setup_inputs(seed, part) draws one part's arguments, and reference() takes and returns one part's arrays. A program takes and returns all parts, laid end to end along the dimension named above; an argument that names none is the same for every part. Nothing has to cross between parts.
Inputs may be any that keep to these rules, and one draw needn't show every extreme that they name: `routes`: each row names 2 different experts; within each aligned block of 128 rows (the tokens of one device) no expert is named more than 48 times, a bound that some block reaches.
All inputs are finite; a program needn't handle non-finite values.
Results may differ from the reference program's by a relative error of at most 0.014.
Values may be sent and summed in bfloat16 or wider, within the bound.
No kernel may reach another device: no remote copies, remote signals or barrier semaphores. Data moves between devices by JAX's collectives and lax.ppermute only.
A program may use at most 128 MiB of HBM per device.

```python
import math
import jax
import jax.numpy as jnp
import numpy as np
from jax import lax

D = 2048
FF = 768
ROUTES = 2
H = 32
KVH = 2
HD = 128
TOK_DEV = 128
GROUP = 16
EXPERTS = 8
SEQ = 2048
CAP = 48
N_BLK = 16


def shared_keys(key):
    base = jax.random.truncated_normal(jax.random.fold_in(key, 101), -5.0, 5.0, (SEQ, KVH * HD), jnp.float32)
    return base


def draw_key_heads(key, part):
    base = shared_keys(key)
    return base.astype(jnp.bfloat16)


def draw_queries(key, part):
    key = jax.random.fold_in(key, 2)
    return jax.random.truncated_normal(key, -5.0, 5.0, (SEQ, H * HD), jnp.float32).astype(jnp.bfloat16)


def block_scale(own_key, shape, pieces, least, top_value):
    gain, own = 1.0, jax.random.fold_in(own_key, 6)
    for dim, blocks in pieces:
        heights = jnp.exp(jax.random.uniform(jax.random.fold_in(own, dim), (blocks,), jnp.float32, least / len(pieces), top_value / len(pieces)))
        gain = gain * jnp.repeat(heights, shape[dim] // blocks).reshape([-1 if axis == dim else 1 for axis in range(len(shape))])
    return gain


def profile(count, total, most, skew):
    portions = [(1 << 20) // math.isqrt(rank ** skew) + 1 for rank in range(2, count + 1)]
    rest, counts = total - most - (count - 1), [1] * (count - 1)
    while rest > 0:
        free = [i for i in range(count - 1) if counts[i] < most]
        whole, budget = sum([portions[i] for i in free]), rest
        for i in free:
            extra = min(most - counts[i], max(1, budget * portions[i] // whole), rest)
            counts[i] = counts[i] + extra
            rest = rest - extra
    return np.array([most] + counts)


def uneven(key, number_of, total, most, skew):
    if number_of == 2:
        one = jax.random.randint(key, (), max(1, total - most), min(most, total - 1) + 1)
        return jnp.stack([one, total - one])
    tallies = jnp.asarray(profile(number_of, total, most, skew), jnp.int32)
    twos = (number_of - 1) // 2
    source_of, taker = tallies[1:1 + 2 * twos:2], tallies[2:2 + 2 * twos:2]
    margin = jnp.minimum(source_of - 1, most - taker)
    shifted = jax.random.randint(jax.random.fold_in(key, 1), (twos,), 0, 1 << 20) % (margin + 1)
    tallies = tallies.at[1:1 + 2 * twos:2].set(source_of - shifted).at[2:2 + 2 * twos:2].set(taker + shifted)
    return tallies[jax.random.permutation(jax.random.fold_in(key, 2), number_of)]


def assign_block(key, own, number, rows, count, top, limit, slope):
    sequence = jax.random.permutation(key, count)
    crowded, usual = portions_of(count, rows * top, limit, slope, True), portions_of(count, rows * top, limit, slope, False)
    places = jnp.arange(count)

    def named(lengths, rotation):
        used = int((lengths > 0).sum())
        fixed = max(1, used // 4)
        passed = fixed + (places - fixed + rotation * (used - fixed)) % max(1, count - fixed)
        return jnp.zeros((count,), jnp.int32).at[sequence[jnp.where(places < fixed, places, passed)]].set(jnp.asarray(lengths, jnp.int32))

    lengths = jnp.where(number % 4 == 0, named(crowded, number // 4), named(usual, number - number // 4 - 1))
    mixed = jax.random.permutation(jax.random.fold_in(own, 3), count)
    giver, receiver = mixed[0:count // 2 * 2:2], mixed[1:count // 2 * 2:2]
    room = jnp.minimum(lengths[giver] - 1, limit - lengths[receiver]) // 2
    room = jnp.where((giver == sequence[0]) | (receiver == sequence[0]) | (lengths[receiver] == 0), 0, jnp.maximum(room, 0))
    passed = jax.random.randint(jax.random.fold_in(own, 4), (count // 2,), 0, 1 << 20) % (room + 1)
    lengths = lengths.at[giver].add(-passed).at[receiver].add(passed)
    labels = jnp.searchsorted(jnp.cumsum(lengths), jnp.arange(rows * top), side="right").astype(jnp.int32)
    listing = labels.reshape(top, rows).T
    listing = listing[jax.random.permutation(jax.random.fold_in(own, 1), rows)]
    rotation = jax.random.randint(jax.random.fold_in(own, 2), (rows, 1), 0, top)
    return jnp.take_along_axis(listing, (jnp.arange(top)[None, :] + rotation) % top, axis=1)


def portions_of(count, total, reach, slope, full):
    weights = [(1 << 20) // math.isqrt(grade ** slope) + 1 for grade in range(1, count + 1)]
    largest = reach if full else min(reach, max(-(-total // count), total * weights[0] // sum(weights)))
    least = 1 if total - largest >= count - 1 else 0
    holding, surplus = [largest] + [least] * (count - 1), total - largest - least * (count - 1)
    while surplus > 0:
        movable = [i for i in range(1, count) if holding[i] < largest] or [i for i in range(1, count) if holding[i] < reach]
        mass, budget = sum([weights[i] for i in movable]), surplus
        for i in movable:
            more = min(reach - holding[i], max(1, budget * weights[i] // mass), surplus)
            holding[i] = holding[i] + more
            surplus = surplus - more
    return np.array(holding)


def scatter_about(own_key, dims, scale, limit, cuts=(), held_as=jnp.bfloat16):
    level = block_scale(own_key, dims, cuts, -0.22, 0.18) if cuts else 1.0
    values = jax.random.normal(own_key, dims, jnp.float32) * scale * level
    return jnp.minimum(jnp.maximum(values, -limit), limit).astype(held_as)


def setup_inputs(seed: int = 0, part: int = 0) -> dict:
    splits = jax.random.split(jax.random.key(seed), 13)
    part_keys = jax.random.split(jax.random.fold_in(splits[12], part), 13)
    moe_input = scatter_about(part_keys[0], (SEQ, D), 1.0, 6.0, ((0, 16),))
    moe_grad = scatter_about(part_keys[1], (SEQ, D), 1.0, 6.0, ((0, 16),))
    routes_keys = jax.random.split(jax.random.fold_in(part_keys[2], 1), SEQ // TOK_DEV)
    routes_turns = jax.random.permutation(jax.random.fold_in(part_keys[2], 3), SEQ // TOK_DEV)
    routes = jax.vmap(lambda own, number: assign_block(jax.random.fold_in(part_keys[2], 2), own, number, TOK_DEV, EXPERTS, ROUTES, CAP, 2))(routes_keys, routes_turns).reshape((SEQ, ROUTES))
    route_weight = jnp.clip(jnp.exp(math.log(1.0) - 2.3025851 * jax.random.uniform(part_keys[3], (SEQ, ROUTES), jnp.float32) ** block_scale(part_keys[3], (SEQ, ROUTES), ((0, 16),), -0.2, 0.2)), 0.1, 1.0)
    w_gate = scatter_about(splits[4], (D, EXPERTS * FF), D ** -0.5, 0.125, ((1, 16),))
    w_up = scatter_about(splits[5], (D, EXPERTS * FF), D ** -0.5, 0.125, ((1, 16),))
    w_down = scatter_about(splits[6], (EXPERTS * FF, D), FF ** -0.5, 0.21875, ((0, 16),))
    w_out = scatter_about(splits[7], (D, H * HD), D ** -0.5, 0.125, ((0, 16),))
    queries = draw_queries(jax.random.fold_in(jax.random.fold_in(splits[12], part), 71), part)
    key_heads = draw_key_heads(jax.random.fold_in(jax.random.fold_in(splits[12], part), 71), part)
    value_heads = scatter_about(part_keys[10], (SEQ, KVH * HD), 1.0, 6.0, ((0, 16),))
    segments = jnp.searchsorted(jnp.cumsum(uneven(part_keys[11], SEQ // TOK_DEV, SEQ, 3 * TOK_DEV, 1)), jnp.arange(SEQ), side="right").astype(jnp.int32)
    return dict(moe_input=moe_input, moe_grad=moe_grad, routes=routes, route_weight=route_weight, w_gate=w_gate, w_up=w_up, w_down=w_down, w_out=w_out, queries=queries, key_heads=key_heads, value_heads=value_heads, segments=segments)


floor_score = -1.0e30


def expert_terms(rows_in, grads_in, gate_cols, up_cols, down_rows):
    gate_pre = jnp.dot(rows_in, gate_cols, preferred_element_type=jnp.float32)
    up_pre = jnp.dot(rows_in, up_cols, preferred_element_type=jnp.float32)
    down_grad = jnp.dot(grads_in, down_rows.T, preferred_element_type=jnp.float32)
    sigmoid_gate = jax.nn.sigmoid(gate_pre)
    gate_grad = (down_grad * up_pre * sigmoid_gate * (1.0 + gate_pre * (1.0 - sigmoid_gate))).astype(jnp.bfloat16)
    up_grad = (down_grad * gate_pre * sigmoid_gate).astype(jnp.bfloat16)
    first = jnp.dot(gate_grad, gate_cols.T, preferred_element_type=jnp.float32)
    second = jnp.dot(up_grad, up_cols.T, preferred_element_type=jnp.float32)
    return first + second


def attend(q_rows, grad_rows, key_all, value_all, visible):
    row_count = q_rows.shape[0]
    span_count = key_all.shape[0]
    score_scale = HD ** -0.5
    query_split = q_rows.astype(jnp.float32).reshape(row_count, KVH, GROUP, HD)
    grad_split = grad_rows.astype(jnp.float32).reshape(row_count, KVH, GROUP, HD)
    key_split = key_all.astype(jnp.float32).reshape(span_count, KVH, HD)
    value_split = value_all.astype(jnp.float32).reshape(span_count, KVH, HD)
    scores = jnp.einsum('tgih,sgh->gits', query_split, key_split) * score_scale
    masked = jnp.where(visible[None, None], scores, floor_score)
    row_peak = jnp.max(masked, axis=-1, keepdims=True)
    raised = jnp.where(visible[None, None], jnp.exp(masked - row_peak), 0.0)
    shares = raised / jnp.sum(raised, axis=-1, keepdims=True)
    shares_low = shares.astype(jnp.bfloat16)
    attn_out = jnp.einsum('gits,sgh->tgih', shares_low.astype(jnp.float32), value_split)
    row_dot = jnp.transpose(jnp.sum(attn_out * grad_split, axis=-1), (1, 2, 0))
    prob_grad = jnp.einsum('tgih,sgh->gits', grad_split, value_split)
    score_grad = (shares * (prob_grad - row_dot[..., None]) * score_scale).astype(jnp.bfloat16)
    query_part = jnp.einsum('gits,sgh->tgih', score_grad.astype(jnp.float32), key_split)
    query_part = query_part.reshape(row_count, H * HD).astype(jnp.bfloat16)
    key_part = jnp.einsum('gits,tgih->sgh', score_grad.astype(jnp.float32), query_split).reshape(span_count, KVH * HD)
    value_part = jnp.einsum('gits,tgih->sgh', shares_low.astype(jnp.float32), grad_split).reshape(span_count, KVH * HD)
    return query_part, key_part, value_part


def fold_back(parts):
    own_part = parts[:, TOK_DEV:]
    earlier = parts[:, :TOK_DEV]
    later = jnp.concatenate([earlier[1:], jnp.zeros_like(earlier[:1])], axis=0)
    return (own_part + later).reshape(-1, parts.shape[-1])


def reference(moe_input, moe_grad, routes, route_weight, w_gate, w_up, w_down, w_out, queries, key_heads, value_heads, segments):
    flat_expert = routes.reshape(-1)
    flat_weight = route_weight.reshape(-1)
    bound = N_BLK * CAP

    def one_expert(carry, expert):
        member = flat_expert == expert
        picked = jnp.nonzero(member, size=bound, fill_value=0)[0].astype(jnp.int32)
        filled = jnp.arange(bound) < jnp.sum(member.astype(jnp.int32))
        token_of = (picked // ROUTES).astype(jnp.int32)
        rows_in = moe_input[token_of]
        grads_in = (flat_weight[picked][:, None] * moe_grad[token_of].astype(jnp.float32)).astype(jnp.bfloat16)
        first_col = (expert * FF).astype(jnp.int32)
        gate_cols = lax.dynamic_slice_in_dim(w_gate, first_col, FF, 1)
        up_cols = lax.dynamic_slice_in_dim(w_up, first_col, FF, 1)
        down_rows = lax.dynamic_slice_in_dim(w_down, first_col, FF, 0)
        terms = expert_terms(rows_in, grads_in, gate_cols, up_cols, down_rows)
        carry = carry.at[token_of].add(jnp.where(filled[:, None], terms, jnp.zeros_like(terms)))
        return carry, None

    total, unused = lax.scan(one_expert, jnp.zeros((SEQ, D), jnp.float32), jnp.arange(EXPERTS, dtype=jnp.int32))
    moe_input_grad = total.astype(jnp.bfloat16)
    stream_grad = (moe_grad.astype(jnp.float32) + moe_input_grad.astype(jnp.float32)).astype(jnp.bfloat16)
    head_grad = jnp.dot(stream_grad, w_out, preferred_element_type=jnp.float32).astype(jnp.bfloat16)

    block_count = SEQ // TOK_DEV

    def one_block(block_index):
        start = (block_index * TOK_DEV).astype(jnp.int32)
        before = (jnp.maximum(block_index - 1, 0) * TOK_DEV).astype(jnp.int32)
        q_rows = lax.dynamic_slice_in_dim(queries, start, TOK_DEV, 0)
        grad_rows = lax.dynamic_slice_in_dim(head_grad, start, TOK_DEV, 0)
        seg_own = lax.dynamic_slice_in_dim(segments, start, TOK_DEV, 0)
        seg_prev = lax.dynamic_slice_in_dim(segments, before, TOK_DEV, 0)
        position = jnp.arange(TOK_DEV)
        own_visible = (position[None, :] <= position[:, None]) & (seg_own[None, :] == seg_own[:, None])
        prev_visible = (seg_prev[None, :] == seg_own[:, None]) & (block_index >= 1)
        visible = jnp.concatenate([prev_visible, own_visible], axis=1)
        key_all = jnp.concatenate([lax.dynamic_slice_in_dim(key_heads, before, TOK_DEV, 0), lax.dynamic_slice_in_dim(key_heads, start, TOK_DEV, 0)], axis=0)
        value_all = jnp.concatenate([lax.dynamic_slice_in_dim(value_heads, before, TOK_DEV, 0), lax.dynamic_slice_in_dim(value_heads, start, TOK_DEV, 0)], axis=0)
        return attend(q_rows, grad_rows, key_all, value_all, visible)

    query_blocks, key_blocks, value_blocks = lax.map(one_block, jnp.arange(block_count, dtype=jnp.int32))
    query_grad = query_blocks.reshape(SEQ, H * HD)
    key_grad = fold_back(key_blocks)
    value_grad = fold_back(value_blocks)
    return moe_input_grad, query_grad, key_grad, value_grad
```

```python
import functools

import jax
import jax.numpy as jnp
from jax import lax
from jax.experimental import pallas as pl
from jax.experimental.pallas import tpu as pltpu
from jax.sharding import PartitionSpec as P

KVH = 2
GROUP = 16
HD = 128
FLOOR = -1e30
MIB = 1 << 20

NT = (((1,), (1,)), ((), ()))
TN = (((0,), (0,)), ((), ()))


def dot(a, b, dims=(((1,), (0,)), ((), ()))):
    return lax.dot_general(a, b, dims, preferred_element_type=jnp.float32)


def params(mib):
    return pltpu.CompilerParams(vmem_limit_bytes=mib * MIB)


def pick_kernel(owners, depth, routes_ref, weight_ref, input_ref, grad_ref, rows_ref, place_ref):
    tokens = input_ref.shape[0]
    slots = owners * depth
    first = routes_ref[0:1, :]
    second = routes_ref[1:2, :]
    expert = lax.broadcasted_iota(jnp.int32, (owners, tokens), 0)
    is_first = first == expert
    is_second = second == expert
    member = jnp.where(is_first | is_second, 1.0, 0.0)
    before = lax.broadcasted_iota(jnp.int32, (tokens, tokens), 0) < lax.broadcasted_iota(
        jnp.int32, (tokens, tokens), 1
    )
    rank = dot(member.astype(jnp.bfloat16), jnp.where(before, 1.0, 0.0).astype(jnp.bfloat16))
    spot = (expert * depth).astype(jnp.float32) + rank
    slot_first = jnp.sum(jnp.where(is_first, spot, 0.0), axis=0, keepdims=True).astype(jnp.int32)
    slot_second = jnp.sum(jnp.where(is_second, spot, 0.0), axis=0, keepdims=True).astype(jnp.int32)
    slot = lax.broadcasted_iota(jnp.int32, (slots, tokens), 0)
    at_first = slot == slot_first
    at_second = slot == slot_second
    place = jnp.where(at_first | at_second, 1.0, 0.0).astype(jnp.bfloat16)
    place_ref[...] = place
    scale = jnp.sum(
        jnp.where(at_first, weight_ref[0:1, :], 0.0) + jnp.where(at_second, weight_ref[1:2, :], 0.0),
        axis=1,
        keepdims=True,
    )
    width = input_ref.shape[1]
    rows_ref[:, :width] = dot(place, input_ref[...]).astype(jnp.bfloat16)
    rows_ref[:, width:] = (scale * dot(place, grad_ref[...])).astype(jnp.bfloat16)


def pick(routes, route_weight, moe_input, moe_grad, owners, depth):
    tokens, width = moe_input.shape
    slots = owners * depth
    return pl.pallas_call(
        functools.partial(pick_kernel, owners, depth),
        out_shape=(
            jax.ShapeDtypeStruct((slots, 2 * width), jnp.bfloat16),
            jax.ShapeDtypeStruct((slots, tokens), jnp.bfloat16),
        ),
        compiler_params=params(32),
        cost_estimate=pl.CostEstimate(
            flops=4 * slots * tokens * width, bytes_accessed=8 * MIB, transcendentals=0
        ),
        name="pick_rows",
    )(routes.T, route_weight.T, moe_input, moe_grad)


def expert_kernel(rows_ref, *refs):
    own, other, out_ref, total = refs[:3], refs[3:6], refs[6], refs[7]
    step = pl.program_id(0)
    width = rows_ref.shape[1] // 2
    inputs = rows_ref[:, :width]
    grads = rows_ref[:, width:]
    part = None
    for gate_ref, up_ref, down_ref in (own, other):
        gate_cols = gate_ref[...]
        up_cols = up_ref[...]
        gate_pre = dot(inputs, gate_cols)
        up_pre = dot(inputs, up_cols)
        down_grad = dot(grads, down_ref[...], NT)
        sig = jax.nn.sigmoid(gate_pre)
        gate_grad = (down_grad * up_pre * sig * (1.0 + gate_pre * (1.0 - sig))).astype(jnp.bfloat16)
        up_grad = (down_grad * gate_pre * sig).astype(jnp.bfloat16)
        term = dot(gate_grad, gate_cols, NT) + dot(up_grad, up_cols, NT)
        part = term if part is None else part + term

    @pl.when(step == 0)
    def _():
        total[...] = part

    @pl.when(step > 0)
    def _():
        total[...] += part

    @pl.when(step == pl.num_programs(0) - 1)
    def _():
        out_ref[...] = total[...].astype(jnp.bfloat16)


def experts(rows, own, other):
    count, twice = rows.shape
    width = twice // 2
    half = own[0].shape[1]
    tile = 128
    cols = pl.BlockSpec((width, tile), lambda i: (0, i))
    down = pl.BlockSpec((tile, width), lambda i: (i, 0))
    return pl.pallas_call(
        expert_kernel,
        grid=(half // tile,),
        in_specs=[pl.BlockSpec((count, twice), lambda i: (0, 0))] + [cols, cols, down] * 2,
        out_specs=pl.BlockSpec((count, width), lambda i: (0, 0)),
        out_shape=jax.ShapeDtypeStruct((count, width), jnp.bfloat16),
        scratch_shapes=[pltpu.VMEM((count, width), jnp.float32)],
        compiler_params=params(48),
        cost_estimate=pl.CostEstimate(
            flops=2 * count * width * half * 10, bytes_accessed=12 * width * half + 6 * count * width,
            transcendentals=2 * count * half,
        ),
        name="expert_terms",
    )(rows, *own, *other)


def shares_kernel(q_ref, key_ref, seen_ref, out_ref):
    seen = seen_ref[...] > 0.5
    keys = key_ref[...]
    for head in range(GROUP):
        query = q_ref[:, head * HD : (head + 1) * HD]
        scores = dot(query, keys, NT) * (HD**-0.5)
        masked = jnp.where(seen, scores, FLOOR)
        raised = jnp.where(seen, jnp.exp(masked - jnp.max(masked, axis=1, keepdims=True)), 0.0)
        shares = raised / jnp.sum(raised, axis=1, keepdims=True)
        out_ref[:, head * 2 * HD : (head + 1) * 2 * HD] = shares.astype(jnp.bfloat16)


def attention_shares(queries, key_all, seen):
    tokens, width = queries.shape
    span = key_all.shape[0]
    per = GROUP * HD
    return pl.pallas_call(
        shares_kernel,
        grid=(KVH,),
        in_specs=[
            pl.BlockSpec((tokens, per), lambda i: (0, i)),
            pl.BlockSpec((span, HD), lambda i: (0, i)),
            pl.BlockSpec((tokens, span), lambda i: (0, 0)),
        ],
        out_specs=pl.BlockSpec((tokens, GROUP * span), lambda i: (0, i)),
        out_shape=jax.ShapeDtypeStruct((tokens, KVH * GROUP * span), jnp.bfloat16),
        compiler_params=params(32),
        cost_estimate=pl.CostEstimate(
            flops=2 * tokens * width * span, bytes_accessed=4 * MIB,
            transcendentals=tokens * span * KVH * GROUP,
        ),
        name="attention_shares",
    )(queries, key_all, seen)


def tail_kernel(
    per_step, back_ref, place_ref, grad_ref, w_ref, share_ref, q_ref, key_ref, value_ref,
    moe_ref, query_out, key_out, value_out, stream,
):
    group = pl.program_id(0)
    step = pl.program_id(1)
    span = key_ref.shape[0]

    @pl.when((group == 0) & (step == 0))
    def _():
        moe = dot(place_ref[...], back_ref[...], TN).astype(jnp.bfloat16)
        moe_ref[...] = moe
        stream[...] = (grad_ref[...].astype(jnp.float32) + moe.astype(jnp.float32)).astype(jnp.bfloat16)

    head_grad = dot(stream[...], w_ref[...]).astype(jnp.bfloat16)
    keys = key_ref[...]
    values = value_ref[...]
    key_part = None
    value_part = None
    for head in range(per_step):
        cols = slice(head * HD, (head + 1) * HD)
        grad = head_grad[:, cols]
        low = share_ref[:, head * span : (head + 1) * span]
        shares = low.astype(jnp.float32)
        prob_grad = dot(grad, values, NT)
        row_dot = jnp.sum(shares * prob_grad, axis=1, keepdims=True)
        score_grad = (shares * (prob_grad - row_dot) * (HD**-0.5)).astype(jnp.bfloat16)
        query_out[:, cols] = dot(score_grad, keys).astype(jnp.bfloat16)
        key_term = dot(score_grad, q_ref[:, cols], TN)
        value_term = dot(low, grad, TN)
        key_part = key_term if key_part is None else key_part + key_term
        value_part = value_term if value_part is None else value_part + value_term

    @pl.when(step == 0)
    def _():
        key_out[...] = key_part
        value_out[...] = value_part

    @pl.when(step > 0)
    def _():
        key_out[...] += key_part
        value_out[...] += value_part


def tail(back, place, moe_grad, w_all, shares, queries, key_all, value_all):
    tokens, width = moe_grad.shape
    slots = back.shape[0]
    span = key_all.shape[0]
    per_step = 4
    steps = GROUP // per_step
    tile = per_step * HD
    whole = lambda shape: pl.BlockSpec(shape, lambda g, i: (0, 0))
    kv = pl.BlockSpec((span, HD), lambda g, i: (0, g))
    heads = pl.BlockSpec((tokens, tile), lambda g, i: (0, g * steps + i))
    return pl.pallas_call(
        functools.partial(tail_kernel, per_step),
        grid=(KVH, steps),
        in_specs=[
            whole((slots, width)),
            whole((slots, tokens)),
            whole((tokens, width)),
            pl.BlockSpec((None, width, tile), lambda g, i: (g, 0, i)),
            pl.BlockSpec((tokens, per_step * span), lambda g, i: (0, g * steps + i)),
            heads,
            kv,
            kv,
        ],
        out_specs=[whole((tokens, width)), heads, kv, kv],
        out_shape=(
            jax.ShapeDtypeStruct((tokens, width), jnp.bfloat16),
            jax.ShapeDtypeStruct(queries.shape, jnp.bfloat16),
            jax.ShapeDtypeStruct((span, KVH * HD), jnp.float32),
            jax.ShapeDtypeStruct((span, KVH * HD), jnp.float32),
        ),
        scratch_shapes=[pltpu.VMEM((tokens, width), jnp.bfloat16)],
        compiler_params=params(48),
        cost_estimate=pl.CostEstimate(
            flops=2 * tokens * width * KVH * GROUP * HD, bytes_accessed=22 * MIB, transcendentals=0
        ),
        name="tail_attention",
    )(back, place, moe_grad, w_all, shares, queries, key_all, value_all)


def local(
    moe_input,
    moe_grad,
    routes,
    route_weight,
    w_gate,
    w_up,
    w_down,
    w_out,
    queries,
    key_heads,
    value_heads,
    segments,
):
    count = lax.axis_size("blk")
    parts = lax.axis_size("groups")
    tokens, width = moe_input.shape
    owners = count // 2
    depth = 2 * max(1, 3 * tokens * routes.shape[1] // (2 * count))
    same_core = [[2 * chip + core for chip in range(owners)] for core in range(2)]
    partner = [(i, i ^ 1) for i in range(count)]
    onward = [(i, i + 1) for i in range(count - 1)]
    backward = [(i + 1, i) for i in range(count - 1)]

    share_cols = w_out.shape[1] // parts
    w_share = lax.dynamic_slice_in_dim(w_out, lax.axis_index("groups") * share_cols, share_cols, 1)
    w_all = lax.all_gather(w_share, ("groups", "blk"), axis=0, tiled=True)
    w_all = w_all.reshape(parts, width, share_cols)

    rows, place = pick(routes, route_weight, moe_input, moe_grad, owners, depth)
    rows_in = lax.all_to_all(
        rows.reshape(owners, depth, 2 * width), "blk", 0, 0, axis_index_groups=same_core, tiled=True
    )
    own = (w_gate, w_up, w_down)
    other = tuple(lax.ppermute(w, "blk", partner) for w in own)

    kv = jnp.concatenate([key_heads, value_heads], axis=1)
    prev_kv, prev_segment = lax.ppermute((kv, segments), "blk", onward)
    key_all = jnp.concatenate([prev_kv[:, : KVH * HD], key_heads], axis=0)
    value_all = jnp.concatenate([prev_kv[:, KVH * HD :], value_heads], axis=0)
    position = jnp.arange(tokens)
    own_seen = (position[None, :] <= position[:, None]) & (segments[None, :] == segments[:, None])
    prev_seen = (prev_segment[None, :] == segments[:, None]) & (lax.axis_index("blk") >= 1)
    seen = jnp.concatenate([prev_seen, own_seen], axis=1).astype(jnp.float32)
    shares = attention_shares(queries, key_all, seen)

    terms = experts(rows_in.reshape(owners * depth, 2 * width), own, other)
    back = lax.all_to_all(
        terms.reshape(owners, depth, width), "blk", 0, 0, axis_index_groups=same_core, tiled=True
    )
    moe_input_grad, query_grad, key_part, value_part = tail(
        back.reshape(owners * depth, width), place, moe_grad, w_all, shares, queries, key_all, value_all
    )
    sent = jnp.concatenate([key_part[:tokens], value_part[:tokens]], axis=1).astype(jnp.bfloat16)
    later = lax.ppermute(sent, "blk", backward).astype(jnp.float32)
    key_grad = key_part[tokens:] + later[:, : KVH * HD]
    value_grad = value_part[tokens:] + later[:, KVH * HD :]
    return (moe_input_grad, query_grad, key_grad, value_grad)


def solution(mesh):
    by_tokens = P(("groups", "blk"), None)
    return jax.shard_map(
        local,
        mesh=mesh,
        in_specs=(
            by_tokens,
            by_tokens,
            by_tokens,
            by_tokens,
            P(None, "blk"),
            P(None, "blk"),
            P("blk", None),
            P("blk", None),
            by_tokens,
            by_tokens,
            by_tokens,
            P(("groups", "blk")),
        ),
        out_specs=(by_tokens,) * 4,
        check_vma=False,
    )
```

```python
import functools

import jax
import jax.numpy as jnp
from jax import lax
from jax.experimental import pallas as pl
from jax.experimental.pallas import tpu as pltpu
from jax.sharding import PartitionSpec as P

KVH = 2
GROUP = 16
HD = 128
FLOOR = -1e30
MIB = 1 << 20

NT = (((1,), (1,)), ((), ()))
TN = (((0,), (0,)), ((), ()))


def dot(a, b, dims=(((1,), (0,)), ((), ()))):
    return lax.dot_general(a, b, dims, preferred_element_type=jnp.float32)


def params(mib):
    return pltpu.CompilerParams(vmem_limit_bytes=mib * MIB)


def pick_kernel(owners, depth, routes_ref, weight_ref, input_ref, grad_ref, rows_ref, place_ref):
    tokens = input_ref.shape[0]
    slots = owners * depth
    first = routes_ref[0:1, :]
    second = routes_ref[1:2, :]
    expert = lax.broadcasted_iota(jnp.int32, (owners, tokens), 0)
    is_first = first == expert
    is_second = second == expert
    member = jnp.where(is_first | is_second, 1.0, 0.0)
    before = lax.broadcasted_iota(jnp.int32, (tokens, tokens), 0) < lax.broadcasted_iota(
        jnp.int32, (tokens, tokens), 1
    )
    rank = dot(member.astype(jnp.bfloat16), jnp.where(before, 1.0, 0.0).astype(jnp.bfloat16))
    spot = (expert * depth).astype(jnp.float32) + rank
    slot_first = jnp.sum(jnp.where(is_first, spot, 0.0), axis=0, keepdims=True).astype(jnp.int32)
    slot_second = jnp.sum(jnp.where(is_second, spot, 0.0), axis=0, keepdims=True).astype(jnp.int32)
    slot = lax.broadcasted_iota(jnp.int32, (slots, tokens), 0)
    at_first = slot == slot_first
    at_second = slot == slot_second
    place = jnp.where(at_first | at_second, 1.0, 0.0).astype(jnp.bfloat16)
    place_ref[...] = place
    scale = jnp.sum(
        jnp.where(at_first, weight_ref[0:1, :], 0.0) + jnp.where(at_second, weight_ref[1:2, :], 0.0),
        axis=1,
        keepdims=True,
    )
    width = input_ref.shape[1]
    rows_ref[:, :width] = dot(place, input_ref[...]).astype(jnp.bfloat16)
    rows_ref[:, width:] = (scale * dot(place, grad_ref[...])).astype(jnp.bfloat16)


def pick(routes, route_weight, moe_input, moe_grad, owners, depth):
    tokens, width = moe_input.shape
    slots = owners * depth
    return pl.pallas_call(
        functools.partial(pick_kernel, owners, depth),
        out_shape=(
            jax.ShapeDtypeStruct((slots, 2 * width), jnp.bfloat16),
            jax.ShapeDtypeStruct((slots, tokens), jnp.bfloat16),
        ),
        compiler_params=params(32),
        cost_estimate=pl.CostEstimate(
            flops=4 * slots * tokens * width, bytes_accessed=8 * MIB, transcendentals=0
        ),
        name="pick_rows",
    )(routes.T, route_weight.T, moe_input, moe_grad)


def weights_kernel(*refs):
    own, other, (cols_ref, down_ref, rows_ref) = refs[:3], refs[3:6], refs[6:]
    tile = own[0].shape[1]
    for place, (gate_ref, up_ref, low_ref) in enumerate((own, other)):
        for kind, ref in enumerate((gate_ref, up_ref)):
            spot = slice((2 * kind + place) * tile, (2 * kind + place + 1) * tile)
            cols_ref[0, :, spot] = ref[...]
            rows_ref[0, spot, :] = ref[...].T
        down_ref[0, :, place * tile : (place + 1) * tile] = low_ref[...].T


def prepare_weights(own, other):
    width, half = own[0].shape
    tile = 128
    steps = half // tile
    cols = pl.BlockSpec((width, tile), lambda i: (0, i))
    down = pl.BlockSpec((tile, width), lambda i: (i, 0))
    return pl.pallas_call(
        weights_kernel,
        grid=(steps,),
        in_specs=[cols, cols, down] * 2,
        out_specs=[
            pl.BlockSpec((1, width, 4 * tile), lambda i: (i, 0, 0)),
            pl.BlockSpec((1, width, 2 * tile), lambda i: (i, 0, 0)),
            pl.BlockSpec((1, 4 * tile, width), lambda i: (i, 0, 0)),
        ],
        out_shape=(
            jax.ShapeDtypeStruct((steps, width, 4 * tile), jnp.bfloat16),
            jax.ShapeDtypeStruct((steps, width, 2 * tile), jnp.bfloat16),
            jax.ShapeDtypeStruct((steps, 4 * tile, width), jnp.bfloat16),
        ),
        compiler_params=params(48),
        cost_estimate=pl.CostEstimate(
            flops=0, bytes_accessed=32 * width * half, transcendentals=0
        ),
        name="prepare_weights",
    )(*own, *other)


def expert_kernel(steps, rows_ref, cols_ref, down_ref, back_ref, out_ref, hidden):
    step = pl.program_id(0)
    width = rows_ref.shape[1] // 2
    pair = down_ref.shape[2]

    @pl.when(step < steps)
    def _():
        both_pre = dot(rows_ref[:, :width], cols_ref[0])
        gate_pre = both_pre[:, :pair]
        up_pre = both_pre[:, pair:]
        down_grad = dot(rows_ref[:, width:], down_ref[0])
        sig = jax.nn.sigmoid(gate_pre)
        hidden[step, :, :pair] = (
            down_grad * up_pre * sig * (1.0 + gate_pre * (1.0 - sig))
        ).astype(jnp.bfloat16)
        hidden[step, :, pair:] = (down_grad * gate_pre * sig).astype(jnp.bfloat16)

    @pl.when(step >= steps)
    def _():
        total = dot(hidden[0], back_ref[0])
        for i in range(1, steps):
            total += dot(hidden[i], back_ref[i])
        out_ref[...] = total.astype(jnp.bfloat16)


def experts(rows, cols, down, back):
    count, twice = rows.shape
    steps, width, quad = cols.shape
    tile = 512
    last = steps - 1
    turn = lambda i: jnp.maximum(i - steps, 0)
    return pl.pallas_call(
        functools.partial(expert_kernel, steps),
        grid=(steps + width // tile,),
        in_specs=[
            pl.BlockSpec((count, twice), lambda i: (0, 0)),
            pl.BlockSpec((1, width, quad), lambda i: (jnp.minimum(i, last), 0, 0)),
            pl.BlockSpec((1, width, quad // 2), lambda i: (jnp.minimum(i, last), 0, 0)),
            pl.BlockSpec((steps, quad, tile), lambda i: (0, 0, turn(i))),
        ],
        out_specs=pl.BlockSpec((count, tile), lambda i: (0, turn(i))),
        out_shape=jax.ShapeDtypeStruct((count, width), jnp.bfloat16),
        scratch_shapes=[pltpu.VMEM((steps, count, quad), jnp.bfloat16)],
        compiler_params=params(48),
        cost_estimate=pl.CostEstimate(
            flops=5 * count * width * steps * quad, bytes_accessed=20 * MIB,
            transcendentals=count * steps * quad,
        ),
        name="expert_terms",
    )(rows, cols, down, back)


def shares_kernel(q_ref, key_ref, seen_ref, out_ref):
    seen = seen_ref[...] > 0.5
    keys = key_ref[...]
    for head in range(GROUP):
        query = q_ref[:, head * HD : (head + 1) * HD]
        scores = dot(query, keys, NT) * (HD**-0.5)
        masked = jnp.where(seen, scores, FLOOR)
        raised = jnp.where(seen, jnp.exp(masked - jnp.max(masked, axis=1, keepdims=True)), 0.0)
        shares = raised / jnp.sum(raised, axis=1, keepdims=True)
        out_ref[:, head * 2 * HD : (head + 1) * 2 * HD] = shares.astype(jnp.bfloat16)


def attention_shares(queries, key_all, seen):
    tokens, width = queries.shape
    span = key_all.shape[0]
    per = GROUP * HD
    return pl.pallas_call(
        shares_kernel,
        grid=(KVH,),
        in_specs=[
            pl.BlockSpec((tokens, per), lambda i: (0, i)),
            pl.BlockSpec((span, HD), lambda i: (0, i)),
            pl.BlockSpec((tokens, span), lambda i: (0, 0)),
        ],
        out_specs=pl.BlockSpec((tokens, GROUP * span), lambda i: (0, i)),
        out_shape=jax.ShapeDtypeStruct((tokens, KVH * GROUP * span), jnp.bfloat16),
        compiler_params=params(32),
        cost_estimate=pl.CostEstimate(
            flops=2 * tokens * width * span, bytes_accessed=4 * MIB,
            transcendentals=tokens * span * KVH * GROUP,
        ),
        name="attention_shares",
    )(queries, key_all, seen)


def tail_kernel(
    per_step, order, back_ref, place_ref, grad_ref, w_ref, share_ref, q_ref, key_ref, value_ref,
    moe_ref, query_out, key_out, value_out, stream,
):
    group = pl.program_id(0)
    step = pl.program_id(1)
    span = key_ref.shape[0]

    @pl.when((group == 0) & (step == 0))
    def _():
        moe = dot(place_ref[...], back_ref[...], TN).astype(jnp.bfloat16)
        moe_ref[...] = moe
        added = (grad_ref[...].astype(jnp.float32) + moe.astype(jnp.float32)).astype(jnp.bfloat16)
        size = added.shape[1] // len(order)
        for to, source in enumerate(order):
            stream[:, to * size : (to + 1) * size] = added[:, source * size : (source + 1) * size]

    head_grad = dot(stream[...], w_ref[...]).astype(jnp.bfloat16)
    keys = key_ref[...]
    values = value_ref[...]
    key_part = None
    value_part = None
    for head in range(per_step):
        cols = slice(head * HD, (head + 1) * HD)
        grad = head_grad[:, cols]
        low = share_ref[:, head * span : (head + 1) * span]
        shares = low.astype(jnp.float32)
        prob_grad = dot(grad, values, NT)
        row_dot = jnp.sum(shares * prob_grad, axis=1, keepdims=True)
        score_grad = (shares * (prob_grad - row_dot) * (HD**-0.5)).astype(jnp.bfloat16)
        query_out[:, cols] = dot(score_grad, keys).astype(jnp.bfloat16)
        key_term = dot(score_grad, q_ref[:, cols], TN)
        value_term = dot(low, grad, TN)
        key_part = key_term if key_part is None else key_part + key_term
        value_part = value_term if value_part is None else value_part + value_term

    @pl.when(step == 0)
    def _():
        key_out[...] = key_part
        value_out[...] = value_part

    @pl.when(step > 0)
    def _():
        key_out[...] += key_part
        value_out[...] += value_part


def tail(order, back, place, moe_grad, w_all, shares, queries, key_all, value_all):
    tokens, width = moe_grad.shape
    slots = back.shape[0]
    span = key_all.shape[0]
    per_step = 4
    steps = GROUP // per_step
    tile = per_step * HD
    whole = lambda shape: pl.BlockSpec(shape, lambda g, i: (0, 0))
    kv = pl.BlockSpec((span, HD), lambda g, i: (0, g))
    heads = pl.BlockSpec((tokens, tile), lambda g, i: (0, g * steps + i))
    return pl.pallas_call(
        functools.partial(tail_kernel, per_step, order),
        grid=(KVH, steps),
        in_specs=[
            whole((slots, width)),
            whole((slots, tokens)),
            whole((tokens, width)),
            pl.BlockSpec((None, width, tile), lambda g, i: (g, 0, i)),
            pl.BlockSpec((tokens, per_step * span), lambda g, i: (0, g * steps + i)),
            heads,
            kv,
            kv,
        ],
        out_specs=[whole((tokens, width)), heads, kv, kv],
        out_shape=(
            jax.ShapeDtypeStruct((tokens, width), jnp.bfloat16),
            jax.ShapeDtypeStruct(queries.shape, jnp.bfloat16),
            jax.ShapeDtypeStruct((span, KVH * HD), jnp.float32),
            jax.ShapeDtypeStruct((span, KVH * HD), jnp.float32),
        ),
        scratch_shapes=[pltpu.VMEM((tokens, width), jnp.bfloat16)],
        compiler_params=params(48),
        cost_estimate=pl.CostEstimate(
            flops=2 * tokens * width * KVH * GROUP * HD, bytes_accessed=22 * MIB, transcendentals=0
        ),
        name="tail_attention",
    )(back, place, moe_grad, w_all, shares, queries, key_all, value_all)


def far_first(share):
    for axis in ("far", "near"):
        moved = lax.ppermute(share, axis, [(0, 1), (1, 0)])
        mine = lax.axis_index(axis) == 0
        share = jnp.where(mine, jnp.stack([share, moved]), jnp.stack([moved, share]))
    return share


def local(
    moe_input,
    moe_grad,
    routes,
    route_weight,
    w_gate,
    w_up,
    w_down,
    w_out,
    queries,
    key_heads,
    value_heads,
    segments,
):
    chips = ("far", "near", "low")
    blk = chips + ("core",)
    low = lax.axis_size("low")
    owners = 4 * low
    count = 2 * owners
    parts = lax.axis_size("groups")
    tokens, width = moe_input.shape
    depth = 2 * max(1, 3 * tokens * routes.shape[1] // (2 * count))
    onward = [(i, i + 1) for i in range(count - 1)]
    backward = [(i + 1, i) for i in range(count - 1)]

    share_cols = w_out.shape[1] // parts
    w_share = lax.dynamic_slice_in_dim(w_out, lax.axis_index("groups") * share_cols, share_cols, 1)
    w_plane = far_first(w_share)
    w_all = lax.all_gather(w_plane, ("groups", "low", "core"), axis=0, tiled=False)
    block = w_out.shape[0]
    w_all = w_all.reshape(parts, 2 * low, 2, 2, block, share_cols)
    order = tuple(
        (2 * far + near) * 2 * low + rest
        for rest in range(2 * low)
        for near in range(2)
        for far in range(2)
    )
    if block % 128:
        w_all = w_all.transpose(0, 3, 2, 1, 4, 5)
        order = (0,)
    w_all = w_all.reshape(parts, width, share_cols)

    rows, place = pick(routes, route_weight, moe_input, moe_grad, owners, depth)
    rows_in = lax.all_to_all(rows.reshape(owners, depth, 2 * width), chips, 0, 0, tiled=True)
    own = (w_gate, w_up, w_down)
    other = tuple(lax.ppermute(w, "core", [(0, 1), (1, 0)]) for w in own)
    prepared = prepare_weights(own, other)

    kv = jnp.concatenate([key_heads, value_heads], axis=1)
    prev_kv, prev_segment = lax.ppermute((kv, segments), blk, onward)
    key_all = jnp.concatenate([prev_kv[:, : KVH * HD], key_heads], axis=0)
    value_all = jnp.concatenate([prev_kv[:, KVH * HD :], value_heads], axis=0)
    position = jnp.arange(tokens)
    own_seen = (position[None, :] <= position[:, None]) & (segments[None, :] == segments[:, None])
    prev_seen = (prev_segment[None, :] == segments[:, None]) & (lax.axis_index(blk) >= 1)
    seen = jnp.concatenate([prev_seen, own_seen], axis=1).astype(jnp.float32)
    shares = attention_shares(queries, key_all, seen)

    prepared, shares, rows_in = lax.optimization_barrier((prepared, shares, rows_in))
    terms = experts(rows_in.reshape(owners * depth, 2 * width), *prepared)
    back = lax.all_to_all(terms.reshape(owners, depth, width), chips, 0, 0, tiled=True)
    moe_input_grad, query_grad, key_part, value_part = tail(
        order, back.reshape(owners * depth, width), place, moe_grad, w_all, shares, queries,
        key_all, value_all,
    )
    sent = jnp.concatenate([key_part[:tokens], value_part[:tokens]], axis=1).astype(jnp.bfloat16)
    later = lax.ppermute(sent, blk, backward).astype(jnp.float32)
    key_grad = key_part[tokens:] + later[:, : KVH * HD]
    value_grad = value_part[tokens:] + later[:, KVH * HD :]
    return (moe_input_grad, query_grad, key_grad, value_grad)


def solution(mesh):
    names = ("groups", "far", "near", "low", "core")
    shape = (mesh.shape["groups"], 2, 2, mesh.shape["blk"] // 8, 2)
    fine = jax.sharding.Mesh(mesh.devices.reshape(shape), names)
    blk = names[1:]
    by_tokens = P(names, None)
    return jax.shard_map(
        local,
        mesh=fine,
        in_specs=(
            by_tokens,
            by_tokens,
            by_tokens,
            by_tokens,
            P(None, blk),
            P(None, blk),
            P(blk, None),
            P(blk, None),
            by_tokens,
            by_tokens,
            by_tokens,
            P(names),
        ),
        out_specs=(by_tokens,) * 4,
        check_vma=False,
    )
```

```python
import functools

import jax
import jax.numpy as jnp
from jax import lax
from jax.experimental import pallas as pl
from jax.experimental.pallas import tpu as pltpu
from jax.sharding import PartitionSpec as P

KVH = 2
GROUP = 16
HD = 128
FLOOR = -1e30
MIB = 1 << 20

NT = (((1,), (1,)), ((), ()))
TN = (((0,), (0,)), ((), ()))


def dot(a, b, dims=(((1,), (0,)), ((), ()))):
    return lax.dot_general(a, b, dims, preferred_element_type=jnp.float32)


def params(mib):
    return pltpu.CompilerParams(vmem_limit_bytes=mib * MIB)


def pick_kernel(owners, depth, routes_ref, weight_ref, input_ref, grad_ref, rows_ref, back_ref, place, scale):
    tokens = input_ref.shape[0]
    slots = owners * depth
    step = pl.program_id(0)
    half = pl.num_programs(0) // 2

    @pl.when(step == 0)
    def _():
        first = routes_ref[0:1, :]
        second = routes_ref[1:2, :]
        expert = lax.broadcasted_iota(jnp.int32, (owners, tokens), 0)
        is_first = first == expert
        is_second = second == expert
        member = jnp.where(is_first | is_second, 1.0, 0.0)
        before = lax.broadcasted_iota(jnp.int32, (tokens, tokens), 0) < lax.broadcasted_iota(
            jnp.int32, (tokens, tokens), 1
        )
        rank = dot(member.astype(jnp.bfloat16), jnp.where(before, 1.0, 0.0).astype(jnp.bfloat16))
        spot = (expert * depth).astype(jnp.float32) + rank
        slot_first = jnp.sum(jnp.where(is_first, spot, 0.0), axis=0, keepdims=True).astype(jnp.int32)
        slot_second = jnp.sum(jnp.where(is_second, spot, 0.0), axis=0, keepdims=True).astype(jnp.int32)
        slot = lax.broadcasted_iota(jnp.int32, (slots, tokens), 0)
        at_first = slot == slot_first
        at_second = slot == slot_second
        chosen = jnp.where(at_first | at_second, 1.0, 0.0).astype(jnp.bfloat16)
        place[...] = chosen
        back_ref[...] = chosen.T
        scale[...] = jnp.sum(
            jnp.where(at_first, weight_ref[0:1, :], 0.0) + jnp.where(at_second, weight_ref[1:2, :], 0.0),
            axis=1,
            keepdims=True,
        )

    @pl.when(step < half)
    def _():
        rows_ref[...] = dot(place[...], input_ref[...]).astype(jnp.bfloat16)

    @pl.when(step >= half)
    def _():
        rows_ref[...] = (scale[...] * dot(place[...], grad_ref[...])).astype(jnp.bfloat16)


def pick(routes, route_weight, moe_input, moe_grad, owners, depth):
    tokens, width = moe_input.shape
    slots = owners * depth
    tile = 1024
    half = width // tile
    return pl.pallas_call(
        functools.partial(pick_kernel, owners, depth),
        grid=(2 * half,),
        in_specs=[
            pl.BlockSpec((2, tokens), lambda i: (0, 0)),
            pl.BlockSpec((2, tokens), lambda i: (0, 0)),
            pl.BlockSpec((tokens, tile), lambda i: (0, jnp.minimum(i, half - 1))),
            pl.BlockSpec((tokens, tile), lambda i: (0, jnp.maximum(i - half, 0))),
        ],
        out_specs=[
            pl.BlockSpec((slots, tile), lambda i: (0, i)),
            pl.BlockSpec((tokens, slots), lambda i: (0, 0)),
        ],
        out_shape=(
            jax.ShapeDtypeStruct((slots, 2 * width), jnp.bfloat16),
            jax.ShapeDtypeStruct((tokens, slots), jnp.bfloat16),
        ),
        scratch_shapes=[pltpu.VMEM((slots, tokens), jnp.bfloat16), pltpu.VMEM((slots, 1), jnp.float32)],
        compiler_params=params(60),
        cost_estimate=pl.CostEstimate(
            flops=4 * slots * tokens * width, bytes_accessed=8 * MIB, transcendentals=0
        ),
        name="pick_rows",
    )(routes.T, route_weight.T, moe_input, moe_grad)


def weights_kernel(*refs):
    own, other, (cols_ref, down_ref, rows_ref) = refs[:3], refs[3:6], refs[6:]
    tile = own[0].shape[1]
    for place, (gate_ref, up_ref, low_ref) in enumerate((own, other)):
        for kind, ref in enumerate((gate_ref, up_ref)):
            spot = slice((2 * kind + place) * tile, (2 * kind + place + 1) * tile)
            cols_ref[0, :, spot] = ref[...]
            rows_ref[0, spot, :] = ref[...].T
        down_ref[0, :, place * tile : (place + 1) * tile] = low_ref[...].T


def prepare_weights(own, other):
    width, half = own[0].shape
    tile = 128
    steps = half // tile
    cols = pl.BlockSpec((width, tile), lambda i: (0, i))
    down = pl.BlockSpec((tile, width), lambda i: (i, 0))
    return pl.pallas_call(
        weights_kernel,
        grid=(steps,),
        in_specs=[cols, cols, down] * 2,
        out_specs=[
            pl.BlockSpec((1, width, 4 * tile), lambda i: (i, 0, 0)),
            pl.BlockSpec((1, width, 2 * tile), lambda i: (i, 0, 0)),
            pl.BlockSpec((1, 4 * tile, width), lambda i: (i, 0, 0)),
        ],
        out_shape=(
            jax.ShapeDtypeStruct((steps, width, 4 * tile), jnp.bfloat16),
            jax.ShapeDtypeStruct((steps, width, 2 * tile), jnp.bfloat16),
            jax.ShapeDtypeStruct((steps, 4 * tile, width), jnp.bfloat16),
        ),
        compiler_params=params(48),
        cost_estimate=pl.CostEstimate(
            flops=0, bytes_accessed=32 * width * half, transcendentals=0
        ),
        name="prepare_weights",
    )(*own, *other)


def expert_kernel(steps, rows_ref, cols_ref, down_ref, back_ref, out_ref, hidden):
    step = pl.program_id(0)
    width = rows_ref.shape[1] // 2
    pair = down_ref.shape[2]

    @pl.when(step < steps)
    def _():
        both_pre = dot(rows_ref[:, :width], cols_ref[0])
        gate_pre = both_pre[:, :pair]
        up_pre = both_pre[:, pair:]
        down_grad = dot(rows_ref[:, width:], down_ref[0])
        sig = jax.nn.sigmoid(gate_pre)
        hidden[step, :, :pair] = (
            down_grad * up_pre * sig * (1.0 + gate_pre * (1.0 - sig))
        ).astype(jnp.bfloat16)
        hidden[step, :, pair:] = (down_grad * gate_pre * sig).astype(jnp.bfloat16)

    @pl.when(step >= steps)
    def _():
        total = dot(hidden[0], back_ref[0])
        for i in range(1, steps):
            total += dot(hidden[i], back_ref[i])
        out_ref[...] = total.astype(jnp.bfloat16)


def experts(rows, cols, down, back):
    count, twice = rows.shape
    steps, width, quad = cols.shape
    tile = 512
    last = steps - 1
    turn = lambda i: jnp.maximum(i - steps, 0)
    return pl.pallas_call(
        functools.partial(expert_kernel, steps),
        grid=(steps + width // tile,),
        in_specs=[
            pl.BlockSpec((count, twice), lambda i: (0, 0)),
            pl.BlockSpec((1, width, quad), lambda i: (jnp.minimum(i, last), 0, 0)),
            pl.BlockSpec((1, width, quad // 2), lambda i: (jnp.minimum(i, last), 0, 0)),
            pl.BlockSpec((steps, quad, tile), lambda i: (0, 0, turn(i))),
        ],
        out_specs=pl.BlockSpec((count, tile), lambda i: (0, turn(i))),
        out_shape=jax.ShapeDtypeStruct((count, width), jnp.bfloat16),
        scratch_shapes=[pltpu.VMEM((steps, count, quad), jnp.bfloat16)],
        compiler_params=params(48),
        cost_estimate=pl.CostEstimate(
            flops=5 * count * width * steps * quad, bytes_accessed=20 * MIB,
            transcendentals=count * steps * quad,
        ),
        name="expert_terms",
    )(rows, cols, down, back)


def shares_kernel(
    q_ref, key_ref, value_ref, prev_key_ref, prev_value_ref, prev_seg_ref, seg_row_ref, seg_col_ref,
    low_ref, turned_ref, query_ref, key_out, value_out,
):
    tokens = q_ref.shape[0]
    seg_col = seg_col_ref[...]
    row = lax.broadcasted_iota(jnp.int32, (tokens, tokens), 0)
    col = lax.broadcasted_iota(jnp.int32, (tokens, tokens), 1)
    own_seen = jnp.where((col <= row) & (seg_row_ref[...] == seg_col), 1.0, 0.0)
    prev_seg = prev_seg_ref[tokens : tokens + 16, :].astype(jnp.float32)[0:1, :]
    prev_seen = jnp.where(prev_seg == seg_col, 1.0, 0.0)
    seen = jnp.concatenate([prev_seen, own_seen], axis=1) > 0.5
    keys = jnp.concatenate([prev_key_ref[:tokens, :], key_ref[...]], axis=0)
    values = jnp.concatenate([prev_value_ref[:tokens, :], value_ref[...]], axis=0)
    key_out[0] = keys
    value_out[0] = values.T
    for head in range(GROUP):
        rows = slice(head * tokens, (head + 1) * tokens)
        query = q_ref[:, head * HD : (head + 1) * HD]
        scores = dot(query, keys, NT) * (HD**-0.5)
        masked = jnp.where(seen, scores, FLOOR)
        raised = jnp.where(seen, jnp.exp(masked - jnp.max(masked, axis=1, keepdims=True)), 0.0)
        shares = raised / jnp.sum(raised, axis=1, keepdims=True)
        low = shares.astype(jnp.bfloat16)
        low_ref[0, rows, :] = low
        turned_ref[0, :, rows] = low.T
        query_ref[0, rows, :] = query


def attention_shares(queries, key_heads, value_heads, prev, segs):
    tokens, width = queries.shape
    span = 2 * tokens
    stack = GROUP * tokens
    high = prev.shape[0]
    own = pl.BlockSpec((tokens, HD), lambda g: (0, g))
    group = lambda shape: pl.BlockSpec((1,) + shape, lambda g: (g, 0, 0))
    made = lambda shape: jax.ShapeDtypeStruct((KVH,) + shape, jnp.bfloat16)
    shapes = ((stack, span), (span, stack), (stack, HD), (span, HD), (HD, span))
    return pl.pallas_call(
        shares_kernel,
        grid=(KVH,),
        in_specs=[
            pl.BlockSpec((tokens, GROUP * HD), lambda g: (0, g)),
            own,
            own,
            pl.BlockSpec((high, HD), lambda g: (0, g)),
            pl.BlockSpec((high, HD), lambda g: (0, KVH + g)),
            pl.BlockSpec((high, HD), lambda g: (0, 0)),
            pl.BlockSpec((1, tokens), lambda g: (0, 0)),
            pl.BlockSpec((tokens, 1), lambda g: (0, 0)),
        ],
        out_specs=[group(shape) for shape in shapes],
        out_shape=[made(shape) for shape in shapes],
        compiler_params=params(32),
        cost_estimate=pl.CostEstimate(
            flops=2 * tokens * width * span, bytes_accessed=8 * MIB,
            transcendentals=tokens * span * KVH * GROUP,
        ),
        name="attention_shares",
    )(queries, key_heads, value_heads, prev, prev, prev, segs[None, :], segs[:, None])


def tail_kernel(plan, *refs):
    order, first, last, heads, tiles = plan
    refs = list(refs)
    take = lambda n: [refs.pop(0) for _ in range(n)]
    step = pl.program_id(0)
    if first:
        back_ref, place_ref, grad_ref = take(3)
    else:
        stream_in, sums_in, _ = take(3)
    w_ref, low_ref, turned_ref, q_ref, key_ref, value_ref = take(6)
    if first:
        moe_ref, stream = take(2)
    else:
        stream = stream_in
    (query_out,) = take(1)
    if last:
        key_out, value_out, sent_out = take(3)
    else:
        (sums_out,) = take(1)
    held, sums = take(2)
    tokens = query_out.shape[0]

    @pl.when(step == 0)
    def _():
        if first:
            moe = dot(place_ref[...], back_ref[...]).astype(jnp.bfloat16)
            moe_ref[...] = moe
            added = (grad_ref[...].astype(jnp.float32) + moe.astype(jnp.float32)).astype(jnp.bfloat16)
            size = added.shape[1] // len(order)
            for to, source in enumerate(order):
                stream[:, to * size : (to + 1) * size] = added[:, source * size : (source + 1) * size]
        held[...] = jnp.zeros_like(held)

    @pl.when((step == 0) | ((step > 1) & ((step - 1) % tiles == 0)))
    def _():
        if first:
            sums[...] = jnp.zeros_like(sums)
        else:
            sums[...] = sums_in[...]

    grads = held[...]
    head_grad = dot(stream[...], w_ref[0]).astype(jnp.bfloat16)
    low = low_ref[0].astype(jnp.float32)
    prob_grad = dot(grads, value_ref[0])
    row_dot = jnp.sum(low * prob_grad, axis=1, keepdims=True)
    score_grad = (low * (prob_grad - row_dot) * (HD**-0.5)).astype(jnp.bfloat16)
    query_grad = dot(score_grad, key_ref[0]).astype(jnp.bfloat16)
    sums[0] += dot(score_grad, q_ref[0], TN)
    sums[1] += dot(turned_ref[0], grads)
    for head in range(heads):
        cols = slice(head * HD, (head + 1) * HD)
        rows = slice(head * tokens, (head + 1) * tokens)
        query_out[:, cols] = query_grad[rows, :]
        held[rows, :] = head_grad[:, cols]

    @pl.when((step > 0) & (step % tiles == 0))
    def _():
        if last:
            key_out[...] = sums[0, tokens:, :]
            value_out[...] = sums[1, tokens:, :]
            sent_out[...] = sums[:, :tokens, :].astype(jnp.bfloat16)
        else:
            sums_out[...] = sums[...]


def tail(chunk, chunks, order, carried, w_part, low, turned, query, keys, values):
    first, last = chunk == 0, chunk == chunks - 1
    width, cols = w_part.shape[1:]
    span = keys.shape[1]
    tokens = span // 2
    heads = 4
    tile = heads * HD
    tiles = cols // tile
    steps = KVH * tiles
    per_group = tiles * chunks
    now = lambda i: jnp.minimum(i, steps - 1)
    was = lambda i: jnp.maximum(i - 1, 0)
    spot = lambda i: chunk * tiles + was(i) % tiles
    whole = lambda shape: pl.BlockSpec(shape, lambda i: (0,) * len(shape))
    group = lambda shape: pl.BlockSpec((1,) + shape, lambda i: (was(i) // tiles, 0, 0))
    rows = lambda shape: pl.BlockSpec((1,) + shape, lambda i: (was(i) // tiles, spot(i), 0))
    sums = pl.BlockSpec((2, span, HD), lambda i: (0, 0, was(i) // tiles))
    if first:
        in_specs = [whole(array.shape) for array in carried]
        out_specs = [whole((tokens, width)), whole((tokens, width))]
        out_shape = [jax.ShapeDtypeStruct((tokens, width), jnp.bfloat16)] * 2
    else:
        in_specs = [whole((tokens, width)), sums, pl.BlockSpec(memory_space=pl.ANY)]
        out_specs, out_shape = [], []
    in_specs += [
        pl.BlockSpec((1, width, tile), lambda i: (now(i) // tiles, 0, now(i) % tiles)),
        rows((heads * tokens, span)),
        pl.BlockSpec((1, span, heads * tokens), lambda i: (was(i) // tiles, 0, spot(i))),
        rows((heads * tokens, HD)),
        group((span, HD)),
        group((HD, span)),
    ]
    out_specs.append(
        pl.BlockSpec((tokens, tile), lambda i: (0, (was(i) // tiles) * per_group + spot(i)))
    )
    out_shape.append(jax.ShapeDtypeStruct((tokens, KVH * chunks * cols), jnp.bfloat16))
    if last:
        half = pl.BlockSpec((tokens, HD), lambda i: (0, was(i) // tiles))
        out_specs += [half, half, pl.BlockSpec((2, tokens, HD), lambda i: (0, 0, was(i) // tiles))]
        out_shape += [jax.ShapeDtypeStruct((tokens, KVH * HD), jnp.float32)] * 2
        out_shape.append(jax.ShapeDtypeStruct((2, tokens, KVH * HD), jnp.bfloat16))
    else:
        out_specs.append(sums)
        out_shape.append(jax.ShapeDtypeStruct((2, span, KVH * HD), jnp.float32))
    return pl.pallas_call(
        functools.partial(tail_kernel, (order, first, last, heads, tiles)),
        grid=(steps + 1,),
        in_specs=in_specs,
        out_specs=out_specs,
        out_shape=out_shape,
        scratch_shapes=[
            pltpu.VMEM((heads * tokens, HD), jnp.bfloat16),
            pltpu.VMEM((2, span, HD), jnp.float32),
        ],
        input_output_aliases={} if first else {2: 0},
        compiler_params=params(60),
        cost_estimate=pl.CostEstimate(
            flops=2 * tokens * width * KVH * cols, bytes_accessed=22 * MIB // chunks, transcendentals=0
        ),
        name="tail_attention",
    )(*carried, w_part, low, turned, query, keys, values)


def far_first(share):
    for axis in ("far", "near"):
        moved = lax.ppermute(share, axis, [(0, 1), (1, 0)])
        mine = lax.axis_index(axis) == 0
        share = jnp.where(mine, jnp.stack([share, moved]), jnp.stack([moved, share]))
    return share


def local(
    moe_input,
    moe_grad,
    routes,
    route_weight,
    w_gate,
    w_up,
    w_down,
    w_out,
    queries,
    key_heads,
    value_heads,
    segments,
):
    chips = ("far", "near", "low")
    blk = chips + ("core",)
    low = lax.axis_size("low")
    owners = 4 * low
    count = 2 * owners
    parts = lax.axis_size("groups")
    tokens, width = moe_input.shape
    depth = 2 * max(1, 3 * tokens * routes.shape[1] // (2 * count))
    onward = [(i, i + 1) for i in range(count - 1)]
    backward = [(i + 1, i) for i in range(count - 1)]

    kv = jnp.concatenate([key_heads, value_heads], axis=1)
    segs = (segments + 1).astype(jnp.float32)
    seg_rows = jnp.zeros((16, kv.shape[1]), jnp.bfloat16).at[0, :tokens].set(segs.astype(jnp.bfloat16))
    prev = lax.ppermute(jnp.concatenate([kv, seg_rows], axis=0), blk, onward)
    rows, place = pick(routes, route_weight, moe_input, moe_grad, owners, depth)
    rows, prev, w_out = lax.optimization_barrier((rows, prev, w_out))
    rows_in = lax.all_to_all(rows.reshape(owners, depth, 2 * width), chips, 0, 0, tiled=True)

    chunks = 2
    block = w_out.shape[0]
    share_cols = w_out.shape[1] // parts
    cols = share_cols // chunks
    order = tuple(
        (2 * far + near) * 2 * low + rest
        for rest in range(2 * low)
        for near in range(2)
        for far in range(2)
    )
    w_parts = []
    for chunk in range(chunks):
        start = lax.axis_index("groups") * share_cols + chunk * cols
        w_plane = far_first(lax.dynamic_slice_in_dim(w_out, start, cols, 1))
        w_part = lax.all_gather(w_plane, ("groups", "low", "core"), axis=0, tiled=False)
        w_part = w_part.reshape(parts, 2 * low, 2, 2, block, cols)
        if block % 128:
            w_part = w_part.transpose(0, 3, 2, 1, 4, 5)
        w_parts.append(w_part.reshape(parts, width, cols))
    if block % 128:
        order = (0,)

    own = (w_gate, w_up, w_down)
    other = tuple(lax.ppermute(w, "core", [(0, 1), (1, 0)]) for w in own)
    prepared = prepare_weights(own, other)
    attention = attention_shares(queries, key_heads, value_heads, prev, segs)

    prepared, attention, rows_in = lax.optimization_barrier((prepared, attention, rows_in))
    terms = experts(rows_in.reshape(owners * depth, 2 * width), *prepared)
    back = lax.all_to_all(terms.reshape(owners, depth, width), chips, 0, 0, tiled=True)

    carried = (back.reshape(owners * depth, width), place, moe_grad)
    for chunk in range(chunks):
        outs = tail(chunk, chunks, order, carried, w_parts[chunk], *attention)
        if chunk == 0:
            moe_input_grad, stream = outs[:2]
            outs = outs[2:]
        carried = (stream, outs[1], outs[0])
    query_grad, key_part, value_part, sent = outs
    later = lax.ppermute(sent, blk, backward).astype(jnp.float32)
    return (moe_input_grad, query_grad, key_part + later[0], value_part + later[1])


def solution(mesh):
    names = ("groups", "far", "near", "low", "core")
    shape = (mesh.shape["groups"], 2, 2, mesh.shape["blk"] // 8, 2)
    fine = jax.sharding.Mesh(mesh.devices.reshape(shape), names)
    blk = names[1:]
    by_tokens = P(names, None)
    return jax.shard_map(
        local,
        mesh=fine,
        in_specs=(
            by_tokens,
            by_tokens,
            by_tokens,
            by_tokens,
            P(None, blk),
            P(None, blk),
            P(blk, None),
            P(blk, None),
            by_tokens,
            by_tokens,
            by_tokens,
            P(names),
        ),
        out_specs=(by_tokens,) * 4,
        check_vma=False,
    )
```

```python
import functools

import jax
import jax.numpy as jnp
from jax import lax
from jax.experimental import pallas as pl
from jax.experimental.pallas import tpu as pltpu
from jax.sharding import PartitionSpec as P

KVH = 2
GROUP = 16
HD = 128
FLOOR = -1e30
MIB = 1 << 20

NT = (((1,), (1,)), ((), ()))
TN = (((0,), (0,)), ((), ()))


def dot(a, b, dims=(((1,), (0,)), ((), ()))):
    return lax.dot_general(a, b, dims, preferred_element_type=jnp.float32)


def params(mib):
    return pltpu.CompilerParams(vmem_limit_bytes=mib * MIB)


def pick_kernel(owners, depth, routes_ref, weight_ref, input_ref, grad_ref, rows_ref, back_ref):
    tokens = input_ref.shape[0]
    slots = owners * depth
    first = routes_ref[0:1, :]
    second = routes_ref[1:2, :]
    expert = lax.broadcasted_iota(jnp.int32, (owners, tokens), 0)
    is_first = first == expert
    is_second = second == expert
    member = jnp.where(is_first | is_second, 1.0, 0.0)
    before = lax.broadcasted_iota(jnp.int32, (tokens, tokens), 0) < lax.broadcasted_iota(
        jnp.int32, (tokens, tokens), 1
    )
    rank = dot(member.astype(jnp.bfloat16), jnp.where(before, 1.0, 0.0).astype(jnp.bfloat16))
    spot = (expert * depth).astype(jnp.float32) + rank
    slot_first = jnp.sum(jnp.where(is_first, spot, 0.0), axis=0, keepdims=True).astype(jnp.int32)
    slot_second = jnp.sum(jnp.where(is_second, spot, 0.0), axis=0, keepdims=True).astype(jnp.int32)
    slot = lax.broadcasted_iota(jnp.int32, (slots, tokens), 0)
    at_first = slot == slot_first
    at_second = slot == slot_second
    place = jnp.where(at_first | at_second, 1.0, 0.0).astype(jnp.bfloat16)
    back_ref[...] = place.T
    scale = jnp.sum(
        jnp.where(at_first, weight_ref[0:1, :], 0.0) + jnp.where(at_second, weight_ref[1:2, :], 0.0),
        axis=1,
        keepdims=True,
    )
    width = input_ref.shape[1]
    rows_ref[:, :width] = dot(place, input_ref[...]).astype(jnp.bfloat16)
    rows_ref[:, width:] = (scale * dot(place, grad_ref[...])).astype(jnp.bfloat16)


def pick(routes, route_weight, moe_input, moe_grad, owners, depth):
    tokens, width = moe_input.shape
    slots = owners * depth
    return pl.pallas_call(
        functools.partial(pick_kernel, owners, depth),
        out_shape=(
            jax.ShapeDtypeStruct((slots, 2 * width), jnp.bfloat16),
            jax.ShapeDtypeStruct((tokens, slots), jnp.bfloat16),
        ),
        compiler_params=params(32),
        cost_estimate=pl.CostEstimate(
            flops=4 * slots * tokens * width, bytes_accessed=8 * MIB, transcendentals=0
        ),
        name="pick_rows",
    )(routes.T, route_weight.T, moe_input, moe_grad)


def weights_kernel(*refs):
    own, other, (cols_ref, down_ref, rows_ref) = refs[:3], refs[3:6], refs[6:]
    tile = own[0].shape[1]
    for place, (gate_ref, up_ref, low_ref) in enumerate((own, other)):
        for kind, ref in enumerate((gate_ref, up_ref)):
            spot = slice((2 * kind + place) * tile, (2 * kind + place + 1) * tile)
            cols_ref[0, :, spot] = ref[...]
            rows_ref[0, spot, :] = ref[...].T
        down_ref[0, :, place * tile : (place + 1) * tile] = low_ref[...].T


def prepare_weights(own, other):
    width, half = own[0].shape
    tile = 128
    steps = half // tile
    cols = pl.BlockSpec((width, tile), lambda i: (0, i))
    down = pl.BlockSpec((tile, width), lambda i: (i, 0))
    return pl.pallas_call(
        weights_kernel,
        grid=(steps,),
        in_specs=[cols, cols, down] * 2,
        out_specs=[
            pl.BlockSpec((1, width, 4 * tile), lambda i: (i, 0, 0)),
            pl.BlockSpec((1, width, 2 * tile), lambda i: (i, 0, 0)),
            pl.BlockSpec((1, 4 * tile, width), lambda i: (i, 0, 0)),
        ],
        out_shape=(
            jax.ShapeDtypeStruct((steps, width, 4 * tile), jnp.bfloat16),
            jax.ShapeDtypeStruct((steps, width, 2 * tile), jnp.bfloat16),
            jax.ShapeDtypeStruct((steps, 4 * tile, width), jnp.bfloat16),
        ),
        compiler_params=params(48),
        cost_estimate=pl.CostEstimate(
            flops=0, bytes_accessed=32 * width * half, transcendentals=0
        ),
        name="prepare_weights",
    )(*own, *other)


def expert_kernel(steps, rows_ref, cols_ref, down_ref, back_ref, out_ref, hidden):
    step = pl.program_id(0)
    width = rows_ref.shape[1] // 2
    pair = down_ref.shape[2]

    @pl.when(step < steps)
    def _():
        both_pre = dot(rows_ref[:, :width], cols_ref[0])
        gate_pre = both_pre[:, :pair]
        up_pre = both_pre[:, pair:]
        down_grad = dot(rows_ref[:, width:], down_ref[0])
        sig = jax.nn.sigmoid(gate_pre)
        hidden[step, :, :pair] = (
            down_grad * up_pre * sig * (1.0 + gate_pre * (1.0 - sig))
        ).astype(jnp.bfloat16)
        hidden[step, :, pair:] = (down_grad * gate_pre * sig).astype(jnp.bfloat16)

    @pl.when(step >= steps)
    def _():
        total = dot(hidden[0], back_ref[0])
        for i in range(1, steps):
            total += dot(hidden[i], back_ref[i])
        out_ref[...] = total.astype(jnp.bfloat16)


def experts(rows, cols, down, back):
    count, twice = rows.shape
    steps, width, quad = cols.shape
    tile = 512
    last = steps - 1
    turn = lambda i: jnp.maximum(i - steps, 0)
    return pl.pallas_call(
        functools.partial(expert_kernel, steps),
        grid=(steps + width // tile,),
        in_specs=[
            pl.BlockSpec((count, twice), lambda i: (0, 0)),
            pl.BlockSpec((1, width, quad), lambda i: (jnp.minimum(i, last), 0, 0)),
            pl.BlockSpec((1, width, quad // 2), lambda i: (jnp.minimum(i, last), 0, 0)),
            pl.BlockSpec((steps, quad, tile), lambda i: (0, 0, turn(i))),
        ],
        out_specs=pl.BlockSpec((count, tile), lambda i: (0, turn(i))),
        out_shape=jax.ShapeDtypeStruct((count, width), jnp.bfloat16),
        scratch_shapes=[pltpu.VMEM((steps, count, quad), jnp.bfloat16)],
        compiler_params=params(48),
        cost_estimate=pl.CostEstimate(
            flops=100 * count * width * steps * quad, bytes_accessed=20 * MIB,
            transcendentals=count * steps * quad,
        ),
        name="expert_terms",
    )(rows, cols, down, back)


def shares_kernel(
    q_ref, key_ref, value_ref, prev_key_ref, prev_value_ref, prev_seg_ref, seg_row_ref, seg_col_ref,
    low_ref, turned_ref, query_ref, key_out, value_out,
):
    tokens = q_ref.shape[0]
    seg_col = seg_col_ref[...]
    row = lax.broadcasted_iota(jnp.int32, (tokens, tokens), 0)
    col = lax.broadcasted_iota(jnp.int32, (tokens, tokens), 1)
    own_seen = jnp.where((col <= row) & (seg_row_ref[...] == seg_col), 1.0, 0.0)
    prev_seg = prev_seg_ref[tokens : tokens + 16, :].astype(jnp.float32)[0:1, :]
    prev_seen = jnp.where(prev_seg == seg_col, 1.0, 0.0)
    seen = jnp.concatenate([prev_seen, own_seen], axis=1) > 0.5
    keys = jnp.concatenate([prev_key_ref[:tokens, :], key_ref[...]], axis=0)
    values = jnp.concatenate([prev_value_ref[:tokens, :], value_ref[...]], axis=0)
    key_out[0] = keys
    value_out[0] = values.T
    for head in range(GROUP):
        rows = slice(head * tokens, (head + 1) * tokens)
        query = q_ref[:, head * HD : (head + 1) * HD]
        scores = dot(query, keys, NT) * (HD**-0.5)
        masked = jnp.where(seen, scores, FLOOR)
        raised = jnp.where(seen, jnp.exp(masked - jnp.max(masked, axis=1, keepdims=True)), 0.0)
        shares = raised / jnp.sum(raised, axis=1, keepdims=True)
        low = shares.astype(jnp.bfloat16)
        low_ref[0, rows, :] = low
        turned_ref[0, :, rows] = low.T
        query_ref[0, rows, :] = query


def attention_shares(queries, key_heads, value_heads, prev, segs):
    tokens, width = queries.shape
    span = 2 * tokens
    stack = GROUP * tokens
    high = prev.shape[0]
    own = pl.BlockSpec((tokens, HD), lambda g: (0, g))
    group = lambda shape: pl.BlockSpec((1,) + shape, lambda g: (g, 0, 0))
    made = lambda shape: jax.ShapeDtypeStruct((KVH,) + shape, jnp.bfloat16)
    shapes = ((stack, span), (span, stack), (stack, HD), (span, HD), (HD, span))
    return pl.pallas_call(
        shares_kernel,
        grid=(KVH,),
        in_specs=[
            pl.BlockSpec((tokens, GROUP * HD), lambda g: (0, g)),
            own,
            own,
            pl.BlockSpec((high, HD), lambda g: (0, g)),
            pl.BlockSpec((high, HD), lambda g: (0, KVH + g)),
            pl.BlockSpec((high, HD), lambda g: (0, 0)),
            pl.BlockSpec((1, tokens), lambda g: (0, 0)),
            pl.BlockSpec((tokens, 1), lambda g: (0, 0)),
        ],
        out_specs=[group(shape) for shape in shapes],
        out_shape=[made(shape) for shape in shapes],
        compiler_params=params(32),
        cost_estimate=pl.CostEstimate(
            flops=2 * tokens * width * span, bytes_accessed=8 * MIB,
            transcendentals=tokens * span * KVH * GROUP,
        ),
        name="attention_shares",
    )(queries, key_heads, value_heads, prev, prev, prev, segs[None, :], segs[:, None])


def tail_kernel(
    plan, back_ref, place_ref, grad_ref, own_ref, other_ref, low_ref, turned_ref, q_ref, key_ref, value_ref,
    moe_ref, query_out, key_out, value_out, sent_out, stream, held, sums,
):
    orders, heads, tiles = plan
    step = pl.program_id(0)
    tokens = query_out.shape[0]
    half = own_ref.shape[1]

    @pl.when(step == 0)
    def _():
        moe = dot(place_ref[...], back_ref[...]).astype(jnp.bfloat16)
        moe_ref[...] = moe
        added = (grad_ref[...].astype(jnp.float32) + moe.astype(jnp.float32)).astype(jnp.bfloat16)
        size = added.shape[1] // len(orders[0])
        for core, order in enumerate(orders):

            @pl.when(lax.axis_index("core") == core)
            def _():
                for to, source in enumerate(order):
                    stream[:, to * size : (to + 1) * size] = added[:, source * size : (source + 1) * size]

        held[...] = jnp.zeros_like(held)

    @pl.when((step == 0) | ((step > 1) & ((step - 1) % tiles == 0)))
    def _():
        sums[...] = jnp.zeros_like(sums)

    grads = held[...]
    head_grad = (dot(stream[:, :half], own_ref[0]) + dot(stream[:, half:], other_ref[0])).astype(jnp.bfloat16)
    low = low_ref[0].astype(jnp.float32)
    prob_grad = dot(grads, value_ref[0])
    row_dot = jnp.sum(low * prob_grad, axis=1, keepdims=True)
    score_grad = (low * (prob_grad - row_dot) * (HD**-0.5)).astype(jnp.bfloat16)
    query_grad = dot(score_grad, key_ref[0]).astype(jnp.bfloat16)
    sums[0] += dot(score_grad, q_ref[0], TN)
    sums[1] += dot(turned_ref[0], grads)
    for head in range(heads):
        cols = slice(head * HD, (head + 1) * HD)
        rows = slice(head * tokens, (head + 1) * tokens)
        query_out[:, cols] = query_grad[rows, :]
        held[rows, :] = head_grad[:, cols]

    @pl.when((step > 0) & (step % tiles == 0))
    def _():
        key_out[...] = sums[0, tokens:, :]
        value_out[...] = sums[1, tokens:, :]
        sent_out[...] = sums[:, :tokens, :].astype(jnp.bfloat16)


def tail(orders, back, place, moe_grad, w_own, w_other, low, turned, query, keys, values):
    tokens, width = moe_grad.shape
    half, cols = w_own.shape[1:]
    span = keys.shape[1]
    heads = 4
    tile = heads * HD
    tiles = cols // tile
    steps = KVH * tiles
    now = lambda i: jnp.minimum(i, steps - 1)
    was = lambda i: jnp.maximum(i - 1, 0)
    whole = lambda shape: pl.BlockSpec(shape, lambda i: (0,) * len(shape))
    group = lambda shape: pl.BlockSpec((1,) + shape, lambda i: (was(i) // tiles, 0, 0))
    rows = lambda shape: pl.BlockSpec((1,) + shape, lambda i: (was(i) // tiles, was(i) % tiles, 0))
    w_spec = pl.BlockSpec((1, half, tile), lambda i: (now(i) // tiles, 0, now(i) % tiles))
    kv = pl.BlockSpec((tokens, HD), lambda i: (0, was(i) // tiles))
    return pl.pallas_call(
        functools.partial(tail_kernel, (orders, heads, tiles)),
        grid=(steps + 1,),
        in_specs=[
            whole(back.shape),
            whole(place.shape),
            whole(moe_grad.shape),
            w_spec,
            w_spec,
            rows((heads * tokens, span)),
            pl.BlockSpec((1, span, heads * tokens), lambda i: (was(i) // tiles, 0, was(i) % tiles)),
            rows((heads * tokens, HD)),
            group((span, HD)),
            group((HD, span)),
        ],
        out_specs=[
            whole((tokens, width)),
            pl.BlockSpec((tokens, tile), lambda i: (0, was(i))),
            kv,
            kv,
            pl.BlockSpec((2, tokens, HD), lambda i: (0, 0, was(i) // tiles)),
        ],
        out_shape=(
            jax.ShapeDtypeStruct((tokens, width), jnp.bfloat16),
            jax.ShapeDtypeStruct((tokens, KVH * cols), jnp.bfloat16),
            jax.ShapeDtypeStruct((tokens, KVH * HD), jnp.float32),
            jax.ShapeDtypeStruct((tokens, KVH * HD), jnp.float32),
            jax.ShapeDtypeStruct((2, tokens, KVH * HD), jnp.bfloat16),
        ),
        scratch_shapes=[
            pltpu.VMEM((tokens, width), jnp.bfloat16),
            pltpu.VMEM((heads * tokens, HD), jnp.bfloat16),
            pltpu.VMEM((2, span, HD), jnp.float32),
        ],
        compiler_params=params(56),
        cost_estimate=pl.CostEstimate(
            flops=2 * tokens * width * KVH * cols, bytes_accessed=22 * MIB, transcendentals=0
        ),
        name="tail_attention",
    )(back, place, moe_grad, w_own, w_other, low, turned, query, keys, values)


def local(
    moe_input,
    moe_grad,
    routes,
    route_weight,
    w_gate,
    w_up,
    w_down,
    w_out,
    queries,
    key_heads,
    value_heads,
    segments,
):
    chips = ("far", "near", "low")
    blk = chips + ("core",)
    low = lax.axis_size("low")
    owners = 4 * low
    count = 2 * owners
    parts = lax.axis_size("groups")
    tokens, width = moe_input.shape
    depth = 2 * max(1, 3 * tokens * routes.shape[1] // (2 * count))
    swap = [(0, 1), (1, 0)]
    onward = [(i, i + 1) for i in range(count - 1)]
    backward = [(i + 1, i) for i in range(count - 1)]

    rows, place = pick(routes, route_weight, moe_input, moe_grad, owners, depth)
    rows, w_out = lax.optimization_barrier((rows, w_out))
    rows_in = lax.all_to_all(rows.reshape(owners, depth, 2 * width), chips, 0, 0, tiled=True)

    block = w_out.shape[0]
    share_cols = w_out.shape[1] // parts
    w_share = lax.dynamic_slice_in_dim(w_out, lax.axis_index("groups") * share_cols, share_cols, 1)
    w_line = lax.all_gather(w_share, ("far", "near"), axis=0, tiled=True)
    w_own = lax.all_gather(w_line, ("groups", "low"), axis=0, tiled=False)
    w_own = w_own.reshape(parts, low, 4, block, share_cols)
    if block % 128:
        w_own = w_own.transpose(0, 2, 1, 3, 4)
    w_own = w_own.reshape(parts, width // 2, share_cols)
    w_other = lax.ppermute(w_own, "core", swap)
    orders = tuple(
        tuple(
            (z * low + rest) * 2 + (core ^ flip)
            for flip in range(2)
            for z, rest in (
                [(z, rest) for rest in range(low) for z in range(4)]
                if block % 128 == 0
                else [(z, rest) for z in range(4) for rest in range(low)]
            )
        )
        for core in range(2)
    )

    own = (w_gate, w_up, w_down)
    other = tuple(lax.ppermute(w, "core", swap) for w in own)
    prepared = prepare_weights(own, other)

    kv = jnp.concatenate([key_heads, value_heads], axis=1)
    segs = (segments + 1).astype(jnp.float32)
    seg_rows = jnp.zeros((16, kv.shape[1]), jnp.bfloat16).at[0, :tokens].set(segs.astype(jnp.bfloat16))
    prev = lax.ppermute(jnp.concatenate([kv, seg_rows], axis=0), blk, onward)

    prepared, prev, rows_in = lax.optimization_barrier((prepared, prev, rows_in))
    terms = experts(rows_in.reshape(owners * depth, 2 * width), *prepared)
    prev, terms = lax.optimization_barrier((prev, terms))
    back = lax.all_to_all(terms.reshape(owners, depth, width), chips, 0, 0, tiled=True)
    attention = attention_shares(queries, key_heads, value_heads, prev, segs)

    moe_input_grad, query_grad, key_part, value_part, sent = tail(
        orders, back.reshape(owners * depth, width), place, moe_grad, w_own, w_other, *attention
    )
    later = lax.ppermute(sent, blk, backward).astype(jnp.float32)
    return (moe_input_grad, query_grad, key_part + later[0], value_part + later[1])


def solution(mesh):
    names = ("groups", "far", "near", "low", "core")
    shape = (mesh.shape["groups"], 2, 2, mesh.shape["blk"] // 8, 2)
    fine = jax.sharding.Mesh(mesh.devices.reshape(shape), names)
    blk = names[1:]
    by_tokens = P(names, None)
    return jax.shard_map(
        local,
        mesh=fine,
        in_specs=(
            by_tokens,
            by_tokens,
            by_tokens,
            by_tokens,
            P(None, blk),
            P(None, blk),
            P(blk, None),
            P(blk, None),
            by_tokens,
            by_tokens,
            by_tokens,
            P(names),
        ),
        out_specs=(by_tokens,) * 4,
        check_vma=False,
    )
```

```python
import functools

import jax
import jax.numpy as jnp
from jax import lax
from jax.experimental import pallas as pl
from jax.experimental.pallas import tpu as pltpu
from jax.sharding import PartitionSpec as P

KVH = 2
GROUP = 16
HD = 128
FLOOR = -1e30
MIB = 1 << 20

NT = (((1,), (1,)), ((), ()))
TN = (((0,), (0,)), ((), ()))


def dot(a, b, dims=(((1,), (0,)), ((), ()))):
    return lax.dot_general(a, b, dims, preferred_element_type=jnp.float32)


def params(mib):
    return pltpu.CompilerParams(vmem_limit_bytes=mib * MIB)


def pick_kernel(owners, depth, routes_ref, weight_ref, input_ref, grad_ref, rows_ref, back_ref):
    tokens = input_ref.shape[0]
    slots = owners * depth
    first = routes_ref[0:1, :]
    second = routes_ref[1:2, :]
    expert = lax.broadcasted_iota(jnp.int32, (owners, tokens), 0)
    is_first = first == expert
    is_second = second == expert
    member = jnp.where(is_first | is_second, 1.0, 0.0)
    before = lax.broadcasted_iota(jnp.int32, (tokens, tokens), 0) < lax.broadcasted_iota(
        jnp.int32, (tokens, tokens), 1
    )
    rank = dot(member.astype(jnp.bfloat16), jnp.where(before, 1.0, 0.0).astype(jnp.bfloat16))
    spot = (expert * depth).astype(jnp.float32) + rank
    slot_first = jnp.sum(jnp.where(is_first, spot, 0.0), axis=0, keepdims=True).astype(jnp.int32)
    slot_second = jnp.sum(jnp.where(is_second, spot, 0.0), axis=0, keepdims=True).astype(jnp.int32)
    slot = lax.broadcasted_iota(jnp.int32, (slots, tokens), 0)
    at_first = slot == slot_first
    at_second = slot == slot_second
    place = jnp.where(at_first | at_second, 1.0, 0.0).astype(jnp.bfloat16)
    back_ref[...] = place.T
    scale = jnp.sum(
        jnp.where(at_first, weight_ref[0:1, :], 0.0) + jnp.where(at_second, weight_ref[1:2, :], 0.0),
        axis=1,
        keepdims=True,
    )
    width = input_ref.shape[1]
    rows_ref[:, :width] = dot(place, input_ref[...]).astype(jnp.bfloat16)
    rows_ref[:, width:] = (scale * dot(place, grad_ref[...])).astype(jnp.bfloat16)


def pick(routes, route_weight, moe_input, moe_grad, owners, depth):
    tokens, width = moe_input.shape
    slots = owners * depth
    return pl.pallas_call(
        functools.partial(pick_kernel, owners, depth),
        out_shape=(
            jax.ShapeDtypeStruct((slots, 2 * width), jnp.bfloat16),
            jax.ShapeDtypeStruct((tokens, slots), jnp.bfloat16),
        ),
        compiler_params=params(32),
        cost_estimate=pl.CostEstimate(
            flops=4 * slots * tokens * width, bytes_accessed=8 * MIB, transcendentals=0
        ),
        name="pick_rows",
    )(routes.T, route_weight.T, moe_input, moe_grad)


def weights_kernel(*refs):
    own, other, (cols_ref, down_ref, rows_ref) = refs[:3], refs[3:6], refs[6:]
    tile = own[0].shape[1]
    for place, (gate_ref, up_ref, low_ref) in enumerate((own, other)):
        for kind, ref in enumerate((gate_ref, up_ref)):
            spot = slice((2 * kind + place) * tile, (2 * kind + place + 1) * tile)
            cols_ref[0, :, spot] = ref[...]
            rows_ref[0, spot, :] = ref[...].T
        down_ref[0, :, place * tile : (place + 1) * tile] = low_ref[...].T


def prepare_weights(own, other):
    width, half = own[0].shape
    tile = 128
    steps = half // tile
    cols = pl.BlockSpec((width, tile), lambda i: (0, i))
    down = pl.BlockSpec((tile, width), lambda i: (i, 0))
    return pl.pallas_call(
        weights_kernel,
        grid=(steps,),
        in_specs=[cols, cols, down] * 2,
        out_specs=[
            pl.BlockSpec((1, width, 4 * tile), lambda i: (i, 0, 0)),
            pl.BlockSpec((1, width, 2 * tile), lambda i: (i, 0, 0)),
            pl.BlockSpec((1, 4 * tile, width), lambda i: (i, 0, 0)),
        ],
        out_shape=(
            jax.ShapeDtypeStruct((steps, width, 4 * tile), jnp.bfloat16),
            jax.ShapeDtypeStruct((steps, width, 2 * tile), jnp.bfloat16),
            jax.ShapeDtypeStruct((steps, 4 * tile, width), jnp.bfloat16),
        ),
        compiler_params=params(48),
        cost_estimate=pl.CostEstimate(
            flops=0, bytes_accessed=32 * width * half, transcendentals=0
        ),
        name="prepare_weights",
    )(*own, *other)


def expert_kernel(steps, rows_ref, cols_ref, down_ref, back_ref, out_ref, hidden):
    step = pl.program_id(0)
    width = rows_ref.shape[1] // 2
    pair = down_ref.shape[2]

    @pl.when(step < steps)
    def _():
        both_pre = dot(rows_ref[:, :width], cols_ref[0])
        gate_pre = both_pre[:, :pair]
        up_pre = both_pre[:, pair:]
        down_grad = dot(rows_ref[:, width:], down_ref[0])
        sig = jax.nn.sigmoid(gate_pre)
        hidden[step, :, :pair] = (
            down_grad * up_pre * sig * (1.0 + gate_pre * (1.0 - sig))
        ).astype(jnp.bfloat16)
        hidden[step, :, pair:] = (down_grad * gate_pre * sig).astype(jnp.bfloat16)

    @pl.when(step >= steps)
    def _():
        total = dot(hidden[0], back_ref[0])
        for i in range(1, steps):
            total += dot(hidden[i], back_ref[i])
        out_ref[...] = total.astype(jnp.bfloat16)


def experts(rows, cols, down, back):
    count, twice = rows.shape
    steps, width, quad = cols.shape
    tile = 512
    last = steps - 1
    turn = lambda i: jnp.maximum(i - steps, 0)
    return pl.pallas_call(
        functools.partial(expert_kernel, steps),
        grid=(steps + width // tile,),
        in_specs=[
            pl.BlockSpec((count, twice), lambda i: (0, 0)),
            pl.BlockSpec((1, width, quad), lambda i: (jnp.minimum(i, last), 0, 0)),
            pl.BlockSpec((1, width, quad // 2), lambda i: (jnp.minimum(i, last), 0, 0)),
            pl.BlockSpec((steps, quad, tile), lambda i: (0, 0, turn(i))),
        ],
        out_specs=pl.BlockSpec((count, tile), lambda i: (0, turn(i))),
        out_shape=jax.ShapeDtypeStruct((count, width), jnp.bfloat16),
        scratch_shapes=[pltpu.VMEM((steps, count, quad), jnp.bfloat16)],
        compiler_params=params(48),
        cost_estimate=pl.CostEstimate(
            flops=5 * count * width * steps * quad, bytes_accessed=20 * MIB,
            transcendentals=count * steps * quad,
        ),
        name="expert_terms",
    )(rows, cols, down, back)


def shares_kernel(
    q_ref, key_ref, value_ref, prev_key_ref, prev_value_ref, prev_seg_ref, seg_row_ref, seg_col_ref,
    low_ref, turned_ref, query_ref, key_out, value_out,
):
    tokens = q_ref.shape[0]
    seg_col = seg_col_ref[...]
    row = lax.broadcasted_iota(jnp.int32, (tokens, tokens), 0)
    col = lax.broadcasted_iota(jnp.int32, (tokens, tokens), 1)
    own_seen = jnp.where((col <= row) & (seg_row_ref[...] == seg_col), 1.0, 0.0)
    prev_seg = prev_seg_ref[tokens : tokens + 16, :].astype(jnp.float32)[0:1, :]
    prev_seen = jnp.where(prev_seg == seg_col, 1.0, 0.0)
    seen = jnp.concatenate([prev_seen, own_seen], axis=1) > 0.5
    keys = jnp.concatenate([prev_key_ref[:tokens, :], key_ref[...]], axis=0)
    values = jnp.concatenate([prev_value_ref[:tokens, :], value_ref[...]], axis=0)
    key_out[0] = keys
    value_out[0] = values.T
    for head in range(GROUP):
        rows = slice(head * tokens, (head + 1) * tokens)
        query = q_ref[:, head * HD : (head + 1) * HD]
        scores = dot(query, keys, NT) * (HD**-0.5)
        masked = jnp.where(seen, scores, FLOOR)
        raised = jnp.where(seen, jnp.exp(masked - jnp.max(masked, axis=1, keepdims=True)), 0.0)
        shares = raised / jnp.sum(raised, axis=1, keepdims=True)
        low = shares.astype(jnp.bfloat16)
        low_ref[0, rows, :] = low
        turned_ref[0, :, rows] = low.T
        query_ref[0, rows, :] = query


def attention_shares(queries, key_heads, value_heads, prev, segs):
    tokens, width = queries.shape
    span = 2 * tokens
    stack = GROUP * tokens
    high = prev.shape[0]
    own = pl.BlockSpec((tokens, HD), lambda g: (0, g))
    group = lambda shape: pl.BlockSpec((1,) + shape, lambda g: (g, 0, 0))
    made = lambda shape: jax.ShapeDtypeStruct((KVH,) + shape, jnp.bfloat16)
    shapes = ((stack, span), (span, stack), (stack, HD), (span, HD), (HD, span))
    return pl.pallas_call(
        shares_kernel,
        grid=(KVH,),
        in_specs=[
            pl.BlockSpec((tokens, GROUP * HD), lambda g: (0, g)),
            own,
            own,
            pl.BlockSpec((high, HD), lambda g: (0, g)),
            pl.BlockSpec((high, HD), lambda g: (0, KVH + g)),
            pl.BlockSpec((high, HD), lambda g: (0, 0)),
            pl.BlockSpec((1, tokens), lambda g: (0, 0)),
            pl.BlockSpec((tokens, 1), lambda g: (0, 0)),
        ],
        out_specs=[group(shape) for shape in shapes],
        out_shape=[made(shape) for shape in shapes],
        compiler_params=params(32),
        cost_estimate=pl.CostEstimate(
            flops=2 * tokens * width * span, bytes_accessed=8 * MIB,
            transcendentals=tokens * span * KVH * GROUP,
        ),
        name="attention_shares",
    )(queries, key_heads, value_heads, prev, prev, prev, segs[None, :], segs[:, None])


def tail_kernel(
    plan, back_ref, place_ref, grad_ref, own_ref, other_ref, low_ref, turned_ref, q_ref, key_ref, value_ref,
    moe_ref, query_out, key_out, value_out, sent_out, stream, held, sums,
):
    heads, tiles = plan
    step = pl.program_id(0)
    tokens = query_out.shape[0]
    half = own_ref.shape[1]

    @pl.when(step == 0)
    def _():
        moe = dot(place_ref[...], back_ref[...]).astype(jnp.bfloat16)
        moe_ref[...] = moe
        added = (grad_ref[...].astype(jnp.float32) + moe.astype(jnp.float32)).astype(jnp.bfloat16)
        low_half = lax.axis_index("far") == 0
        stream[:, :half] = jnp.where(low_half, added[:, :half], added[:, half:])
        stream[:, half:] = jnp.where(low_half, added[:, half:], added[:, :half])
        held[...] = jnp.zeros_like(held)

    @pl.when((step == 0) | ((step > 1) & ((step - 1) % tiles == 0)))
    def _():
        sums[...] = jnp.zeros_like(sums)

    grads = held[...]
    head_grad = (dot(stream[:, :half], own_ref[0]) + dot(stream[:, half:], other_ref[0])).astype(jnp.bfloat16)
    low = low_ref[0].astype(jnp.float32)
    prob_grad = dot(grads, value_ref[0])
    row_dot = jnp.sum(low * prob_grad, axis=1, keepdims=True)
    score_grad = (low * (prob_grad - row_dot) * (HD**-0.5)).astype(jnp.bfloat16)
    query_grad = dot(score_grad, key_ref[0]).astype(jnp.bfloat16)
    sums[0] += dot(score_grad, q_ref[0], TN)
    sums[1] += dot(turned_ref[0], grads)
    for head in range(heads):
        cols = slice(head * HD, (head + 1) * HD)
        rows = slice(head * tokens, (head + 1) * tokens)
        query_out[:, cols] = query_grad[rows, :]
        held[rows, :] = head_grad[:, cols]

    @pl.when((step > 0) & (step % tiles == 0))
    def _():
        key_out[...] = sums[0, tokens:, :]
        value_out[...] = sums[1, tokens:, :]
        sent_out[...] = sums[:, :tokens, :].astype(jnp.bfloat16)


def tail(back, place, moe_grad, w_own, w_other, low, turned, query, keys, values):
    tokens, width = moe_grad.shape
    half, cols = w_own.shape[1:]
    span = keys.shape[1]
    heads = 4
    tile = heads * HD
    tiles = cols // tile
    steps = KVH * tiles
    now = lambda i: jnp.minimum(i, steps - 1)
    was = lambda i: jnp.maximum(i - 1, 0)
    whole = lambda shape: pl.BlockSpec(shape, lambda i: (0,) * len(shape))
    group = lambda shape: pl.BlockSpec((1,) + shape, lambda i: (was(i) // tiles, 0, 0))
    rows = lambda shape: pl.BlockSpec((1,) + shape, lambda i: (was(i) // tiles, was(i) % tiles, 0))
    w_spec = pl.BlockSpec((1, half, tile), lambda i: (now(i) // tiles, 0, now(i) % tiles))
    kv = pl.BlockSpec((tokens, HD), lambda i: (0, was(i) // tiles))
    return pl.pallas_call(
        functools.partial(tail_kernel, (heads, tiles)),
        grid=(steps + 1,),
        in_specs=[
            whole(back.shape),
            whole(place.shape),
            whole(moe_grad.shape),
            w_spec,
            w_spec,
            rows((heads * tokens, span)),
            pl.BlockSpec((1, span, heads * tokens), lambda i: (was(i) // tiles, 0, was(i) % tiles)),
            rows((heads * tokens, HD)),
            group((span, HD)),
            group((HD, span)),
        ],
        out_specs=[
            whole((tokens, width)),
            pl.BlockSpec((tokens, tile), lambda i: (0, was(i))),
            kv,
            kv,
            pl.BlockSpec((2, tokens, HD), lambda i: (0, 0, was(i) // tiles)),
        ],
        out_shape=(
            jax.ShapeDtypeStruct((tokens, width), jnp.bfloat16),
            jax.ShapeDtypeStruct((tokens, KVH * cols), jnp.bfloat16),
            jax.ShapeDtypeStruct((tokens, KVH * HD), jnp.float32),
            jax.ShapeDtypeStruct((tokens, KVH * HD), jnp.float32),
            jax.ShapeDtypeStruct((2, tokens, KVH * HD), jnp.bfloat16),
        ),
        scratch_shapes=[
            pltpu.VMEM((tokens, width), jnp.bfloat16),
            pltpu.VMEM((heads * tokens, HD), jnp.bfloat16),
            pltpu.VMEM((2, span, HD), jnp.float32),
        ],
        compiler_params=params(56),
        cost_estimate=pl.CostEstimate(
            flops=2 * tokens * width * KVH * cols, bytes_accessed=22 * MIB, transcendentals=0
        ),
        name="tail_attention",
    )(back, place, moe_grad, w_own, w_other, low, turned, query, keys, values)


def local(
    moe_input,
    moe_grad,
    routes,
    route_weight,
    w_gate,
    w_up,
    w_down,
    w_out,
    queries,
    key_heads,
    value_heads,
    segments,
):
    chips = ("far", "near", "low")
    blk = chips + ("core",)
    low = lax.axis_size("low")
    owners = 4 * low
    count = 2 * owners
    parts = lax.axis_size("groups")
    tokens, width = moe_input.shape
    depth = 2 * max(1, 3 * tokens * routes.shape[1] // (2 * count))
    swap = [(0, 1), (1, 0)]
    onward = [(i, i + 1) for i in range(count - 1)]
    backward = [(i + 1, i) for i in range(count - 1)]

    rows, place = pick(routes, route_weight, moe_input, moe_grad, owners, depth)
    rows_in = lax.all_to_all(rows.reshape(owners, depth, 2 * width), chips, 0, 0, tiled=True)

    share_cols = w_out.shape[1] // parts
    w_share = lax.dynamic_slice_in_dim(w_out, lax.axis_index("groups") * share_cols, share_cols, 1)
    w_mirror = lax.ppermute(w_share, "far", swap)
    own = (w_gate, w_up, w_down)
    other = tuple(lax.ppermute(w, "core", swap) for w in own)
    prepared = prepare_weights(own, other)

    kv = jnp.concatenate([key_heads, value_heads], axis=1)
    segs = (segments + 1).astype(jnp.float32)
    seg_rows = jnp.zeros((16, kv.shape[1]), jnp.bfloat16).at[0, :tokens].set(segs.astype(jnp.bfloat16))
    prev = lax.ppermute(jnp.concatenate([kv, seg_rows], axis=0), blk, onward)

    w_mirror, prepared, prev, rows_in = lax.optimization_barrier((w_mirror, prepared, prev, rows_in))
    w_own, w_other = (
        lax.all_gather(part, ("groups", "near", "low", "core"), axis=0, tiled=True).reshape(
            parts, width // 2, share_cols
        )
        for part in (w_share, w_mirror)
    )

    terms = experts(rows_in.reshape(owners * depth, 2 * width), *prepared)
    prev, terms = lax.optimization_barrier((prev, terms))
    back = lax.all_to_all(terms.reshape(owners, depth, width), chips, 0, 0, tiled=True)
    attention = attention_shares(queries, key_heads, value_heads, prev, segs)

    moe_input_grad, query_grad, key_part, value_part, sent = tail(
        back.reshape(owners * depth, width), place, moe_grad, w_own, w_other, *attention
    )
    later = lax.ppermute(sent, blk, backward).astype(jnp.float32)
    return (moe_input_grad, query_grad, key_part + later[0], value_part + later[1])


def solution(mesh):
    names = ("groups", "far", "near", "low", "core")
    shape = (mesh.shape["groups"], 2, 2, mesh.shape["blk"] // 8, 2)
    fine = jax.sharding.Mesh(mesh.devices.reshape(shape), names)
    blk = names[1:]
    by_tokens = P(names, None)
    return jax.shard_map(
        local,
        mesh=fine,
        in_specs=(
            by_tokens,
            by_tokens,
            by_tokens,
            by_tokens,
            P(None, blk),
            P(None, blk),
            P(blk, None),
            P(blk, None),
            by_tokens,
            by_tokens,
            by_tokens,
            P(names),
        ),
        out_specs=(by_tokens,) * 4,
        check_vma=False,
    )
```

```python
import functools

import jax
import jax.numpy as jnp
from jax import lax
from jax.experimental import pallas as pl
from jax.experimental.pallas import tpu as pltpu
from jax.sharding import PartitionSpec as P

KVH = 2
GROUP = 16
HD = 128
FLOOR = -1e30
MIB = 1 << 20

NT = (((1,), (1,)), ((), ()))
TN = (((0,), (0,)), ((), ()))


def dot(a, b, dims=(((1,), (0,)), ((), ()))):
    return lax.dot_general(a, b, dims, preferred_element_type=jnp.float32)


def params(mib):
    return pltpu.CompilerParams(vmem_limit_bytes=mib * MIB)


def pick_kernel(owners, depth, routes_ref, weight_ref, input_ref, grad_ref, rows_ref, back_ref):
    tokens = input_ref.shape[0]
    slots = owners * depth
    first = routes_ref[0:1, :]
    second = routes_ref[1:2, :]
    expert = lax.broadcasted_iota(jnp.int32, (owners, tokens), 0)
    is_first = first == expert
    is_second = second == expert
    member = jnp.where(is_first | is_second, 1.0, 0.0)
    before = lax.broadcasted_iota(jnp.int32, (tokens, tokens), 0) < lax.broadcasted_iota(
        jnp.int32, (tokens, tokens), 1
    )
    rank = dot(member.astype(jnp.bfloat16), jnp.where(before, 1.0, 0.0).astype(jnp.bfloat16))
    spot = (expert * depth).astype(jnp.float32) + rank
    slot_first = jnp.sum(jnp.where(is_first, spot, 0.0), axis=0, keepdims=True).astype(jnp.int32)
    slot_second = jnp.sum(jnp.where(is_second, spot, 0.0), axis=0, keepdims=True).astype(jnp.int32)
    slot = lax.broadcasted_iota(jnp.int32, (slots, tokens), 0)
    at_first = slot == slot_first
    at_second = slot == slot_second
    place = jnp.where(at_first | at_second, 1.0, 0.0).astype(jnp.bfloat16)
    back_ref[...] = place.T
    scale = jnp.sum(
        jnp.where(at_first, weight_ref[0:1, :], 0.0) + jnp.where(at_second, weight_ref[1:2, :], 0.0),
        axis=1,
        keepdims=True,
    )
    width = input_ref.shape[1]
    rows_ref[:, :width] = dot(place, input_ref[...]).astype(jnp.bfloat16)
    rows_ref[:, width:] = (scale * dot(place, grad_ref[...])).astype(jnp.bfloat16)


def pick(routes, route_weight, moe_input, moe_grad, owners, depth):
    tokens, width = moe_input.shape
    slots = owners * depth
    return pl.pallas_call(
        functools.partial(pick_kernel, owners, depth),
        out_shape=(
            jax.ShapeDtypeStruct((slots, 2 * width), jnp.bfloat16),
            jax.ShapeDtypeStruct((tokens, slots), jnp.bfloat16),
        ),
        compiler_params=params(32),
        cost_estimate=pl.CostEstimate(
            flops=4 * slots * tokens * width, bytes_accessed=8 * MIB, transcendentals=0
        ),
        name="pick_rows",
    )(routes.T, route_weight.T, moe_input, moe_grad)


def weights_kernel(*refs):
    own, other, (cols_ref, down_ref, rows_ref) = refs[:3], refs[3:6], refs[6:]
    tile = own[0].shape[1]
    for place, (gate_ref, up_ref, low_ref) in enumerate((own, other)):
        for kind, ref in enumerate((gate_ref, up_ref)):
            spot = slice((2 * kind + place) * tile, (2 * kind + place + 1) * tile)
            cols_ref[0, :, spot] = ref[...]
            rows_ref[0, spot, :] = ref[...].T
        down_ref[0, :, place * tile : (place + 1) * tile] = low_ref[...].T


def prepare_weights(own, other):
    width, half = own[0].shape
    tile = 128
    steps = half // tile
    cols = pl.BlockSpec((width, tile), lambda i: (0, i))
    down = pl.BlockSpec((tile, width), lambda i: (i, 0))
    return pl.pallas_call(
        weights_kernel,
        grid=(steps,),
        in_specs=[cols, cols, down] * 2,
        out_specs=[
            pl.BlockSpec((1, width, 4 * tile), lambda i: (i, 0, 0)),
            pl.BlockSpec((1, width, 2 * tile), lambda i: (i, 0, 0)),
            pl.BlockSpec((1, 4 * tile, width), lambda i: (i, 0, 0)),
        ],
        out_shape=(
            jax.ShapeDtypeStruct((steps, width, 4 * tile), jnp.bfloat16),
            jax.ShapeDtypeStruct((steps, width, 2 * tile), jnp.bfloat16),
            jax.ShapeDtypeStruct((steps, 4 * tile, width), jnp.bfloat16),
        ),
        compiler_params=params(48),
        cost_estimate=pl.CostEstimate(
            flops=0, bytes_accessed=32 * width * half, transcendentals=0
        ),
        name="prepare_weights",
    )(*own, *other)


def expert_kernel(steps, rows_ref, cols_ref, down_ref, back_ref, out_ref, hidden):
    step = pl.program_id(0)
    width = rows_ref.shape[1] // 2
    pair = down_ref.shape[2]

    @pl.when(step < steps)
    def _():
        both_pre = dot(rows_ref[:, :width], cols_ref[0])
        gate_pre = both_pre[:, :pair]
        up_pre = both_pre[:, pair:]
        down_grad = dot(rows_ref[:, width:], down_ref[0])
        sig = jax.nn.sigmoid(gate_pre)
        hidden[step, :, :pair] = (
            down_grad * up_pre * sig * (1.0 + gate_pre * (1.0 - sig))
        ).astype(jnp.bfloat16)
        hidden[step, :, pair:] = (down_grad * gate_pre * sig).astype(jnp.bfloat16)

    @pl.when(step >= steps)
    def _():
        total = dot(hidden[0], back_ref[0])
        for i in range(1, steps):
            total += dot(hidden[i], back_ref[i])
        out_ref[...] = total.astype(jnp.bfloat16)


def experts(rows, cols, down, back):
    count, twice = rows.shape
    steps, width, quad = cols.shape
    tile = 512
    last = steps - 1
    turn = lambda i: jnp.maximum(i - steps, 0)
    return pl.pallas_call(
        functools.partial(expert_kernel, steps),
        grid=(steps + width // tile,),
        in_specs=[
            pl.BlockSpec((count, twice), lambda i: (0, 0)),
            pl.BlockSpec((1, width, quad), lambda i: (jnp.minimum(i, last), 0, 0)),
            pl.BlockSpec((1, width, quad // 2), lambda i: (jnp.minimum(i, last), 0, 0)),
            pl.BlockSpec((steps, quad, tile), lambda i: (0, 0, turn(i))),
        ],
        out_specs=pl.BlockSpec((count, tile), lambda i: (0, turn(i))),
        out_shape=jax.ShapeDtypeStruct((count, width), jnp.bfloat16),
        scratch_shapes=[pltpu.VMEM((steps, count, quad), jnp.bfloat16)],
        compiler_params=params(48),
        cost_estimate=pl.CostEstimate(
            flops=5 * count * width * steps * quad, bytes_accessed=20 * MIB,
            transcendentals=count * steps * quad,
        ),
        name="expert_terms",
    )(rows, cols, down, back)


def shares_kernel(
    q_ref, key_ref, value_ref, prev_key_ref, prev_value_ref, prev_seg_ref, seg_row_ref, seg_col_ref,
    low_ref, turned_ref, query_ref, key_out, value_out,
):
    tokens = q_ref.shape[0]
    seg_col = seg_col_ref[...]
    row = lax.broadcasted_iota(jnp.int32, (tokens, tokens), 0)
    col = lax.broadcasted_iota(jnp.int32, (tokens, tokens), 1)
    own_seen = jnp.where((col <= row) & (seg_row_ref[...] == seg_col), 1.0, 0.0)
    prev_seg = prev_seg_ref[tokens : tokens + 16, :].astype(jnp.float32)[0:1, :]
    prev_seen = jnp.where(prev_seg == seg_col, 1.0, 0.0)
    seen = jnp.concatenate([prev_seen, own_seen], axis=1) > 0.5
    keys = jnp.concatenate([prev_key_ref[:tokens, :], key_ref[...]], axis=0)
    values = jnp.concatenate([prev_value_ref[:tokens, :], value_ref[...]], axis=0)
    key_out[0] = keys
    value_out[0] = values.T
    for head in range(GROUP):
        rows = slice(head * tokens, (head + 1) * tokens)
        query = q_ref[:, head * HD : (head + 1) * HD]
        scores = dot(query, keys, NT) * (HD**-0.5)
        masked = jnp.where(seen, scores, FLOOR)
        raised = jnp.where(seen, jnp.exp(masked - jnp.max(masked, axis=1, keepdims=True)), 0.0)
        shares = raised / jnp.sum(raised, axis=1, keepdims=True)
        low = shares.astype(jnp.bfloat16)
        low_ref[0, rows, :] = low
        turned_ref[0, :, rows] = low.T
        query_ref[0, rows, :] = query


def attention_shares(queries, key_heads, value_heads, prev, segs):
    tokens, width = queries.shape
    span = 2 * tokens
    stack = GROUP * tokens
    high = prev.shape[0]
    own = pl.BlockSpec((tokens, HD), lambda g: (0, g))
    group = lambda shape: pl.BlockSpec((1,) + shape, lambda g: (g, 0, 0))
    made = lambda shape: jax.ShapeDtypeStruct((KVH,) + shape, jnp.bfloat16)
    shapes = ((stack, span), (span, stack), (stack, HD), (span, HD), (HD, span))
    return pl.pallas_call(
        shares_kernel,
        grid=(KVH,),
        in_specs=[
            pl.BlockSpec((tokens, GROUP * HD), lambda g: (0, g)),
            own,
            own,
            pl.BlockSpec((high, HD), lambda g: (0, g)),
            pl.BlockSpec((high, HD), lambda g: (0, KVH + g)),
            pl.BlockSpec((high, HD), lambda g: (0, 0)),
            pl.BlockSpec((1, tokens), lambda g: (0, 0)),
            pl.BlockSpec((tokens, 1), lambda g: (0, 0)),
        ],
        out_specs=[group(shape) for shape in shapes],
        out_shape=[made(shape) for shape in shapes],
        compiler_params=params(32),
        cost_estimate=pl.CostEstimate(
            flops=2 * tokens * width * span, bytes_accessed=8 * MIB,
            transcendentals=tokens * span * KVH * GROUP,
        ),
        name="attention_shares",
    )(queries, key_heads, value_heads, prev, prev, prev, segs[None, :], segs[:, None])


def tail_kernel(
    plan, place_info, back_ref, place_ref, grad_ref, *refs
):
    heads, tiles, blocks = plan
    own_refs, other_refs, refs = refs[:4], refs[4:8], refs[8:]
    low_ref, turned_ref, q_ref, key_ref, value_ref, *refs = refs
    moe_ref, query_out, key_out, value_out, sent_out, stream, held, sums = refs
    step = pl.program_id(0)
    tokens = query_out.shape[0]

    @pl.when(step == 0)
    def _():
        moe = dot(place_ref[...], back_ref[...]).astype(jnp.bfloat16)
        moe_ref[...] = moe
        added = (grad_ref[...].astype(jnp.float32) + moe.astype(jnp.float32)).astype(jnp.bfloat16)
        size = added.shape[1] // (4 * blocks)
        for far in range(2):
            for core in range(2):
                for rest in range(blocks):
                    source = (far * blocks + rest) * 2 + core
                    stream[2 * far + core, :, rest * size : (rest + 1) * size] = added[
                        :, source * size : (source + 1) * size
                    ]
        held[...] = jnp.zeros_like(held)

    @pl.when((step == 0) | ((step > 1) & ((step - 1) % tiles == 0)))
    def _():
        sums[...] = jnp.zeros_like(sums)

    def advance(w_refs):
        far, core = place_info[1], place_info[2]
        grads = held[...]
        head_grad = None
        for k, w_ref in enumerate(w_refs):
            part = dot(stream[2 * (far ^ (k // 2)) + (core ^ (k % 2))], w_ref[...])
            head_grad = part if head_grad is None else head_grad + part
        head_grad = head_grad.astype(jnp.bfloat16)
        low = low_ref[0].astype(jnp.float32)
        prob_grad = dot(grads, value_ref[0])
        row_dot = jnp.sum(low * prob_grad, axis=1, keepdims=True)
        score_grad = (low * (prob_grad - row_dot) * (HD**-0.5)).astype(jnp.bfloat16)
        query_grad = dot(score_grad, key_ref[0]).astype(jnp.bfloat16)
        sums[0] += dot(score_grad, q_ref[0], TN)
        sums[1] += dot(turned_ref[0], grads)
        for head in range(heads):
            cols = slice(head * HD, (head + 1) * HD)
            rows = slice(head * tokens, (head + 1) * tokens)
            query_out[:, cols] = query_grad[rows, :]
            held[rows, :] = head_grad[:, cols]

    @pl.when(step < tiles)
    def _():
        advance(own_refs)

    @pl.when(step >= tiles)
    def _():
        advance(other_refs)

    @pl.when((step > 0) & (step % tiles == 0))
    def _():
        key_out[...] = sums[0, tokens:, :]
        value_out[...] = sums[1, tokens:, :]
        sent_out[...] = sums[:, :tokens, :].astype(jnp.bfloat16)


def tail(place_info, blocks, back, place, moe_grad, w_own, w_other, low, turned, query, keys, values):
    tokens, width = moe_grad.shape
    quarter, cols = w_own[0].shape
    span = keys.shape[1]
    heads = 4
    tile = heads * HD
    tiles = cols // tile
    steps = KVH * tiles
    was = lambda i: jnp.maximum(i - 1, 0)
    kv_group = lambda i, info: (was(i) // tiles) ^ info[0]
    whole = lambda shape: pl.BlockSpec(shape, lambda i, info: (0,) * len(shape))
    group = lambda shape: pl.BlockSpec((1,) + shape, lambda i, info: (kv_group(i, info), 0, 0))
    rows = lambda shape: pl.BlockSpec((1,) + shape, lambda i, info: (kv_group(i, info), was(i) % tiles, 0))
    own_spec = pl.BlockSpec((quarter, tile), lambda i, info: (0, jnp.minimum(i, tiles - 1)))
    other_spec = pl.BlockSpec(
        (quarter, tile), lambda i, info: (0, jnp.minimum(jnp.maximum(i - tiles, 0), tiles - 1))
    )
    kv = pl.BlockSpec((tokens, HD), lambda i, info: (0, kv_group(i, info)))
    return pl.pallas_call(
        functools.partial(tail_kernel, (heads, tiles, blocks)),
        grid_spec=pltpu.PrefetchScalarGridSpec(
            num_scalar_prefetch=1,
            grid=(steps + 1,),
            in_specs=[whole(back.shape), whole(place.shape), whole(moe_grad.shape)]
            + [own_spec] * 4
            + [other_spec] * 4
            + [
                rows((heads * tokens, span)),
                pl.BlockSpec(
                    (1, span, heads * tokens), lambda i, info: (kv_group(i, info), 0, was(i) % tiles)
                ),
                rows((heads * tokens, HD)),
                group((span, HD)),
                group((HD, span)),
            ],
            out_specs=[
                whole((tokens, width)),
                pl.BlockSpec(
                    (tokens, tile), lambda i, info: (0, kv_group(i, info) * tiles + was(i) % tiles)
                ),
                kv,
                kv,
                pl.BlockSpec((2, tokens, HD), lambda i, info: (0, 0, kv_group(i, info))),
            ],
            scratch_shapes=[
                pltpu.VMEM((4, tokens, quarter), jnp.bfloat16),
                pltpu.VMEM((heads * tokens, HD), jnp.bfloat16),
                pltpu.VMEM((2, span, HD), jnp.float32),
            ],
        ),
        out_shape=(
            jax.ShapeDtypeStruct((tokens, width), jnp.bfloat16),
            jax.ShapeDtypeStruct((tokens, KVH * cols), jnp.bfloat16),
            jax.ShapeDtypeStruct((tokens, KVH * HD), jnp.float32),
            jax.ShapeDtypeStruct((tokens, KVH * HD), jnp.float32),
            jax.ShapeDtypeStruct((2, tokens, KVH * HD), jnp.bfloat16),
        ),
        compiler_params=params(56),
        cost_estimate=pl.CostEstimate(
            flops=2 * tokens * width * KVH * cols, bytes_accessed=22 * MIB, transcendentals=0
        ),
        name="tail_attention",
    )(place_info, back, place, moe_grad, *w_own, *w_other, low, turned, query, keys, values)


def local(
    moe_input,
    moe_grad,
    routes,
    route_weight,
    w_gate,
    w_up,
    w_down,
    w_out,
    queries,
    key_heads,
    value_heads,
    segments,
):
    chips = ("far", "near", "low")
    blk = chips + ("core",)
    low = lax.axis_size("low")
    owners = 4 * low
    count = 2 * owners
    parts = lax.axis_size("groups")
    tokens, width = moe_input.shape
    depth = 2 * max(1, 3 * tokens * routes.shape[1] // (2 * count))
    swap = [(0, 1), (1, 0)]
    onward = [(i, i + 1) for i in range(count - 1)]
    backward = [(i + 1, i) for i in range(count - 1)]

    share_cols = w_out.shape[1] // parts
    w_share = lax.dynamic_slice_in_dim(w_out, lax.axis_index("groups") * share_cols, share_cols, 1)
    w_mirror = lax.ppermute(w_share, "far", swap)
    w_near, w_far = (
        lax.all_gather(part, ("near", "low"), axis=0, tiled=True) for part in (w_share, w_mirror)
    )

    rows, place = pick(routes, route_weight, moe_input, moe_grad, owners, depth)
    rows_in = lax.all_to_all(rows.reshape(owners, depth, 2 * width), chips, 0, 0, tiled=True)
    x_near = lax.ppermute(w_near, "groups", swap)

    own = (w_gate, w_up, w_down)
    other = tuple(lax.ppermute(w, "core", swap) for w in own)
    prepared = prepare_weights(own, other)

    kv = jnp.concatenate([key_heads, value_heads], axis=1)
    segs = (segments + 1).astype(jnp.float32)
    seg_rows = jnp.zeros((16, kv.shape[1]), jnp.bfloat16).at[0, :tokens].set(segs.astype(jnp.bfloat16))
    prev = lax.ppermute(jnp.concatenate([kv, seg_rows], axis=0), blk, onward)

    rows_in, prepared, prev, w_near, w_far, x_near = lax.optimization_barrier(
        (rows_in, prepared, prev, w_near, w_far, x_near)
    )
    x_far = lax.ppermute(w_far, "groups", swap)
    terms = experts(rows_in.reshape(owners * depth, 2 * width), *prepared)
    prev, terms = lax.optimization_barrier((prev, terms))
    back = lax.all_to_all(terms.reshape(owners, depth, width), chips, 0, 0, tiled=True)
    attention = attention_shares(queries, key_heads, value_heads, prev, segs)
    both_cores = lambda *pieces: [w for piece in pieces for w in (piece, lax.ppermute(piece, "core", swap))]

    moe_input_grad, query_grad, key_part, value_part, sent = tail(
        jnp.stack([lax.axis_index(axis) for axis in ("groups", "far", "core")]).astype(jnp.int32),
        2 * low, back.reshape(owners * depth, width), place, moe_grad,
        both_cores(w_near, w_far), both_cores(x_near, x_far), *attention,
    )
    later = lax.ppermute(sent, blk, backward).astype(jnp.float32)
    return (moe_input_grad, query_grad, key_part + later[0], value_part + later[1])


def solution(mesh):
    names = ("groups", "far", "near", "low", "core")
    shape = (mesh.shape["groups"], 2, 2, mesh.shape["blk"] // 8, 2)
    fine = jax.sharding.Mesh(mesh.devices.reshape(shape), names)
    blk = names[1:]
    by_tokens = P(names, None)
    return jax.shard_map(
        local,
        mesh=fine,
        in_specs=(
            by_tokens,
            by_tokens,
            by_tokens,
            by_tokens,
            P(None, blk),
            P(None, blk),
            P(blk, None),
            P(blk, None),
            by_tokens,
            by_tokens,
            by_tokens,
            P(names),
        ),
        out_specs=(by_tokens,) * 4,
        check_vma=False,
    )
```

```python
import functools

import jax
import jax.numpy as jnp
from jax import lax
from jax.experimental import pallas as pl
from jax.experimental.pallas import tpu as pltpu
from jax.sharding import PartitionSpec as P

KVH = 2
GROUP = 16
HD = 128
FLOOR = -1e30
MIB = 1 << 20
LIGHT = pl.CostEstimate(flops=0, bytes_accessed=0, transcendentals=0)

NT = (((1,), (1,)), ((), ()))
TN = (((0,), (0,)), ((), ()))


def dot(a, b, dims=(((1,), (0,)), ((), ()))):
    return lax.dot_general(a, b, dims, preferred_element_type=jnp.float32)


def params(mib):
    return pltpu.CompilerParams(vmem_limit_bytes=mib * MIB)


def pick_kernel(owners, depth, routes_ref, weight_ref, input_ref, grad_ref, rows_ref, back_ref):
    tokens = input_ref.shape[0]
    slots = owners * depth
    first = routes_ref[0:1, :]
    second = routes_ref[1:2, :]
    expert = lax.broadcasted_iota(jnp.int32, (owners, tokens), 0)
    is_first = first == expert
    is_second = second == expert
    member = jnp.where(is_first | is_second, 1.0, 0.0)
    before = lax.broadcasted_iota(jnp.int32, (tokens, tokens), 0) < lax.broadcasted_iota(
        jnp.int32, (tokens, tokens), 1
    )
    rank = dot(member.astype(jnp.bfloat16), jnp.where(before, 1.0, 0.0).astype(jnp.bfloat16))
    spot = (expert * depth).astype(jnp.float32) + rank
    slot_first = jnp.sum(jnp.where(is_first, spot, 0.0), axis=0, keepdims=True).astype(jnp.int32)
    slot_second = jnp.sum(jnp.where(is_second, spot, 0.0), axis=0, keepdims=True).astype(jnp.int32)
    slot = lax.broadcasted_iota(jnp.int32, (slots, tokens), 0)
    at_first = slot == slot_first
    at_second = slot == slot_second
    place = jnp.where(at_first | at_second, 1.0, 0.0).astype(jnp.bfloat16)
    back_ref[...] = place.T
    scale = jnp.sum(
        jnp.where(at_first, weight_ref[0:1, :], 0.0) + jnp.where(at_second, weight_ref[1:2, :], 0.0),
        axis=1,
        keepdims=True,
    )
    width = input_ref.shape[1]
    rows_ref[:, :width] = dot(place, input_ref[...]).astype(jnp.bfloat16)
    rows_ref[:, width:] = (scale * dot(place, grad_ref[...])).astype(jnp.bfloat16)


def pick(routes, route_weight, moe_input, moe_grad, owners, depth):
    tokens, width = moe_input.shape
    slots = owners * depth
    return pl.pallas_call(
        functools.partial(pick_kernel, owners, depth),
        out_shape=(
            jax.ShapeDtypeStruct((slots, 2 * width), jnp.bfloat16),
            jax.ShapeDtypeStruct((tokens, slots), jnp.bfloat16),
        ),
        compiler_params=params(32),
        cost_estimate=pl.CostEstimate(
            flops=4 * slots * tokens * width, bytes_accessed=8 * MIB, transcendentals=0
        ),
        name="pick_rows",
    )(routes.T, route_weight.T, moe_input, moe_grad)


def weights_kernel(*refs):
    own, other, (cols_ref, down_ref, rows_ref) = refs[:3], refs[3:6], refs[6:]
    tile = own[0].shape[1]
    for place, (gate_ref, up_ref, low_ref) in enumerate((own, other)):
        for kind, ref in enumerate((gate_ref, up_ref)):
            spot = slice((2 * kind + place) * tile, (2 * kind + place + 1) * tile)
            cols_ref[0, :, spot] = ref[...]
            rows_ref[0, spot, :] = ref[...].T
        down_ref[0, :, place * tile : (place + 1) * tile] = low_ref[...].T


def prepare_weights(own, other):
    width, half = own[0].shape
    tile = 128
    steps = half // tile
    cols = pl.BlockSpec((width, tile), lambda i: (0, i))
    down = pl.BlockSpec((tile, width), lambda i: (i, 0))
    return pl.pallas_call(
        weights_kernel,
        grid=(steps,),
        in_specs=[cols, cols, down] * 2,
        out_specs=[
            pl.BlockSpec((1, width, 4 * tile), lambda i: (i, 0, 0)),
            pl.BlockSpec((1, width, 2 * tile), lambda i: (i, 0, 0)),
            pl.BlockSpec((1, 4 * tile, width), lambda i: (i, 0, 0)),
        ],
        out_shape=(
            jax.ShapeDtypeStruct((steps, width, 4 * tile), jnp.bfloat16),
            jax.ShapeDtypeStruct((steps, width, 2 * tile), jnp.bfloat16),
            jax.ShapeDtypeStruct((steps, 4 * tile, width), jnp.bfloat16),
        ),
        compiler_params=params(48),
        cost_estimate=LIGHT,
        name="prepare_weights",
    )(*own, *other)


def expert_kernel(steps, rows_ref, cols_ref, down_ref, back_ref, out_ref, hidden):
    step = pl.program_id(0)
    width = rows_ref.shape[1] // 2
    pair = down_ref.shape[2]

    @pl.when(step < steps)
    def _():
        both_pre = dot(rows_ref[:, :width], cols_ref[0])
        gate_pre = both_pre[:, :pair]
        up_pre = both_pre[:, pair:]
        down_grad = dot(rows_ref[:, width:], down_ref[0])
        sig = jax.nn.sigmoid(gate_pre)
        hidden[step, :, :pair] = (
            down_grad * up_pre * sig * (1.0 + gate_pre * (1.0 - sig))
        ).astype(jnp.bfloat16)
        hidden[step, :, pair:] = (down_grad * gate_pre * sig).astype(jnp.bfloat16)

    @pl.when(step >= steps)
    def _():
        total = dot(hidden[0], back_ref[0])
        for i in range(1, steps):
            total += dot(hidden[i], back_ref[i])
        out_ref[...] = total.astype(jnp.bfloat16)


def experts(rows, cols, down, back):
    count, twice = rows.shape
    steps, width, quad = cols.shape
    tile = 512
    last = steps - 1
    turn = lambda i: jnp.maximum(i - steps, 0)
    return pl.pallas_call(
        functools.partial(expert_kernel, steps),
        grid=(steps + width // tile,),
        in_specs=[
            pl.BlockSpec((count, twice), lambda i: (0, 0)),
            pl.BlockSpec((1, width, quad), lambda i: (jnp.minimum(i, last), 0, 0)),
            pl.BlockSpec((1, width, quad // 2), lambda i: (jnp.minimum(i, last), 0, 0)),
            pl.BlockSpec((steps, quad, tile), lambda i: (0, 0, turn(i))),
        ],
        out_specs=pl.BlockSpec((count, tile), lambda i: (0, turn(i))),
        out_shape=jax.ShapeDtypeStruct((count, width), jnp.bfloat16),
        scratch_shapes=[pltpu.VMEM((steps, count, quad), jnp.bfloat16)],
        compiler_params=params(48),
        cost_estimate=LIGHT,
        name="expert_terms",
    )(rows, cols, down, back)


def shares_kernel(
    q_ref, key_ref, value_ref, prev_key_ref, prev_value_ref, prev_seg_ref, seg_row_ref, seg_col_ref,
    low_ref, turned_ref, query_ref, key_out, value_out,
):
    tokens = q_ref.shape[0]
    seg_col = seg_col_ref[...]
    row = lax.broadcasted_iota(jnp.int32, (tokens, tokens), 0)
    col = lax.broadcasted_iota(jnp.int32, (tokens, tokens), 1)
    own_seen = jnp.where((col <= row) & (seg_row_ref[...] == seg_col), 1.0, 0.0)
    prev_seg = prev_seg_ref[tokens : tokens + 16, :].astype(jnp.float32)[0:1, :]
    prev_seen = jnp.where(prev_seg == seg_col, 1.0, 0.0)
    seen = jnp.concatenate([prev_seen, own_seen], axis=1) > 0.5
    keys = jnp.concatenate([prev_key_ref[:tokens, :], key_ref[...]], axis=0)
    values = jnp.concatenate([prev_value_ref[:tokens, :], value_ref[...]], axis=0)
    key_out[0] = keys
    value_out[0] = values.T
    for head in range(GROUP):
        rows = slice(head * tokens, (head + 1) * tokens)
        query = q_ref[:, head * HD : (head + 1) * HD]
        scores = dot(query, keys, NT) * (HD**-0.5)
        masked = jnp.where(seen, scores, FLOOR)
        raised = jnp.where(seen, jnp.exp(masked - jnp.max(masked, axis=1, keepdims=True)), 0.0)
        shares = raised / jnp.sum(raised, axis=1, keepdims=True)
        low = shares.astype(jnp.bfloat16)
        low_ref[0, rows, :] = low
        turned_ref[0, :, rows] = low.T
        query_ref[0, rows, :] = query


def attention_shares(queries, key_heads, value_heads, prev, segs):
    tokens, width = queries.shape
    span = 2 * tokens
    stack = GROUP * tokens
    high = prev.shape[0]
    own = pl.BlockSpec((tokens, HD), lambda g: (0, g))
    group = lambda shape: pl.BlockSpec((1,) + shape, lambda g: (g, 0, 0))
    made = lambda shape: jax.ShapeDtypeStruct((KVH,) + shape, jnp.bfloat16)
    shapes = ((stack, span), (span, stack), (stack, HD), (span, HD), (HD, span))
    return pl.pallas_call(
        shares_kernel,
        grid=(KVH,),
        in_specs=[
            pl.BlockSpec((tokens, GROUP * HD), lambda g: (0, g)),
            own,
            own,
            pl.BlockSpec((high, HD), lambda g: (0, g)),
            pl.BlockSpec((high, HD), lambda g: (0, KVH + g)),
            pl.BlockSpec((high, HD), lambda g: (0, 0)),
            pl.BlockSpec((1, tokens), lambda g: (0, 0)),
            pl.BlockSpec((tokens, 1), lambda g: (0, 0)),
        ],
        out_specs=[group(shape) for shape in shapes],
        out_shape=[made(shape) for shape in shapes],
        compiler_params=params(32),
        cost_estimate=LIGHT,
        name="attention_shares",
    )(queries, key_heads, value_heads, prev, prev, prev, segs[None, :], segs[:, None])


def tail_kernel(
    plan, back_ref, place_ref, grad_ref, own_ref, pair_ref, last_ref, low_ref, turned_ref, q_ref, key_ref, value_ref,
    moe_ref, query_out, key_out, value_out, sent_out, stream, held, sums,
):
    heads, tiles = plan
    step = pl.program_id(0)
    tokens = query_out.shape[0]
    spread, size = last_ref.shape[1:3]

    @pl.when(step == 0)
    def _():
        moe = dot(place_ref[...], back_ref[...]).astype(jnp.bfloat16)
        moe_ref[...] = moe
        added = (grad_ref[...].astype(jnp.float32) + moe.astype(jnp.float32)).astype(jnp.bfloat16)
        for z in range(4):
            for rest in range(spread):
                source = z * spread + rest
                stream[z, :, rest * size : (rest + 1) * size] = added[:, source * size : (source + 1) * size]
        held[...] = jnp.zeros_like(held)

    @pl.when((step == 0) | ((step > 1) & ((step - 1) % tiles == 0)))
    def _():
        sums[...] = jnp.zeros_like(sums)

    grads = held[...]
    here = 2 * lax.axis_index("far") + lax.axis_index("near")
    tile = last_ref.shape[3]
    head_grad = dot(stream[here], own_ref[0].reshape(spread * size, tile))
    for turn in range(2):
        head_grad += dot(stream[here ^ (turn + 1)], pair_ref[0, :, turn].reshape(spread * size, tile))
    head_grad += dot(stream[3 - here], last_ref[0].reshape(spread * size, tile))
    head_grad = head_grad.astype(jnp.bfloat16)
    low = low_ref[0].astype(jnp.float32)
    prob_grad = dot(grads, value_ref[0])
    row_dot = jnp.sum(low * prob_grad, axis=1, keepdims=True)
    score_grad = (low * (prob_grad - row_dot) * (HD**-0.5)).astype(jnp.bfloat16)
    query_grad = dot(score_grad, key_ref[0]).astype(jnp.bfloat16)
    sums[0] += dot(score_grad, q_ref[0], TN)
    sums[1] += dot(turned_ref[0], grads)
    for head in range(heads):
        cols = slice(head * HD, (head + 1) * HD)
        rows = slice(head * tokens, (head + 1) * tokens)
        query_out[:, cols] = query_grad[rows, :]
        held[rows, :] = head_grad[:, cols]

    @pl.when((step > 0) & (step % tiles == 0))
    def _():
        key_out[...] = sums[0, tokens:, :]
        value_out[...] = sums[1, tokens:, :]
        sent_out[...] = sums[:, :tokens, :].astype(jnp.bfloat16)


def tail(back, place, moe_grad, w_own, w_pair, w_last, low, turned, query, keys, values):
    tokens, width = moe_grad.shape
    spread, size, cols = w_last.shape[1:]
    span = keys.shape[1]
    heads = 4
    tile = heads * HD
    tiles = cols // tile
    steps = KVH * tiles
    now = lambda i: jnp.minimum(i, steps - 1)
    was = lambda i: jnp.maximum(i - 1, 0)
    whole = lambda shape: pl.BlockSpec(shape, lambda i: (0,) * len(shape))
    group = lambda shape: pl.BlockSpec((1,) + shape, lambda i: (was(i) // tiles, 0, 0))
    rows = lambda shape: pl.BlockSpec((1,) + shape, lambda i: (was(i) // tiles, was(i) % tiles, 0))
    pair_spec = pl.BlockSpec(
        (1, spread, 2, size, tile), lambda i: (now(i) // tiles, 0, 0, 0, now(i) % tiles)
    )
    one_spec = pl.BlockSpec((1, spread, size, tile), lambda i: (now(i) // tiles, 0, 0, now(i) % tiles))
    kv = pl.BlockSpec((tokens, HD), lambda i: (0, was(i) // tiles))
    return pl.pallas_call(
        functools.partial(tail_kernel, (heads, tiles)),
        grid=(steps + 1,),
        in_specs=[
            whole(back.shape),
            whole(place.shape),
            whole(moe_grad.shape),
            one_spec,
            pair_spec,
            one_spec,
            rows((heads * tokens, span)),
            pl.BlockSpec((1, span, heads * tokens), lambda i: (was(i) // tiles, 0, was(i) % tiles)),
            rows((heads * tokens, HD)),
            group((span, HD)),
            group((HD, span)),
        ],
        out_specs=[
            whole((tokens, width)),
            pl.BlockSpec((tokens, tile), lambda i: (0, was(i))),
            kv,
            kv,
            pl.BlockSpec((2, tokens, HD), lambda i: (0, 0, was(i) // tiles)),
        ],
        out_shape=(
            jax.ShapeDtypeStruct((tokens, width), jnp.bfloat16),
            jax.ShapeDtypeStruct((tokens, KVH * cols), jnp.bfloat16),
            jax.ShapeDtypeStruct((tokens, KVH * HD), jnp.float32),
            jax.ShapeDtypeStruct((tokens, KVH * HD), jnp.float32),
            jax.ShapeDtypeStruct((2, tokens, KVH * HD), jnp.bfloat16),
        ),
        scratch_shapes=[
            pltpu.VMEM((4, tokens, width // 4), jnp.bfloat16),
            pltpu.VMEM((heads * tokens, HD), jnp.bfloat16),
            pltpu.VMEM((2, span, HD), jnp.float32),
        ],
        compiler_params=params(56),
        cost_estimate=pl.CostEstimate(
            flops=2 * tokens * width * KVH * cols, bytes_accessed=22 * MIB, transcendentals=0
        ),
        name="tail_attention",
    )(back, place, moe_grad, w_own, w_pair, w_last, low, turned, query, keys, values)


def local(
    moe_input,
    moe_grad,
    routes,
    route_weight,
    w_gate,
    w_up,
    w_down,
    w_out,
    queries,
    key_heads,
    value_heads,
    segments,
):
    chips = ("far", "near", "low")
    blk = chips + ("core",)
    low = lax.axis_size("low")
    owners = 4 * low
    count = 2 * owners
    parts = lax.axis_size("groups")
    tokens, width = moe_input.shape
    depth = 2 * max(1, 3 * tokens * routes.shape[1] // (2 * count))
    swap = [(0, 1), (1, 0)]
    onward = [(i, i + 1) for i in range(count - 1)]
    backward = [(i + 1, i) for i in range(count - 1)]

    share_cols = w_out.shape[1] // parts
    w_share = lax.dynamic_slice_in_dim(w_out, lax.axis_index("groups") * share_cols, share_cols, 1)
    w_near = lax.ppermute(w_share, "near", swap)
    w_far = lax.ppermute(w_share, "far", swap)

    kv = jnp.concatenate([key_heads, value_heads], axis=1)
    segs = (segments + 1).astype(jnp.float32)
    seg_rows = jnp.zeros((16, kv.shape[1]), jnp.bfloat16).at[0, :tokens].set(segs.astype(jnp.bfloat16))
    prev = lax.ppermute(jnp.concatenate([kv, seg_rows], axis=0), blk, onward)

    own = (w_gate, w_up, w_down)
    other = tuple(lax.ppermute(w, "core", swap) for w in own)
    rows, place = pick(routes, route_weight, moe_input, moe_grad, owners, depth)
    rows, w_near, w_far, prev, other = lax.optimization_barrier((rows, w_near, w_far, prev, other))

    rows_in = lax.all_to_all(rows.reshape(owners, depth, 2 * width), chips, 0, 0, tiled=True)
    plane = ("groups", "low", "core")
    w_own = lax.all_gather(w_share, plane, axis=0, tiled=False)
    w_pair = lax.all_gather(jnp.stack([w_near, w_far]), plane, axis=0, tiled=False)
    w_last = lax.ppermute(w_far, "near", swap)
    prepared = prepare_weights(own, other)
    attention = attention_shares(queries, key_heads, value_heads, prev, segs)

    rows_in, prepared, attention, w_last = lax.optimization_barrier((rows_in, prepared, attention, w_last))
    w_last = lax.all_gather(w_last, plane, axis=0, tiled=False)
    split = lambda w: w.reshape((parts, 2 * low) + w.shape[1:])
    terms = experts(rows_in.reshape(owners * depth, 2 * width), *prepared)
    terms, w_pair = lax.optimization_barrier((terms, w_pair))
    back = lax.all_to_all(terms.reshape(owners, depth, width), chips, 0, 0, tiled=True)

    moe_input_grad, query_grad, key_part, value_part, sent = tail(
        back.reshape(owners * depth, width), place, moe_grad,
        split(w_own), split(w_pair), split(w_last), *attention,
    )
    later = lax.ppermute(sent, blk, backward).astype(jnp.float32)
    return (moe_input_grad, query_grad, key_part + later[0], value_part + later[1])


def solution(mesh):
    names = ("groups", "far", "near", "low", "core")
    shape = (mesh.shape["groups"], 2, 2, mesh.shape["blk"] // 8, 2)
    fine = jax.sharding.Mesh(mesh.devices.reshape(shape), names)
    blk = names[1:]
    by_tokens = P(names, None)
    return jax.shard_map(
        local,
        mesh=fine,
        in_specs=(
            by_tokens,
            by_tokens,
            by_tokens,
            by_tokens,
            P(None, blk),
            P(None, blk),
            P(blk, None),
            P(blk, None),
            by_tokens,
            by_tokens,
            by_tokens,
            P(names),
        ),
        out_specs=(by_tokens,) * 4,
        check_vma=False,
    )
```

```python
import functools

import jax
import jax.numpy as jnp
from jax import lax
from jax.experimental import pallas as pl
from jax.experimental.pallas import tpu as pltpu
from jax.sharding import PartitionSpec as P

KVH = 2
GROUP = 16
HD = 128
FLOOR = -1e30
MIB = 1 << 20
LIGHT = pl.CostEstimate(flops=0, bytes_accessed=0, transcendentals=0)

NT = (((1,), (1,)), ((), ()))
TN = (((0,), (0,)), ((), ()))


def dot(a, b, dims=(((1,), (0,)), ((), ()))):
    return lax.dot_general(a, b, dims, preferred_element_type=jnp.float32)


def params(mib):
    return pltpu.CompilerParams(vmem_limit_bytes=mib * MIB)


def pick_kernel(owners, depth, routes_ref, weight_ref, input_ref, grad_ref, rows_ref, back_ref):
    tokens = input_ref.shape[0]
    slots = owners * depth
    first = routes_ref[0:1, :]
    second = routes_ref[1:2, :]
    expert = lax.broadcasted_iota(jnp.int32, (owners, tokens), 0)
    is_first = first == expert
    is_second = second == expert
    member = jnp.where(is_first | is_second, 1.0, 0.0)
    before = lax.broadcasted_iota(jnp.int32, (tokens, tokens), 0) < lax.broadcasted_iota(
        jnp.int32, (tokens, tokens), 1
    )
    rank = dot(member.astype(jnp.bfloat16), jnp.where(before, 1.0, 0.0).astype(jnp.bfloat16))
    spot = (expert * depth).astype(jnp.float32) + rank
    slot_first = jnp.sum(jnp.where(is_first, spot, 0.0), axis=0, keepdims=True).astype(jnp.int32)
    slot_second = jnp.sum(jnp.where(is_second, spot, 0.0), axis=0, keepdims=True).astype(jnp.int32)
    slot = lax.broadcasted_iota(jnp.int32, (slots, tokens), 0)
    at_first = slot == slot_first
    at_second = slot == slot_second
    place = jnp.where(at_first | at_second, 1.0, 0.0).astype(jnp.bfloat16)
    back_ref[...] = place.T
    scale = jnp.sum(
        jnp.where(at_first, weight_ref[0:1, :], 0.0) + jnp.where(at_second, weight_ref[1:2, :], 0.0),
        axis=1,
        keepdims=True,
    )
    width = input_ref.shape[1]
    rows_ref[:, :width] = dot(place, input_ref[...]).astype(jnp.bfloat16)
    rows_ref[:, width:] = (scale * dot(place, grad_ref[...])).astype(jnp.bfloat16)


def pick(routes, route_weight, moe_input, moe_grad, owners, depth):
    tokens, width = moe_input.shape
    slots = owners * depth
    return pl.pallas_call(
        functools.partial(pick_kernel, owners, depth),
        out_shape=(
            jax.ShapeDtypeStruct((slots, 2 * width), jnp.bfloat16),
            jax.ShapeDtypeStruct((tokens, slots), jnp.bfloat16),
        ),
        compiler_params=params(32),
        cost_estimate=pl.CostEstimate(
            flops=4 * slots * tokens * width, bytes_accessed=8 * MIB, transcendentals=0
        ),
        name="pick_rows",
    )(routes.T, route_weight.T, moe_input, moe_grad)


def weights_kernel(*refs):
    own, other, (cols_ref, down_ref, rows_ref) = refs[:3], refs[3:6], refs[6:]
    tile = own[0].shape[1]
    for place, (gate_ref, up_ref, low_ref) in enumerate((own, other)):
        for kind, ref in enumerate((gate_ref, up_ref)):
            spot = slice((2 * kind + place) * tile, (2 * kind + place + 1) * tile)
            cols_ref[0, :, spot] = ref[...]
            rows_ref[0, spot, :] = ref[...].T
        down_ref[0, :, place * tile : (place + 1) * tile] = low_ref[...].T


def prepare_weights(own, other):
    width, half = own[0].shape
    tile = 128
    steps = half // tile
    cols = pl.BlockSpec((width, tile), lambda i: (0, i))
    down = pl.BlockSpec((tile, width), lambda i: (i, 0))
    return pl.pallas_call(
        weights_kernel,
        grid=(steps,),
        in_specs=[cols, cols, down] * 2,
        out_specs=[
            pl.BlockSpec((1, width, 4 * tile), lambda i: (i, 0, 0)),
            pl.BlockSpec((1, width, 2 * tile), lambda i: (i, 0, 0)),
            pl.BlockSpec((1, 4 * tile, width), lambda i: (i, 0, 0)),
        ],
        out_shape=(
            jax.ShapeDtypeStruct((steps, width, 4 * tile), jnp.bfloat16),
            jax.ShapeDtypeStruct((steps, width, 2 * tile), jnp.bfloat16),
            jax.ShapeDtypeStruct((steps, 4 * tile, width), jnp.bfloat16),
        ),
        compiler_params=params(48),
        cost_estimate=LIGHT,
        name="prepare_weights",
    )(*own, *other)


def expert_kernel(steps, rows_ref, cols_ref, down_ref, back_ref, out_ref, hidden):
    step = pl.program_id(0)
    width = rows_ref.shape[1] // 2
    pair = down_ref.shape[2]

    @pl.when(step < steps)
    def _():
        both_pre = dot(rows_ref[:, :width], cols_ref[0])
        gate_pre = both_pre[:, :pair]
        up_pre = both_pre[:, pair:]
        down_grad = dot(rows_ref[:, width:], down_ref[0])
        sig = jax.nn.sigmoid(gate_pre)
        hidden[step, :, :pair] = (
            down_grad * up_pre * sig * (1.0 + gate_pre * (1.0 - sig))
        ).astype(jnp.bfloat16)
        hidden[step, :, pair:] = (down_grad * gate_pre * sig).astype(jnp.bfloat16)

    @pl.when(step >= steps)
    def _():
        total = dot(hidden[0], back_ref[0])
        for i in range(1, steps):
            total += dot(hidden[i], back_ref[i])
        out_ref[...] = total.astype(jnp.bfloat16)


def experts(rows, cols, down, back):
    count, twice = rows.shape
    steps, width, quad = cols.shape
    tile = 512
    last = steps - 1
    turn = lambda i: jnp.maximum(i - steps, 0)
    return pl.pallas_call(
        functools.partial(expert_kernel, steps),
        grid=(steps + width // tile,),
        in_specs=[
            pl.BlockSpec((count, twice), lambda i: (0, 0)),
            pl.BlockSpec((1, width, quad), lambda i: (jnp.minimum(i, last), 0, 0)),
            pl.BlockSpec((1, width, quad // 2), lambda i: (jnp.minimum(i, last), 0, 0)),
            pl.BlockSpec((steps, quad, tile), lambda i: (0, 0, turn(i))),
        ],
        out_specs=pl.BlockSpec((count, tile), lambda i: (0, turn(i))),
        out_shape=jax.ShapeDtypeStruct((count, width), jnp.bfloat16),
        scratch_shapes=[pltpu.VMEM((steps, count, quad), jnp.bfloat16)],
        compiler_params=params(48),
        cost_estimate=LIGHT,
        name="expert_terms",
    )(rows, cols, down, back)


def shares_kernel(
    q_ref, key_ref, value_ref, prev_key_ref, prev_value_ref, prev_seg_ref, seg_row_ref, seg_col_ref,
    low_ref, turned_ref, query_ref, key_out, value_out,
):
    tokens = q_ref.shape[0]
    seg_col = seg_col_ref[...]
    row = lax.broadcasted_iota(jnp.int32, (tokens, tokens), 0)
    col = lax.broadcasted_iota(jnp.int32, (tokens, tokens), 1)
    own_seen = jnp.where((col <= row) & (seg_row_ref[...] == seg_col), 1.0, 0.0)
    prev_seg = prev_seg_ref[tokens : tokens + 16, :].astype(jnp.float32)[0:1, :]
    prev_seen = jnp.where(prev_seg == seg_col, 1.0, 0.0)
    seen = jnp.concatenate([prev_seen, own_seen], axis=1) > 0.5
    keys = jnp.concatenate([prev_key_ref[:tokens, :], key_ref[...]], axis=0)
    values = jnp.concatenate([prev_value_ref[:tokens, :], value_ref[...]], axis=0)
    key_out[0] = keys
    value_out[0] = values.T
    for head in range(GROUP):
        rows = slice(head * tokens, (head + 1) * tokens)
        query = q_ref[:, head * HD : (head + 1) * HD]
        scores = dot(query, keys, NT) * (HD**-0.5)
        masked = jnp.where(seen, scores, FLOOR)
        raised = jnp.where(seen, jnp.exp(masked - jnp.max(masked, axis=1, keepdims=True)), 0.0)
        shares = raised / jnp.sum(raised, axis=1, keepdims=True)
        low = shares.astype(jnp.bfloat16)
        low_ref[0, rows, :] = low
        turned_ref[0, :, rows] = low.T
        query_ref[0, rows, :] = query


def attention_shares(queries, key_heads, value_heads, prev, segs):
    tokens, width = queries.shape
    span = 2 * tokens
    stack = GROUP * tokens
    high = prev.shape[0]
    own = pl.BlockSpec((tokens, HD), lambda g: (0, g))
    group = lambda shape: pl.BlockSpec((1,) + shape, lambda g: (g, 0, 0))
    made = lambda shape: jax.ShapeDtypeStruct((KVH,) + shape, jnp.bfloat16)
    shapes = ((stack, span), (span, stack), (stack, HD), (span, HD), (HD, span))
    return pl.pallas_call(
        shares_kernel,
        grid=(KVH,),
        in_specs=[
            pl.BlockSpec((tokens, GROUP * HD), lambda g: (0, g)),
            own,
            own,
            pl.BlockSpec((high, HD), lambda g: (0, g)),
            pl.BlockSpec((high, HD), lambda g: (0, KVH + g)),
            pl.BlockSpec((high, HD), lambda g: (0, 0)),
            pl.BlockSpec((1, tokens), lambda g: (0, 0)),
            pl.BlockSpec((tokens, 1), lambda g: (0, 0)),
        ],
        out_specs=[group(shape) for shape in shapes],
        out_shape=[made(shape) for shape in shapes],
        compiler_params=params(32),
        cost_estimate=LIGHT,
        name="attention_shares",
    )(queries, key_heads, value_heads, prev, prev, prev, segs[None, :], segs[:, None])


def tail_kernel(
    plan, back_ref, place_ref, grad_ref, w_ref, low_ref, turned_ref, q_ref, key_ref, value_ref,
    moe_ref, query_out, key_out, value_out, sent_out, stream, held, sums,
):
    heads, tiles = plan
    step = pl.program_id(0)
    tokens = query_out.shape[0]

    @pl.when(step == 0)
    def _():
        moe = dot(place_ref[...], back_ref[...]).astype(jnp.bfloat16)
        moe_ref[...] = moe
        stream[...] = (grad_ref[...].astype(jnp.float32) + moe.astype(jnp.float32)).astype(jnp.bfloat16)
        held[...] = jnp.zeros_like(held)

    @pl.when((step == 0) | ((step > 1) & ((step - 1) % tiles == 0)))
    def _():
        sums[...] = jnp.zeros_like(sums)

    grads = held[...]
    head_grad = dot(stream[...], w_ref[0]).astype(jnp.bfloat16)
    low = low_ref[0].astype(jnp.float32)
    prob_grad = dot(grads, value_ref[0])
    row_dot = jnp.sum(low * prob_grad, axis=1, keepdims=True)
    score_grad = (low * (prob_grad - row_dot) * (HD**-0.5)).astype(jnp.bfloat16)
    query_grad = dot(score_grad, key_ref[0]).astype(jnp.bfloat16)
    sums[0] += dot(score_grad, q_ref[0], TN)
    sums[1] += dot(turned_ref[0], grads)
    for head in range(heads):
        cols = slice(head * HD, (head + 1) * HD)
        rows = slice(head * tokens, (head + 1) * tokens)
        query_out[:, cols] = query_grad[rows, :]
        held[rows, :] = head_grad[:, cols]

    @pl.when((step > 0) & (step % tiles == 0))
    def _():
        key_out[...] = sums[0, tokens:, :]
        value_out[...] = sums[1, tokens:, :]
        sent_out[...] = sums[:, :tokens, :].astype(jnp.bfloat16)


def tail(back, place, moe_grad, w_all, low, turned, query, keys, values):
    tokens, width = moe_grad.shape
    cols = w_all.shape[2]
    span = keys.shape[1]
    heads = 4
    tile = heads * HD
    tiles = cols // tile
    steps = KVH * tiles
    now = lambda i: jnp.minimum(i, steps - 1)
    was = lambda i: jnp.maximum(i - 1, 0)
    whole = lambda shape: pl.BlockSpec(shape, lambda i: (0,) * len(shape))
    group = lambda shape: pl.BlockSpec((1,) + shape, lambda i: (was(i) // tiles, 0, 0))
    rows = lambda shape: pl.BlockSpec((1,) + shape, lambda i: (was(i) // tiles, was(i) % tiles, 0))
    w_spec = pl.BlockSpec((1, width, tile), lambda i: (now(i) // tiles, 0, now(i) % tiles))
    kv = pl.BlockSpec((tokens, HD), lambda i: (0, was(i) // tiles))
    return pl.pallas_call(
        functools.partial(tail_kernel, (heads, tiles)),
        grid=(steps + 1,),
        in_specs=[
            whole(back.shape),
            whole(place.shape),
            whole(moe_grad.shape),
            w_spec,
            rows((heads * tokens, span)),
            pl.BlockSpec((1, span, heads * tokens), lambda i: (was(i) // tiles, 0, was(i) % tiles)),
            rows((heads * tokens, HD)),
            group((span, HD)),
            group((HD, span)),
        ],
        out_specs=[
            whole((tokens, width)),
            pl.BlockSpec((tokens, tile), lambda i: (0, was(i))),
            kv,
            kv,
            pl.BlockSpec((2, tokens, HD), lambda i: (0, 0, was(i) // tiles)),
        ],
        out_shape=(
            jax.ShapeDtypeStruct((tokens, width), jnp.bfloat16),
            jax.ShapeDtypeStruct((tokens, KVH * cols), jnp.bfloat16),
            jax.ShapeDtypeStruct((tokens, KVH * HD), jnp.float32),
            jax.ShapeDtypeStruct((tokens, KVH * HD), jnp.float32),
            jax.ShapeDtypeStruct((2, tokens, KVH * HD), jnp.bfloat16),
        ),
        scratch_shapes=[
            pltpu.VMEM((tokens, width), jnp.bfloat16),
            pltpu.VMEM((heads * tokens, HD), jnp.bfloat16),
            pltpu.VMEM((2, span, HD), jnp.float32),
        ],
        compiler_params=params(56),
        cost_estimate=pl.CostEstimate(
            flops=2 * tokens * width * KVH * cols, bytes_accessed=22 * MIB, transcendentals=0
        ),
        name="tail_attention",
    )(back, place, moe_grad, w_all, low, turned, query, keys, values)


def local(
    moe_input,
    moe_grad,
    routes,
    route_weight,
    w_gate,
    w_up,
    w_down,
    w_out,
    queries,
    key_heads,
    value_heads,
    segments,
):
    chips = ("far", "near", "low")
    blk = chips + ("core",)
    low = lax.axis_size("low")
    owners = 4 * low
    count = 2 * owners
    parts = lax.axis_size("groups")
    tokens, width = moe_input.shape
    depth = 2 * max(1, 3 * tokens * routes.shape[1] // (2 * count))
    swap = [(0, 1), (1, 0)]
    onward = [(i, i + 1) for i in range(count - 1)]
    backward = [(i + 1, i) for i in range(count - 1)]

    share_cols = w_out.shape[1] // parts
    w_share = lax.dynamic_slice_in_dim(w_out, lax.axis_index("groups") * share_cols, share_cols, 1)
    w_all = lax.all_gather(w_share, ("groups",) + blk, axis=0, tiled=True).reshape(parts, width, share_cols)
    rows, place = pick(routes, route_weight, moe_input, moe_grad, owners, depth)
    rows_in = lax.all_to_all(rows.reshape(owners, depth, 2 * width), chips, 0, 0, tiled=True)

    kv = jnp.concatenate([key_heads, value_heads], axis=1)
    segs = (segments + 1).astype(jnp.float32)
    seg_rows = jnp.zeros((16, kv.shape[1]), jnp.bfloat16).at[0, :tokens].set(segs.astype(jnp.bfloat16))
    prev = lax.ppermute(jnp.concatenate([kv, seg_rows], axis=0), blk, onward)

    own = (w_gate, w_up, w_down)
    other = tuple(lax.ppermute(w, "core", swap) for w in own)
    prepared = prepare_weights(own, other)
    rows_in, prepared, prev = lax.optimization_barrier((rows_in, prepared, prev))
    terms = experts(rows_in.reshape(owners * depth, 2 * width), *prepared)
    terms, prev = lax.optimization_barrier((terms, prev))
    back = lax.all_to_all(terms.reshape(owners, depth, width), chips, 0, 0, tiled=True)
    attention = attention_shares(queries, key_heads, value_heads, prev, segs)

    moe_input_grad, query_grad, key_part, value_part, sent = tail(
        back.reshape(owners * depth, width), place, moe_grad, w_all, *attention
    )
    later = lax.ppermute(sent, blk, backward).astype(jnp.float32)
    return (moe_input_grad, query_grad, key_part + later[0], value_part + later[1])


def solution(mesh):
    names = ("groups", "far", "near", "low", "core")
    shape = (mesh.shape["groups"], 2, 2, mesh.shape["blk"] // 8, 2)
    fine = jax.sharding.Mesh(mesh.devices.reshape(shape), names)
    blk = names[1:]
    by_tokens = P(names, None)
    return jax.shard_map(
        local,
        mesh=fine,
        in_specs=(
            by_tokens,
            by_tokens,
            by_tokens,
            by_tokens,
            P(None, blk),
            P(None, blk),
            P(blk, None),
            P(blk, None),
            by_tokens,
            by_tokens,
            by_tokens,
            P(names),
        ),
        out_specs=(by_tokens,) * 4,
        check_vma=False,
    )
```

```python
import functools

import jax
import jax.numpy as jnp
from jax import lax
from jax.experimental import pallas as pl
from jax.experimental.pallas import tpu as pltpu
from jax.sharding import PartitionSpec as P

KVH = 2
GROUP = 16
HD = 128
FLOOR = -1e30
MIB = 1 << 20
LIGHT = pl.CostEstimate(flops=0, bytes_accessed=0, transcendentals=0)

NT = (((1,), (1,)), ((), ()))
TN = (((0,), (0,)), ((), ()))


def dot(a, b, dims=(((1,), (0,)), ((), ()))):
    return lax.dot_general(a, b, dims, preferred_element_type=jnp.float32)


def params(mib):
    return pltpu.CompilerParams(vmem_limit_bytes=mib * MIB)


def pick_kernel(owners, depth, routes_ref, weight_ref, input_ref, grad_ref, rows_ref, back_ref):
    tokens = input_ref.shape[0]
    slots = owners * depth
    first = routes_ref[0:1, :]
    second = routes_ref[1:2, :]
    expert = lax.broadcasted_iota(jnp.int32, (owners, tokens), 0)
    is_first = first == expert
    is_second = second == expert
    member = jnp.where(is_first | is_second, 1.0, 0.0)
    before = lax.broadcasted_iota(jnp.int32, (tokens, tokens), 0) < lax.broadcasted_iota(
        jnp.int32, (tokens, tokens), 1
    )
    rank = dot(member.astype(jnp.bfloat16), jnp.where(before, 1.0, 0.0).astype(jnp.bfloat16))
    spot = (expert * depth).astype(jnp.float32) + rank
    slot_first = jnp.sum(jnp.where(is_first, spot, 0.0), axis=0, keepdims=True).astype(jnp.int32)
    slot_second = jnp.sum(jnp.where(is_second, spot, 0.0), axis=0, keepdims=True).astype(jnp.int32)
    slot = lax.broadcasted_iota(jnp.int32, (slots, tokens), 0)
    at_first = slot == slot_first
    at_second = slot == slot_second
    place = jnp.where(at_first | at_second, 1.0, 0.0).astype(jnp.bfloat16)
    back_ref[...] = place.T
    scale = jnp.sum(
        jnp.where(at_first, weight_ref[0:1, :], 0.0) + jnp.where(at_second, weight_ref[1:2, :], 0.0),
        axis=1,
        keepdims=True,
    )
    width = input_ref.shape[1]
    rows_ref[:, :width] = dot(place, input_ref[...]).astype(jnp.bfloat16)
    rows_ref[:, width:] = (scale * dot(place, grad_ref[...])).astype(jnp.bfloat16)


def pick(routes, route_weight, moe_input, moe_grad, owners, depth):
    tokens, width = moe_input.shape
    slots = owners * depth
    return pl.pallas_call(
        functools.partial(pick_kernel, owners, depth),
        out_shape=(
            jax.ShapeDtypeStruct((slots, 2 * width), jnp.bfloat16),
            jax.ShapeDtypeStruct((tokens, slots), jnp.bfloat16),
        ),
        compiler_params=params(32),
        cost_estimate=pl.CostEstimate(
            flops=4 * slots * tokens * width, bytes_accessed=8 * MIB, transcendentals=0
        ),
        name="pick_rows",
    )(routes.T, route_weight.T, moe_input, moe_grad)


def weights_kernel(*refs):
    own, other, (cols_ref, down_ref, rows_ref) = refs[:3], refs[3:6], refs[6:]
    tile = own[0].shape[1]
    for place, (gate_ref, up_ref, low_ref) in enumerate((own, other)):
        for kind, ref in enumerate((gate_ref, up_ref)):
            spot = slice((2 * kind + place) * tile, (2 * kind + place + 1) * tile)
            cols_ref[0, :, spot] = ref[...]
            rows_ref[0, spot, :] = ref[...].T
        down_ref[0, :, place * tile : (place + 1) * tile] = low_ref[...].T


def prepare_weights(own, other):
    width, half = own[0].shape
    tile = 128
    steps = half // tile
    cols = pl.BlockSpec((width, tile), lambda i: (0, i))
    down = pl.BlockSpec((tile, width), lambda i: (i, 0))
    return pl.pallas_call(
        weights_kernel,
        grid=(steps,),
        in_specs=[cols, cols, down] * 2,
        out_specs=[
            pl.BlockSpec((1, width, 4 * tile), lambda i: (i, 0, 0)),
            pl.BlockSpec((1, width, 2 * tile), lambda i: (i, 0, 0)),
            pl.BlockSpec((1, 4 * tile, width), lambda i: (i, 0, 0)),
        ],
        out_shape=(
            jax.ShapeDtypeStruct((steps, width, 4 * tile), jnp.bfloat16),
            jax.ShapeDtypeStruct((steps, width, 2 * tile), jnp.bfloat16),
            jax.ShapeDtypeStruct((steps, 4 * tile, width), jnp.bfloat16),
        ),
        compiler_params=params(48),
        cost_estimate=LIGHT,
        name="prepare_weights",
    )(*own, *other)


def expert_kernel(steps, rows_ref, cols_ref, down_ref, back_ref, out_ref, hidden):
    step = pl.program_id(0)
    width = rows_ref.shape[1] // 2
    pair = down_ref.shape[2]

    @pl.when(step < steps)
    def _():
        both_pre = dot(rows_ref[:, :width], cols_ref[0])
        gate_pre = both_pre[:, :pair]
        up_pre = both_pre[:, pair:]
        down_grad = dot(rows_ref[:, width:], down_ref[0])
        sig = jax.nn.sigmoid(gate_pre)
        hidden[step, :, :pair] = (
            down_grad * up_pre * sig * (1.0 + gate_pre * (1.0 - sig))
        ).astype(jnp.bfloat16)
        hidden[step, :, pair:] = (down_grad * gate_pre * sig).astype(jnp.bfloat16)

    @pl.when(step >= steps)
    def _():
        total = dot(hidden[0], back_ref[0])
        for i in range(1, steps):
            total += dot(hidden[i], back_ref[i])
        out_ref[...] = total.astype(jnp.bfloat16)


def experts(rows, cols, down, back):
    count, twice = rows.shape
    steps, width, quad = cols.shape
    tile = 512
    last = steps - 1
    turn = lambda i: jnp.maximum(i - steps, 0)
    return pl.pallas_call(
        functools.partial(expert_kernel, steps),
        grid=(steps + width // tile,),
        in_specs=[
            pl.BlockSpec((count, twice), lambda i: (0, 0)),
            pl.BlockSpec((1, width, quad), lambda i: (jnp.minimum(i, last), 0, 0)),
            pl.BlockSpec((1, width, quad // 2), lambda i: (jnp.minimum(i, last), 0, 0)),
            pl.BlockSpec((steps, quad, tile), lambda i: (0, 0, turn(i))),
        ],
        out_specs=pl.BlockSpec((count, tile), lambda i: (0, turn(i))),
        out_shape=jax.ShapeDtypeStruct((count, width), jnp.bfloat16),
        scratch_shapes=[pltpu.VMEM((steps, count, quad), jnp.bfloat16)],
        compiler_params=params(48),
        cost_estimate=LIGHT,
        name="expert_terms",
    )(rows, cols, down, back)


def shares_kernel(
    q_ref, key_ref, value_ref, prev_key_ref, prev_value_ref, prev_seg_ref, seg_row_ref, seg_col_ref,
    low_ref, turned_ref, query_ref, key_out, value_out,
):
    tokens = q_ref.shape[0]
    seg_col = seg_col_ref[...]
    row = lax.broadcasted_iota(jnp.int32, (tokens, tokens), 0)
    col = lax.broadcasted_iota(jnp.int32, (tokens, tokens), 1)
    own_seen = jnp.where((col <= row) & (seg_row_ref[...] == seg_col), 1.0, 0.0)
    prev_seg = prev_seg_ref[tokens : tokens + 16, :].astype(jnp.float32)[0:1, :]
    prev_seen = jnp.where(prev_seg == seg_col, 1.0, 0.0)
    seen = jnp.concatenate([prev_seen, own_seen], axis=1) > 0.5
    keys = jnp.concatenate([prev_key_ref[:tokens, :], key_ref[...]], axis=0)
    values = jnp.concatenate([prev_value_ref[:tokens, :], value_ref[...]], axis=0)
    key_out[0] = keys
    value_out[0] = values.T
    for head in range(GROUP):
        rows = slice(head * tokens, (head + 1) * tokens)
        query = q_ref[:, head * HD : (head + 1) * HD]
        scores = dot(query, keys, NT) * (HD**-0.5)
        masked = jnp.where(seen, scores, FLOOR)
        raised = jnp.where(seen, jnp.exp(masked - jnp.max(masked, axis=1, keepdims=True)), 0.0)
        shares = raised / jnp.sum(raised, axis=1, keepdims=True)
        low = shares.astype(jnp.bfloat16)
        low_ref[0, rows, :] = low
        turned_ref[0, :, rows] = low.T
        query_ref[0, rows, :] = query


def attention_shares(queries, key_heads, value_heads, prev, segs):
    tokens, width = queries.shape
    span = 2 * tokens
    stack = GROUP * tokens
    high = prev.shape[0]
    own = pl.BlockSpec((tokens, HD), lambda g: (0, g))
    group = lambda shape: pl.BlockSpec((1,) + shape, lambda g: (g, 0, 0))
    made = lambda shape: jax.ShapeDtypeStruct((KVH,) + shape, jnp.bfloat16)
    shapes = ((stack, span), (span, stack), (stack, HD), (span, HD), (HD, span))
    return pl.pallas_call(
        shares_kernel,
        grid=(KVH,),
        in_specs=[
            pl.BlockSpec((tokens, GROUP * HD), lambda g: (0, g)),
            own,
            own,
            pl.BlockSpec((high, HD), lambda g: (0, g)),
            pl.BlockSpec((high, HD), lambda g: (0, KVH + g)),
            pl.BlockSpec((high, HD), lambda g: (0, 0)),
            pl.BlockSpec((1, tokens), lambda g: (0, 0)),
            pl.BlockSpec((tokens, 1), lambda g: (0, 0)),
        ],
        out_specs=[group(shape) for shape in shapes],
        out_shape=[made(shape) for shape in shapes],
        compiler_params=params(32),
        cost_estimate=LIGHT,
        name="attention_shares",
    )(queries, key_heads, value_heads, prev, prev, prev, segs[None, :], segs[:, None])


def tail_kernel(
    plan, place_info, back_ref, place_ref, grad_ref, *refs
):
    heads, tiles = plan
    own_ref, pair_ref, own_across, own_swapped, pair_across, pair_swapped, last_ref, low_ref, turned_ref, q_ref, key_ref, value_ref, *refs = refs
    moe_ref, query_out, key_out, value_out, sent_out, stream, held, sums = refs
    step = pl.program_id(0)
    tokens = query_out.shape[0]
    part_size = stream.shape[2]
    half = last_ref.shape[1] // 2
    here, core = place_info[1], place_info[2]

    @pl.when(step == 0)
    def _():
        moe = dot(place_ref[...], back_ref[...]).astype(jnp.bfloat16)
        moe_ref[...] = moe
        added = (grad_ref[...].astype(jnp.float32) + moe.astype(jnp.float32)).astype(jnp.bfloat16)
        for eighth in range(8):
            stream[eighth] = added[:, eighth * part_size : (eighth + 1) * part_size]
        held[...] = jnp.zeros_like(held)

    @pl.when((step == 0) | ((step > 1) & ((step - 1) % tiles == 0)))
    def _():
        sums[...] = jnp.zeros_like(sums)

    def advance(pieces):
        grads = held[...]
        head_grad = None
        for turn, side, piece in pieces:
            rows = stream[2 * (here ^ turn) + side]
            part = dot(rows, piece.reshape(part_size, piece.shape[-1]))
            head_grad = part if head_grad is None else head_grad + part
        head_grad = head_grad.astype(jnp.bfloat16)
        low = low_ref[0].astype(jnp.float32)
        prob_grad = dot(grads, value_ref[0])
        row_dot = jnp.sum(low * prob_grad, axis=1, keepdims=True)
        score_grad = (low * (prob_grad - row_dot) * (HD**-0.5)).astype(jnp.bfloat16)
        query_grad = dot(score_grad, key_ref[0]).astype(jnp.bfloat16)
        sums[0] += dot(score_grad, q_ref[0], TN)
        sums[1] += dot(turned_ref[0], grads)
        for head in range(heads):
            cols = slice(head * HD, (head + 1) * HD)
            rows = slice(head * tokens, (head + 1) * tokens)
            query_out[:, cols] = query_grad[rows, :]
            held[rows, :] = head_grad[:, cols]

    sides = [(side, slice(side * half, (side + 1) * half)) for side in range(2)]
    last_pieces = [(3, side, last_ref[0, part]) for side, part in sides]

    @pl.when(step < tiles)
    def _():
        pieces = [(0, side, own_ref[part]) for side, part in sides]
        pieces += [(1 + i, side, pair_ref[part, i]) for i in range(2) for side, part in sides]
        advance(pieces + last_pieces)

    @pl.when(step >= tiles)
    def _():
        pieces = [(0, core, own_across[...]), (0, 1 - core, own_swapped[...])]
        for i in range(2):
            pieces += [(1 + i, core, pair_across[:, i]), (1 + i, 1 - core, pair_swapped[:, i])]
        advance(pieces + last_pieces)

    @pl.when((step > 0) & (step % tiles == 0))
    def _():
        key_out[...] = sums[0, tokens:, :]
        value_out[...] = sums[1, tokens:, :]
        sent_out[...] = sums[:, :tokens, :].astype(jnp.bfloat16)


def tail(place_info, back, place, moe_grad, pieces, w_last, low, turned, query, keys, values):
    tokens, width = moe_grad.shape
    spread, size, cols = w_last.shape[1:]
    span = keys.shape[1]
    heads = 4
    tile = heads * HD
    tiles = cols // tile
    steps = KVH * tiles
    was = lambda i: jnp.maximum(i - 1, 0)
    kv_group = lambda i, info: (was(i) // tiles) ^ info[0]
    whole = lambda shape: pl.BlockSpec(shape, lambda i, info: (0,) * len(shape))
    group = lambda shape: pl.BlockSpec((1,) + shape, lambda i, info: (kv_group(i, info), 0, 0))
    rows = lambda shape: pl.BlockSpec((1,) + shape, lambda i, info: (kv_group(i, info), was(i) % tiles, 0))
    now = lambda i: jnp.minimum(i, steps - 1)
    own_tile = lambda i: jnp.minimum(i, tiles - 1)
    other_tile = lambda i: jnp.minimum(jnp.maximum(i - tiles, 0), tiles - 1)
    both_spec = pl.BlockSpec(
        (1, spread, size, tile), lambda i, info: ((now(i) // tiles) ^ info[0], 0, 0, now(i) % tiles)
    )
    one = lambda count, turn: pl.BlockSpec((count, size, tile), lambda i, info: (0, 0, turn(i)))
    two = lambda count, turn: pl.BlockSpec((count, 2, size, tile), lambda i, info: (0, 0, 0, turn(i)))
    kv = pl.BlockSpec((tokens, HD), lambda i, info: (0, kv_group(i, info)))
    return pl.pallas_call(
        functools.partial(tail_kernel, (heads, tiles)),
        grid_spec=pltpu.PrefetchScalarGridSpec(
            num_scalar_prefetch=1,
            grid=(steps + 1,),
            in_specs=[whole(back.shape), whole(place.shape), whole(moe_grad.shape)]
            + [one(spread, own_tile), two(spread, own_tile)]
            + [one(spread // 2, other_tile)] * 2
            + [two(spread // 2, other_tile)] * 2
            + [both_spec]
            + [
                rows((heads * tokens, span)),
                pl.BlockSpec(
                    (1, span, heads * tokens), lambda i, info: (kv_group(i, info), 0, was(i) % tiles)
                ),
                rows((heads * tokens, HD)),
                group((span, HD)),
                group((HD, span)),
            ],
            out_specs=[
                whole((tokens, width)),
                pl.BlockSpec(
                    (tokens, tile), lambda i, info: (0, kv_group(i, info) * tiles + was(i) % tiles)
                ),
                kv,
                kv,
                pl.BlockSpec((2, tokens, HD), lambda i, info: (0, 0, kv_group(i, info))),
            ],
            scratch_shapes=[
                pltpu.VMEM((8, tokens, spread * size // 2), jnp.bfloat16),
                pltpu.VMEM((heads * tokens, HD), jnp.bfloat16),
                pltpu.VMEM((2, span, HD), jnp.float32),
            ],
        ),
        out_shape=(
            jax.ShapeDtypeStruct((tokens, width), jnp.bfloat16),
            jax.ShapeDtypeStruct((tokens, KVH * cols), jnp.bfloat16),
            jax.ShapeDtypeStruct((tokens, KVH * HD), jnp.float32),
            jax.ShapeDtypeStruct((tokens, KVH * HD), jnp.float32),
            jax.ShapeDtypeStruct((2, tokens, KVH * HD), jnp.bfloat16),
        ),
        compiler_params=params(56),
        cost_estimate=pl.CostEstimate(
            flops=2 * tokens * width * KVH * cols, bytes_accessed=22 * MIB, transcendentals=0
        ),
        name="tail_attention",
    )(place_info, back, place, moe_grad, *pieces, w_last, low, turned, query, keys, values)


def local(
    moe_input,
    moe_grad,
    routes,
    route_weight,
    w_gate,
    w_up,
    w_down,
    w_out,
    queries,
    key_heads,
    value_heads,
    segments,
):
    chips = ("far", "near", "low")
    blk = chips + ("core",)
    low = lax.axis_size("low")
    owners = 4 * low
    count = 2 * owners
    parts = lax.axis_size("groups")
    tokens, width = moe_input.shape
    depth = 2 * max(1, 3 * tokens * routes.shape[1] // (2 * count))
    swap = [(0, 1), (1, 0)]
    onward = [(i, i + 1) for i in range(count - 1)]
    backward = [(i + 1, i) for i in range(count - 1)]

    share_cols = w_out.shape[1] // parts
    w_share = lax.dynamic_slice_in_dim(w_out, lax.axis_index("groups") * share_cols, share_cols, 1)
    w_near = lax.ppermute(w_share, "near", swap)
    w_far = lax.ppermute(w_share, "far", swap)

    kv = jnp.concatenate([key_heads, value_heads], axis=1)
    segs = (segments + 1).astype(jnp.float32)
    seg_rows = jnp.zeros((16, kv.shape[1]), jnp.bfloat16).at[0, :tokens].set(segs.astype(jnp.bfloat16))
    prev = lax.ppermute(jnp.concatenate([kv, seg_rows], axis=0), blk, onward)

    own = (w_gate, w_up, w_down)
    other = tuple(lax.ppermute(w, "core", swap) for w in own)
    rows, place = pick(routes, route_weight, moe_input, moe_grad, owners, depth)
    plane = ("groups", "low", "core")
    core = lax.axis_index("core")
    w_own = lax.all_gather(w_share, plane[1:], axis=0, tiled=False)
    rows, w_near, w_far, w_own, prev, other = lax.optimization_barrier((rows, w_near, w_far, w_own, prev, other))

    half_of = lambda w: lax.dynamic_slice_in_dim(w, core * low, low, 0)
    rows_in = lax.all_to_all(rows.reshape(owners, depth, 2 * width), chips, 0, 0, tiled=True)
    own_across = lax.ppermute(half_of(w_own), "groups", swap)
    w_pair = lax.all_gather(jnp.stack([w_near, w_far]), plane[1:], axis=0, tiled=False)
    w_half = half_of(w_pair)
    w_last = lax.ppermute(w_far, "near", swap)
    prepared = prepare_weights(own, other)
    attention = attention_shares(queries, key_heads, value_heads, prev, segs)

    rows_in, prepared, attention, own_across, w_pair, w_half, w_last = lax.optimization_barrier(
        (rows_in, prepared, attention, own_across, w_pair, w_half, w_last)
    )
    own_swapped = lax.ppermute(own_across, "core", swap)
    pair_across = lax.ppermute(w_half, "groups", swap)
    pair_swapped = lax.ppermute(pair_across, "core", swap)
    w_last = lax.all_gather(w_last, plane, axis=0, tiled=False).reshape(parts, 2 * low, *w_share.shape)
    terms = experts(rows_in.reshape(owners * depth, 2 * width), *prepared)
    back = lax.all_to_all(terms.reshape(owners, depth, width), chips, 0, 0, tiled=True)

    z = 2 * lax.axis_index("far") + lax.axis_index("near")
    moe_input_grad, query_grad, key_part, value_part, sent = tail(
        jnp.stack([lax.axis_index("groups"), z, core]).astype(jnp.int32),
        back.reshape(owners * depth, width), place, moe_grad,
        (w_own, w_pair, own_across, own_swapped, pair_across, pair_swapped), w_last, *attention,
    )
    later = lax.ppermute(sent, blk, backward).astype(jnp.float32)
    return (moe_input_grad, query_grad, key_part + later[0], value_part + later[1])


def solution(mesh):
    names = ("groups", "far", "near", "low", "core")
    shape = (mesh.shape["groups"], 2, 2, mesh.shape["blk"] // 8, 2)
    fine = jax.sharding.Mesh(mesh.devices.reshape(shape), names)
    blk = names[1:]
    by_tokens = P(names, None)
    return jax.shard_map(
        local,
        mesh=fine,
        in_specs=(
            by_tokens,
            by_tokens,
            by_tokens,
            by_tokens,
            P(None, blk),
            P(None, blk),
            P(blk, None),
            P(blk, None),
            by_tokens,
            by_tokens,
            by_tokens,
            P(names),
        ),
        out_specs=(by_tokens,) * 4,
        check_vma=False,
    )
```

```python
import functools

import jax
import jax.numpy as jnp
from jax import lax
from jax.experimental import pallas as pl
from jax.experimental.pallas import tpu as pltpu
from jax.sharding import PartitionSpec as P

KVH = 2
GROUP = 16
HD = 128
FLOOR = -1e30
MIB = 1 << 20
LIGHT = pl.CostEstimate(flops=0, bytes_accessed=0, transcendentals=0)

NT = (((1,), (1,)), ((), ()))
TN = (((0,), (0,)), ((), ()))


def dot(a, b, dims=(((1,), (0,)), ((), ()))):
    return lax.dot_general(a, b, dims, preferred_element_type=jnp.float32)


def params(mib):
    return pltpu.CompilerParams(vmem_limit_bytes=mib * MIB)


def pick_kernel(owners, depth, routes_ref, weight_ref, input_ref, grad_ref, rows_ref, back_ref):
    tokens = input_ref.shape[0]
    slots = owners * depth
    first = routes_ref[0:1, :]
    second = routes_ref[1:2, :]
    expert = lax.broadcasted_iota(jnp.int32, (owners, tokens), 0)
    is_first = first == expert
    is_second = second == expert
    member = jnp.where(is_first | is_second, 1.0, 0.0)
    before = lax.broadcasted_iota(jnp.int32, (tokens, tokens), 0) < lax.broadcasted_iota(
        jnp.int32, (tokens, tokens), 1
    )
    rank = dot(member.astype(jnp.bfloat16), jnp.where(before, 1.0, 0.0).astype(jnp.bfloat16))
    spot = (expert * depth).astype(jnp.float32) + rank
    slot_first = jnp.sum(jnp.where(is_first, spot, 0.0), axis=0, keepdims=True).astype(jnp.int32)
    slot_second = jnp.sum(jnp.where(is_second, spot, 0.0), axis=0, keepdims=True).astype(jnp.int32)
    slot = lax.broadcasted_iota(jnp.int32, (slots, tokens), 0)
    at_first = slot == slot_first
    at_second = slot == slot_second
    place = jnp.where(at_first | at_second, 1.0, 0.0).astype(jnp.bfloat16)
    back_ref[...] = place.T
    scale = jnp.sum(
        jnp.where(at_first, weight_ref[0:1, :], 0.0) + jnp.where(at_second, weight_ref[1:2, :], 0.0),
        axis=1,
        keepdims=True,
    )
    width = input_ref.shape[1]
    rows_ref[:, :width] = dot(place, input_ref[...]).astype(jnp.bfloat16)
    rows_ref[:, width:] = (scale * dot(place, grad_ref[...])).astype(jnp.bfloat16)


def pick(routes, route_weight, moe_input, moe_grad, owners, depth):
    tokens, width = moe_input.shape
    slots = owners * depth
    return pl.pallas_call(
        functools.partial(pick_kernel, owners, depth),
        out_shape=(
            jax.ShapeDtypeStruct((slots, 2 * width), jnp.bfloat16),
            jax.ShapeDtypeStruct((tokens, slots), jnp.bfloat16),
        ),
        compiler_params=params(32),
        cost_estimate=pl.CostEstimate(
            flops=4 * slots * tokens * width, bytes_accessed=8 * MIB, transcendentals=0
        ),
        name="pick_rows",
    )(routes.T, route_weight.T, moe_input, moe_grad)


def weights_kernel(*refs):
    own, other, (cols_ref, down_ref, rows_ref) = refs[:3], refs[3:6], refs[6:]
    tile = own[0].shape[1]
    for place, (gate_ref, up_ref, low_ref) in enumerate((own, other)):
        for kind, ref in enumerate((gate_ref, up_ref)):
            spot = slice((2 * kind + place) * tile, (2 * kind + place + 1) * tile)
            cols_ref[0, :, spot] = ref[...]
            rows_ref[0, spot, :] = ref[...].T
        down_ref[0, :, place * tile : (place + 1) * tile] = low_ref[...].T


def prepare_weights(own, other):
    width, half = own[0].shape
    tile = 128
    steps = half // tile
    cols = pl.BlockSpec((width, tile), lambda i: (0, i))
    down = pl.BlockSpec((tile, width), lambda i: (i, 0))
    return pl.pallas_call(
        weights_kernel,
        grid=(steps,),
        in_specs=[cols, cols, down] * 2,
        out_specs=[
            pl.BlockSpec((1, width, 4 * tile), lambda i: (i, 0, 0)),
            pl.BlockSpec((1, width, 2 * tile), lambda i: (i, 0, 0)),
            pl.BlockSpec((1, 4 * tile, width), lambda i: (i, 0, 0)),
        ],
        out_shape=(
            jax.ShapeDtypeStruct((steps, width, 4 * tile), jnp.bfloat16),
            jax.ShapeDtypeStruct((steps, width, 2 * tile), jnp.bfloat16),
            jax.ShapeDtypeStruct((steps, 4 * tile, width), jnp.bfloat16),
        ),
        compiler_params=params(48),
        cost_estimate=LIGHT,
        name="prepare_weights",
    )(*own, *other)


def expert_kernel(steps, rows_ref, cols_ref, down_ref, back_ref, out_ref, hidden):
    step = pl.program_id(0)
    width = rows_ref.shape[1] // 2
    pair = down_ref.shape[2]

    @pl.when(step < steps)
    def _():
        both_pre = dot(rows_ref[:, :width], cols_ref[0])
        gate_pre = both_pre[:, :pair]
        up_pre = both_pre[:, pair:]
        down_grad = dot(rows_ref[:, width:], down_ref[0])
        sig = jax.nn.sigmoid(gate_pre)
        hidden[step, :, :pair] = (
            down_grad * up_pre * sig * (1.0 + gate_pre * (1.0 - sig))
        ).astype(jnp.bfloat16)
        hidden[step, :, pair:] = (down_grad * gate_pre * sig).astype(jnp.bfloat16)

    @pl.when(step >= steps)
    def _():
        total = dot(hidden[0], back_ref[0])
        for i in range(1, steps):
            total += dot(hidden[i], back_ref[i])
        out_ref[...] = total.astype(jnp.bfloat16)


def experts(rows, cols, down, back):
    count, twice = rows.shape
    steps, width, quad = cols.shape
    tile = 512
    last = steps - 1
    turn = lambda i: jnp.maximum(i - steps, 0)
    return pl.pallas_call(
        functools.partial(expert_kernel, steps),
        grid=(steps + width // tile,),
        in_specs=[
            pl.BlockSpec((count, twice), lambda i: (0, 0)),
            pl.BlockSpec((1, width, quad), lambda i: (jnp.minimum(i, last), 0, 0)),
            pl.BlockSpec((1, width, quad // 2), lambda i: (jnp.minimum(i, last), 0, 0)),
            pl.BlockSpec((steps, quad, tile), lambda i: (0, 0, turn(i))),
        ],
        out_specs=pl.BlockSpec((count, tile), lambda i: (0, turn(i))),
        out_shape=jax.ShapeDtypeStruct((count, width), jnp.bfloat16),
        scratch_shapes=[pltpu.VMEM((steps, count, quad), jnp.bfloat16)],
        compiler_params=params(24),
        cost_estimate=LIGHT,
        name="expert_terms",
    )(rows, cols, down, back)


def shares_kernel(
    q_ref, key_ref, value_ref, prev_key_ref, prev_value_ref, prev_seg_ref, seg_row_ref, seg_col_ref,
    low_ref, turned_ref, query_ref, key_out, value_out,
):
    tokens = q_ref.shape[0]
    seg_col = seg_col_ref[...]
    row = lax.broadcasted_iota(jnp.int32, (tokens, tokens), 0)
    col = lax.broadcasted_iota(jnp.int32, (tokens, tokens), 1)
    own_seen = jnp.where((col <= row) & (seg_row_ref[...] == seg_col), 1.0, 0.0)
    prev_seg = prev_seg_ref[tokens : tokens + 16, :].astype(jnp.float32)[0:1, :]
    prev_seen = jnp.where(prev_seg == seg_col, 1.0, 0.0)
    seen = jnp.concatenate([prev_seen, own_seen], axis=1) > 0.5
    keys = jnp.concatenate([prev_key_ref[:tokens, :], key_ref[...]], axis=0)
    values = jnp.concatenate([prev_value_ref[:tokens, :], value_ref[...]], axis=0)
    key_out[0] = keys
    value_out[0] = values.T
    for head in range(GROUP):
        rows = slice(head * tokens, (head + 1) * tokens)
        query = q_ref[:, head * HD : (head + 1) * HD]
        scores = dot(query, keys, NT) * (HD**-0.5)
        masked = jnp.where(seen, scores, FLOOR)
        raised = jnp.where(seen, jnp.exp(masked - jnp.max(masked, axis=1, keepdims=True)), 0.0)
        shares = raised / jnp.sum(raised, axis=1, keepdims=True)
        low = shares.astype(jnp.bfloat16)
        low_ref[0, rows, :] = low
        turned_ref[0, :, rows] = low.T
        query_ref[0, rows, :] = query


def attention_shares(queries, key_heads, value_heads, prev, segs):
    tokens, width = queries.shape
    span = 2 * tokens
    stack = GROUP * tokens
    high = prev.shape[0]
    own = pl.BlockSpec((tokens, HD), lambda g: (0, g))
    group = lambda shape: pl.BlockSpec((1,) + shape, lambda g: (g, 0, 0))
    made = lambda shape: jax.ShapeDtypeStruct((KVH,) + shape, jnp.bfloat16)
    shapes = ((stack, span), (span, stack), (stack, HD), (span, HD), (HD, span))
    return pl.pallas_call(
        shares_kernel,
        grid=(KVH,),
        in_specs=[
            pl.BlockSpec((tokens, GROUP * HD), lambda g: (0, g)),
            own,
            own,
            pl.BlockSpec((high, HD), lambda g: (0, g)),
            pl.BlockSpec((high, HD), lambda g: (0, KVH + g)),
            pl.BlockSpec((high, HD), lambda g: (0, 0)),
            pl.BlockSpec((1, tokens), lambda g: (0, 0)),
            pl.BlockSpec((tokens, 1), lambda g: (0, 0)),
        ],
        out_specs=[group(shape) for shape in shapes],
        out_shape=[made(shape) for shape in shapes],
        compiler_params=params(32),
        cost_estimate=LIGHT,
        name="attention_shares",
    )(queries, key_heads, value_heads, prev, prev, prev, segs[None, :], segs[:, None])


def tail_kernel(
    plan, place_info, back_ref, place_ref, grad_ref, *refs
):
    heads, tiles = plan
    mine, across, swapped, refs = refs[:3], refs[3:6], refs[6:9], refs[9:]
    last_ref, low_ref, turned_ref, q_ref, key_ref, value_ref, *refs = refs
    moe_ref, query_out, kept_out, sent_out, stream, held, sums = refs
    step = pl.program_id(0)
    tokens = query_out.shape[0]
    part_size = stream.shape[2]
    half = last_ref.shape[1] // 2
    here, core = place_info[1], place_info[2]

    @pl.when(step == 0)
    def _():
        moe = dot(place_ref[...], back_ref[...]).astype(jnp.bfloat16)
        moe_ref[...] = moe
        added = (grad_ref[...].astype(jnp.float32) + moe.astype(jnp.float32)).astype(jnp.bfloat16)
        for eighth in range(8):
            stream[eighth] = added[:, eighth * part_size : (eighth + 1) * part_size]

    @pl.when((step > 0) & ((step - 1) % tiles == 0))
    def _():
        sums[...] = jnp.zeros_like(sums)

    def project(pieces):
        head_grad = None
        for turn, side, piece in pieces:
            rows = stream[2 * (here ^ turn) + side]
            part = dot(rows, piece.reshape(part_size, piece.shape[-1]))
            head_grad = part if head_grad is None else head_grad + part
        return head_grad.astype(jnp.bfloat16)

    def hold(head_grad):
        for head in range(heads):
            held[head * tokens : (head + 1) * tokens, :] = head_grad[:, head * HD : (head + 1) * HD]

    def attend():
        grads = held[...]
        low = low_ref[0].astype(jnp.float32)
        prob_grad = dot(grads, value_ref[0])
        row_dot = jnp.sum(low * prob_grad, axis=1, keepdims=True)
        score_grad = (low * (prob_grad - row_dot) * (HD**-0.5)).astype(jnp.bfloat16)
        query_grad = dot(score_grad, key_ref[0]).astype(jnp.bfloat16)
        sums[0] += dot(score_grad, q_ref[0], TN)
        sums[1] += dot(turned_ref[0], grads)
        for head in range(heads):
            query_out[:, head * HD : (head + 1) * HD] = query_grad[head * tokens : (head + 1) * tokens, :]

    sides = [(side, slice(side * half, (side + 1) * half)) for side in range(2)]

    def own_pieces():
        pieces = [(turn, side, mine[turn][part]) for turn in range(3) for side, part in sides]
        return pieces + [(3, side, last_ref[0, part]) for side, part in sides]

    def other_pieces():
        pieces = []
        for turn in range(3):
            pieces += [(turn, core, across[turn][...]), (turn, 1 - core, swapped[turn][...])]
        return pieces + [(3, side, last_ref[0, part]) for side, part in sides]

    @pl.when(step == 0)
    def _():
        hold(project(own_pieces()))

    @pl.when((step > 0) & (step < tiles))
    def _():
        head_grad = project(own_pieces())
        attend()
        hold(head_grad)

    @pl.when((step >= tiles) & (step < 2 * tiles))
    def _():
        head_grad = project(other_pieces())
        attend()
        hold(head_grad)

    @pl.when(step == 2 * tiles)
    def _():
        attend()

    @pl.when((step > 0) & (step % tiles == 0))
    def _():
        kept_out[...] = sums[:, tokens:, :]
        sent_out[...] = sums[:, :tokens, :].astype(jnp.bfloat16)


def tail(place_info, back, place, moe_grad, pieces, w_last, low, turned, query, keys, values):
    tokens, width = moe_grad.shape
    spread, size, cols = w_last.shape[1:]
    span = keys.shape[1]
    heads = 4
    tile = heads * HD
    tiles = cols // tile
    steps = KVH * tiles
    was = lambda i: jnp.maximum(i - 1, 0)
    kv_group = lambda i, info: (was(i) // tiles) ^ info[0]
    whole = lambda shape: pl.BlockSpec(shape, lambda i, info: (0,) * len(shape))
    group = lambda shape: pl.BlockSpec((1,) + shape, lambda i, info: (kv_group(i, info), 0, 0))
    rows = lambda shape: pl.BlockSpec((1,) + shape, lambda i, info: (kv_group(i, info), was(i) % tiles, 0))
    now = lambda i: jnp.minimum(i, steps - 1)
    own_tile = lambda i: jnp.minimum(i, tiles - 1)
    other_tile = lambda i: jnp.minimum(jnp.maximum(i - tiles, 0), tiles - 1)
    both_spec = pl.BlockSpec(
        (1, spread, size, tile), lambda i, info: ((now(i) // tiles) ^ info[0], 0, 0, now(i) % tiles)
    )
    one = lambda count, turn: pl.BlockSpec((count, size, tile), lambda i, info: (0, 0, turn(i)))
    kv = pl.BlockSpec((2, tokens, HD), lambda i, info: (0, 0, kv_group(i, info)))
    return pl.pallas_call(
        functools.partial(tail_kernel, (heads, tiles)),
        grid_spec=pltpu.PrefetchScalarGridSpec(
            num_scalar_prefetch=1,
            grid=(steps + 1,),
            in_specs=[whole(back.shape), whole(place.shape), whole(moe_grad.shape)]
            + [one(spread, own_tile)] * 3
            + [one(spread // 2, other_tile)] * 6
            + [both_spec]
            + [
                rows((heads * tokens, span)),
                pl.BlockSpec(
                    (1, span, heads * tokens), lambda i, info: (kv_group(i, info), 0, was(i) % tiles)
                ),
                rows((heads * tokens, HD)),
                group((span, HD)),
                group((HD, span)),
            ],
            out_specs=[
                whole((tokens, width)),
                pl.BlockSpec(
                    (tokens, tile), lambda i, info: (0, kv_group(i, info) * tiles + was(i) % tiles)
                ),
                kv,
                kv,
            ],
            scratch_shapes=[
                pltpu.VMEM((8, tokens, spread * size // 2), jnp.bfloat16),
                pltpu.VMEM((heads * tokens, HD), jnp.bfloat16),
                pltpu.VMEM((2, span, HD), jnp.float32),
            ],
        ),
        out_shape=(
            jax.ShapeDtypeStruct((tokens, width), jnp.bfloat16),
            jax.ShapeDtypeStruct((tokens, KVH * cols), jnp.bfloat16),
            jax.ShapeDtypeStruct((2, tokens, KVH * HD), jnp.float32),
            jax.ShapeDtypeStruct((2, tokens, KVH * HD), jnp.bfloat16),
        ),
        compiler_params=params(40),
        cost_estimate=pl.CostEstimate(
            flops=2 * tokens * width * KVH * cols, bytes_accessed=22 * MIB, transcendentals=0
        ),
        name="tail_attention",
    )(place_info, back, place, moe_grad, *pieces, w_last, low, turned, query, keys, values)


def finish_kernel(kept_ref, later_ref, key_ref, value_ref):
    for kind, out_ref in enumerate((key_ref, value_ref)):
        out_ref[...] = kept_ref[kind] + later_ref[kind].astype(jnp.float32)


def finish(kept, later):
    out = jax.ShapeDtypeStruct(kept.shape[1:], jnp.float32)
    return pl.pallas_call(
        finish_kernel, out_shape=(out, out), compiler_params=params(16), cost_estimate=LIGHT, name="finish"
    )(kept, later)


def local(
    moe_input,
    moe_grad,
    routes,
    route_weight,
    w_gate,
    w_up,
    w_down,
    w_out,
    queries,
    key_heads,
    value_heads,
    segments,
):
    chips = ("far", "near", "low")
    blk = chips + ("core",)
    low = lax.axis_size("low")
    owners = 4 * low
    count = 2 * owners
    parts = lax.axis_size("groups")
    tokens, width = moe_input.shape
    depth = 2 * max(1, 3 * tokens * routes.shape[1] // (2 * count))
    swap = [(0, 1), (1, 0)]
    onward = [(i, i + 1) for i in range(count - 1)]
    backward = [(i + 1, i) for i in range(count - 1)]

    share_cols = w_out.shape[1] // parts
    w_share = lax.dynamic_slice_in_dim(w_out, lax.axis_index("groups") * share_cols, share_cols, 1)
    w_near = lax.ppermute(w_share, "near", swap)
    w_far = lax.ppermute(w_share, "far", swap)

    own = (w_gate, w_up, w_down)
    other = tuple(lax.ppermute(w, "core", swap) for w in own)
    rows, place = pick(routes, route_weight, moe_input, moe_grad, owners, depth)
    plane = ("groups", "low", "core")
    core = lax.axis_index("core")
    w_own = lax.all_gather(w_share, plane[1:], axis=0, tiled=False)
    rows, w_near, w_far, w_own = lax.optimization_barrier((rows, w_near, w_far, w_own))

    half_of = lambda w: lax.dynamic_slice_in_dim(w, core * low, low, 0)
    rows_in = lax.all_to_all(rows.reshape(owners, depth, 2 * width), chips, 0, 0, tiled=True)
    own_across = lax.ppermute(half_of(w_own), "groups", swap)
    near_rows = lax.all_gather(w_near, plane[1:], axis=0, tiled=False)
    near_across = lax.ppermute(half_of(near_rows), "groups", swap)
    far_rows = lax.all_gather(w_far, plane[1:], axis=0, tiled=False)
    far_half = half_of(far_rows)
    w_last = lax.ppermute(w_far, "near", swap)
    prepared = prepare_weights(own, other)
    kv = jnp.concatenate([key_heads, value_heads], axis=1)
    segs = (segments + 1).astype(jnp.float32)
    seg_rows = jnp.zeros((16, kv.shape[1]), jnp.bfloat16).at[0, :tokens].set(segs.astype(jnp.bfloat16))
    prev = lax.ppermute(jnp.concatenate([kv, seg_rows], axis=0), blk, onward)

    rows_in, prepared, prev, own_across, near_across, far_rows, far_half, w_last = lax.optimization_barrier(
        (rows_in, prepared, prev, own_across, near_across, far_rows, far_half, w_last)
    )
    far_across = lax.ppermute(far_half, "groups", swap)
    across = (own_across, near_across, far_across)
    swapped = tuple(lax.ppermute(w, "core", swap) for w in across)
    w_last = lax.all_gather(w_last, plane, axis=0, tiled=False).reshape(parts, 2 * low, *w_share.shape)
    terms = experts(rows_in.reshape(owners * depth, 2 * width), *prepared)
    terms, prev = lax.optimization_barrier((terms, prev))
    back = lax.all_to_all(terms.reshape(owners, depth, width), chips, 0, 0, tiled=True)
    attention = attention_shares(queries, key_heads, value_heads, prev, segs)

    z = 2 * lax.axis_index("far") + lax.axis_index("near")
    moe_input_grad, query_grad, kept, sent = tail(
        jnp.stack([lax.axis_index("groups"), z, core]).astype(jnp.int32),
        back.reshape(owners * depth, width), place, moe_grad,
        (w_own, near_rows, far_rows, *across, *swapped), w_last, *attention,
    )
    return (moe_input_grad, query_grad, *finish(kept, lax.ppermute(sent, blk, backward)))


def solution(mesh):
    names = ("groups", "far", "near", "low", "core")
    shape = (mesh.shape["groups"], 2, 2, mesh.shape["blk"] // 8, 2)
    fine = jax.sharding.Mesh(mesh.devices.reshape(shape), names)
    blk = names[1:]
    by_tokens = P(names, None)
    return jax.shard_map(
        local,
        mesh=fine,
        in_specs=(
            by_tokens,
            by_tokens,
            by_tokens,
            by_tokens,
            P(None, blk),
            P(None, blk),
            P(blk, None),
            P(blk, None),
            by_tokens,
            by_tokens,
            by_tokens,
            P(names),
        ),
        out_specs=(by_tokens,) * 4,
        check_vma=False,
    )
```

```python
import functools

import jax
import jax.numpy as jnp
from jax import lax
from jax.experimental import pallas as pl
from jax.experimental.pallas import tpu as pltpu
from jax.sharding import PartitionSpec as P

KVH = 2
GROUP = 16
HD = 128
FLOOR = -1e30
MIB = 1 << 20
LIGHT = pl.CostEstimate(flops=0, bytes_accessed=0, transcendentals=0)

NT = (((1,), (1,)), ((), ()))
TN = (((0,), (0,)), ((), ()))


def dot(a, b, dims=(((1,), (0,)), ((), ()))):
    return lax.dot_general(a, b, dims, preferred_element_type=jnp.float32)


def params(mib):
    return pltpu.CompilerParams(vmem_limit_bytes=mib * MIB)


def pick_kernel(owners, depth, routes_ref, weight_ref, input_ref, grad_ref, rows_ref, back_ref):
    tokens = input_ref.shape[0]
    slots = owners * depth
    first = routes_ref[0:1, :]
    second = routes_ref[1:2, :]
    expert = lax.broadcasted_iota(jnp.int32, (owners, tokens), 0)
    is_first = first == expert
    is_second = second == expert
    member = jnp.where(is_first | is_second, 1.0, 0.0)
    before = lax.broadcasted_iota(jnp.int32, (tokens, tokens), 0) < lax.broadcasted_iota(
        jnp.int32, (tokens, tokens), 1
    )
    rank = dot(member.astype(jnp.bfloat16), jnp.where(before, 1.0, 0.0).astype(jnp.bfloat16))
    spot = (expert * depth).astype(jnp.float32) + rank
    slot_first = jnp.sum(jnp.where(is_first, spot, 0.0), axis=0, keepdims=True).astype(jnp.int32)
    slot_second = jnp.sum(jnp.where(is_second, spot, 0.0), axis=0, keepdims=True).astype(jnp.int32)
    slot = lax.broadcasted_iota(jnp.int32, (slots, tokens), 0)
    at_first = slot == slot_first
    at_second = slot == slot_second
    place = jnp.where(at_first | at_second, 1.0, 0.0).astype(jnp.bfloat16)
    back_ref[...] = place.T
    scale = jnp.sum(
        jnp.where(at_first, weight_ref[0:1, :], 0.0) + jnp.where(at_second, weight_ref[1:2, :], 0.0),
        axis=1,
        keepdims=True,
    )
    width = input_ref.shape[1]
    rows_ref[:, :width] = dot(place, input_ref[...]).astype(jnp.bfloat16)
    rows_ref[:, width:] = (scale * dot(place, grad_ref[...])).astype(jnp.bfloat16)


def pick(routes, route_weight, moe_input, moe_grad, owners, depth):
    tokens, width = moe_input.shape
    slots = owners * depth
    return pl.pallas_call(
        functools.partial(pick_kernel, owners, depth),
        out_shape=(
            jax.ShapeDtypeStruct((slots, 2 * width), jnp.bfloat16),
            jax.ShapeDtypeStruct((tokens, slots), jnp.bfloat16),
        ),
        compiler_params=params(32),
        cost_estimate=pl.CostEstimate(
            flops=4 * slots * tokens * width, bytes_accessed=8 * MIB, transcendentals=0
        ),
        name="pick_rows",
    )(routes.T, route_weight.T, moe_input, moe_grad)


def weights_kernel(*refs):
    own, other, (cols_ref, down_ref, rows_ref) = refs[:3], refs[3:6], refs[6:]
    tile = own[0].shape[1]
    for place, (gate_ref, up_ref, low_ref) in enumerate((own, other)):
        for kind, ref in enumerate((gate_ref, up_ref)):
            spot = slice((2 * kind + place) * tile, (2 * kind + place + 1) * tile)
            cols_ref[0, :, spot] = ref[...]
            rows_ref[0, spot, :] = ref[...].T
        down_ref[0, :, place * tile : (place + 1) * tile] = low_ref[...].T


def prepare_weights(own, other):
    width, half = own[0].shape
    tile = 128
    steps = half // tile
    cols = pl.BlockSpec((width, tile), lambda i: (0, i))
    down = pl.BlockSpec((tile, width), lambda i: (i, 0))
    return pl.pallas_call(
        weights_kernel,
        grid=(steps,),
        in_specs=[cols, cols, down] * 2,
        out_specs=[
            pl.BlockSpec((1, width, 4 * tile), lambda i: (i, 0, 0)),
            pl.BlockSpec((1, width, 2 * tile), lambda i: (i, 0, 0)),
            pl.BlockSpec((1, 4 * tile, width), lambda i: (i, 0, 0)),
        ],
        out_shape=(
            jax.ShapeDtypeStruct((steps, width, 4 * tile), jnp.bfloat16),
            jax.ShapeDtypeStruct((steps, width, 2 * tile), jnp.bfloat16),
            jax.ShapeDtypeStruct((steps, 4 * tile, width), jnp.bfloat16),
        ),
        compiler_params=params(20),
        cost_estimate=LIGHT,
        name="prepare_weights",
    )(*own, *other)


def expert_kernel(steps, rows_ref, cols_ref, down_ref, back_ref, out_ref, hidden):
    step = pl.program_id(0)
    width = rows_ref.shape[1] // 2
    pair = down_ref.shape[2]

    @pl.when(step < steps)
    def _():
        both_pre = dot(rows_ref[:, :width], cols_ref[0])
        gate_pre = both_pre[:, :pair]
        up_pre = both_pre[:, pair:]
        down_grad = dot(rows_ref[:, width:], down_ref[0])
        sig = jax.nn.sigmoid(gate_pre)
        hidden[step, :, :pair] = (
            down_grad * up_pre * sig * (1.0 + gate_pre * (1.0 - sig))
        ).astype(jnp.bfloat16)
        hidden[step, :, pair:] = (down_grad * gate_pre * sig).astype(jnp.bfloat16)

    @pl.when(step >= steps)
    def _():
        total = dot(hidden[0], back_ref[0])
        for i in range(1, steps):
            total += dot(hidden[i], back_ref[i])
        out_ref[...] = total.astype(jnp.bfloat16)


def experts(rows, cols, down, back):
    count, twice = rows.shape
    steps, width, quad = cols.shape
    tile = 512
    last = steps - 1
    turn = lambda i: jnp.maximum(i - steps, 0)
    return pl.pallas_call(
        functools.partial(expert_kernel, steps),
        grid=(steps + width // tile,),
        in_specs=[
            pl.BlockSpec((count, twice), lambda i: (0, 0)),
            pl.BlockSpec((1, width, quad), lambda i: (jnp.minimum(i, last), 0, 0)),
            pl.BlockSpec((1, width, quad // 2), lambda i: (jnp.minimum(i, last), 0, 0)),
            pl.BlockSpec((steps, quad, tile), lambda i: (0, 0, turn(i))),
        ],
        out_specs=pl.BlockSpec((count, tile), lambda i: (0, turn(i))),
        out_shape=jax.ShapeDtypeStruct((count, width), jnp.bfloat16),
        scratch_shapes=[pltpu.VMEM((steps, count, quad), jnp.bfloat16)],
        compiler_params=params(24),
        cost_estimate=LIGHT,
        name="expert_terms",
    )(rows, cols, down, back)


def shares_kernel(
    q_ref, key_ref, value_ref, prev_key_ref, prev_value_ref, prev_seg_ref, seg_row_ref, seg_col_ref,
    low_ref, turned_ref, query_ref, key_out, value_out,
):
    tokens = q_ref.shape[0]
    seg_col = seg_col_ref[...]
    row = lax.broadcasted_iota(jnp.int32, (tokens, tokens), 0)
    col = lax.broadcasted_iota(jnp.int32, (tokens, tokens), 1)
    own_seen = jnp.where((col <= row) & (seg_row_ref[...] == seg_col), 1.0, 0.0)
    prev_seg = prev_seg_ref[tokens : tokens + 16, :].astype(jnp.float32)[0:1, :]
    prev_seen = jnp.where(prev_seg == seg_col, 1.0, 0.0)
    seen = jnp.concatenate([prev_seen, own_seen], axis=1) > 0.5
    keys = jnp.concatenate([prev_key_ref[:tokens, :], key_ref[...]], axis=0)
    values = jnp.concatenate([prev_value_ref[:tokens, :], value_ref[...]], axis=0)
    key_out[0] = keys
    value_out[0] = values.T
    for head in range(GROUP):
        rows = slice(head * tokens, (head + 1) * tokens)
        query = q_ref[:, head * HD : (head + 1) * HD]
        scores = dot(query, keys, NT) * (HD**-0.5)
        masked = jnp.where(seen, scores, FLOOR)
        raised = jnp.where(seen, jnp.exp(masked - jnp.max(masked, axis=1, keepdims=True)), 0.0)
        shares = raised / jnp.sum(raised, axis=1, keepdims=True)
        low = shares.astype(jnp.bfloat16)
        low_ref[0, rows, :] = low
        turned_ref[0, :, rows] = low.T
        query_ref[0, rows, :] = query


def attention_shares(queries, key_heads, value_heads, prev, segs):
    tokens, width = queries.shape
    span = 2 * tokens
    stack = GROUP * tokens
    high = prev.shape[0]
    own = pl.BlockSpec((tokens, HD), lambda g: (0, g))
    group = lambda shape: pl.BlockSpec((1,) + shape, lambda g: (g, 0, 0))
    made = lambda shape: jax.ShapeDtypeStruct((KVH,) + shape, jnp.bfloat16)
    shapes = ((stack, span), (span, stack), (stack, HD), (span, HD), (HD, span))
    return pl.pallas_call(
        shares_kernel,
        grid=(KVH,),
        in_specs=[
            pl.BlockSpec((tokens, GROUP * HD), lambda g: (0, g)),
            own,
            own,
            pl.BlockSpec((high, HD), lambda g: (0, g)),
            pl.BlockSpec((high, HD), lambda g: (0, KVH + g)),
            pl.BlockSpec((high, HD), lambda g: (0, 0)),
            pl.BlockSpec((1, tokens), lambda g: (0, 0)),
            pl.BlockSpec((tokens, 1), lambda g: (0, 0)),
        ],
        out_specs=[group(shape) for shape in shapes],
        out_shape=[made(shape) for shape in shapes],
        compiler_params=params(16),
        cost_estimate=LIGHT,
        name="attention_shares",
    )(queries, key_heads, value_heads, prev, prev, prev, segs[None, :], segs[:, None])


def tail_kernel(
    plan, place_info, back_ref, place_ref, grad_ref, *refs
):
    heads, tiles = plan
    mine, across, refs = refs[:8], refs[8:16], refs[16:]
    low_ref, turned_ref, q_ref, key_ref, value_ref, *refs = refs
    moe_ref, query_out, kept_out, sent_out, stream, held, sums = refs
    step = pl.program_id(0)
    tokens = query_out.shape[0]
    part_size = stream.shape[2]
    size = mine[0].shape[1]
    spread = part_size // size
    here, core = place_info[1], place_info[2]

    @pl.when(step == 0)
    def _():
        moe = dot(place_ref[...], back_ref[...]).astype(jnp.bfloat16)
        moe_ref[...] = moe
        added = (grad_ref[...].astype(jnp.float32) + moe.astype(jnp.float32)).astype(jnp.bfloat16)
        for z in range(4):
            for rest in range(spread):
                for side in range(2):
                    source = ((z * spread + rest) * 2 + side) * size
                    stream[2 * z + side, :, rest * size : (rest + 1) * size] = added[:, source : source + size]

    @pl.when((step > 0) & ((step - 1) % tiles == 0))
    def _():
        sums[...] = jnp.zeros_like(sums)

    def project(pieces):
        head_grad = None
        for i, piece in enumerate(pieces):
            rows = stream[2 * (here ^ (i // 2)) + (core ^ (i % 2))]
            part = dot(rows, piece[...].reshape(part_size, piece.shape[-1]))
            head_grad = part if head_grad is None else head_grad + part
        return head_grad.astype(jnp.bfloat16)

    def hold(head_grad):
        for head in range(heads):
            held[head * tokens : (head + 1) * tokens, :] = head_grad[:, head * HD : (head + 1) * HD]

    def attend():
        grads = held[...]
        low = low_ref[0].astype(jnp.float32)
        prob_grad = dot(grads, value_ref[0])
        row_dot = jnp.sum(low * prob_grad, axis=1, keepdims=True)
        score_grad = (low * (prob_grad - row_dot) * (HD**-0.5)).astype(jnp.bfloat16)
        query_grad = dot(score_grad, key_ref[0]).astype(jnp.bfloat16)
        sums[0] += dot(score_grad, q_ref[0], TN)
        sums[1] += dot(turned_ref[0], grads)
        for head in range(heads):
            query_out[:, head * HD : (head + 1) * HD] = query_grad[head * tokens : (head + 1) * tokens, :]

    @pl.when(step == 0)
    def _():
        hold(project(mine))

    @pl.when((step > 0) & (step < tiles))
    def _():
        head_grad = project(mine)
        attend()
        hold(head_grad)

    @pl.when((step >= tiles) & (step < 2 * tiles))
    def _():
        head_grad = project(across)
        attend()
        hold(head_grad)

    @pl.when(step == 2 * tiles)
    def _():
        attend()

    @pl.when((step > 0) & (step % tiles == 0))
    def _():
        kept_out[...] = sums[:, tokens:, :]
        sent_out[...] = sums[:, :tokens, :].astype(jnp.bfloat16)


def tail(place_info, back, place, moe_grad, pieces, low, turned, query, keys, values):
    tokens, width = moe_grad.shape
    spread, size, cols = pieces[0].shape
    span = keys.shape[1]
    heads = 4
    tile = heads * HD
    tiles = cols // tile
    steps = KVH * tiles
    was = lambda i: jnp.maximum(i - 1, 0)
    kv_group = lambda i, info: (was(i) // tiles) ^ info[0]
    whole = lambda shape: pl.BlockSpec(shape, lambda i, info: (0,) * len(shape))
    group = lambda shape: pl.BlockSpec((1,) + shape, lambda i, info: (kv_group(i, info), 0, 0))
    rows = lambda shape: pl.BlockSpec((1,) + shape, lambda i, info: (kv_group(i, info), was(i) % tiles, 0))
    own_tile = lambda i: jnp.minimum(i, tiles - 1)
    other_tile = lambda i: jnp.minimum(jnp.maximum(i - tiles, 0), tiles - 1)
    piece = lambda turn: pl.BlockSpec((spread, size, tile), lambda i, info: (0, 0, turn(i)))
    kv = pl.BlockSpec((2, tokens, HD), lambda i, info: (0, 0, kv_group(i, info)))
    return pl.pallas_call(
        functools.partial(tail_kernel, (heads, tiles)),
        grid_spec=pltpu.PrefetchScalarGridSpec(
            num_scalar_prefetch=1,
            grid=(steps + 1,),
            in_specs=[whole(back.shape), whole(place.shape), whole(moe_grad.shape)]
            + [piece(own_tile)] * 8
            + [piece(other_tile)] * 8
            + [
                rows((heads * tokens, span)),
                pl.BlockSpec(
                    (1, span, heads * tokens), lambda i, info: (kv_group(i, info), 0, was(i) % tiles)
                ),
                rows((heads * tokens, HD)),
                group((span, HD)),
                group((HD, span)),
            ],
            out_specs=[
                whole((tokens, width)),
                pl.BlockSpec(
                    (tokens, tile), lambda i, info: (0, kv_group(i, info) * tiles + was(i) % tiles)
                ),
                kv,
                kv,
            ],
            scratch_shapes=[
                pltpu.VMEM((8, tokens, spread * size), jnp.bfloat16),
                pltpu.VMEM((heads * tokens, HD), jnp.bfloat16),
                pltpu.VMEM((2, span, HD), jnp.float32),
            ],
        ),
        out_shape=(
            jax.ShapeDtypeStruct((tokens, width), jnp.bfloat16),
            jax.ShapeDtypeStruct((tokens, KVH * cols), jnp.bfloat16),
            jax.ShapeDtypeStruct((2, tokens, KVH * HD), jnp.float32),
            jax.ShapeDtypeStruct((2, tokens, KVH * HD), jnp.bfloat16),
        ),
        compiler_params=params(56),
        cost_estimate=pl.CostEstimate(
            flops=2 * tokens * width * KVH * cols, bytes_accessed=22 * MIB, transcendentals=0
        ),
        name="tail_attention",
    )(place_info, back, place, moe_grad, *pieces, low, turned, query, keys, values)


def finish_kernel(kept_ref, later_ref, key_ref, value_ref):
    for kind, out_ref in enumerate((key_ref, value_ref)):
        out_ref[...] = kept_ref[kind] + later_ref[kind].astype(jnp.float32)


def finish(kept, later):
    out = jax.ShapeDtypeStruct(kept.shape[1:], jnp.float32)
    return pl.pallas_call(
        finish_kernel, out_shape=(out, out), compiler_params=params(16), cost_estimate=LIGHT, name="finish"
    )(kept, later)


def local(
    moe_input,
    moe_grad,
    routes,
    route_weight,
    w_gate,
    w_up,
    w_down,
    w_out,
    queries,
    key_heads,
    value_heads,
    segments,
):
    chips = ("far", "near", "low")
    blk = chips + ("core",)
    low = lax.axis_size("low")
    owners = 4 * low
    count = 2 * owners
    parts = lax.axis_size("groups")
    tokens, width = moe_input.shape
    depth = 2 * max(1, 3 * tokens * routes.shape[1] // (2 * count))
    swap = [(0, 1), (1, 0)]
    onward = [(i, i + 1) for i in range(count - 1)]
    backward = [(i + 1, i) for i in range(count - 1)]

    share_cols = w_out.shape[1] // parts
    w_share = lax.dynamic_slice_in_dim(w_out, lax.axis_index("groups") * share_cols, share_cols, 1)
    w_near = lax.ppermute(w_share, "near", swap)
    w_far = lax.ppermute(w_share, "far", swap)

    rows, place = pick(routes, route_weight, moe_input, moe_grad, owners, depth)
    line = lambda w: lax.all_gather(w, "low", axis=0, tiled=False)
    cross = lambda w: lax.ppermute(w, "groups", swap)
    other_core = lambda w: lax.ppermute(w, "core", swap)
    own = (w_gate, w_up, w_down)
    other = tuple(other_core(w) for w in own)

    key_heads, value_heads, segments, place = lax.optimization_barrier((key_heads, value_heads, segments, place))
    kv = jnp.concatenate([key_heads, value_heads], axis=1)
    segs = (segments + 1).astype(jnp.float32)
    seg_rows = jnp.zeros((16, kv.shape[1]), jnp.bfloat16).at[0, :tokens].set(segs.astype(jnp.bfloat16))
    prev = lax.ppermute(jnp.concatenate([kv, seg_rows], axis=0), blk, onward)
    own_line = line(w_share)
    rows, w_near, w_far, own_line, prev = lax.optimization_barrier((rows, w_near, w_far, own_line, prev))

    rows_in = lax.all_to_all(rows.reshape(owners, depth, 2 * width), chips, 0, 0, tiled=True)
    lines = [own_line, line(w_near), line(w_far)]
    crossed = [cross(w) for w in lines]
    w_last = lax.ppermute(w_far, "near", swap)
    prepared = prepare_weights(own, other)
    attention = attention_shares(queries, key_heads, value_heads, prev, segs)
    rows_in, prepared, attention, lines, crossed, w_last = lax.optimization_barrier(
        (rows_in, prepared, attention, lines, crossed, w_last)
    )
    last_line = line(w_last)
    last_crossed = cross(last_line)
    terms = experts(rows_in.reshape(owners * depth, 2 * width), *prepared)
    terms, lines, crossed = lax.optimization_barrier((terms, lines, crossed))
    back = lax.all_to_all(terms.reshape(owners, depth, width), chips, 0, 0, tiled=True)
    both = lambda pieces: [w for piece in pieces for w in (piece, other_core(piece))]

    z = 2 * lax.axis_index("far") + lax.axis_index("near")
    moe_input_grad, query_grad, kept, sent = tail(
        jnp.stack([lax.axis_index("groups"), z, lax.axis_index("core")]).astype(jnp.int32),
        back.reshape(owners * depth, width), place, moe_grad,
        both(lines + [last_line]) + both(crossed + [last_crossed]), *attention,
    )
    return (moe_input_grad, query_grad, *finish(kept, lax.ppermute(sent, blk, backward)))


def solution(mesh):
    names = ("groups", "far", "near", "low", "core")
    shape = (mesh.shape["groups"], 2, 2, mesh.shape["blk"] // 8, 2)
    fine = jax.sharding.Mesh(mesh.devices.reshape(shape), names)
    blk = names[1:]
    by_tokens = P(names, None)
    return jax.shard_map(
        local,
        mesh=fine,
        in_specs=(
            by_tokens,
            by_tokens,
            by_tokens,
            by_tokens,
            P(None, blk),
            P(None, blk),
            P(blk, None),
            P(blk, None),
            by_tokens,
            by_tokens,
            by_tokens,
            P(names),
        ),
        out_specs=(by_tokens,) * 4,
        check_vma=False,
    )
```

```python
import functools

import jax
import jax.numpy as jnp
from jax import lax
from jax.experimental import pallas as pl
from jax.experimental.pallas import tpu as pltpu
from jax.sharding import PartitionSpec as P

KVH = 2
GROUP = 16
HD = 128
FLOOR = -1e30
MIB = 1 << 20
LIGHT = pl.CostEstimate(flops=0, bytes_accessed=0, transcendentals=0)

NT = (((1,), (1,)), ((), ()))
TN = (((0,), (0,)), ((), ()))


def dot(a, b, dims=(((1,), (0,)), ((), ()))):
    return lax.dot_general(a, b, dims, preferred_element_type=jnp.float32)


def params(mib):
    return pltpu.CompilerParams(vmem_limit_bytes=mib * MIB)


def pick_kernel(owners, depth, routes_ref, weight_ref, input_ref, grad_ref, rows_ref, back_ref):
    tokens = input_ref.shape[0]
    slots = owners * depth
    first = routes_ref[0:1, :]
    second = routes_ref[1:2, :]
    expert = lax.broadcasted_iota(jnp.int32, (owners, tokens), 0)
    is_first = first == expert
    is_second = second == expert
    member = jnp.where(is_first | is_second, 1.0, 0.0)
    before = lax.broadcasted_iota(jnp.int32, (tokens, tokens), 0) < lax.broadcasted_iota(
        jnp.int32, (tokens, tokens), 1
    )
    rank = dot(member.astype(jnp.bfloat16), jnp.where(before, 1.0, 0.0).astype(jnp.bfloat16))
    spot = (expert * depth).astype(jnp.float32) + rank
    slot_first = jnp.sum(jnp.where(is_first, spot, 0.0), axis=0, keepdims=True).astype(jnp.int32)
    slot_second = jnp.sum(jnp.where(is_second, spot, 0.0), axis=0, keepdims=True).astype(jnp.int32)
    slot = lax.broadcasted_iota(jnp.int32, (slots, tokens), 0)
    at_first = slot == slot_first
    at_second = slot == slot_second
    place = jnp.where(at_first | at_second, 1.0, 0.0).astype(jnp.bfloat16)
    back_ref[...] = place.T
    scale = jnp.sum(
        jnp.where(at_first, weight_ref[0:1, :], 0.0) + jnp.where(at_second, weight_ref[1:2, :], 0.0),
        axis=1,
        keepdims=True,
    )
    width = input_ref.shape[1]
    rows_ref[:, :width] = dot(place, input_ref[...]).astype(jnp.bfloat16)
    rows_ref[:, width:] = (scale * dot(place, grad_ref[...])).astype(jnp.bfloat16)


def pick(routes, route_weight, moe_input, moe_grad, owners, depth):
    tokens, width = moe_input.shape
    slots = owners * depth
    return pl.pallas_call(
        functools.partial(pick_kernel, owners, depth),
        out_shape=(
            jax.ShapeDtypeStruct((slots, 2 * width), jnp.bfloat16),
            jax.ShapeDtypeStruct((tokens, slots), jnp.bfloat16),
        ),
        compiler_params=params(32),
        cost_estimate=pl.CostEstimate(
            flops=4 * slots * tokens * width, bytes_accessed=8 * MIB, transcendentals=0
        ),
        name="pick_rows",
    )(routes.T, route_weight.T, moe_input, moe_grad)


def weights_kernel(*refs):
    own, other, (cols_ref, down_ref, rows_ref) = refs[:3], refs[3:6], refs[6:]
    tile = own[0].shape[1]
    for place, (gate_ref, up_ref, low_ref) in enumerate((own, other)):
        for kind, ref in enumerate((gate_ref, up_ref)):
            spot = slice((2 * kind + place) * tile, (2 * kind + place + 1) * tile)
            cols_ref[0, :, spot] = ref[...]
            rows_ref[0, spot, :] = ref[...].T
        down_ref[0, :, place * tile : (place + 1) * tile] = low_ref[...].T


def prepare_weights(own, other):
    width, half = own[0].shape
    tile = 128
    steps = half // tile
    cols = pl.BlockSpec((width, tile), lambda i: (0, i))
    down = pl.BlockSpec((tile, width), lambda i: (i, 0))
    return pl.pallas_call(
        weights_kernel,
        grid=(steps,),
        in_specs=[cols, cols, down] * 2,
        out_specs=[
            pl.BlockSpec((1, width, 4 * tile), lambda i: (i, 0, 0)),
            pl.BlockSpec((1, width, 2 * tile), lambda i: (i, 0, 0)),
            pl.BlockSpec((1, 4 * tile, width), lambda i: (i, 0, 0)),
        ],
        out_shape=(
            jax.ShapeDtypeStruct((steps, width, 4 * tile), jnp.bfloat16),
            jax.ShapeDtypeStruct((steps, width, 2 * tile), jnp.bfloat16),
            jax.ShapeDtypeStruct((steps, 4 * tile, width), jnp.bfloat16),
        ),
        compiler_params=params(48),
        cost_estimate=LIGHT,
        name="prepare_weights",
    )(*own, *other)


def expert_kernel(steps, rows_ref, cols_ref, down_ref, back_ref, out_ref, hidden):
    step = pl.program_id(0)
    width = rows_ref.shape[1] // 2
    pair = down_ref.shape[2]

    @pl.when(step < steps)
    def _():
        both_pre = dot(rows_ref[:, :width], cols_ref[0])
        gate_pre = both_pre[:, :pair]
        up_pre = both_pre[:, pair:]
        down_grad = dot(rows_ref[:, width:], down_ref[0])
        sig = jax.nn.sigmoid(gate_pre)
        hidden[step, :, :pair] = (
            down_grad * up_pre * sig * (1.0 + gate_pre * (1.0 - sig))
        ).astype(jnp.bfloat16)
        hidden[step, :, pair:] = (down_grad * gate_pre * sig).astype(jnp.bfloat16)

    @pl.when(step >= steps)
    def _():
        total = dot(hidden[0], back_ref[0])
        for i in range(1, steps):
            total += dot(hidden[i], back_ref[i])
        out_ref[...] = total.astype(jnp.bfloat16)


def experts(rows, cols, down, back):
    count, twice = rows.shape
    steps, width, quad = cols.shape
    tile = 512
    last = steps - 1
    turn = lambda i: jnp.maximum(i - steps, 0)
    return pl.pallas_call(
        functools.partial(expert_kernel, steps),
        grid=(steps + width // tile,),
        in_specs=[
            pl.BlockSpec((count, twice), lambda i: (0, 0)),
            pl.BlockSpec((1, width, quad), lambda i: (jnp.minimum(i, last), 0, 0)),
            pl.BlockSpec((1, width, quad // 2), lambda i: (jnp.minimum(i, last), 0, 0)),
            pl.BlockSpec((steps, quad, tile), lambda i: (0, 0, turn(i))),
        ],
        out_specs=pl.BlockSpec((count, tile), lambda i: (0, turn(i))),
        out_shape=jax.ShapeDtypeStruct((count, width), jnp.bfloat16),
        scratch_shapes=[pltpu.VMEM((steps, count, quad), jnp.bfloat16)],
        compiler_params=params(48),
        cost_estimate=LIGHT,
        name="expert_terms",
    )(rows, cols, down, back)


def shares_kernel(
    q_ref, key_ref, value_ref, prev_key_ref, prev_value_ref, prev_seg_ref, seg_row_ref, seg_col_ref,
    low_ref, turned_ref, query_ref, key_out, value_out,
):
    tokens = q_ref.shape[0]
    seg_col = seg_col_ref[...]
    row = lax.broadcasted_iota(jnp.int32, (tokens, tokens), 0)
    col = lax.broadcasted_iota(jnp.int32, (tokens, tokens), 1)
    own_seen = jnp.where((col <= row) & (seg_row_ref[...] == seg_col), 1.0, 0.0)
    prev_seg = prev_seg_ref[tokens : tokens + 16, :].astype(jnp.float32)[0:1, :]
    prev_seen = jnp.where(prev_seg == seg_col, 1.0, 0.0)
    seen = jnp.concatenate([prev_seen, own_seen], axis=1) > 0.5
    keys = jnp.concatenate([prev_key_ref[:tokens, :], key_ref[...]], axis=0)
    values = jnp.concatenate([prev_value_ref[:tokens, :], value_ref[...]], axis=0)
    key_out[0] = keys
    value_out[0] = values.T
    for head in range(GROUP):
        rows = slice(head * tokens, (head + 1) * tokens)
        query = q_ref[:, head * HD : (head + 1) * HD]
        scores = dot(query, keys, NT) * (HD**-0.5)
        masked = jnp.where(seen, scores, FLOOR)
        raised = jnp.where(seen, jnp.exp(masked - jnp.max(masked, axis=1, keepdims=True)), 0.0)
        shares = raised / jnp.sum(raised, axis=1, keepdims=True)
        low = shares.astype(jnp.bfloat16)
        low_ref[0, rows, :] = low
        turned_ref[0, :, rows] = low.T
        query_ref[0, rows, :] = query


def attention_shares(queries, key_heads, value_heads, prev, segs):
    tokens, width = queries.shape
    span = 2 * tokens
    stack = GROUP * tokens
    high = prev.shape[0]
    own = pl.BlockSpec((tokens, HD), lambda g: (0, g))
    group = lambda shape: pl.BlockSpec((1,) + shape, lambda g: (g, 0, 0))
    made = lambda shape: jax.ShapeDtypeStruct((KVH,) + shape, jnp.bfloat16)
    shapes = ((stack, span), (span, stack), (stack, HD), (span, HD), (HD, span))
    return pl.pallas_call(
        shares_kernel,
        grid=(KVH,),
        in_specs=[
            pl.BlockSpec((tokens, GROUP * HD), lambda g: (0, g)),
            own,
            own,
            pl.BlockSpec((high, HD), lambda g: (0, g)),
            pl.BlockSpec((high, HD), lambda g: (0, KVH + g)),
            pl.BlockSpec((high, HD), lambda g: (0, 0)),
            pl.BlockSpec((1, tokens), lambda g: (0, 0)),
            pl.BlockSpec((tokens, 1), lambda g: (0, 0)),
        ],
        out_specs=[group(shape) for shape in shapes],
        out_shape=[made(shape) for shape in shapes],
        compiler_params=params(32),
        cost_estimate=LIGHT,
        name="attention_shares",
    )(queries, key_heads, value_heads, prev, prev, prev, segs[None, :], segs[:, None])


def tail_kernel(
    plan, place_info, back_ref, place_ref, grad_ref, *refs
):
    heads, tiles = plan
    mine, across, refs = refs[:8], refs[8:16], refs[16:]
    low_ref, turned_ref, q_ref, key_ref, value_ref, *refs = refs
    moe_ref, query_out, kept_out, sent_out, stream, held, sums = refs
    step = pl.program_id(0)
    tokens = query_out.shape[0]
    part_size = stream.shape[2]
    size = mine[0].shape[1]
    spread = part_size // size
    here, core = place_info[1], place_info[2]

    @pl.when(step == 0)
    def _():
        moe = dot(place_ref[...], back_ref[...]).astype(jnp.bfloat16)
        moe_ref[...] = moe
        added = (grad_ref[...].astype(jnp.float32) + moe.astype(jnp.float32)).astype(jnp.bfloat16)
        for z in range(4):
            for rest in range(spread):
                for side in range(2):
                    source = ((z * spread + rest) * 2 + side) * size
                    stream[2 * z + side, :, rest * size : (rest + 1) * size] = added[:, source : source + size]

    @pl.when((step > 0) & ((step - 1) % tiles == 0))
    def _():
        sums[...] = jnp.zeros_like(sums)

    def project(pieces):
        head_grad = None
        for i, piece in enumerate(pieces):
            rows = stream[2 * (here ^ (i // 2)) + (core ^ (i % 2))]
            part = dot(rows, piece[...].reshape(part_size, piece.shape[-1]))
            head_grad = part if head_grad is None else head_grad + part
        return head_grad.astype(jnp.bfloat16)

    def hold(head_grad):
        for head in range(heads):
            held[head * tokens : (head + 1) * tokens, :] = head_grad[:, head * HD : (head + 1) * HD]

    def attend():
        grads = held[...]
        low = low_ref[0].astype(jnp.float32)
        prob_grad = dot(grads, value_ref[0])
        row_dot = jnp.sum(low * prob_grad, axis=1, keepdims=True)
        score_grad = (low * (prob_grad - row_dot) * (HD**-0.5)).astype(jnp.bfloat16)
        query_grad = dot(score_grad, key_ref[0]).astype(jnp.bfloat16)
        sums[0] += dot(score_grad, q_ref[0], TN)
        sums[1] += dot(turned_ref[0], grads)
        for head in range(heads):
            query_out[:, head * HD : (head + 1) * HD] = query_grad[head * tokens : (head + 1) * tokens, :]

    @pl.when(step == 0)
    def _():
        hold(project(mine))

    @pl.when((step > 0) & (step < tiles))
    def _():
        head_grad = project(mine)
        attend()
        hold(head_grad)

    @pl.when((step >= tiles) & (step < 2 * tiles))
    def _():
        head_grad = project(across)
        attend()
        hold(head_grad)

    @pl.when(step == 2 * tiles)
    def _():
        attend()

    @pl.when((step > 0) & (step % tiles == 0))
    def _():
        kept_out[...] = sums[:, tokens:, :]
        sent_out[...] = sums[:, :tokens, :].astype(jnp.bfloat16)


def tail(place_info, back, place, moe_grad, pieces, low, turned, query, keys, values):
    tokens, width = moe_grad.shape
    spread, size, cols = pieces[0].shape
    span = keys.shape[1]
    heads = 4
    tile = heads * HD
    tiles = cols // tile
    steps = KVH * tiles
    was = lambda i: jnp.maximum(i - 1, 0)
    kv_group = lambda i, info: (was(i) // tiles) ^ info[0]
    whole = lambda shape: pl.BlockSpec(shape, lambda i, info: (0,) * len(shape))
    group = lambda shape: pl.BlockSpec((1,) + shape, lambda i, info: (kv_group(i, info), 0, 0))
    rows = lambda shape: pl.BlockSpec((1,) + shape, lambda i, info: (kv_group(i, info), was(i) % tiles, 0))
    own_tile = lambda i: jnp.minimum(i, tiles - 1)
    other_tile = lambda i: jnp.minimum(jnp.maximum(i - tiles, 0), tiles - 1)
    piece = lambda turn: pl.BlockSpec((spread, size, tile), lambda i, info: (0, 0, turn(i)))
    kv = pl.BlockSpec((2, tokens, HD), lambda i, info: (0, 0, kv_group(i, info)))
    return pl.pallas_call(
        functools.partial(tail_kernel, (heads, tiles)),
        grid_spec=pltpu.PrefetchScalarGridSpec(
            num_scalar_prefetch=1,
            grid=(steps + 1,),
            in_specs=[whole(back.shape), whole(place.shape), whole(moe_grad.shape)]
            + [piece(own_tile)] * 8
            + [piece(other_tile)] * 8
            + [
                rows((heads * tokens, span)),
                pl.BlockSpec(
                    (1, span, heads * tokens), lambda i, info: (kv_group(i, info), 0, was(i) % tiles)
                ),
                rows((heads * tokens, HD)),
                group((span, HD)),
                group((HD, span)),
            ],
            out_specs=[
                whole((tokens, width)),
                pl.BlockSpec(
                    (tokens, tile), lambda i, info: (0, kv_group(i, info) * tiles + was(i) % tiles)
                ),
                kv,
                kv,
            ],
            scratch_shapes=[
                pltpu.VMEM((8, tokens, spread * size), jnp.bfloat16),
                pltpu.VMEM((heads * tokens, HD), jnp.bfloat16),
                pltpu.VMEM((2, span, HD), jnp.float32),
            ],
        ),
        out_shape=(
            jax.ShapeDtypeStruct((tokens, width), jnp.bfloat16),
            jax.ShapeDtypeStruct((tokens, KVH * cols), jnp.bfloat16),
            jax.ShapeDtypeStruct((2, tokens, KVH * HD), jnp.float32),
            jax.ShapeDtypeStruct((2, tokens, KVH * HD), jnp.bfloat16),
        ),
        compiler_params=params(56),
        cost_estimate=pl.CostEstimate(
            flops=2 * tokens * width * KVH * cols, bytes_accessed=22 * MIB, transcendentals=0
        ),
        name="tail_attention",
    )(place_info, back, place, moe_grad, *pieces, low, turned, query, keys, values)


def finish_kernel(kept_ref, later_ref, key_ref, value_ref):
    for kind, out_ref in enumerate((key_ref, value_ref)):
        out_ref[...] = kept_ref[kind] + later_ref[kind].astype(jnp.float32)


def finish(kept, later):
    out = jax.ShapeDtypeStruct(kept.shape[1:], jnp.float32)
    return pl.pallas_call(
        finish_kernel, out_shape=(out, out), compiler_params=params(16), cost_estimate=LIGHT, name="finish"
    )(kept, later)


def local(
    moe_input,
    moe_grad,
    routes,
    route_weight,
    w_gate,
    w_up,
    w_down,
    w_out,
    queries,
    key_heads,
    value_heads,
    segments,
):
    chips = ("far", "near", "low")
    blk = chips + ("core",)
    low = lax.axis_size("low")
    owners = 4 * low
    count = 2 * owners
    parts = lax.axis_size("groups")
    tokens, width = moe_input.shape
    depth = 2 * max(1, 3 * tokens * routes.shape[1] // (2 * count))
    swap = [(0, 1), (1, 0)]
    onward = [(i, i + 1) for i in range(count - 1)]
    backward = [(i + 1, i) for i in range(count - 1)]

    share_cols = w_out.shape[1] // parts
    w_share = lax.dynamic_slice_in_dim(w_out, lax.axis_index("groups") * share_cols, share_cols, 1)
    w_near = lax.ppermute(w_share, "near", swap)
    w_far = lax.ppermute(w_share, "far", swap)

    rows, place = pick(routes, route_weight, moe_input, moe_grad, owners, depth)
    line = lambda w: lax.all_gather(w, "low", axis=0, tiled=False)
    cross = lambda w: lax.ppermute(w, "groups", swap)
    other_core = lambda w: lax.ppermute(w, "core", swap)
    own = (w_gate, w_up, w_down)
    other = tuple(other_core(w) for w in own)

    key_heads, value_heads, segments, place = lax.optimization_barrier((key_heads, value_heads, segments, place))
    kv = jnp.concatenate([key_heads, value_heads], axis=1)
    segs = (segments + 1).astype(jnp.float32)
    seg_rows = jnp.zeros((16, kv.shape[1]), jnp.bfloat16).at[0, :tokens].set(segs.astype(jnp.bfloat16))
    prev = lax.ppermute(jnp.concatenate([kv, seg_rows], axis=0), blk, onward)
    own_line = line(w_share)
    rows, w_near, w_far, own_line, prev = lax.optimization_barrier((rows, w_near, w_far, own_line, prev))

    rows_in = lax.all_to_all(rows.reshape(owners, depth, 2 * width), chips, 0, 0, tiled=True)
    near_line, far_line = line(w_near), line(w_far)
    w_last = lax.ppermute(w_far, "near", swap)
    prepared = prepare_weights(own, other)
    attention = attention_shares(queries, key_heads, value_heads, prev, segs)
    near_line, prepared, attention = lax.optimization_barrier((near_line, prepared, attention))
    crossed = [cross(own_line), cross(near_line)]
    rows_in, prepared, attention, near_line, far_line, crossed, w_last = lax.optimization_barrier(
        (rows_in, prepared, attention, near_line, far_line, crossed, w_last)
    )
    lines = [own_line, near_line, far_line]
    last_line = line(w_last)
    far_crossed = cross(far_line)
    last_crossed = cross(last_line)
    terms = experts(rows_in.reshape(owners * depth, 2 * width), *prepared)
    terms, lines, crossed = lax.optimization_barrier((terms, lines, crossed))
    back = lax.all_to_all(terms.reshape(owners, depth, width), chips, 0, 0, tiled=True)
    both = lambda pieces: [w for piece in pieces for w in (piece, other_core(piece))]

    z = 2 * lax.axis_index("far") + lax.axis_index("near")
    moe_input_grad, query_grad, kept, sent = tail(
        jnp.stack([lax.axis_index("groups"), z, lax.axis_index("core")]).astype(jnp.int32),
        back.reshape(owners * depth, width), place, moe_grad,
        both(lines + [last_line]) + both(crossed + [far_crossed, last_crossed]), *attention,
    )
    return (moe_input_grad, query_grad, *finish(kept, lax.ppermute(sent, blk, backward)))


def solution(mesh):
    names = ("groups", "far", "near", "low", "core")
    shape = (mesh.shape["groups"], 2, 2, mesh.shape["blk"] // 8, 2)
    fine = jax.sharding.Mesh(mesh.devices.reshape(shape), names)
    blk = names[1:]
    by_tokens = P(names, None)
    return jax.shard_map(
        local,
        mesh=fine,
        in_specs=(
            by_tokens,
            by_tokens,
            by_tokens,
            by_tokens,
            P(None, blk),
            P(None, blk),
            P(blk, None),
            P(blk, None),
            by_tokens,
            by_tokens,
            by_tokens,
            P(names),
        ),
        out_specs=(by_tokens,) * 4,
        check_vma=False,
    )
```

```python
import functools

import jax
import jax.numpy as jnp
from jax import lax
from jax.experimental import pallas as pl
from jax.experimental.pallas import tpu as pltpu
from jax.sharding import PartitionSpec as P

KVH = 2
GROUP = 16
HD = 128
FLOOR = -1e30
MIB = 1 << 20
LIGHT = pl.CostEstimate(flops=0, bytes_accessed=0, transcendentals=0)

NT = (((1,), (1,)), ((), ()))
TN = (((0,), (0,)), ((), ()))


def dot(a, b, dims=(((1,), (0,)), ((), ()))):
    return lax.dot_general(a, b, dims, preferred_element_type=jnp.float32)


def params(mib):
    return pltpu.CompilerParams(vmem_limit_bytes=mib * MIB)


def pick_kernel(owners, depth, routes_ref, weight_ref, input_ref, grad_ref, rows_ref, back_ref):
    tokens = input_ref.shape[0]
    slots = owners * depth
    first = routes_ref[0:1, :]
    second = routes_ref[1:2, :]
    expert = lax.broadcasted_iota(jnp.int32, (owners, tokens), 0)
    is_first = first == expert
    is_second = second == expert
    member = jnp.where(is_first | is_second, 1.0, 0.0)
    before = lax.broadcasted_iota(jnp.int32, (tokens, tokens), 0) < lax.broadcasted_iota(
        jnp.int32, (tokens, tokens), 1
    )
    rank = dot(member.astype(jnp.bfloat16), jnp.where(before, 1.0, 0.0).astype(jnp.bfloat16))
    spot = (expert * depth).astype(jnp.float32) + rank
    slot_first = jnp.sum(jnp.where(is_first, spot, 0.0), axis=0, keepdims=True).astype(jnp.int32)
    slot_second = jnp.sum(jnp.where(is_second, spot, 0.0), axis=0, keepdims=True).astype(jnp.int32)
    slot = lax.broadcasted_iota(jnp.int32, (slots, tokens), 0)
    at_first = slot == slot_first
    at_second = slot == slot_second
    place = jnp.where(at_first | at_second, 1.0, 0.0).astype(jnp.bfloat16)
    back_ref[...] = place.T
    scale = jnp.sum(
        jnp.where(at_first, weight_ref[0:1, :], 0.0) + jnp.where(at_second, weight_ref[1:2, :], 0.0),
        axis=1,
        keepdims=True,
    )
    width = input_ref.shape[1]
    rows_ref[:, :width] = dot(place, input_ref[...]).astype(jnp.bfloat16)
    rows_ref[:, width:] = (scale * dot(place, grad_ref[...])).astype(jnp.bfloat16)


def pick(routes, route_weight, moe_input, moe_grad, owners, depth):
    tokens, width = moe_input.shape
    slots = owners * depth
    return pl.pallas_call(
        functools.partial(pick_kernel, owners, depth),
        out_shape=(
            jax.ShapeDtypeStruct((slots, 2 * width), jnp.bfloat16),
            jax.ShapeDtypeStruct((tokens, slots), jnp.bfloat16),
        ),
        compiler_params=params(32),
        cost_estimate=pl.CostEstimate(
            flops=4 * slots * tokens * width, bytes_accessed=8 * MIB, transcendentals=0
        ),
        name="pick_rows",
    )(routes.T, route_weight.T, moe_input, moe_grad)


def weights_kernel(*refs):
    own, other, (cols_ref, down_ref, rows_ref, token_ref) = refs[:3], refs[3:6], refs[6:]
    token_ref[...] = jnp.zeros_like(token_ref)
    tile = own[0].shape[1]
    for place, (gate_ref, up_ref, low_ref) in enumerate((own, other)):
        for kind, ref in enumerate((gate_ref, up_ref)):
            spot = slice((2 * kind + place) * tile, (2 * kind + place + 1) * tile)
            cols_ref[0, :, spot] = ref[...]
            rows_ref[0, spot, :] = ref[...].T
        down_ref[0, :, place * tile : (place + 1) * tile] = low_ref[...].T


def prepare_weights(own, other):
    width, half = own[0].shape
    tile = 128
    steps = half // tile
    cols = pl.BlockSpec((width, tile), lambda i: (0, i))
    down = pl.BlockSpec((tile, width), lambda i: (i, 0))
    return pl.pallas_call(
        weights_kernel,
        grid=(steps,),
        in_specs=[cols, cols, down] * 2,
        out_specs=[
            pl.BlockSpec((1, width, 4 * tile), lambda i: (i, 0, 0)),
            pl.BlockSpec((1, width, 2 * tile), lambda i: (i, 0, 0)),
            pl.BlockSpec((1, 4 * tile, width), lambda i: (i, 0, 0)),
            pl.BlockSpec((8, 128), lambda i: (0, 0)),
        ],
        out_shape=(
            jax.ShapeDtypeStruct((steps, width, 4 * tile), jnp.bfloat16),
            jax.ShapeDtypeStruct((steps, width, 2 * tile), jnp.bfloat16),
            jax.ShapeDtypeStruct((steps, 4 * tile, width), jnp.bfloat16),
            jax.ShapeDtypeStruct((8, 128), jnp.float32),
        ),
        compiler_params=params(20),
        cost_estimate=LIGHT,
        name="prepare_weights",
    )(*own, *other)


def expert_kernel(steps, rows_ref, cols_ref, down_ref, back_ref, token_ref, out_ref, hidden):
    step = pl.program_id(0)
    width = rows_ref.shape[1] // 2
    pair = down_ref.shape[2]

    @pl.when(step < steps)
    def _():
        both_pre = dot(rows_ref[:, :width], cols_ref[0])
        gate_pre = both_pre[:, :pair]
        up_pre = both_pre[:, pair:]
        down_grad = dot(rows_ref[:, width:], down_ref[0])
        sig = jax.nn.sigmoid(gate_pre)
        hidden[step, :, :pair] = (
            down_grad * up_pre * sig * (1.0 + gate_pre * (1.0 - sig))
        ).astype(jnp.bfloat16)
        hidden[step, :, pair:] = (down_grad * gate_pre * sig).astype(jnp.bfloat16)

    @pl.when(step >= steps)
    def _():
        total = dot(hidden[0], back_ref[0])
        for i in range(1, steps):
            total += dot(hidden[i], back_ref[i])
        out_ref[...] = total.astype(jnp.bfloat16)


def experts(rows, cols, down, back, token):
    count, twice = rows.shape
    steps, width, quad = cols.shape
    tile = 512
    last = steps - 1
    turn = lambda i: jnp.maximum(i - steps, 0)
    return pl.pallas_call(
        functools.partial(expert_kernel, steps),
        grid=(steps + width // tile,),
        in_specs=[
            pl.BlockSpec((count, twice), lambda i: (0, 0)),
            pl.BlockSpec((1, width, quad), lambda i: (jnp.minimum(i, last), 0, 0)),
            pl.BlockSpec((1, width, quad // 2), lambda i: (jnp.minimum(i, last), 0, 0)),
            pl.BlockSpec((steps, quad, tile), lambda i: (0, 0, turn(i))),
            pl.BlockSpec((8, 128), lambda i: (0, 0)),
        ],
        out_specs=pl.BlockSpec((count, tile), lambda i: (0, turn(i))),
        out_shape=jax.ShapeDtypeStruct((count, width), jnp.bfloat16),
        scratch_shapes=[pltpu.VMEM((steps, count, quad), jnp.bfloat16)],
        compiler_params=params(24),
        cost_estimate=LIGHT,
        name="expert_terms",
    )(rows, cols, down, back, token)


def shares_kernel(
    q_ref, key_ref, value_ref, prev_key_ref, prev_value_ref, prev_seg_ref, seg_row_ref, seg_col_ref,
    low_ref, turned_ref, query_ref, key_out, value_out,
):
    tokens = q_ref.shape[0]
    seg_col = seg_col_ref[...]
    row = lax.broadcasted_iota(jnp.int32, (tokens, tokens), 0)
    col = lax.broadcasted_iota(jnp.int32, (tokens, tokens), 1)
    own_seen = jnp.where((col <= row) & (seg_row_ref[...] == seg_col), 1.0, 0.0)
    prev_seg = prev_seg_ref[tokens : tokens + 16, :].astype(jnp.float32)[0:1, :]
    prev_seen = jnp.where(prev_seg == seg_col, 1.0, 0.0)
    seen = jnp.concatenate([prev_seen, own_seen], axis=1) > 0.5
    keys = jnp.concatenate([prev_key_ref[:tokens, :], key_ref[...]], axis=0)
    values = jnp.concatenate([prev_value_ref[:tokens, :], value_ref[...]], axis=0)
    key_out[0] = keys
    value_out[0] = values.T
    for head in range(GROUP):
        rows = slice(head * tokens, (head + 1) * tokens)
        query = q_ref[:, head * HD : (head + 1) * HD]
        scores = dot(query, keys, NT) * (HD**-0.5)
        masked = jnp.where(seen, scores, FLOOR)
        raised = jnp.where(seen, jnp.exp(masked - jnp.max(masked, axis=1, keepdims=True)), 0.0)
        shares = raised / jnp.sum(raised, axis=1, keepdims=True)
        low = shares.astype(jnp.bfloat16)
        low_ref[0, rows, :] = low
        turned_ref[0, :, rows] = low.T
        query_ref[0, rows, :] = query


def attention_shares(queries, key_heads, value_heads, prev, segs):
    tokens, width = queries.shape
    span = 2 * tokens
    stack = GROUP * tokens
    high = prev.shape[0]
    own = pl.BlockSpec((tokens, HD), lambda g: (0, g))
    group = lambda shape: pl.BlockSpec((1,) + shape, lambda g: (g, 0, 0))
    made = lambda shape: jax.ShapeDtypeStruct((KVH,) + shape, jnp.bfloat16)
    shapes = ((stack, span), (span, stack), (stack, HD), (span, HD), (HD, span))
    return pl.pallas_call(
        shares_kernel,
        grid=(KVH,),
        in_specs=[
            pl.BlockSpec((tokens, GROUP * HD), lambda g: (0, g)),
            own,
            own,
            pl.BlockSpec((high, HD), lambda g: (0, g)),
            pl.BlockSpec((high, HD), lambda g: (0, KVH + g)),
            pl.BlockSpec((high, HD), lambda g: (0, 0)),
            pl.BlockSpec((1, tokens), lambda g: (0, 0)),
            pl.BlockSpec((tokens, 1), lambda g: (0, 0)),
        ],
        out_specs=[group(shape) for shape in shapes],
        out_shape=[made(shape) for shape in shapes],
        compiler_params=params(16),
        cost_estimate=LIGHT,
        name="attention_shares",
    )(queries, key_heads, value_heads, prev, prev, prev, segs[None, :], segs[:, None])


def tail_kernel(
    plan, place_info, back_ref, place_ref, grad_ref, *refs
):
    heads, tiles = plan
    mine, across, whole, refs = refs[:4], refs[4:8], refs[8:12], refs[12:]
    low_ref, turned_ref, q_ref, key_ref, value_ref, *refs = refs
    moe_ref, query_out, kept_out, sent_out, stream, held, sums = refs
    step = pl.program_id(0)
    tokens = query_out.shape[0]
    part_size = stream.shape[2]
    size = mine[0].shape[1]
    mine, across = mine + whole, across + whole
    spread = part_size // size
    here, core = place_info[1], place_info[2]

    @pl.when(step == 0)
    def _():
        moe = dot(place_ref[...], back_ref[...]).astype(jnp.bfloat16)
        moe_ref[...] = moe
        added = (grad_ref[...].astype(jnp.float32) + moe.astype(jnp.float32)).astype(jnp.bfloat16)
        for z in range(4):
            for rest in range(spread):
                for side in range(2):
                    source = ((z * spread + rest) * 2 + side) * size
                    stream[2 * z + side, :, rest * size : (rest + 1) * size] = added[:, source : source + size]

    @pl.when((step > 0) & ((step - 1) % tiles == 0))
    def _():
        sums[...] = jnp.zeros_like(sums)

    def project(pieces):
        head_grad = None
        for i, piece in enumerate(pieces):
            rows = stream[2 * (here ^ (i // 2)) + (core ^ (i % 2))]
            part = dot(rows, piece[...].reshape(part_size, piece.shape[-1]))
            head_grad = part if head_grad is None else head_grad + part
        return head_grad.astype(jnp.bfloat16)

    def hold(head_grad):
        for head in range(heads):
            held[head * tokens : (head + 1) * tokens, :] = head_grad[:, head * HD : (head + 1) * HD]

    def attend():
        grads = held[...]
        low = low_ref[0].astype(jnp.float32)
        prob_grad = dot(grads, value_ref[0])
        row_dot = jnp.sum(low * prob_grad, axis=1, keepdims=True)
        score_grad = (low * (prob_grad - row_dot) * (HD**-0.5)).astype(jnp.bfloat16)
        query_grad = dot(score_grad, key_ref[0]).astype(jnp.bfloat16)
        sums[0] += dot(score_grad, q_ref[0], TN)
        sums[1] += dot(turned_ref[0], grads)
        for head in range(heads):
            query_out[:, head * HD : (head + 1) * HD] = query_grad[head * tokens : (head + 1) * tokens, :]

    @pl.when(step == 0)
    def _():
        hold(project(mine))

    @pl.when((step > 0) & (step < tiles))
    def _():
        head_grad = project(mine)
        attend()
        hold(head_grad)

    @pl.when((step >= tiles) & (step < 2 * tiles))
    def _():
        head_grad = project(across)
        attend()
        hold(head_grad)

    @pl.when(step == 2 * tiles)
    def _():
        attend()

    @pl.when((step > 0) & (step % tiles == 0))
    def _():
        kept_out[...] = sums[:, tokens:, :]
        sent_out[...] = sums[:, :tokens, :].astype(jnp.bfloat16)


def tail(place_info, back, place, moe_grad, pieces, low, turned, query, keys, values):
    tokens, width = moe_grad.shape
    spread, size, cols = pieces[0].shape
    span = keys.shape[1]
    heads = 4
    tile = heads * HD
    tiles = cols // tile
    steps = KVH * tiles
    was = lambda i: jnp.maximum(i - 1, 0)
    kv_group = lambda i, info: (was(i) // tiles) ^ info[0]
    whole = lambda shape: pl.BlockSpec(shape, lambda i, info: (0,) * len(shape))
    group = lambda shape: pl.BlockSpec((1,) + shape, lambda i, info: (kv_group(i, info), 0, 0))
    rows = lambda shape: pl.BlockSpec((1,) + shape, lambda i, info: (kv_group(i, info), was(i) % tiles, 0))
    own_tile = lambda i: jnp.minimum(i, tiles - 1)
    other_tile = lambda i: jnp.minimum(jnp.maximum(i - tiles, 0), tiles - 1)
    now = lambda i: jnp.minimum(i, steps - 1)
    both = pl.BlockSpec(
        (1, spread, size, tile), lambda i, info: ((now(i) // tiles) ^ info[0], 0, 0, now(i) % tiles)
    )
    piece = lambda turn: pl.BlockSpec((spread, size, tile), lambda i, info: (0, 0, turn(i)))
    kv = pl.BlockSpec((2, tokens, HD), lambda i, info: (0, 0, kv_group(i, info)))
    return pl.pallas_call(
        functools.partial(tail_kernel, (heads, tiles)),
        grid_spec=pltpu.PrefetchScalarGridSpec(
            num_scalar_prefetch=1,
            grid=(steps + 1,),
            in_specs=[whole(back.shape), whole(place.shape), whole(moe_grad.shape)]
            + [piece(own_tile)] * 4
            + [piece(other_tile)] * 4
            + [both] * 4
            + [
                rows((heads * tokens, span)),
                pl.BlockSpec(
                    (1, span, heads * tokens), lambda i, info: (kv_group(i, info), 0, was(i) % tiles)
                ),
                rows((heads * tokens, HD)),
                group((span, HD)),
                group((HD, span)),
            ],
            out_specs=[
                whole((tokens, width)),
                pl.BlockSpec(
                    (tokens, tile), lambda i, info: (0, kv_group(i, info) * tiles + was(i) % tiles)
                ),
                kv,
                kv,
            ],
            scratch_shapes=[
                pltpu.VMEM((8, tokens, spread * size), jnp.bfloat16),
                pltpu.VMEM((heads * tokens, HD), jnp.bfloat16),
                pltpu.VMEM((2, span, HD), jnp.float32),
            ],
        ),
        out_shape=(
            jax.ShapeDtypeStruct((tokens, width), jnp.bfloat16),
            jax.ShapeDtypeStruct((tokens, KVH * cols), jnp.bfloat16),
            jax.ShapeDtypeStruct((2, tokens, KVH * HD), jnp.float32),
            jax.ShapeDtypeStruct((2, tokens, KVH * HD), jnp.bfloat16),
        ),
        compiler_params=params(56),
        cost_estimate=pl.CostEstimate(
            flops=2 * tokens * width * KVH * cols, bytes_accessed=22 * MIB, transcendentals=0
        ),
        name="tail_attention",
    )(place_info, back, place, moe_grad, *pieces, low, turned, query, keys, values)


def finish_kernel(kept_ref, later_ref, key_ref, value_ref):
    for kind, out_ref in enumerate((key_ref, value_ref)):
        out_ref[...] = kept_ref[kind] + later_ref[kind].astype(jnp.float32)


def finish(kept, later):
    out = jax.ShapeDtypeStruct(kept.shape[1:], jnp.float32)
    return pl.pallas_call(
        finish_kernel, out_shape=(out, out), compiler_params=params(16), cost_estimate=LIGHT, name="finish"
    )(kept, later)


def local(
    moe_input,
    moe_grad,
    routes,
    route_weight,
    w_gate,
    w_up,
    w_down,
    w_out,
    queries,
    key_heads,
    value_heads,
    segments,
):
    chips = ("far", "near", "low")
    blk = chips + ("core",)
    low = lax.axis_size("low")
    owners = 4 * low
    count = 2 * owners
    parts = lax.axis_size("groups")
    tokens, width = moe_input.shape
    depth = 2 * max(1, 3 * tokens * routes.shape[1] // (2 * count))
    swap = [(0, 1), (1, 0)]
    onward = [(i, i + 1) for i in range(count - 1)]
    backward = [(i + 1, i) for i in range(count - 1)]

    share_cols = w_out.shape[1] // parts
    w_share = lax.dynamic_slice_in_dim(w_out, lax.axis_index("groups") * share_cols, share_cols, 1)
    w_near = lax.ppermute(w_share, "near", swap)
    w_far = lax.ppermute(w_share, "far", swap)

    rows, place = pick(routes, route_weight, moe_input, moe_grad, owners, depth)
    line = lambda w: lax.all_gather(w, "low", axis=0, tiled=False)
    cross = lambda w: lax.ppermute(w, "groups", swap)
    other_core = lambda w: lax.ppermute(w, "core", swap)
    own = (w_gate, w_up, w_down)
    other = tuple(other_core(w) for w in own)

    key_heads, value_heads, segments, place = lax.optimization_barrier((key_heads, value_heads, segments, place))
    kv = jnp.concatenate([key_heads, value_heads], axis=1)
    segs = (segments + 1).astype(jnp.float32)
    seg_rows = jnp.zeros((16, kv.shape[1]), jnp.bfloat16).at[0, :tokens].set(segs.astype(jnp.bfloat16))
    prev = lax.ppermute(jnp.concatenate([kv, seg_rows], axis=0), blk, onward)
    own_line = line(w_share)
    rows, w_near, w_far, own_line, prev = lax.optimization_barrier((rows, w_near, w_far, own_line, prev))

    rows_in = lax.all_to_all(rows.reshape(owners, depth, 2 * width), chips, 0, 0, tiled=True)
    plane = lambda w: lax.all_gather(w, ("groups", "low"), axis=0, tiled=False).reshape(parts, low, *w.shape)
    near_line, far_plane = line(w_near), plane(w_far)
    w_last = lax.ppermute(w_far, "near", swap)
    *prepared, token = prepare_weights(own, other)
    attention = attention_shares(queries, key_heads, value_heads, prev, segs)
    near_line, token, attention = lax.optimization_barrier((near_line, token, attention))
    crossed = [cross(own_line), cross(near_line)]
    rows_in, token, attention, near_line, crossed, w_last = lax.optimization_barrier(
        (rows_in, token, attention, near_line, crossed, w_last)
    )
    lines = [own_line, near_line]
    last_plane = plane(w_last)
    terms = experts(rows_in.reshape(owners * depth, 2 * width), *prepared, token)
    terms, lines, crossed = lax.optimization_barrier((terms, lines, crossed))
    back = lax.all_to_all(terms.reshape(owners, depth, width), chips, 0, 0, tiled=True)
    both = lambda pieces: [w for piece in pieces for w in (piece, other_core(piece))]

    z = 2 * lax.axis_index("far") + lax.axis_index("near")
    moe_input_grad, query_grad, kept, sent = tail(
        jnp.stack([lax.axis_index("groups"), z, lax.axis_index("core")]).astype(jnp.int32),
        back.reshape(owners * depth, width), place, moe_grad,
        both(lines) + both(crossed) + both([far_plane, last_plane]), *attention,
    )
    return (moe_input_grad, query_grad, *finish(kept, lax.ppermute(sent, blk, backward)))


def solution(mesh):
    names = ("groups", "far", "near", "low", "core")
    shape = (mesh.shape["groups"], 2, 2, mesh.shape["blk"] // 8, 2)
    fine = jax.sharding.Mesh(mesh.devices.reshape(shape), names)
    blk = names[1:]
    by_tokens = P(names, None)
    return jax.shard_map(
        local,
        mesh=fine,
        in_specs=(
            by_tokens,
            by_tokens,
            by_tokens,
            by_tokens,
            P(None, blk),
            P(None, blk),
            P(blk, None),
            P(blk, None),
            by_tokens,
            by_tokens,
            by_tokens,
            P(names),
        ),
        out_specs=(by_tokens,) * 4,
        check_vma=False,
    )
```

```python
import functools

import jax
import jax.numpy as jnp
from jax import lax
from jax.experimental import pallas as pl
from jax.experimental.pallas import tpu as pltpu
from jax.sharding import PartitionSpec as P

KVH = 2
GROUP = 16
HD = 128
FLOOR = -1e30
MIB = 1 << 20
LIGHT = pl.CostEstimate(flops=0, bytes_accessed=0, transcendentals=0)

NT = (((1,), (1,)), ((), ()))
TN = (((0,), (0,)), ((), ()))


def dot(a, b, dims=(((1,), (0,)), ((), ()))):
    return lax.dot_general(a, b, dims, preferred_element_type=jnp.float32)


def params(mib):
    return pltpu.CompilerParams(vmem_limit_bytes=mib * MIB)


def pick_kernel(owners, depth, routes_ref, weight_ref, input_ref, grad_ref, rows_ref, back_ref):
    tokens = input_ref.shape[0]
    slots = owners * depth
    first = routes_ref[0:1, :]
    second = routes_ref[1:2, :]
    expert = lax.broadcasted_iota(jnp.int32, (owners, tokens), 0)
    is_first = first == expert
    is_second = second == expert
    member = jnp.where(is_first | is_second, 1.0, 0.0)
    before = lax.broadcasted_iota(jnp.int32, (tokens, tokens), 0) < lax.broadcasted_iota(
        jnp.int32, (tokens, tokens), 1
    )
    rank = dot(member.astype(jnp.bfloat16), jnp.where(before, 1.0, 0.0).astype(jnp.bfloat16))
    spot = (expert * depth).astype(jnp.float32) + rank
    slot_first = jnp.sum(jnp.where(is_first, spot, 0.0), axis=0, keepdims=True).astype(jnp.int32)
    slot_second = jnp.sum(jnp.where(is_second, spot, 0.0), axis=0, keepdims=True).astype(jnp.int32)
    slot = lax.broadcasted_iota(jnp.int32, (slots, tokens), 0)
    at_first = slot == slot_first
    at_second = slot == slot_second
    place = jnp.where(at_first | at_second, 1.0, 0.0).astype(jnp.bfloat16)
    back_ref[...] = place.T
    scale = jnp.sum(
        jnp.where(at_first, weight_ref[0:1, :], 0.0) + jnp.where(at_second, weight_ref[1:2, :], 0.0),
        axis=1,
        keepdims=True,
    )
    width = input_ref.shape[1]
    rows_ref[:, :width] = dot(place, input_ref[...]).astype(jnp.bfloat16)
    rows_ref[:, width:] = (scale * dot(place, grad_ref[...])).astype(jnp.bfloat16)


def pick(routes, route_weight, moe_input, moe_grad, owners, depth):
    tokens, width = moe_input.shape
    slots = owners * depth
    return pl.pallas_call(
        functools.partial(pick_kernel, owners, depth),
        out_shape=(
            jax.ShapeDtypeStruct((slots, 2 * width), jnp.bfloat16),
            jax.ShapeDtypeStruct((tokens, slots), jnp.bfloat16),
        ),
        compiler_params=params(32),
        cost_estimate=pl.CostEstimate(
            flops=4 * slots * tokens * width, bytes_accessed=8 * MIB, transcendentals=0
        ),
        name="pick_rows",
    )(routes.T, route_weight.T, moe_input, moe_grad)


def weights_kernel(*refs):
    own, other, (cols_ref, down_ref, rows_ref) = refs[:3], refs[3:6], refs[6:]
    tile = own[0].shape[1]
    for place, (gate_ref, up_ref, low_ref) in enumerate((own, other)):
        for kind, ref in enumerate((gate_ref, up_ref)):
            spot = slice((2 * kind + place) * tile, (2 * kind + place + 1) * tile)
            cols_ref[0, :, spot] = ref[...]
            rows_ref[0, spot, :] = ref[...].T
        down_ref[0, :, place * tile : (place + 1) * tile] = low_ref[...].T


def prepare_weights(own, other):
    width, half = own[0].shape
    tile = 128
    steps = half // tile
    cols = pl.BlockSpec((width, tile), lambda i: (0, i))
    down = pl.BlockSpec((tile, width), lambda i: (i, 0))
    return pl.pallas_call(
        weights_kernel,
        grid=(steps,),
        in_specs=[cols, cols, down] * 2,
        out_specs=[
            pl.BlockSpec((1, width, 4 * tile), lambda i: (i, 0, 0)),
            pl.BlockSpec((1, width, 2 * tile), lambda i: (i, 0, 0)),
            pl.BlockSpec((1, 4 * tile, width), lambda i: (i, 0, 0)),
        ],
        out_shape=(
            jax.ShapeDtypeStruct((steps, width, 4 * tile), jnp.bfloat16),
            jax.ShapeDtypeStruct((steps, width, 2 * tile), jnp.bfloat16),
            jax.ShapeDtypeStruct((steps, 4 * tile, width), jnp.bfloat16),
        ),
        compiler_params=params(48),
        cost_estimate=LIGHT,
        name="prepare_weights",
    )(*own, *other)


def expert_kernel(steps, rows_ref, cols_ref, down_ref, back_ref, out_ref, hidden):
    step = pl.program_id(0)
    width = rows_ref.shape[1] // 2
    pair = down_ref.shape[2]

    @pl.when(step < steps)
    def _():
        both_pre = dot(rows_ref[:, :width], cols_ref[0])
        gate_pre = both_pre[:, :pair]
        up_pre = both_pre[:, pair:]
        down_grad = dot(rows_ref[:, width:], down_ref[0])
        sig = jax.nn.sigmoid(gate_pre)
        hidden[step, :, :pair] = (
            down_grad * up_pre * sig * (1.0 + gate_pre * (1.0 - sig))
        ).astype(jnp.bfloat16)
        hidden[step, :, pair:] = (down_grad * gate_pre * sig).astype(jnp.bfloat16)

    @pl.when(step >= steps)
    def _():
        total = dot(hidden[0], back_ref[0])
        for i in range(1, steps):
            total += dot(hidden[i], back_ref[i])
        out_ref[...] = total.astype(jnp.bfloat16)


def experts(rows, cols, down, back):
    count, twice = rows.shape
    steps, width, quad = cols.shape
    tile = 512
    last = steps - 1
    turn = lambda i: jnp.maximum(i - steps, 0)
    return pl.pallas_call(
        functools.partial(expert_kernel, steps),
        grid=(steps + width // tile,),
        in_specs=[
            pl.BlockSpec((count, twice), lambda i: (0, 0)),
            pl.BlockSpec((1, width, quad), lambda i: (jnp.minimum(i, last), 0, 0)),
            pl.BlockSpec((1, width, quad // 2), lambda i: (jnp.minimum(i, last), 0, 0)),
            pl.BlockSpec((steps, quad, tile), lambda i: (0, 0, turn(i))),
        ],
        out_specs=pl.BlockSpec((count, tile), lambda i: (0, turn(i))),
        out_shape=jax.ShapeDtypeStruct((count, width), jnp.bfloat16),
        scratch_shapes=[pltpu.VMEM((steps, count, quad), jnp.bfloat16)],
        compiler_params=params(48),
        cost_estimate=LIGHT,
        name="expert_terms",
    )(rows, cols, down, back)


def shares_kernel(
    q_ref, key_ref, value_ref, prev_key_ref, prev_value_ref, prev_seg_ref, seg_row_ref, seg_col_ref,
    low_ref, turned_ref, query_ref, key_out, value_out,
):
    tokens = q_ref.shape[0]
    seg_col = seg_col_ref[...]
    row = lax.broadcasted_iota(jnp.int32, (tokens, tokens), 0)
    col = lax.broadcasted_iota(jnp.int32, (tokens, tokens), 1)
    own_seen = jnp.where((col <= row) & (seg_row_ref[...] == seg_col), 1.0, 0.0)
    prev_seg = prev_seg_ref[tokens : tokens + 16, :].astype(jnp.float32)[0:1, :]
    prev_seen = jnp.where(prev_seg == seg_col, 1.0, 0.0)
    seen = jnp.concatenate([prev_seen, own_seen], axis=1) > 0.5
    keys = jnp.concatenate([prev_key_ref[:tokens, :], key_ref[...]], axis=0)
    values = jnp.concatenate([prev_value_ref[:tokens, :], value_ref[...]], axis=0)
    key_out[0] = keys
    value_out[0] = values.T
    for head in range(GROUP):
        rows = slice(head * tokens, (head + 1) * tokens)
        query = q_ref[:, head * HD : (head + 1) * HD]
        scores = dot(query, keys, NT) * (HD**-0.5)
        masked = jnp.where(seen, scores, FLOOR)
        raised = jnp.where(seen, jnp.exp(masked - jnp.max(masked, axis=1, keepdims=True)), 0.0)
        shares = raised / jnp.sum(raised, axis=1, keepdims=True)
        low = shares.astype(jnp.bfloat16)
        low_ref[0, rows, :] = low
        turned_ref[0, :, rows] = low.T
        query_ref[0, rows, :] = query


def attention_shares(queries, key_heads, value_heads, prev, segs):
    tokens, width = queries.shape
    span = 2 * tokens
    stack = GROUP * tokens
    high = prev.shape[0]
    own = pl.BlockSpec((tokens, HD), lambda g: (0, g))
    group = lambda shape: pl.BlockSpec((1,) + shape, lambda g: (g, 0, 0))
    made = lambda shape: jax.ShapeDtypeStruct((KVH,) + shape, jnp.bfloat16)
    shapes = ((stack, span), (span, stack), (stack, HD), (span, HD), (HD, span))
    return pl.pallas_call(
        shares_kernel,
        grid=(KVH,),
        in_specs=[
            pl.BlockSpec((tokens, GROUP * HD), lambda g: (0, g)),
            own,
            own,
            pl.BlockSpec((high, HD), lambda g: (0, g)),
            pl.BlockSpec((high, HD), lambda g: (0, KVH + g)),
            pl.BlockSpec((high, HD), lambda g: (0, 0)),
            pl.BlockSpec((1, tokens), lambda g: (0, 0)),
            pl.BlockSpec((tokens, 1), lambda g: (0, 0)),
        ],
        out_specs=[group(shape) for shape in shapes],
        out_shape=[made(shape) for shape in shapes],
        compiler_params=params(32),
        cost_estimate=LIGHT,
        name="attention_shares",
    )(queries, key_heads, value_heads, prev, prev, prev, segs[None, :], segs[:, None])


def tail_kernel(
    plan, place_info, back_ref, place_ref, grad_ref, *refs
):
    heads, tiles = plan
    mine, across, refs = refs[:8], refs[8:16], refs[16:]
    low_ref, turned_ref, q_ref, key_ref, value_ref, *refs = refs
    moe_ref, query_out, kept_out, sent_out, by_place, stream, held, sums = refs
    step = pl.program_id(0)
    tokens = query_out.shape[0]
    part_size = by_place.shape[2]
    size = mine[0].shape[1]
    spread = part_size // size
    here, core = place_info[1], place_info[2]

    @pl.when(step == 0)
    def _():
        moe = dot(place_ref[...], back_ref[...]).astype(jnp.bfloat16)
        moe_ref[...] = moe
        added = (grad_ref[...].astype(jnp.float32) + moe.astype(jnp.float32)).astype(jnp.bfloat16)
        for z in range(4):
            for rest in range(spread):
                for side in range(2):
                    source = ((z * spread + rest) * 2 + side) * size
                    by_place[2 * z + side, :, rest * size : (rest + 1) * size] = added[:, source : source + size]
        for i in range(8):
            spot = slice(i * part_size, (i + 1) * part_size)
            stream[:, spot] = by_place[2 * (here ^ (i // 2)) + (core ^ (i % 2))]

    @pl.when((step > 0) & ((step - 1) % tiles == 0))
    def _():
        sums[...] = jnp.zeros_like(sums)

    def project(pieces):
        columns = jnp.concatenate([piece[...].reshape(part_size, piece.shape[-1]) for piece in pieces], axis=0)
        return dot(stream[...], columns).astype(jnp.bfloat16)

    def hold(head_grad):
        for head in range(heads):
            held[head * tokens : (head + 1) * tokens, :] = head_grad[:, head * HD : (head + 1) * HD]

    def attend():
        grads = held[...]
        low = low_ref[0].astype(jnp.float32)
        prob_grad = dot(grads, value_ref[0])
        row_dot = jnp.sum(low * prob_grad, axis=1, keepdims=True)
        score_grad = (low * (prob_grad - row_dot) * (HD**-0.5)).astype(jnp.bfloat16)
        query_grad = dot(score_grad, key_ref[0]).astype(jnp.bfloat16)
        sums[0] += dot(score_grad, q_ref[0], TN)
        sums[1] += dot(turned_ref[0], grads)
        for head in range(heads):
            query_out[:, head * HD : (head + 1) * HD] = query_grad[head * tokens : (head + 1) * tokens, :]

    @pl.when(step == 0)
    def _():
        hold(project(mine))

    @pl.when((step > 0) & (step < tiles))
    def _():
        head_grad = project(mine)
        attend()
        hold(head_grad)

    @pl.when((step >= tiles) & (step < 2 * tiles))
    def _():
        head_grad = project(across)
        attend()
        hold(head_grad)

    @pl.when(step == 2 * tiles)
    def _():
        attend()

    @pl.when((step > 0) & (step % tiles == 0))
    def _():
        kept_out[...] = sums[:, tokens:, :]
        sent_out[...] = sums[:, :tokens, :].astype(jnp.bfloat16)


def tail(place_info, back, place, moe_grad, pieces, low, turned, query, keys, values):
    tokens, width = moe_grad.shape
    spread, size, cols = pieces[0].shape
    span = keys.shape[1]
    heads = 4
    tile = heads * HD
    tiles = cols // tile
    steps = KVH * tiles
    was = lambda i: jnp.maximum(i - 1, 0)
    kv_group = lambda i, info: (was(i) // tiles) ^ info[0]
    whole = lambda shape: pl.BlockSpec(shape, lambda i, info: (0,) * len(shape))
    group = lambda shape: pl.BlockSpec((1,) + shape, lambda i, info: (kv_group(i, info), 0, 0))
    rows = lambda shape: pl.BlockSpec((1,) + shape, lambda i, info: (kv_group(i, info), was(i) % tiles, 0))
    own_tile = lambda i: jnp.minimum(i, tiles - 1)
    other_tile = lambda i: jnp.minimum(jnp.maximum(i - tiles, 0), tiles - 1)
    piece = lambda turn: pl.BlockSpec((spread, size, tile), lambda i, info: (0, 0, turn(i)))
    kv = pl.BlockSpec((2, tokens, HD), lambda i, info: (0, 0, kv_group(i, info)))
    return pl.pallas_call(
        functools.partial(tail_kernel, (heads, tiles)),
        grid_spec=pltpu.PrefetchScalarGridSpec(
            num_scalar_prefetch=1,
            grid=(steps + 1,),
            in_specs=[whole(back.shape), whole(place.shape), whole(moe_grad.shape)]
            + [piece(own_tile)] * 8
            + [piece(other_tile)] * 8
            + [
                rows((heads * tokens, span)),
                pl.BlockSpec(
                    (1, span, heads * tokens), lambda i, info: (kv_group(i, info), 0, was(i) % tiles)
                ),
                rows((heads * tokens, HD)),
                group((span, HD)),
                group((HD, span)),
            ],
            out_specs=[
                whole((tokens, width)),
                pl.BlockSpec(
                    (tokens, tile), lambda i, info: (0, kv_group(i, info) * tiles + was(i) % tiles)
                ),
                kv,
                kv,
            ],
            scratch_shapes=[
                pltpu.VMEM((8, tokens, spread * size), jnp.bfloat16),
                pltpu.VMEM((tokens, width), jnp.bfloat16),
                pltpu.VMEM((heads * tokens, HD), jnp.bfloat16),
                pltpu.VMEM((2, span, HD), jnp.float32),
            ],
        ),
        out_shape=(
            jax.ShapeDtypeStruct((tokens, width), jnp.bfloat16),
            jax.ShapeDtypeStruct((tokens, KVH * cols), jnp.bfloat16),
            jax.ShapeDtypeStruct((2, tokens, KVH * HD), jnp.float32),
            jax.ShapeDtypeStruct((2, tokens, KVH * HD), jnp.bfloat16),
        ),
        compiler_params=params(56),
        cost_estimate=pl.CostEstimate(
            flops=2 * tokens * width * KVH * cols, bytes_accessed=22 * MIB, transcendentals=0
        ),
        name="tail_attention",
    )(place_info, back, place, moe_grad, *pieces, low, turned, query, keys, values)


def finish_kernel(kept_ref, later_ref, key_ref, value_ref):
    for kind, out_ref in enumerate((key_ref, value_ref)):
        out_ref[...] = kept_ref[kind] + later_ref[kind].astype(jnp.float32)


def finish(kept, later):
    out = jax.ShapeDtypeStruct(kept.shape[1:], jnp.float32)
    return pl.pallas_call(
        finish_kernel, out_shape=(out, out), compiler_params=params(60), cost_estimate=LIGHT, name="finish"
    )(kept, later)


def local(
    moe_input,
    moe_grad,
    routes,
    route_weight,
    w_gate,
    w_up,
    w_down,
    w_out,
    queries,
    key_heads,
    value_heads,
    segments,
):
    chips = ("far", "near", "low")
    blk = chips + ("core",)
    low = lax.axis_size("low")
    owners = 4 * low
    count = 2 * owners
    parts = lax.axis_size("groups")
    tokens, width = moe_input.shape
    depth = 2 * max(1, 3 * tokens * routes.shape[1] // (2 * count))
    swap = [(0, 1), (1, 0)]
    onward = [(i, i + 1) for i in range(count - 1)]
    backward = [(i + 1, i) for i in range(count - 1)]

    share_cols = w_out.shape[1] // parts
    w_share = lax.dynamic_slice_in_dim(w_out, lax.axis_index("groups") * share_cols, share_cols, 1)
    w_near = lax.ppermute(w_share, "near", swap)
    w_far = lax.ppermute(w_share, "far", swap)

    rows, place = pick(routes, route_weight, moe_input, moe_grad, owners, depth)
    line = lambda w: lax.all_gather(w, "low", axis=0, tiled=False)
    cross = lambda w: lax.ppermute(w, "groups", swap)
    other_core = lambda w: lax.ppermute(w, "core", swap)
    own = (w_gate, w_up, w_down)
    other = tuple(other_core(w) for w in own)

    key_heads, value_heads, segments, place = lax.optimization_barrier((key_heads, value_heads, segments, place))
    kv = jnp.concatenate([key_heads, value_heads], axis=1)
    segs = (segments + 1).astype(jnp.float32)
    seg_rows = jnp.zeros((16, kv.shape[1]), jnp.bfloat16).at[0, :tokens].set(segs.astype(jnp.bfloat16))
    prev = lax.ppermute(jnp.concatenate([kv, seg_rows], axis=0), blk, onward)
    own_line = line(w_share)
    rows, w_near, w_far, own_line, prev = lax.optimization_barrier((rows, w_near, w_far, own_line, prev))

    rows_in = lax.all_to_all(rows.reshape(owners, depth, 2 * width), chips, 0, 0, tiled=True)
    near_line, far_line = line(w_near), line(w_far)
    w_last = lax.ppermute(w_far, "near", swap)
    prepared = prepare_weights(own, other)
    attention = attention_shares(queries, key_heads, value_heads, prev, segs)
    near_line, prepared, attention = lax.optimization_barrier((near_line, prepared, attention))
    crossed = [cross(own_line), cross(near_line)]
    rows_in, prepared, attention, near_line, far_line, crossed, w_last = lax.optimization_barrier(
        (rows_in, prepared, attention, near_line, far_line, crossed, w_last)
    )
    lines = [own_line, near_line, far_line]
    last_line = line(w_last)
    half = low // 2
    far_first, far_rest = cross(far_line[:half]), cross(far_line[half:])
    last_crossed = cross(last_line)
    terms = experts(rows_in.reshape(owners * depth, 2 * width), *prepared)
    terms, lines, crossed, far_first = lax.optimization_barrier((terms, lines, crossed, far_first))
    far_crossed = jnp.concatenate([far_first, far_rest], axis=0)
    back = lax.all_to_all(terms.reshape(owners, depth, width), chips, 0, 0, tiled=True)
    both = lambda pieces: [w for piece in pieces for w in (piece, other_core(piece))]

    z = 2 * lax.axis_index("far") + lax.axis_index("near")
    moe_input_grad, query_grad, kept, sent = tail(
        jnp.stack([lax.axis_index("groups"), z, lax.axis_index("core")]).astype(jnp.int32),
        back.reshape(owners * depth, width), place, moe_grad,
        both(lines + [last_line]) + both(crossed + [far_crossed, last_crossed]), *attention,
    )
    return (moe_input_grad, query_grad, *finish(kept, lax.ppermute(sent, blk, backward)))


def solution(mesh):
    names = ("groups", "far", "near", "low", "core")
    shape = (mesh.shape["groups"], 2, 2, mesh.shape["blk"] // 8, 2)
    fine = jax.sharding.Mesh(mesh.devices.reshape(shape), names)
    blk = names[1:]
    by_tokens = P(names, None)
    return jax.shard_map(
        local,
        mesh=fine,
        in_specs=(
            by_tokens,
            by_tokens,
            by_tokens,
            by_tokens,
            P(None, blk),
            P(None, blk),
            P(blk, None),
            P(blk, None),
            by_tokens,
            by_tokens,
            by_tokens,
            P(names),
        ),
        out_specs=(by_tokens,) * 4,
        check_vma=False,
    )
```

```python
import functools

import jax
import jax.numpy as jnp
from jax import lax
from jax.experimental import pallas as pl
from jax.experimental.pallas import tpu as pltpu
from jax.sharding import PartitionSpec as P

KVH = 2
GROUP = 16
HD = 128
FLOOR = -1e30
MIB = 1 << 20
LIGHT = pl.CostEstimate(flops=0, bytes_accessed=0, transcendentals=0)

NT = (((1,), (1,)), ((), ()))
TN = (((0,), (0,)), ((), ()))


def dot(a, b, dims=(((1,), (0,)), ((), ()))):
    return lax.dot_general(a, b, dims, preferred_element_type=jnp.float32)


def params(mib):
    return pltpu.CompilerParams(vmem_limit_bytes=mib * MIB)


def pick_kernel(owners, depth, routes_ref, weight_ref, input_ref, grad_ref, rows_ref, back_ref):
    tokens = input_ref.shape[0]
    slots = owners * depth
    first = routes_ref[0:1, :]
    second = routes_ref[1:2, :]
    expert = lax.broadcasted_iota(jnp.int32, (owners, tokens), 0)
    is_first = first == expert
    is_second = second == expert
    member = jnp.where(is_first | is_second, 1.0, 0.0)
    before = lax.broadcasted_iota(jnp.int32, (tokens, tokens), 0) < lax.broadcasted_iota(
        jnp.int32, (tokens, tokens), 1
    )
    rank = dot(member.astype(jnp.bfloat16), jnp.where(before, 1.0, 0.0).astype(jnp.bfloat16))
    spot = (expert * depth).astype(jnp.float32) + rank
    slot_first = jnp.sum(jnp.where(is_first, spot, 0.0), axis=0, keepdims=True).astype(jnp.int32)
    slot_second = jnp.sum(jnp.where(is_second, spot, 0.0), axis=0, keepdims=True).astype(jnp.int32)
    slot = lax.broadcasted_iota(jnp.int32, (slots, tokens), 0)
    at_first = slot == slot_first
    at_second = slot == slot_second
    place = jnp.where(at_first | at_second, 1.0, 0.0).astype(jnp.bfloat16)
    back_ref[...] = place.T
    scale = jnp.sum(
        jnp.where(at_first, weight_ref[0:1, :], 0.0) + jnp.where(at_second, weight_ref[1:2, :], 0.0),
        axis=1,
        keepdims=True,
    )
    width = input_ref.shape[1]
    rows_ref[:, :width] = dot(place, input_ref[...]).astype(jnp.bfloat16)
    rows_ref[:, width:] = (scale * dot(place, grad_ref[...])).astype(jnp.bfloat16)


def pick(routes, route_weight, moe_input, moe_grad, owners, depth):
    tokens, width = moe_input.shape
    slots = owners * depth
    return pl.pallas_call(
        functools.partial(pick_kernel, owners, depth),
        out_shape=(
            jax.ShapeDtypeStruct((slots, 2 * width), jnp.bfloat16),
            jax.ShapeDtypeStruct((tokens, slots), jnp.bfloat16),
        ),
        compiler_params=params(32),
        cost_estimate=pl.CostEstimate(
            flops=4 * slots * tokens * width, bytes_accessed=8 * MIB, transcendentals=0
        ),
        name="pick_rows",
    )(routes.T, route_weight.T, moe_input, moe_grad)


def weights_kernel(*refs):
    own, other, (cols_ref, down_ref, rows_ref) = refs[:3], refs[3:6], refs[6:]
    tile = own[0].shape[1]
    for place, (gate_ref, up_ref, low_ref) in enumerate((own, other)):
        for kind, ref in enumerate((gate_ref, up_ref)):
            spot = slice((2 * kind + place) * tile, (2 * kind + place + 1) * tile)
            cols_ref[0, :, spot] = ref[...]
            rows_ref[0, spot, :] = ref[...].T
        down_ref[0, :, place * tile : (place + 1) * tile] = low_ref[...].T


def prepare_weights(own, other):
    width, half = own[0].shape
    tile = 128
    steps = half // tile
    cols = pl.BlockSpec((width, tile), lambda i: (0, i))
    down = pl.BlockSpec((tile, width), lambda i: (i, 0))
    return pl.pallas_call(
        weights_kernel,
        grid=(steps,),
        in_specs=[cols, cols, down] * 2,
        out_specs=[
            pl.BlockSpec((1, width, 4 * tile), lambda i: (i, 0, 0)),
            pl.BlockSpec((1, width, 2 * tile), lambda i: (i, 0, 0)),
            pl.BlockSpec((1, 4 * tile, width), lambda i: (i, 0, 0)),
        ],
        out_shape=(
            jax.ShapeDtypeStruct((steps, width, 4 * tile), jnp.bfloat16),
            jax.ShapeDtypeStruct((steps, width, 2 * tile), jnp.bfloat16),
            jax.ShapeDtypeStruct((steps, 4 * tile, width), jnp.bfloat16),
        ),
        compiler_params=params(48),
        cost_estimate=LIGHT,
        name="prepare_weights",
    )(*own, *other)


def expert_kernel(steps, rows_ref, cols_ref, down_ref, back_ref, out_ref, hidden):
    step = pl.program_id(0)
    width = rows_ref.shape[1] // 2
    pair = down_ref.shape[2]

    @pl.when(step < steps)
    def _():
        both_pre = dot(rows_ref[:, :width], cols_ref[0])
        gate_pre = both_pre[:, :pair]
        up_pre = both_pre[:, pair:]
        down_grad = dot(rows_ref[:, width:], down_ref[0])
        sig = jax.nn.sigmoid(gate_pre)
        hidden[step, :, :pair] = (
            down_grad * up_pre * sig * (1.0 + gate_pre * (1.0 - sig))
        ).astype(jnp.bfloat16)
        hidden[step, :, pair:] = (down_grad * gate_pre * sig).astype(jnp.bfloat16)

    @pl.when(step >= steps)
    def _():
        total = dot(hidden[0], back_ref[0])
        for i in range(1, steps):
            total += dot(hidden[i], back_ref[i])
        out_ref[...] = total.astype(jnp.bfloat16)


def experts(rows, cols, down, back):
    count, twice = rows.shape
    steps, width, quad = cols.shape
    tile = 512
    last = steps - 1
    turn = lambda i: jnp.maximum(i - steps, 0)
    return pl.pallas_call(
        functools.partial(expert_kernel, steps),
        grid=(steps + width // tile,),
        in_specs=[
            pl.BlockSpec((count, twice), lambda i: (0, 0)),
            pl.BlockSpec((1, width, quad), lambda i: (jnp.minimum(i, last), 0, 0)),
            pl.BlockSpec((1, width, quad // 2), lambda i: (jnp.minimum(i, last), 0, 0)),
            pl.BlockSpec((steps, quad, tile), lambda i: (0, 0, turn(i))),
        ],
        out_specs=pl.BlockSpec((count, tile), lambda i: (0, turn(i))),
        out_shape=jax.ShapeDtypeStruct((count, width), jnp.bfloat16),
        scratch_shapes=[pltpu.VMEM((steps, count, quad), jnp.bfloat16)],
        compiler_params=params(48),
        cost_estimate=LIGHT,
        name="expert_terms",
    )(rows, cols, down, back)


def shares_kernel(
    q_ref, key_ref, value_ref, prev_key_ref, prev_value_ref, prev_seg_ref, seg_row_ref, seg_col_ref,
    low_ref, turned_ref, query_ref, key_out, value_out,
):
    tokens = q_ref.shape[0]
    seg_col = seg_col_ref[...]
    row = lax.broadcasted_iota(jnp.int32, (tokens, tokens), 0)
    col = lax.broadcasted_iota(jnp.int32, (tokens, tokens), 1)
    own_seen = jnp.where((col <= row) & (seg_row_ref[...] == seg_col), 1.0, 0.0)
    prev_seg = prev_seg_ref[tokens : tokens + 16, :].astype(jnp.float32)[0:1, :]
    prev_seen = jnp.where(prev_seg == seg_col, 1.0, 0.0)
    seen = jnp.concatenate([prev_seen, own_seen], axis=1) > 0.5
    keys = jnp.concatenate([prev_key_ref[:tokens, :], key_ref[...]], axis=0)
    values = jnp.concatenate([prev_value_ref[:tokens, :], value_ref[...]], axis=0)
    key_out[0] = keys
    value_out[0] = values.T
    for head in range(GROUP):
        rows = slice(head * tokens, (head + 1) * tokens)
        query = q_ref[:, head * HD : (head + 1) * HD]
        scores = dot(query, keys, NT) * (HD**-0.5)
        masked = jnp.where(seen, scores, FLOOR)
        raised = jnp.where(seen, jnp.exp(masked - jnp.max(masked, axis=1, keepdims=True)), 0.0)
        shares = raised / jnp.sum(raised, axis=1, keepdims=True)
        low = shares.astype(jnp.bfloat16)
        low_ref[0, rows, :] = low
        turned_ref[0, :, rows] = low.T
        query_ref[0, rows, :] = query


def attention_shares(queries, key_heads, value_heads, prev, segs):
    tokens, width = queries.shape
    span = 2 * tokens
    stack = GROUP * tokens
    high = prev.shape[0]
    own = pl.BlockSpec((tokens, HD), lambda g: (0, g))
    group = lambda shape: pl.BlockSpec((1,) + shape, lambda g: (g, 0, 0))
    made = lambda shape: jax.ShapeDtypeStruct((KVH,) + shape, jnp.bfloat16)
    shapes = ((stack, span), (span, stack), (stack, HD), (span, HD), (HD, span))
    return pl.pallas_call(
        shares_kernel,
        grid=(KVH,),
        in_specs=[
            pl.BlockSpec((tokens, GROUP * HD), lambda g: (0, g)),
            own,
            own,
            pl.BlockSpec((high, HD), lambda g: (0, g)),
            pl.BlockSpec((high, HD), lambda g: (0, KVH + g)),
            pl.BlockSpec((high, HD), lambda g: (0, 0)),
            pl.BlockSpec((1, tokens), lambda g: (0, 0)),
            pl.BlockSpec((tokens, 1), lambda g: (0, 0)),
        ],
        out_specs=[group(shape) for shape in shapes],
        out_shape=[made(shape) for shape in shapes],
        compiler_params=params(32),
        cost_estimate=LIGHT,
        name="attention_shares",
    )(queries, key_heads, value_heads, prev, prev, prev, segs[None, :], segs[:, None])


def tail_kernel(
    plan, place_info, back_ref, place_ref, grad_ref, *refs
):
    heads, tiles = plan
    mine, across, last, refs = refs[:6], refs[6:12], refs[12:14], refs[14:]
    low_ref, turned_ref, q_ref, key_ref, value_ref, *refs = refs
    moe_ref, query_out, kept_out, sent_out, by_place, stream, held, sums = refs
    step = pl.program_id(0)
    tokens = query_out.shape[0]
    part_size = by_place.shape[2]
    size = mine[0].shape[1]
    mine, across = mine + last, across + last
    spread = part_size // size
    here, core = place_info[1], place_info[2]

    @pl.when(step == 0)
    def _():
        moe = dot(place_ref[...], back_ref[...]).astype(jnp.bfloat16)
        moe_ref[...] = moe
        added = (grad_ref[...].astype(jnp.float32) + moe.astype(jnp.float32)).astype(jnp.bfloat16)
        for z in range(4):
            for rest in range(spread):
                for side in range(2):
                    source = ((z * spread + rest) * 2 + side) * size
                    by_place[2 * z + side, :, rest * size : (rest + 1) * size] = added[:, source : source + size]
        for i in range(8):
            spot = slice(i * part_size, (i + 1) * part_size)
            stream[:, spot] = by_place[2 * (here ^ (i // 2)) + (core ^ (i % 2))]

    @pl.when((step > 0) & ((step - 1) % tiles == 0))
    def _():
        sums[...] = jnp.zeros_like(sums)

    def project(pieces):
        columns = jnp.concatenate([piece[...].reshape(part_size, piece.shape[-1]) for piece in pieces], axis=0)
        return dot(stream[...], columns).astype(jnp.bfloat16)

    def hold(head_grad):
        for head in range(heads):
            held[head * tokens : (head + 1) * tokens, :] = head_grad[:, head * HD : (head + 1) * HD]

    def attend():
        grads = held[...]
        low = low_ref[0].astype(jnp.float32)
        prob_grad = dot(grads, value_ref[0])
        row_dot = jnp.sum(low * prob_grad, axis=1, keepdims=True)
        score_grad = (low * (prob_grad - row_dot) * (HD**-0.5)).astype(jnp.bfloat16)
        query_grad = dot(score_grad, key_ref[0]).astype(jnp.bfloat16)
        sums[0] += dot(score_grad, q_ref[0], TN)
        sums[1] += dot(turned_ref[0], grads)
        for head in range(heads):
            query_out[:, head * HD : (head + 1) * HD] = query_grad[head * tokens : (head + 1) * tokens, :]

    @pl.when(step == 0)
    def _():
        hold(project(mine))

    @pl.when((step > 0) & (step < tiles))
    def _():
        head_grad = project(mine)
        attend()
        hold(head_grad)

    @pl.when((step >= tiles) & (step < 2 * tiles))
    def _():
        head_grad = project(across)
        attend()
        hold(head_grad)

    @pl.when(step == 2 * tiles)
    def _():
        attend()

    @pl.when((step > 0) & (step % tiles == 0))
    def _():
        kept_out[...] = sums[:, tokens:, :]
        sent_out[...] = sums[:, :tokens, :].astype(jnp.bfloat16)


def tail(place_info, back, place, moe_grad, pieces, low, turned, query, keys, values):
    tokens, width = moe_grad.shape
    spread, size, cols = pieces[0].shape
    span = keys.shape[1]
    heads = 4
    tile = heads * HD
    tiles = cols // tile
    steps = KVH * tiles
    was = lambda i: jnp.maximum(i - 1, 0)
    kv_group = lambda i, info: (was(i) // tiles) ^ info[0]
    whole = lambda shape: pl.BlockSpec(shape, lambda i, info: (0,) * len(shape))
    group = lambda shape: pl.BlockSpec((1,) + shape, lambda i, info: (kv_group(i, info), 0, 0))
    rows = lambda shape: pl.BlockSpec((1,) + shape, lambda i, info: (kv_group(i, info), was(i) % tiles, 0))
    own_tile = lambda i: jnp.minimum(i, tiles - 1)
    other_tile = lambda i: jnp.minimum(jnp.maximum(i - tiles, 0), tiles - 1)
    now = lambda i: jnp.minimum(i, steps - 1)
    last = pl.BlockSpec((spread, 1, size, tile), lambda i, info: (0, now(i) // tiles, 0, now(i) % tiles))
    piece = lambda turn: pl.BlockSpec((spread, size, tile), lambda i, info: (0, 0, turn(i)))
    kv = pl.BlockSpec((2, tokens, HD), lambda i, info: (0, 0, kv_group(i, info)))
    return pl.pallas_call(
        functools.partial(tail_kernel, (heads, tiles)),
        grid_spec=pltpu.PrefetchScalarGridSpec(
            num_scalar_prefetch=1,
            grid=(steps + 1,),
            in_specs=[whole(back.shape), whole(place.shape), whole(moe_grad.shape)]
            + [piece(own_tile)] * 6
            + [piece(other_tile)] * 6
            + [last] * 2
            + [
                rows((heads * tokens, span)),
                pl.BlockSpec(
                    (1, span, heads * tokens), lambda i, info: (kv_group(i, info), 0, was(i) % tiles)
                ),
                rows((heads * tokens, HD)),
                group((span, HD)),
                group((HD, span)),
            ],
            out_specs=[
                whole((tokens, width)),
                pl.BlockSpec(
                    (tokens, tile), lambda i, info: (0, kv_group(i, info) * tiles + was(i) % tiles)
                ),
                kv,
                kv,
            ],
            scratch_shapes=[
                pltpu.VMEM((8, tokens, spread * size), jnp.bfloat16),
                pltpu.VMEM((tokens, width), jnp.bfloat16),
                pltpu.VMEM((heads * tokens, HD), jnp.bfloat16),
                pltpu.VMEM((2, span, HD), jnp.float32),
            ],
        ),
        out_shape=(
            jax.ShapeDtypeStruct((tokens, width), jnp.bfloat16),
            jax.ShapeDtypeStruct((tokens, KVH * cols), jnp.bfloat16),
            jax.ShapeDtypeStruct((2, tokens, KVH * HD), jnp.float32),
            jax.ShapeDtypeStruct((2, tokens, KVH * HD), jnp.bfloat16),
        ),
        compiler_params=params(56),
        cost_estimate=pl.CostEstimate(
            flops=2 * tokens * width * KVH * cols, bytes_accessed=22 * MIB, transcendentals=0
        ),
        name="tail_attention",
    )(place_info, back, place, moe_grad, *pieces, low, turned, query, keys, values)


def finish_kernel(kept_ref, later_ref, key_ref, value_ref):
    for kind, out_ref in enumerate((key_ref, value_ref)):
        out_ref[...] = kept_ref[kind] + later_ref[kind].astype(jnp.float32)


def finish(kept, later):
    out = jax.ShapeDtypeStruct(kept.shape[1:], jnp.float32)
    return pl.pallas_call(
        finish_kernel, out_shape=(out, out), compiler_params=params(60), cost_estimate=LIGHT, name="finish"
    )(kept, later)


def local(
    moe_input,
    moe_grad,
    routes,
    route_weight,
    w_gate,
    w_up,
    w_down,
    w_out,
    queries,
    key_heads,
    value_heads,
    segments,
):
    chips = ("far", "near", "low")
    blk = chips + ("core",)
    low = lax.axis_size("low")
    owners = 4 * low
    count = 2 * owners
    parts = lax.axis_size("groups")
    tokens, width = moe_input.shape
    depth = 2 * max(1, 3 * tokens * routes.shape[1] // (2 * count))
    swap = [(0, 1), (1, 0)]
    onward = [(i, i + 1) for i in range(count - 1)]
    backward = [(i + 1, i) for i in range(count - 1)]

    share_cols = w_out.shape[1] // parts
    w_share = lax.dynamic_slice_in_dim(w_out, lax.axis_index("groups") * share_cols, share_cols, 1)
    w_near = lax.ppermute(w_share, "near", swap)
    w_far = lax.ppermute(w_share, "far", swap)

    rows, place = pick(routes, route_weight, moe_input, moe_grad, owners, depth)
    line = lambda w: lax.all_gather(w, "low", axis=0, tiled=False)
    cross = lambda w: lax.ppermute(w, "groups", swap)
    other_core = lambda w: lax.ppermute(w, "core", swap)
    own = (w_gate, w_up, w_down)
    other = tuple(other_core(w) for w in own)

    key_heads, value_heads, segments, place = lax.optimization_barrier((key_heads, value_heads, segments, place))
    kv = jnp.concatenate([key_heads, value_heads], axis=1)
    segs = (segments + 1).astype(jnp.float32)
    seg_rows = jnp.zeros((16, kv.shape[1]), jnp.bfloat16).at[0, :tokens].set(segs.astype(jnp.bfloat16))
    prev = lax.ppermute(jnp.concatenate([kv, seg_rows], axis=0), blk, onward)
    own_line = line(w_share)
    rows, w_near, w_far, own_line, prev = lax.optimization_barrier((rows, w_near, w_far, own_line, prev))

    rows_in = lax.all_to_all(rows.reshape(owners, depth, 2 * width), chips, 0, 0, tiled=True)
    near_line, far_line = line(w_near), line(w_far)
    w_last = lax.ppermute(w_far, "near", swap)
    prepared = prepare_weights(own, other)
    attention = attention_shares(queries, key_heads, value_heads, prev, segs)
    near_line, prepared, attention = lax.optimization_barrier((near_line, prepared, attention))
    crossed = [cross(own_line), cross(near_line)]
    rows_in, prepared, attention, near_line, far_line, crossed, w_last = lax.optimization_barrier(
        (rows_in, prepared, attention, near_line, far_line, crossed, w_last)
    )
    lines = [own_line, near_line, far_line]
    last_crossed = cross(w_last)
    terms = experts(rows_in.reshape(owners * depth, 2 * width), *prepared)
    terms, lines, crossed, last_crossed = lax.optimization_barrier((terms, lines, crossed, last_crossed))
    last_line = line(jnp.stack([w_last, last_crossed]))
    far_crossed = cross(lines[2])
    back = lax.all_to_all(terms.reshape(owners, depth, width), chips, 0, 0, tiled=True)
    both = lambda pieces: [w for piece in pieces for w in (piece, other_core(piece))]

    z = 2 * lax.axis_index("far") + lax.axis_index("near")
    moe_input_grad, query_grad, kept, sent = tail(
        jnp.stack([lax.axis_index("groups"), z, lax.axis_index("core")]).astype(jnp.int32),
        back.reshape(owners * depth, width), place, moe_grad,
        both(lines) + both(crossed + [far_crossed]) + both([last_line]), *attention,
    )
    return (moe_input_grad, query_grad, *finish(kept, lax.ppermute(sent, blk, backward)))


def solution(mesh):
    names = ("groups", "far", "near", "low", "core")
    shape = (mesh.shape["groups"], 2, 2, mesh.shape["blk"] // 8, 2)
    fine = jax.sharding.Mesh(mesh.devices.reshape(shape), names)
    blk = names[1:]
    by_tokens = P(names, None)
    return jax.shard_map(
        local,
        mesh=fine,
        in_specs=(
            by_tokens,
            by_tokens,
            by_tokens,
            by_tokens,
            P(None, blk),
            P(None, blk),
            P(blk, None),
            P(blk, None),
            by_tokens,
            by_tokens,
            by_tokens,
            P(names),
        ),
        out_specs=(by_tokens,) * 4,
        check_vma=False,
    )
```

```python
import functools

import jax
import jax.numpy as jnp
from jax import lax
from jax.experimental import pallas as pl
from jax.experimental.pallas import tpu as pltpu
from jax.sharding import PartitionSpec as P

KVH = 2
GROUP = 16
HD = 128
FLOOR = -1e30
MIB = 1 << 20
LIGHT = pl.CostEstimate(flops=0, bytes_accessed=0, transcendentals=0)

NT = (((1,), (1,)), ((), ()))
TN = (((0,), (0,)), ((), ()))


def dot(a, b, dims=(((1,), (0,)), ((), ()))):
    return lax.dot_general(a, b, dims, preferred_element_type=jnp.float32)


def params(mib):
    return pltpu.CompilerParams(vmem_limit_bytes=mib * MIB)


def pick_kernel(owners, depth, routes_ref, weight_ref, input_ref, grad_ref, rows_ref, back_ref):
    tokens = input_ref.shape[0]
    slots = owners * depth
    first = routes_ref[0:1, :]
    second = routes_ref[1:2, :]
    expert = lax.broadcasted_iota(jnp.int32, (owners, tokens), 0)
    is_first = first == expert
    is_second = second == expert
    member = jnp.where(is_first | is_second, 1.0, 0.0)
    before = lax.broadcasted_iota(jnp.int32, (tokens, tokens), 0) < lax.broadcasted_iota(
        jnp.int32, (tokens, tokens), 1
    )
    rank = dot(member.astype(jnp.bfloat16), jnp.where(before, 1.0, 0.0).astype(jnp.bfloat16))
    spot = (expert * depth).astype(jnp.float32) + rank
    slot_first = jnp.sum(jnp.where(is_first, spot, 0.0), axis=0, keepdims=True).astype(jnp.int32)
    slot_second = jnp.sum(jnp.where(is_second, spot, 0.0), axis=0, keepdims=True).astype(jnp.int32)
    slot = lax.broadcasted_iota(jnp.int32, (slots, tokens), 0)
    at_first = slot == slot_first
    at_second = slot == slot_second
    place = jnp.where(at_first | at_second, 1.0, 0.0).astype(jnp.bfloat16)
    back_ref[...] = place.T
    scale = jnp.sum(
        jnp.where(at_first, weight_ref[0:1, :], 0.0) + jnp.where(at_second, weight_ref[1:2, :], 0.0),
        axis=1,
        keepdims=True,
    )
    width = input_ref.shape[1]
    rows_ref[:, :width] = dot(place, input_ref[...]).astype(jnp.bfloat16)
    rows_ref[:, width:] = (scale * dot(place, grad_ref[...])).astype(jnp.bfloat16)


def pick(routes, route_weight, moe_input, moe_grad, owners, depth):
    tokens, width = moe_input.shape
    slots = owners * depth
    return pl.pallas_call(
        functools.partial(pick_kernel, owners, depth),
        out_shape=(
            jax.ShapeDtypeStruct((slots, 2 * width), jnp.bfloat16),
            jax.ShapeDtypeStruct((tokens, slots), jnp.bfloat16),
        ),
        compiler_params=params(32),
        cost_estimate=pl.CostEstimate(
            flops=4 * slots * tokens * width, bytes_accessed=8 * MIB, transcendentals=0
        ),
        name="pick_rows",
    )(routes.T, route_weight.T, moe_input, moe_grad)


def weights_kernel(*refs):
    own, other, (cols_ref, down_ref, rows_ref) = refs[:3], refs[3:6], refs[6:]
    tile = own[0].shape[1]
    for place, (gate_ref, up_ref, low_ref) in enumerate((own, other)):
        for kind, ref in enumerate((gate_ref, up_ref)):
            spot = slice((2 * kind + place) * tile, (2 * kind + place + 1) * tile)
            cols_ref[0, :, spot] = ref[...]
            rows_ref[0, spot, :] = ref[...].T
        down_ref[0, :, place * tile : (place + 1) * tile] = low_ref[...].T


def prepare_weights(own, other):
    width, half = own[0].shape
    tile = 128
    steps = half // tile
    cols = pl.BlockSpec((width, tile), lambda i: (0, i))
    down = pl.BlockSpec((tile, width), lambda i: (i, 0))
    return pl.pallas_call(
        weights_kernel,
        grid=(steps,),
        in_specs=[cols, cols, down] * 2,
        out_specs=[
            pl.BlockSpec((1, width, 4 * tile), lambda i: (i, 0, 0)),
            pl.BlockSpec((1, width, 2 * tile), lambda i: (i, 0, 0)),
            pl.BlockSpec((1, 4 * tile, width), lambda i: (i, 0, 0)),
        ],
        out_shape=(
            jax.ShapeDtypeStruct((steps, width, 4 * tile), jnp.bfloat16),
            jax.ShapeDtypeStruct((steps, width, 2 * tile), jnp.bfloat16),
            jax.ShapeDtypeStruct((steps, 4 * tile, width), jnp.bfloat16),
        ),
        compiler_params=params(48),
        cost_estimate=LIGHT,
        name="prepare_weights",
    )(*own, *other)


def expert_kernel(steps, rows_ref, cols_ref, down_ref, back_ref, out_ref, hidden):
    step = pl.program_id(0)
    width = rows_ref.shape[1] // 2
    pair = down_ref.shape[2]

    @pl.when(step < steps)
    def _():
        both_pre = dot(rows_ref[:, :width], cols_ref[0])
        gate_pre = both_pre[:, :pair]
        up_pre = both_pre[:, pair:]
        down_grad = dot(rows_ref[:, width:], down_ref[0])
        sig = jax.nn.sigmoid(gate_pre)
        hidden[step, :, :pair] = (
            down_grad * up_pre * sig * (1.0 + gate_pre * (1.0 - sig))
        ).astype(jnp.bfloat16)
        hidden[step, :, pair:] = (down_grad * gate_pre * sig).astype(jnp.bfloat16)

    @pl.when(step >= steps)
    def _():
        total = dot(hidden[0], back_ref[0])
        for i in range(1, steps):
            total += dot(hidden[i], back_ref[i])
        out_ref[...] = total.astype(jnp.bfloat16)


def experts(rows, cols, down, back):
    count, twice = rows.shape
    steps, width, quad = cols.shape
    tile = 512
    last = steps - 1
    turn = lambda i: jnp.maximum(i - steps, 0)
    return pl.pallas_call(
        functools.partial(expert_kernel, steps),
        grid=(steps + width // tile,),
        in_specs=[
            pl.BlockSpec((count, twice), lambda i: (0, 0)),
            pl.BlockSpec((1, width, quad), lambda i: (jnp.minimum(i, last), 0, 0)),
            pl.BlockSpec((1, width, quad // 2), lambda i: (jnp.minimum(i, last), 0, 0)),
            pl.BlockSpec((steps, quad, tile), lambda i: (0, 0, turn(i))),
        ],
        out_specs=pl.BlockSpec((count, tile), lambda i: (0, turn(i))),
        out_shape=jax.ShapeDtypeStruct((count, width), jnp.bfloat16),
        scratch_shapes=[pltpu.VMEM((steps, count, quad), jnp.bfloat16)],
        compiler_params=params(48),
        cost_estimate=LIGHT,
        name="expert_terms",
    )(rows, cols, down, back)


def shares_kernel(
    q_ref, key_ref, value_ref, prev_key_ref, prev_value_ref, prev_seg_ref, seg_row_ref, seg_col_ref,
    low_ref, turned_ref, query_ref, key_out, value_out,
):
    tokens = q_ref.shape[0]
    seg_col = seg_col_ref[...]
    row = lax.broadcasted_iota(jnp.int32, (tokens, tokens), 0)
    col = lax.broadcasted_iota(jnp.int32, (tokens, tokens), 1)
    own_seen = jnp.where((col <= row) & (seg_row_ref[...] == seg_col), 1.0, 0.0)
    prev_seg = prev_seg_ref[tokens : tokens + 16, :].astype(jnp.float32)[0:1, :]
    prev_seen = jnp.where(prev_seg == seg_col, 1.0, 0.0)
    seen = jnp.concatenate([prev_seen, own_seen], axis=1) > 0.5
    keys = jnp.concatenate([prev_key_ref[:tokens, :], key_ref[...]], axis=0)
    values = jnp.concatenate([prev_value_ref[:tokens, :], value_ref[...]], axis=0)
    key_out[0] = keys
    value_out[0] = values.T
    for head in range(GROUP):
        rows = slice(head * tokens, (head + 1) * tokens)
        query = q_ref[:, head * HD : (head + 1) * HD]
        scores = dot(query, keys, NT) * (HD**-0.5)
        masked = jnp.where(seen, scores, FLOOR)
        raised = jnp.where(seen, jnp.exp(masked - jnp.max(masked, axis=1, keepdims=True)), 0.0)
        shares = raised / jnp.sum(raised, axis=1, keepdims=True)
        low = shares.astype(jnp.bfloat16)
        low_ref[0, rows, :] = low
        turned_ref[0, :, rows] = low.T
        query_ref[0, rows, :] = query


def attention_shares(queries, key_heads, value_heads, prev, segs):
    tokens, width = queries.shape
    span = 2 * tokens
    stack = GROUP * tokens
    high = prev.shape[0]
    own = pl.BlockSpec((tokens, HD), lambda g: (0, g))
    group = lambda shape: pl.BlockSpec((1,) + shape, lambda g: (g, 0, 0))
    made = lambda shape: jax.ShapeDtypeStruct((KVH,) + shape, jnp.bfloat16)
    shapes = ((stack, span), (span, stack), (stack, HD), (span, HD), (HD, span))
    return pl.pallas_call(
        shares_kernel,
        grid=(KVH,),
        in_specs=[
            pl.BlockSpec((tokens, GROUP * HD), lambda g: (0, g)),
            own,
            own,
            pl.BlockSpec((high, HD), lambda g: (0, g)),
            pl.BlockSpec((high, HD), lambda g: (0, KVH + g)),
            pl.BlockSpec((high, HD), lambda g: (0, 0)),
            pl.BlockSpec((1, tokens), lambda g: (0, 0)),
            pl.BlockSpec((tokens, 1), lambda g: (0, 0)),
        ],
        out_specs=[group(shape) for shape in shapes],
        out_shape=[made(shape) for shape in shapes],
        compiler_params=params(32),
        cost_estimate=LIGHT,
        name="attention_shares",
    )(queries, key_heads, value_heads, prev, prev, prev, segs[None, :], segs[:, None])


def tail_kernel(
    plan, place_info, back_ref, place_ref, grad_ref, *refs
):
    heads, tiles = plan
    own, last, twin, refs = refs[:4], refs[4:8], refs[8:12], refs[12:]
    low_ref, turned_ref, q_ref, key_ref, value_ref, *refs = refs
    moe_ref, query_out, kept_out, sent_out, by_place, stream, held, sums = refs
    step = pl.program_id(0)
    tokens = query_out.shape[0]
    part_size = by_place.shape[2]
    size = own[0].shape[1]
    mine, across = own[:2] + twin + last[:2], own[2:] + twin + last[2:]
    spread = part_size // size
    here, core = place_info[1], place_info[2]

    @pl.when(step == 0)
    def _():
        moe = dot(place_ref[...], back_ref[...]).astype(jnp.bfloat16)
        moe_ref[...] = moe
        added = (grad_ref[...].astype(jnp.float32) + moe.astype(jnp.float32)).astype(jnp.bfloat16)
        for z in range(4):
            for rest in range(spread):
                for side in range(2):
                    source = ((z * spread + rest) * 2 + side) * size
                    by_place[2 * z + side, :, rest * size : (rest + 1) * size] = added[:, source : source + size]
        for i in range(8):
            spot = slice(i * part_size, (i + 1) * part_size)
            stream[:, spot] = by_place[2 * (here ^ (i // 2)) + (core ^ (i % 2))]

    @pl.when((step > 0) & ((step - 1) % tiles == 0))
    def _():
        sums[...] = jnp.zeros_like(sums)

    def project(pieces):
        columns = jnp.concatenate([piece[...].reshape(part_size, piece.shape[-1]) for piece in pieces], axis=0)
        return dot(stream[...], columns).astype(jnp.bfloat16)

    def hold(head_grad):
        for head in range(heads):
            held[head * tokens : (head + 1) * tokens, :] = head_grad[:, head * HD : (head + 1) * HD]

    def attend():
        grads = held[...]
        low = low_ref[0].astype(jnp.float32)
        prob_grad = dot(grads, value_ref[0])
        row_dot = jnp.sum(low * prob_grad, axis=1, keepdims=True)
        score_grad = (low * (prob_grad - row_dot) * (HD**-0.5)).astype(jnp.bfloat16)
        query_grad = dot(score_grad, key_ref[0]).astype(jnp.bfloat16)
        sums[0] += dot(score_grad, q_ref[0], TN)
        sums[1] += dot(turned_ref[0], grads)
        for head in range(heads):
            query_out[:, head * HD : (head + 1) * HD] = query_grad[head * tokens : (head + 1) * tokens, :]

    @pl.when(step == 0)
    def _():
        hold(project(mine))

    @pl.when((step > 0) & (step < tiles))
    def _():
        head_grad = project(mine)
        attend()
        hold(head_grad)

    @pl.when((step >= tiles) & (step < 2 * tiles))
    def _():
        head_grad = project(across)
        attend()
        hold(head_grad)

    @pl.when(step == 2 * tiles)
    def _():
        attend()

    @pl.when((step > 0) & (step % tiles == 0))
    def _():
        kept_out[...] = sums[:, tokens:, :]
        sent_out[...] = sums[:, :tokens, :].astype(jnp.bfloat16)


def tail(place_info, back, place, moe_grad, pieces, low, turned, query, keys, values):
    tokens, width = moe_grad.shape
    spread, size, cols = pieces[0].shape
    span = keys.shape[1]
    heads = 4
    tile = heads * HD
    tiles = cols // tile
    steps = KVH * tiles
    was = lambda i: jnp.maximum(i - 1, 0)
    kv_group = lambda i, info: (was(i) // tiles) ^ info[0]
    whole = lambda shape: pl.BlockSpec(shape, lambda i, info: (0,) * len(shape))
    group = lambda shape: pl.BlockSpec((1,) + shape, lambda i, info: (kv_group(i, info), 0, 0))
    rows = lambda shape: pl.BlockSpec((1,) + shape, lambda i, info: (kv_group(i, info), was(i) % tiles, 0))
    own_tile = lambda i: jnp.minimum(i, tiles - 1)
    other_tile = lambda i: jnp.minimum(jnp.maximum(i - tiles, 0), tiles - 1)
    now = lambda i: jnp.minimum(i, steps - 1)
    twin = pl.BlockSpec((spread, 1, size, tile), lambda i, info: (0, now(i) // tiles, 0, now(i) % tiles))
    piece = lambda turn: pl.BlockSpec((spread, size, tile), lambda i, info: (0, 0, turn(i)))
    kv = pl.BlockSpec((2, tokens, HD), lambda i, info: (0, 0, kv_group(i, info)))
    return pl.pallas_call(
        functools.partial(tail_kernel, (heads, tiles)),
        grid_spec=pltpu.PrefetchScalarGridSpec(
            num_scalar_prefetch=1,
            grid=(steps + 1,),
            in_specs=[whole(back.shape), whole(place.shape), whole(moe_grad.shape)]
            + ([piece(own_tile)] * 2 + [piece(other_tile)] * 2) * 2
            + [twin] * 4
            + [
                rows((heads * tokens, span)),
                pl.BlockSpec(
                    (1, span, heads * tokens), lambda i, info: (kv_group(i, info), 0, was(i) % tiles)
                ),
                rows((heads * tokens, HD)),
                group((span, HD)),
                group((HD, span)),
            ],
            out_specs=[
                whole((tokens, width)),
                pl.BlockSpec(
                    (tokens, tile), lambda i, info: (0, kv_group(i, info) * tiles + was(i) % tiles)
                ),
                kv,
                kv,
            ],
            scratch_shapes=[
                pltpu.VMEM((8, tokens, spread * size), jnp.bfloat16),
                pltpu.VMEM((tokens, width), jnp.bfloat16),
                pltpu.VMEM((heads * tokens, HD), jnp.bfloat16),
                pltpu.VMEM((2, span, HD), jnp.float32),
            ],
        ),
        out_shape=(
            jax.ShapeDtypeStruct((tokens, width), jnp.bfloat16),
            jax.ShapeDtypeStruct((tokens, KVH * cols), jnp.bfloat16),
            jax.ShapeDtypeStruct((2, tokens, KVH * HD), jnp.float32),
            jax.ShapeDtypeStruct((2, tokens, KVH * HD), jnp.bfloat16),
        ),
        compiler_params=params(56),
        cost_estimate=pl.CostEstimate(
            flops=2 * tokens * width * KVH * cols, bytes_accessed=22 * MIB, transcendentals=0
        ),
        name="tail_attention",
    )(place_info, back, place, moe_grad, *pieces, low, turned, query, keys, values)


def finish_kernel(kept_ref, later_ref, key_ref, value_ref):
    for kind, out_ref in enumerate((key_ref, value_ref)):
        out_ref[...] = kept_ref[kind] + later_ref[kind].astype(jnp.float32)


def finish(kept, later):
    out = jax.ShapeDtypeStruct(kept.shape[1:], jnp.float32)
    return pl.pallas_call(
        finish_kernel, out_shape=(out, out), compiler_params=params(60), cost_estimate=LIGHT, name="finish"
    )(kept, later)


def local(
    moe_input,
    moe_grad,
    routes,
    route_weight,
    w_gate,
    w_up,
    w_down,
    w_out,
    queries,
    key_heads,
    value_heads,
    segments,
):
    chips = ("far", "near", "low")
    blk = chips + ("core",)
    low = lax.axis_size("low")
    owners = 4 * low
    count = 2 * owners
    parts = lax.axis_size("groups")
    tokens, width = moe_input.shape
    depth = 2 * max(1, 3 * tokens * routes.shape[1] // (2 * count))
    swap = [(0, 1), (1, 0)]
    onward = [(i, i + 1) for i in range(count - 1)]
    backward = [(i + 1, i) for i in range(count - 1)]

    share_cols = w_out.shape[1] // parts
    w_share = lax.dynamic_slice_in_dim(w_out, lax.axis_index("groups") * share_cols, share_cols, 1)
    w_near = lax.ppermute(w_share, "near", swap)
    w_far = lax.ppermute(w_share, "far", swap)

    rows, place = pick(routes, route_weight, moe_input, moe_grad, owners, depth)
    line = lambda w: lax.all_gather(w, "low", axis=0, tiled=False)
    cross = lambda w: lax.ppermute(w, "groups", swap)
    other_core = lambda w: lax.ppermute(w, "core", swap)
    own = (w_gate, w_up, w_down)
    other = tuple(other_core(w) for w in own)

    key_heads, value_heads, segments, place = lax.optimization_barrier((key_heads, value_heads, segments, place))
    kv = jnp.concatenate([key_heads, value_heads], axis=1)
    segs = (segments + 1).astype(jnp.float32)
    seg_rows = jnp.zeros((16, kv.shape[1]), jnp.bfloat16).at[0, :tokens].set(segs.astype(jnp.bfloat16))
    prev = lax.ppermute(jnp.concatenate([kv, seg_rows], axis=0), blk, onward)
    own_line = line(w_share)
    rows, w_near, w_far, own_line, prev = lax.optimization_barrier((rows, w_near, w_far, own_line, prev))

    rows_in = lax.all_to_all(rows.reshape(owners, depth, 2 * width), chips, 0, 0, tiled=True)
    near_crossed, far_crossed = cross(w_near), cross(w_far)
    near_twin = line(jnp.stack([w_near, near_crossed]))
    far_twin = line(jnp.stack([w_far, far_crossed]))
    own_line, near_crossed, far_crossed = lax.optimization_barrier((own_line, near_crossed, far_crossed))
    own_crossed = cross(own_line)
    w_last = lax.ppermute(w_far, "near", swap)
    prepared = prepare_weights(own, other)
    attention = attention_shares(queries, key_heads, value_heads, prev, segs)
    rows_in, prepared, attention, own_line, own_crossed, w_last = lax.optimization_barrier(
        (rows_in, prepared, attention, own_line, own_crossed, w_last)
    )
    if low == 2:
        moved = lax.ppermute(w_last, "low", swap)
        first = lax.axis_index("low") == 0
        last_line = jnp.where(first, jnp.stack([w_last, moved]), jnp.stack([moved, w_last]))
    else:
        last_line = line(w_last)
    terms = experts(rows_in.reshape(owners * depth, 2 * width), *prepared)
    terms, own_line, own_crossed, last_line, near_twin, far_twin = lax.optimization_barrier(
        (terms, own_line, own_crossed, last_line, near_twin, far_twin)
    )
    last_crossed = cross(last_line)
    back = lax.all_to_all(terms.reshape(owners, depth, width), chips, 0, 0, tiled=True)
    both = lambda *pieces: [w for piece in pieces for w in (piece, other_core(piece))]

    z = 2 * lax.axis_index("far") + lax.axis_index("near")
    moe_input_grad, query_grad, kept, sent = tail(
        jnp.stack([lax.axis_index("groups"), z, lax.axis_index("core")]).astype(jnp.int32),
        back.reshape(owners * depth, width), place, moe_grad,
        both(own_line, own_crossed, last_line, last_crossed, near_twin, far_twin), *attention,
    )
    return (moe_input_grad, query_grad, *finish(kept, lax.ppermute(sent, blk, backward)))


def solution(mesh):
    names = ("groups", "far", "near", "low", "core")
    shape = (mesh.shape["groups"], 2, 2, mesh.shape["blk"] // 8, 2)
    fine = jax.sharding.Mesh(mesh.devices.reshape(shape), names)
    blk = names[1:]
    by_tokens = P(names, None)
    return jax.shard_map(
        local,
        mesh=fine,
        in_specs=(
            by_tokens,
            by_tokens,
            by_tokens,
            by_tokens,
            P(None, blk),
            P(None, blk),
            P(blk, None),
            P(blk, None),
            by_tokens,
            by_tokens,
            by_tokens,
            P(names),
        ),
        out_specs=(by_tokens,) * 4,
        check_vma=False,
    )
```

```python
import functools

import jax
import jax.numpy as jnp
from jax import lax
from jax.experimental import pallas as pl
from jax.experimental.pallas import tpu as pltpu
from jax.sharding import PartitionSpec as P

KVH = 2
GROUP = 16
HD = 128
FLOOR = -1e30
MIB = 1 << 20
LIGHT = pl.CostEstimate(flops=0, bytes_accessed=0, transcendentals=0)

NT = (((1,), (1,)), ((), ()))
TN = (((0,), (0,)), ((), ()))


def dot(a, b, dims=(((1,), (0,)), ((), ()))):
    return lax.dot_general(a, b, dims, preferred_element_type=jnp.float32)


def params(mib):
    return pltpu.CompilerParams(vmem_limit_bytes=mib * MIB)


def pick_kernel(owners, depth, routes_ref, weight_ref, input_ref, grad_ref, rows_ref, back_ref):
    tokens = input_ref.shape[0]
    slots = owners * depth
    first = routes_ref[0:1, :]
    second = routes_ref[1:2, :]
    expert = lax.broadcasted_iota(jnp.int32, (owners, tokens), 0)
    is_first = first == expert
    is_second = second == expert
    member = jnp.where(is_first | is_second, 1.0, 0.0)
    before = lax.broadcasted_iota(jnp.int32, (tokens, tokens), 0) < lax.broadcasted_iota(
        jnp.int32, (tokens, tokens), 1
    )
    rank = dot(member.astype(jnp.bfloat16), jnp.where(before, 1.0, 0.0).astype(jnp.bfloat16))
    spot = (expert * depth).astype(jnp.float32) + rank
    slot_first = jnp.sum(jnp.where(is_first, spot, 0.0), axis=0, keepdims=True).astype(jnp.int32)
    slot_second = jnp.sum(jnp.where(is_second, spot, 0.0), axis=0, keepdims=True).astype(jnp.int32)
    slot = lax.broadcasted_iota(jnp.int32, (slots, tokens), 0)
    at_first = slot == slot_first
    at_second = slot == slot_second
    place = jnp.where(at_first | at_second, 1.0, 0.0).astype(jnp.bfloat16)
    back_ref[...] = place.T
    scale = jnp.sum(
        jnp.where(at_first, weight_ref[0:1, :], 0.0) + jnp.where(at_second, weight_ref[1:2, :], 0.0),
        axis=1,
        keepdims=True,
    )
    width = input_ref.shape[1]
    rows_ref[:, :width] = dot(place, input_ref[...]).astype(jnp.bfloat16)
    rows_ref[:, width:] = (scale * dot(place, grad_ref[...])).astype(jnp.bfloat16)


def pick(routes, route_weight, moe_input, moe_grad, owners, depth):
    tokens, width = moe_input.shape
    slots = owners * depth
    return pl.pallas_call(
        functools.partial(pick_kernel, owners, depth),
        out_shape=(
            jax.ShapeDtypeStruct((slots, 2 * width), jnp.bfloat16),
            jax.ShapeDtypeStruct((tokens, slots), jnp.bfloat16),
        ),
        compiler_params=params(32),
        cost_estimate=pl.CostEstimate(
            flops=4 * slots * tokens * width, bytes_accessed=8 * MIB, transcendentals=0
        ),
        name="pick_rows",
    )(routes.T, route_weight.T, moe_input, moe_grad)


def weights_kernel(*refs):
    own, other, (cols_ref, down_ref, rows_ref) = refs[:3], refs[3:6], refs[6:]
    tile = own[0].shape[1]
    for place, (gate_ref, up_ref, low_ref) in enumerate((own, other)):
        for kind, ref in enumerate((gate_ref, up_ref)):
            spot = slice((2 * kind + place) * tile, (2 * kind + place + 1) * tile)
            cols_ref[0, :, spot] = ref[...]
            rows_ref[0, spot, :] = ref[...].T
        down_ref[0, :, place * tile : (place + 1) * tile] = low_ref[...].T


def prepare_weights(own, other):
    width, half = own[0].shape
    tile = 128
    steps = half // tile
    cols = pl.BlockSpec((width, tile), lambda i: (0, i))
    down = pl.BlockSpec((tile, width), lambda i: (i, 0))
    return pl.pallas_call(
        weights_kernel,
        grid=(steps,),
        in_specs=[cols, cols, down] * 2,
        out_specs=[
            pl.BlockSpec((1, width, 4 * tile), lambda i: (i, 0, 0)),
            pl.BlockSpec((1, width, 2 * tile), lambda i: (i, 0, 0)),
            pl.BlockSpec((1, 4 * tile, width), lambda i: (i, 0, 0)),
        ],
        out_shape=(
            jax.ShapeDtypeStruct((steps, width, 4 * tile), jnp.bfloat16),
            jax.ShapeDtypeStruct((steps, width, 2 * tile), jnp.bfloat16),
            jax.ShapeDtypeStruct((steps, 4 * tile, width), jnp.bfloat16),
        ),
        compiler_params=params(48),
        cost_estimate=LIGHT,
        name="prepare_weights",
    )(*own, *other)


def expert_kernel(steps, rows_ref, cols_ref, down_ref, back_ref, out_ref, hidden):
    step = pl.program_id(0)
    width = rows_ref.shape[1] // 2
    pair = down_ref.shape[2]

    @pl.when(step < steps)
    def _():
        both_pre = dot(rows_ref[:, :width], cols_ref[0])
        gate_pre = both_pre[:, :pair]
        up_pre = both_pre[:, pair:]
        down_grad = dot(rows_ref[:, width:], down_ref[0])
        sig = jax.nn.sigmoid(gate_pre)
        hidden[step, :, :pair] = (
            down_grad * up_pre * sig * (1.0 + gate_pre * (1.0 - sig))
        ).astype(jnp.bfloat16)
        hidden[step, :, pair:] = (down_grad * gate_pre * sig).astype(jnp.bfloat16)

    @pl.when(step >= steps)
    def _():
        total = dot(hidden[0], back_ref[0])
        for i in range(1, steps):
            total += dot(hidden[i], back_ref[i])
        out_ref[...] = total.astype(jnp.bfloat16)


def experts(rows, cols, down, back):
    count, twice = rows.shape
    steps, width, quad = cols.shape
    tile = 512
    last = steps - 1
    turn = lambda i: jnp.maximum(i - steps, 0)
    return pl.pallas_call(
        functools.partial(expert_kernel, steps),
        grid=(steps + width // tile,),
        in_specs=[
            pl.BlockSpec((count, twice), lambda i: (0, 0)),
            pl.BlockSpec((1, width, quad), lambda i: (jnp.minimum(i, last), 0, 0)),
            pl.BlockSpec((1, width, quad // 2), lambda i: (jnp.minimum(i, last), 0, 0)),
            pl.BlockSpec((steps, quad, tile), lambda i: (0, 0, turn(i))),
        ],
        out_specs=pl.BlockSpec((count, tile), lambda i: (0, turn(i))),
        out_shape=jax.ShapeDtypeStruct((count, width), jnp.bfloat16),
        scratch_shapes=[pltpu.VMEM((steps, count, quad), jnp.bfloat16)],
        compiler_params=params(48),
        cost_estimate=LIGHT,
        name="expert_terms",
    )(rows, cols, down, back)


def shares_kernel(
    q_ref, key_ref, value_ref, prev_key_ref, prev_value_ref, prev_seg_ref, seg_row_ref, seg_col_ref,
    low_ref, turned_ref, query_ref, key_out, value_out,
):
    tokens = q_ref.shape[0]
    seg_col = seg_col_ref[...]
    row = lax.broadcasted_iota(jnp.int32, (tokens, tokens), 0)
    col = lax.broadcasted_iota(jnp.int32, (tokens, tokens), 1)
    own_seen = jnp.where((col <= row) & (seg_row_ref[...] == seg_col), 1.0, 0.0)
    prev_seg = prev_seg_ref[tokens : tokens + 16, :].astype(jnp.float32)[0:1, :]
    prev_seen = jnp.where(prev_seg == seg_col, 1.0, 0.0)
    seen = jnp.concatenate([prev_seen, own_seen], axis=1) > 0.5
    keys = jnp.concatenate([prev_key_ref[:tokens, :], key_ref[...]], axis=0)
    values = jnp.concatenate([prev_value_ref[:tokens, :], value_ref[...]], axis=0)
    key_out[0] = keys
    value_out[0] = values.T
    for head in range(GROUP):
        rows = slice(head * tokens, (head + 1) * tokens)
        query = q_ref[:, head * HD : (head + 1) * HD]
        scores = dot(query, keys, NT) * (HD**-0.5)
        masked = jnp.where(seen, scores, FLOOR)
        raised = jnp.where(seen, jnp.exp(masked - jnp.max(masked, axis=1, keepdims=True)), 0.0)
        shares = raised / jnp.sum(raised, axis=1, keepdims=True)
        low = shares.astype(jnp.bfloat16)
        low_ref[0, rows, :] = low
        turned_ref[0, :, rows] = low.T
        query_ref[0, rows, :] = query


def attention_shares(queries, key_heads, value_heads, prev, segs):
    tokens, width = queries.shape
    span = 2 * tokens
    stack = GROUP * tokens
    high = prev.shape[0]
    own = pl.BlockSpec((tokens, HD), lambda g: (0, g))
    group = lambda shape: pl.BlockSpec((1,) + shape, lambda g: (g, 0, 0))
    made = lambda shape: jax.ShapeDtypeStruct((KVH,) + shape, jnp.bfloat16)
    shapes = ((stack, span), (span, stack), (stack, HD), (span, HD), (HD, span))
    return pl.pallas_call(
        shares_kernel,
        grid=(KVH,),
        in_specs=[
            pl.BlockSpec((tokens, GROUP * HD), lambda g: (0, g)),
            own,
            own,
            pl.BlockSpec((high, HD), lambda g: (0, g)),
            pl.BlockSpec((high, HD), lambda g: (0, KVH + g)),
            pl.BlockSpec((high, HD), lambda g: (0, 0)),
            pl.BlockSpec((1, tokens), lambda g: (0, 0)),
            pl.BlockSpec((tokens, 1), lambda g: (0, 0)),
        ],
        out_specs=[group(shape) for shape in shapes],
        out_shape=[made(shape) for shape in shapes],
        compiler_params=params(32),
        cost_estimate=LIGHT,
        name="attention_shares",
    )(queries, key_heads, value_heads, prev, prev, prev, segs[None, :], segs[:, None])


def tail_kernel(
    plan, place_info, back_ref, place_ref, grad_ref, *refs
):
    heads, tiles = plan
    mine, across, refs = refs[:8], refs[8:16], refs[16:]
    low_ref, turned_ref, q_ref, key_ref, value_ref, *refs = refs
    moe_ref, query_out, kept_out, sent_out, by_place, stream, held, sums = refs
    step = pl.program_id(0)
    tokens = query_out.shape[0]
    part_size = by_place.shape[2]
    size = mine[0].shape[1]
    spread = part_size // size
    here, core = place_info[1], place_info[2]

    @pl.when(step == 0)
    def _():
        moe = dot(place_ref[...], back_ref[...]).astype(jnp.bfloat16)
        moe_ref[...] = moe
        added = (grad_ref[...].astype(jnp.float32) + moe.astype(jnp.float32)).astype(jnp.bfloat16)
        for z in range(4):
            for rest in range(spread):
                for side in range(2):
                    source = ((z * spread + rest) * 2 + side) * size
                    by_place[2 * z + side, :, rest * size : (rest + 1) * size] = added[:, source : source + size]
        for i in range(8):
            spot = slice(i * part_size, (i + 1) * part_size)
            stream[:, spot] = by_place[2 * (here ^ (i // 2)) + (core ^ (i % 2))]

    @pl.when((step > 0) & ((step - 1) % tiles == 0))
    def _():
        sums[...] = jnp.zeros_like(sums)

    def project(pieces):
        columns = jnp.concatenate([piece[...].reshape(part_size, piece.shape[-1]) for piece in pieces], axis=0)
        return dot(stream[...], columns).astype(jnp.bfloat16)

    def hold(head_grad):
        for head in range(heads):
            held[head * tokens : (head + 1) * tokens, :] = head_grad[:, head * HD : (head + 1) * HD]

    def attend():
        grads = held[...]
        low = low_ref[0].astype(jnp.float32)
        prob_grad = dot(grads, value_ref[0])
        row_dot = jnp.sum(low * prob_grad, axis=1, keepdims=True)
        score_grad = (low * (prob_grad - row_dot) * (HD**-0.5)).astype(jnp.bfloat16)
        query_grad = dot(score_grad, key_ref[0]).astype(jnp.bfloat16)
        sums[0] += dot(score_grad, q_ref[0], TN)
        sums[1] += dot(turned_ref[0], grads)
        for head in range(heads):
            query_out[:, head * HD : (head + 1) * HD] = query_grad[head * tokens : (head + 1) * tokens, :]

    @pl.when(step == 0)
    def _():
        hold(project(mine))

    @pl.when((step > 0) & (step < tiles))
    def _():
        head_grad = project(mine)
        attend()
        hold(head_grad)

    @pl.when((step >= tiles) & (step < 2 * tiles))
    def _():
        head_grad = project(across)
        attend()
        hold(head_grad)

    @pl.when(step == 2 * tiles)
    def _():
        attend()

    @pl.when((step > 0) & (step % tiles == 0))
    def _():
        kept_out[...] = sums[:, tokens:, :]
        sent_out[...] = sums[:, :tokens, :].astype(jnp.bfloat16)


def tail(place_info, back, place, moe_grad, pieces, low, turned, query, keys, values):
    tokens, width = moe_grad.shape
    spread, size, cols = pieces[0].shape
    span = keys.shape[1]
    heads = 4
    tile = heads * HD
    tiles = cols // tile
    steps = KVH * tiles
    was = lambda i: jnp.maximum(i - 1, 0)
    kv_group = lambda i, info: (was(i) // tiles) ^ info[0]
    whole = lambda shape: pl.BlockSpec(shape, lambda i, info: (0,) * len(shape))
    group = lambda shape: pl.BlockSpec((1,) + shape, lambda i, info: (kv_group(i, info), 0, 0))
    rows = lambda shape: pl.BlockSpec((1,) + shape, lambda i, info: (kv_group(i, info), was(i) % tiles, 0))
    own_tile = lambda i: jnp.minimum(i, tiles - 1)
    other_tile = lambda i: jnp.minimum(jnp.maximum(i - tiles, 0), tiles - 1)
    single = lambda turn: pl.BlockSpec((spread, size, tile), lambda i, info: (0, 0, turn(i)))
    paired = lambda turn, which: pl.BlockSpec(
        (spread, 1, size, tile), lambda i, info: (0, which, 0, turn(i))
    )
    pieces_of = lambda turn: (
        [single(turn)] * 2 + [paired(turn, 0)] * 2 + [paired(turn, 1)] * 2 + [single(turn)] * 2
    )
    kv = pl.BlockSpec((2, tokens, HD), lambda i, info: (0, 0, kv_group(i, info)))
    return pl.pallas_call(
        functools.partial(tail_kernel, (heads, tiles)),
        grid_spec=pltpu.PrefetchScalarGridSpec(
            num_scalar_prefetch=1,
            grid=(steps + 1,),
            in_specs=[whole(back.shape), whole(place.shape), whole(moe_grad.shape)]
            + [spec for turn in (own_tile, other_tile) for spec in pieces_of(turn)]
            + [
                rows((heads * tokens, span)),
                pl.BlockSpec(
                    (1, span, heads * tokens), lambda i, info: (kv_group(i, info), 0, was(i) % tiles)
                ),
                rows((heads * tokens, HD)),
                group((span, HD)),
                group((HD, span)),
            ],
            out_specs=[
                whole((tokens, width)),
                pl.BlockSpec(
                    (tokens, tile), lambda i, info: (0, kv_group(i, info) * tiles + was(i) % tiles)
                ),
                kv,
                kv,
            ],
            scratch_shapes=[
                pltpu.VMEM((8, tokens, spread * size), jnp.bfloat16),
                pltpu.VMEM((tokens, width), jnp.bfloat16),
                pltpu.VMEM((heads * tokens, HD), jnp.bfloat16),
                pltpu.VMEM((2, span, HD), jnp.float32),
            ],
        ),
        out_shape=(
            jax.ShapeDtypeStruct((tokens, width), jnp.bfloat16),
            jax.ShapeDtypeStruct((tokens, KVH * cols), jnp.bfloat16),
            jax.ShapeDtypeStruct((2, tokens, KVH * HD), jnp.float32),
            jax.ShapeDtypeStruct((2, tokens, KVH * HD), jnp.bfloat16),
        ),
        compiler_params=params(56),
        cost_estimate=pl.CostEstimate(
            flops=2 * tokens * width * KVH * cols, bytes_accessed=22 * MIB, transcendentals=0
        ),
        name="tail_attention",
    )(place_info, back, place, moe_grad, *pieces, low, turned, query, keys, values)


def finish_kernel(kept_ref, later_ref, key_ref, value_ref):
    for kind, out_ref in enumerate((key_ref, value_ref)):
        out_ref[...] = kept_ref[kind] + later_ref[kind].astype(jnp.float32)


def finish(kept, later):
    out = jax.ShapeDtypeStruct(kept.shape[1:], jnp.float32)
    return pl.pallas_call(
        finish_kernel, out_shape=(out, out), compiler_params=params(60), cost_estimate=LIGHT, name="finish"
    )(kept, later)


def local(
    moe_input,
    moe_grad,
    routes,
    route_weight,
    w_gate,
    w_up,
    w_down,
    w_out,
    queries,
    key_heads,
    value_heads,
    segments,
):
    chips = ("far", "near", "low")
    blk = chips + ("core",)
    low = lax.axis_size("low")
    owners = 4 * low
    count = 2 * owners
    parts = lax.axis_size("groups")
    tokens, width = moe_input.shape
    depth = 2 * max(1, 3 * tokens * routes.shape[1] // (2 * count))
    swap = [(0, 1), (1, 0)]
    onward = [(i, i + 1) for i in range(count - 1)]
    backward = [(i + 1, i) for i in range(count - 1)]

    share_cols = w_out.shape[1] // parts
    w_share = lax.dynamic_slice_in_dim(w_out, lax.axis_index("groups") * share_cols, share_cols, 1)
    w_near = lax.ppermute(w_share, "near", swap)
    w_far = lax.ppermute(w_share, "far", swap)

    rows, place = pick(routes, route_weight, moe_input, moe_grad, owners, depth)
    line = lambda w: lax.all_gather(w, "low", axis=0, tiled=False)
    cross = lambda w: lax.ppermute(w, "groups", swap)
    other_core = lambda w: lax.ppermute(w, "core", swap)
    own = (w_gate, w_up, w_down)
    other = tuple(other_core(w) for w in own)

    key_heads, value_heads, segments, place = lax.optimization_barrier((key_heads, value_heads, segments, place))
    kv = jnp.concatenate([key_heads, value_heads], axis=1)
    segs = (segments + 1).astype(jnp.float32)
    seg_rows = jnp.zeros((16, kv.shape[1]), jnp.bfloat16).at[0, :tokens].set(segs.astype(jnp.bfloat16))
    prev = lax.ppermute(jnp.concatenate([kv, seg_rows], axis=0), blk, onward)
    own_line = line(w_share)
    rows, w_near, w_far, own_line, prev = lax.optimization_barrier((rows, w_near, w_far, own_line, prev))

    rows_in = lax.all_to_all(rows.reshape(owners, depth, 2 * width), chips, 0, 0, tiled=True)
    pair_line = line(jnp.stack([w_near, w_far]))
    w_last = lax.ppermute(w_far, "near", swap)
    prepared = prepare_weights(own, other)
    attention = attention_shares(queries, key_heads, value_heads, prev, segs)
    pair_line, prepared, attention = lax.optimization_barrier((pair_line, prepared, attention))
    own_crossed, pair_crossed = cross(own_line), cross(pair_line)
    rows_in, prepared, attention, own_line, own_crossed, w_last = lax.optimization_barrier(
        (rows_in, prepared, attention, own_line, own_crossed, w_last)
    )
    if low == 2:
        moved = lax.ppermute(w_last, "low", swap)
        first = lax.axis_index("low") == 0
        last_line = jnp.where(first, jnp.stack([w_last, moved]), jnp.stack([moved, w_last]))
    else:
        last_line = line(w_last)
    terms = experts(rows_in.reshape(owners * depth, 2 * width), *prepared)
    terms, own_line, own_crossed, last_line, pair_line, pair_crossed = lax.optimization_barrier(
        (terms, own_line, own_crossed, last_line, pair_line, pair_crossed)
    )
    last_crossed = cross(last_line)
    back = lax.all_to_all(terms.reshape(owners, depth, width), chips, 0, 0, tiled=True)

    def pieces(own_piece, pair_piece, last_piece):
        pairs = [(piece, other_core(piece)) for piece in (own_piece, pair_piece, last_piece)]
        return [*pairs[0], *pairs[1], *pairs[1], *pairs[2]]

    z = 2 * lax.axis_index("far") + lax.axis_index("near")
    moe_input_grad, query_grad, kept, sent = tail(
        jnp.stack([lax.axis_index("groups"), z, lax.axis_index("core")]).astype(jnp.int32),
        back.reshape(owners * depth, width), place, moe_grad,
        pieces(own_line, pair_line, last_line) + pieces(own_crossed, pair_crossed, last_crossed), *attention,
    )
    return (moe_input_grad, query_grad, *finish(kept, lax.ppermute(sent, blk, backward)))


def solution(mesh):
    names = ("groups", "far", "near", "low", "core")
    shape = (mesh.shape["groups"], 2, 2, mesh.shape["blk"] // 8, 2)
    fine = jax.sharding.Mesh(mesh.devices.reshape(shape), names)
    blk = names[1:]
    by_tokens = P(names, None)
    return jax.shard_map(
        local,
        mesh=fine,
        in_specs=(
            by_tokens,
            by_tokens,
            by_tokens,
            by_tokens,
            P(None, blk),
            P(None, blk),
            P(blk, None),
            P(blk, None),
            by_tokens,
            by_tokens,
            by_tokens,
            P(names),
        ),
        out_specs=(by_tokens,) * 4,
        check_vma=False,
    )
```

```python
import functools

import jax
import jax.numpy as jnp
from jax import lax
from jax.experimental import pallas as pl
from jax.experimental.pallas import tpu as pltpu
from jax.sharding import PartitionSpec as P

KVH = 2
GROUP = 16
HD = 128
FLOOR = -1e30
MIB = 1 << 20
LIGHT = pl.CostEstimate(flops=0, bytes_accessed=0, transcendentals=0)

NT = (((1,), (1,)), ((), ()))
TN = (((0,), (0,)), ((), ()))


def dot(a, b, dims=(((1,), (0,)), ((), ()))):
    return lax.dot_general(a, b, dims, preferred_element_type=jnp.float32)


def params(mib):
    return pltpu.CompilerParams(vmem_limit_bytes=mib * MIB)


def pick_kernel(owners, depth, routes_ref, weight_ref, input_ref, grad_ref, rows_ref, back_ref):
    tokens = input_ref.shape[0]
    slots = owners * depth
    first = routes_ref[0:1, :]
    second = routes_ref[1:2, :]
    expert = lax.broadcasted_iota(jnp.int32, (owners, tokens), 0)
    is_first = first == expert
    is_second = second == expert
    member = jnp.where(is_first | is_second, 1.0, 0.0)
    before = lax.broadcasted_iota(jnp.int32, (tokens, tokens), 0) < lax.broadcasted_iota(
        jnp.int32, (tokens, tokens), 1
    )
    rank = dot(member.astype(jnp.bfloat16), jnp.where(before, 1.0, 0.0).astype(jnp.bfloat16))
    spot = (expert * depth).astype(jnp.float32) + rank
    slot_first = jnp.sum(jnp.where(is_first, spot, 0.0), axis=0, keepdims=True).astype(jnp.int32)
    slot_second = jnp.sum(jnp.where(is_second, spot, 0.0), axis=0, keepdims=True).astype(jnp.int32)
    slot = lax.broadcasted_iota(jnp.int32, (slots, tokens), 0)
    at_first = slot == slot_first
    at_second = slot == slot_second
    place = jnp.where(at_first | at_second, 1.0, 0.0).astype(jnp.bfloat16)
    back_ref[...] = place.T
    scale = jnp.sum(
        jnp.where(at_first, weight_ref[0:1, :], 0.0) + jnp.where(at_second, weight_ref[1:2, :], 0.0),
        axis=1,
        keepdims=True,
    )
    width = input_ref.shape[1]
    rows_ref[:, :width] = dot(place, input_ref[...]).astype(jnp.bfloat16)
    rows_ref[:, width:] = (scale * dot(place, grad_ref[...])).astype(jnp.bfloat16)


def pick(routes, route_weight, moe_input, moe_grad, owners, depth):
    tokens, width = moe_input.shape
    slots = owners * depth
    return pl.pallas_call(
        functools.partial(pick_kernel, owners, depth),
        out_shape=(
            jax.ShapeDtypeStruct((slots, 2 * width), jnp.bfloat16),
            jax.ShapeDtypeStruct((tokens, slots), jnp.bfloat16),
        ),
        compiler_params=params(32),
        cost_estimate=pl.CostEstimate(
            flops=4 * slots * tokens * width, bytes_accessed=8 * MIB, transcendentals=0
        ),
        name="pick_rows",
    )(routes.T, route_weight.T, moe_input, moe_grad)


def weights_kernel(*refs):
    own, other, (cols_ref, down_ref, rows_ref) = refs[:3], refs[3:6], refs[6:]
    tile = own[0].shape[1]
    for place, (gate_ref, up_ref, low_ref) in enumerate((own, other)):
        for kind, ref in enumerate((gate_ref, up_ref)):
            spot = slice((2 * kind + place) * tile, (2 * kind + place + 1) * tile)
            cols_ref[0, :, spot] = ref[...]
            rows_ref[0, spot, :] = ref[...].T
        down_ref[0, :, place * tile : (place + 1) * tile] = low_ref[...].T


def prepare_weights(own, other):
    width, half = own[0].shape
    tile = 128
    steps = half // tile
    cols = pl.BlockSpec((width, tile), lambda i: (0, i))
    down = pl.BlockSpec((tile, width), lambda i: (i, 0))
    return pl.pallas_call(
        weights_kernel,
        grid=(steps,),
        in_specs=[cols, cols, down] * 2,
        out_specs=[
            pl.BlockSpec((1, width, 4 * tile), lambda i: (i, 0, 0)),
            pl.BlockSpec((1, width, 2 * tile), lambda i: (i, 0, 0)),
            pl.BlockSpec((1, 4 * tile, width), lambda i: (i, 0, 0)),
        ],
        out_shape=(
            jax.ShapeDtypeStruct((steps, width, 4 * tile), jnp.bfloat16),
            jax.ShapeDtypeStruct((steps, width, 2 * tile), jnp.bfloat16),
            jax.ShapeDtypeStruct((steps, 4 * tile, width), jnp.bfloat16),
        ),
        compiler_params=params(48),
        cost_estimate=LIGHT,
        name="prepare_weights",
    )(*own, *other)


def expert_kernel(steps, rows_ref, cols_ref, down_ref, back_ref, out_ref, hidden):
    step = pl.program_id(0)
    width = rows_ref.shape[1] // 2
    pair = down_ref.shape[2]

    @pl.when(step < steps)
    def _():
        both_pre = dot(rows_ref[:, :width], cols_ref[0])
        gate_pre = both_pre[:, :pair]
        up_pre = both_pre[:, pair:]
        down_grad = dot(rows_ref[:, width:], down_ref[0])
        sig = jax.nn.sigmoid(gate_pre)
        hidden[step, :, :pair] = (
            down_grad * up_pre * sig * (1.0 + gate_pre * (1.0 - sig))
        ).astype(jnp.bfloat16)
        hidden[step, :, pair:] = (down_grad * gate_pre * sig).astype(jnp.bfloat16)

    @pl.when(step >= steps)
    def _():
        total = dot(hidden[0], back_ref[0])
        for i in range(1, steps):
            total += dot(hidden[i], back_ref[i])
        out_ref[...] = total.astype(jnp.bfloat16)


def experts(rows, cols, down, back):
    count, twice = rows.shape
    steps, width, quad = cols.shape
    tile = 512
    last = steps - 1
    turn = lambda i: jnp.maximum(i - steps, 0)
    return pl.pallas_call(
        functools.partial(expert_kernel, steps),
        grid=(steps + width // tile,),
        in_specs=[
            pl.BlockSpec((count, twice), lambda i: (0, 0)),
            pl.BlockSpec((1, width, quad), lambda i: (jnp.minimum(i, last), 0, 0)),
            pl.BlockSpec((1, width, quad // 2), lambda i: (jnp.minimum(i, last), 0, 0)),
            pl.BlockSpec((steps, quad, tile), lambda i: (0, 0, turn(i))),
        ],
        out_specs=pl.BlockSpec((count, tile), lambda i: (0, turn(i))),
        out_shape=jax.ShapeDtypeStruct((count, width), jnp.bfloat16),
        scratch_shapes=[pltpu.VMEM((steps, count, quad), jnp.bfloat16)],
        compiler_params=params(48),
        cost_estimate=LIGHT,
        name="expert_terms",
    )(rows, cols, down, back)


def shares_kernel(
    q_ref, key_ref, value_ref, prev_key_ref, prev_value_ref, prev_seg_ref, seg_row_ref, seg_col_ref,
    low_ref, turned_ref, query_ref, key_out, value_out,
):
    tokens = q_ref.shape[0]
    seg_col = seg_col_ref[...]
    row = lax.broadcasted_iota(jnp.int32, (tokens, tokens), 0)
    col = lax.broadcasted_iota(jnp.int32, (tokens, tokens), 1)
    own_seen = jnp.where((col <= row) & (seg_row_ref[...] == seg_col), 1.0, 0.0)
    prev_seg = prev_seg_ref[tokens : tokens + 16, :].astype(jnp.float32)[0:1, :]
    prev_seen = jnp.where(prev_seg == seg_col, 1.0, 0.0)
    seen = jnp.concatenate([prev_seen, own_seen], axis=1) > 0.5
    keys = jnp.concatenate([prev_key_ref[:tokens, :], key_ref[...]], axis=0)
    values = jnp.concatenate([prev_value_ref[:tokens, :], value_ref[...]], axis=0)
    key_out[0] = keys
    value_out[0] = values.T
    for head in range(GROUP):
        rows = slice(head * tokens, (head + 1) * tokens)
        query = q_ref[:, head * HD : (head + 1) * HD]
        scores = dot(query, keys, NT) * (HD**-0.5)
        masked = jnp.where(seen, scores, FLOOR)
        raised = jnp.where(seen, jnp.exp(masked - jnp.max(masked, axis=1, keepdims=True)), 0.0)
        shares = raised / jnp.sum(raised, axis=1, keepdims=True)
        low = shares.astype(jnp.bfloat16)
        low_ref[0, rows, :] = low
        turned_ref[0, :, rows] = low.T
        query_ref[0, rows, :] = query


def attention_shares(queries, key_heads, value_heads, prev, segs):
    tokens, width = queries.shape
    span = 2 * tokens
    stack = GROUP * tokens
    high = prev.shape[0]
    own = pl.BlockSpec((tokens, HD), lambda g: (0, g))
    group = lambda shape: pl.BlockSpec((1,) + shape, lambda g: (g, 0, 0))
    made = lambda shape: jax.ShapeDtypeStruct((KVH,) + shape, jnp.bfloat16)
    shapes = ((stack, span), (span, stack), (stack, HD), (span, HD), (HD, span))
    return pl.pallas_call(
        shares_kernel,
        grid=(KVH,),
        in_specs=[
            pl.BlockSpec((tokens, GROUP * HD), lambda g: (0, g)),
            own,
            own,
            pl.BlockSpec((high, HD), lambda g: (0, g)),
            pl.BlockSpec((high, HD), lambda g: (0, KVH + g)),
            pl.BlockSpec((high, HD), lambda g: (0, 0)),
            pl.BlockSpec((1, tokens), lambda g: (0, 0)),
            pl.BlockSpec((tokens, 1), lambda g: (0, 0)),
        ],
        out_specs=[group(shape) for shape in shapes],
        out_shape=[made(shape) for shape in shapes],
        compiler_params=params(32),
        cost_estimate=LIGHT,
        name="attention_shares",
    )(queries, key_heads, value_heads, prev, prev, prev, segs[None, :], segs[:, None])


def tail_kernel(
    plan, place_info, back_ref, place_ref, grad_ref, *refs
):
    heads, tiles = plan
    mine, across, refs = refs[:8], refs[8:16], refs[16:]
    low_ref, turned_ref, q_ref, key_ref, value_ref, *refs = refs
    moe_ref, query_out, kept_out, sent_out, by_place, stream, held, sums = refs
    step = pl.program_id(0)
    tokens = query_out.shape[0]
    part_size = by_place.shape[2]
    size = mine[0].shape[1]
    spread = part_size // size
    here, core = place_info[1], place_info[2]

    @pl.when(step == 0)
    def _():
        moe = dot(place_ref[...], back_ref[...]).astype(jnp.bfloat16)
        moe_ref[...] = moe
        added = (grad_ref[...].astype(jnp.float32) + moe.astype(jnp.float32)).astype(jnp.bfloat16)
        for z in range(4):
            for rest in range(spread):
                for side in range(2):
                    source = ((z * spread + rest) * 2 + side) * size
                    by_place[2 * z + side, :, rest * size : (rest + 1) * size] = added[:, source : source + size]
        for i in range(8):
            spot = slice(i * part_size, (i + 1) * part_size)
            stream[:, spot] = by_place[2 * (here ^ (i // 2)) + (core ^ (i % 2))]

    @pl.when((step > 0) & ((step - 1) % tiles == 0))
    def _():
        sums[...] = jnp.zeros_like(sums)

    def project(pieces):
        columns = jnp.concatenate([piece[...].reshape(part_size, piece.shape[-1]) for piece in pieces], axis=0)
        return dot(stream[...], columns).astype(jnp.bfloat16)

    def hold(head_grad):
        for head in range(heads):
            held[head * tokens : (head + 1) * tokens, :] = head_grad[:, head * HD : (head + 1) * HD]

    def attend():
        grads = held[...]
        low = low_ref[0].astype(jnp.float32)
        prob_grad = dot(grads, value_ref[0])
        row_dot = jnp.sum(low * prob_grad, axis=1, keepdims=True)
        score_grad = (low * (prob_grad - row_dot) * (HD**-0.5)).astype(jnp.bfloat16)
        query_grad = dot(score_grad, key_ref[0]).astype(jnp.bfloat16)
        sums[0] += dot(score_grad, q_ref[0], TN)
        sums[1] += dot(turned_ref[0], grads)
        for head in range(heads):
            query_out[:, head * HD : (head + 1) * HD] = query_grad[head * tokens : (head + 1) * tokens, :]

    @pl.when(step == 0)
    def _():
        hold(project(mine))

    @pl.when((step > 0) & (step < tiles))
    def _():
        head_grad = project(mine)
        attend()
        hold(head_grad)

    @pl.when((step >= tiles) & (step < 2 * tiles))
    def _():
        head_grad = project(across)
        attend()
        hold(head_grad)

    @pl.when(step == 2 * tiles)
    def _():
        attend()

    @pl.when((step > 0) & (step % tiles == 0))
    def _():
        kept_out[...] = sums[:, tokens:, :]
        sent_out[...] = sums[:, :tokens, :].astype(jnp.bfloat16)


def tail(place_info, back, place, moe_grad, pieces, low, turned, query, keys, values):
    tokens, width = moe_grad.shape
    spread, size, cols = pieces[0].shape
    span = keys.shape[1]
    heads = 4
    tile = heads * HD
    tiles = cols // tile
    steps = KVH * tiles
    was = lambda i: jnp.maximum(i - 1, 0)
    kv_group = lambda i, info: (was(i) // tiles) ^ info[0]
    whole = lambda shape: pl.BlockSpec(shape, lambda i, info: (0,) * len(shape))
    group = lambda shape: pl.BlockSpec((1,) + shape, lambda i, info: (kv_group(i, info), 0, 0))
    rows = lambda shape: pl.BlockSpec((1,) + shape, lambda i, info: (kv_group(i, info), was(i) % tiles, 0))
    own_tile = lambda i: jnp.minimum(i, tiles - 1)
    other_tile = lambda i: jnp.minimum(jnp.maximum(i - tiles, 0), tiles - 1)
    single = lambda turn: pl.BlockSpec((spread, size, tile), lambda i, info: (0, 0, turn(i)))
    paired = lambda turn, which: pl.BlockSpec(
        (spread, 1, size, tile), lambda i, info: (0, which, 0, turn(i))
    )
    pieces_of = lambda turn, first: (
        [single(turn)] * 2 + [paired(turn, first)] * 2 + [paired(turn, first + 1)] * 2 + [single(turn)] * 2
    )
    kv = pl.BlockSpec((2, tokens, HD), lambda i, info: (0, 0, kv_group(i, info)))
    return pl.pallas_call(
        functools.partial(tail_kernel, (heads, tiles)),
        grid_spec=pltpu.PrefetchScalarGridSpec(
            num_scalar_prefetch=1,
            grid=(steps + 1,),
            in_specs=[whole(back.shape), whole(place.shape), whole(moe_grad.shape)]
            + pieces_of(own_tile, 0)
            + pieces_of(other_tile, 2)
            + [
                rows((heads * tokens, span)),
                pl.BlockSpec(
                    (1, span, heads * tokens), lambda i, info: (kv_group(i, info), 0, was(i) % tiles)
                ),
                rows((heads * tokens, HD)),
                group((span, HD)),
                group((HD, span)),
            ],
            out_specs=[
                whole((tokens, width)),
                pl.BlockSpec(
                    (tokens, tile), lambda i, info: (0, kv_group(i, info) * tiles + was(i) % tiles)
                ),
                kv,
                kv,
            ],
            scratch_shapes=[
                pltpu.VMEM((8, tokens, spread * size), jnp.bfloat16),
                pltpu.VMEM((tokens, width), jnp.bfloat16),
                pltpu.VMEM((heads * tokens, HD), jnp.bfloat16),
                pltpu.VMEM((2, span, HD), jnp.float32),
            ],
        ),
        out_shape=(
            jax.ShapeDtypeStruct((tokens, width), jnp.bfloat16),
            jax.ShapeDtypeStruct((tokens, KVH * cols), jnp.bfloat16),
            jax.ShapeDtypeStruct((2, tokens, KVH * HD), jnp.float32),
            jax.ShapeDtypeStruct((2, tokens, KVH * HD), jnp.bfloat16),
        ),
        compiler_params=params(56),
        cost_estimate=pl.CostEstimate(
            flops=2 * tokens * width * KVH * cols, bytes_accessed=22 * MIB, transcendentals=0
        ),
        name="tail_attention",
    )(place_info, back, place, moe_grad, *pieces, low, turned, query, keys, values)


def finish_kernel(kept_ref, later_ref, key_ref, value_ref):
    for kind, out_ref in enumerate((key_ref, value_ref)):
        out_ref[...] = kept_ref[kind] + later_ref[kind].astype(jnp.float32)


def finish(kept, later):
    out = jax.ShapeDtypeStruct(kept.shape[1:], jnp.float32)
    return pl.pallas_call(
        finish_kernel, out_shape=(out, out), compiler_params=params(60), cost_estimate=LIGHT, name="finish"
    )(kept, later)


def local(
    moe_input,
    moe_grad,
    routes,
    route_weight,
    w_gate,
    w_up,
    w_down,
    w_out,
    queries,
    key_heads,
    value_heads,
    segments,
):
    chips = ("far", "near", "low")
    blk = chips + ("core",)
    low = lax.axis_size("low")
    owners = 4 * low
    count = 2 * owners
    parts = lax.axis_size("groups")
    tokens, width = moe_input.shape
    depth = 2 * max(1, 3 * tokens * routes.shape[1] // (2 * count))
    swap = [(0, 1), (1, 0)]
    onward = [(i, i + 1) for i in range(count - 1)]
    backward = [(i + 1, i) for i in range(count - 1)]

    share_cols = w_out.shape[1] // parts
    w_share = lax.dynamic_slice_in_dim(w_out, lax.axis_index("groups") * share_cols, share_cols, 1)
    w_near = lax.ppermute(w_share, "near", swap)
    w_far = lax.ppermute(w_share, "far", swap)

    rows, place = pick(routes, route_weight, moe_input, moe_grad, owners, depth)
    line = lambda w: lax.all_gather(w, "low", axis=0, tiled=False)
    cross = lambda w: lax.ppermute(w, "groups", swap)
    other_core = lambda w: lax.ppermute(w, "core", swap)
    own = (w_gate, w_up, w_down)
    other = tuple(other_core(w) for w in own)

    key_heads, value_heads, segments, place = lax.optimization_barrier((key_heads, value_heads, segments, place))
    kv = jnp.concatenate([key_heads, value_heads], axis=1)
    segs = (segments + 1).astype(jnp.float32)
    seg_rows = jnp.zeros((16, kv.shape[1]), jnp.bfloat16).at[0, :tokens].set(segs.astype(jnp.bfloat16))
    prev = lax.ppermute(jnp.concatenate([kv, seg_rows], axis=0), blk, onward)
    own_line = line(w_share)
    rows, w_near, w_far, own_line, prev = lax.optimization_barrier((rows, w_near, w_far, own_line, prev))

    rows_in = lax.all_to_all(rows.reshape(owners, depth, 2 * width), chips, 0, 0, tiled=True)
    pair = jnp.stack([w_near, w_far])
    pair_crossed = cross(pair)
    four_lines = line(jnp.concatenate([pair, pair_crossed], axis=0))
    own_line, pair_crossed = lax.optimization_barrier((own_line, pair_crossed))
    own_crossed = cross(own_line)
    w_last = lax.ppermute(w_far, "near", swap)
    prepared = prepare_weights(own, other)
    attention = attention_shares(queries, key_heads, value_heads, prev, segs)
    rows_in, prepared, attention, own_line, own_crossed, w_last = lax.optimization_barrier(
        (rows_in, prepared, attention, own_line, own_crossed, w_last)
    )
    if low == 2:
        moved = lax.ppermute(w_last, "low", swap)
        first = lax.axis_index("low") == 0
        last_line = jnp.where(first, jnp.stack([w_last, moved]), jnp.stack([moved, w_last]))
    else:
        last_line = line(w_last)
    terms = experts(rows_in.reshape(owners * depth, 2 * width), *prepared)
    terms, own_line, own_crossed, last_line, four_lines = lax.optimization_barrier(
        (terms, own_line, own_crossed, last_line, four_lines)
    )
    last_crossed = cross(last_line)
    back = lax.all_to_all(terms.reshape(owners, depth, width), chips, 0, 0, tiled=True)

    four = (four_lines, other_core(four_lines))

    def pieces(own_piece, last_piece):
        return [own_piece, other_core(own_piece), *four, *four, last_piece, other_core(last_piece)]

    z = 2 * lax.axis_index("far") + lax.axis_index("near")
    moe_input_grad, query_grad, kept, sent = tail(
        jnp.stack([lax.axis_index("groups"), z, lax.axis_index("core")]).astype(jnp.int32),
        back.reshape(owners * depth, width), place, moe_grad,
        pieces(own_line, last_line) + pieces(own_crossed, last_crossed), *attention,
    )
    return (moe_input_grad, query_grad, *finish(kept, lax.ppermute(sent, blk, backward)))


def solution(mesh):
    names = ("groups", "far", "near", "low", "core")
    shape = (mesh.shape["groups"], 2, 2, mesh.shape["blk"] // 8, 2)
    fine = jax.sharding.Mesh(mesh.devices.reshape(shape), names)
    blk = names[1:]
    by_tokens = P(names, None)
    return jax.shard_map(
        local,
        mesh=fine,
        in_specs=(
            by_tokens,
            by_tokens,
            by_tokens,
            by_tokens,
            P(None, blk),
            P(None, blk),
            P(blk, None),
            P(blk, None),
            by_tokens,
            by_tokens,
            by_tokens,
            P(names),
        ),
        out_specs=(by_tokens,) * 4,
        check_vma=False,
    )
```

```python
import functools

import jax
import jax.numpy as jnp
from jax import lax
from jax.experimental import pallas as pl
from jax.experimental.pallas import tpu as pltpu
from jax.sharding import PartitionSpec as P

KVH = 2
GROUP = 16
HD = 128
FLOOR = -1e30
MIB = 1 << 20
LIGHT = pl.CostEstimate(flops=0, bytes_accessed=0, transcendentals=0)

NT = (((1,), (1,)), ((), ()))
TN = (((0,), (0,)), ((), ()))


def dot(a, b, dims=(((1,), (0,)), ((), ()))):
    return lax.dot_general(a, b, dims, preferred_element_type=jnp.float32)


def params(mib):
    return pltpu.CompilerParams(vmem_limit_bytes=mib * MIB)


def pick_kernel(owners, depth, routes_ref, weight_ref, input_ref, grad_ref, rows_ref, back_ref):
    tokens = input_ref.shape[0]
    slots = owners * depth
    first = routes_ref[0:1, :]
    second = routes_ref[1:2, :]
    expert = lax.broadcasted_iota(jnp.int32, (owners, tokens), 0)
    is_first = first == expert
    is_second = second == expert
    member = jnp.where(is_first | is_second, 1.0, 0.0)
    before = lax.broadcasted_iota(jnp.int32, (tokens, tokens), 0) < lax.broadcasted_iota(
        jnp.int32, (tokens, tokens), 1
    )
    rank = dot(member.astype(jnp.bfloat16), jnp.where(before, 1.0, 0.0).astype(jnp.bfloat16))
    spot = (expert * depth).astype(jnp.float32) + rank
    slot_first = jnp.sum(jnp.where(is_first, spot, 0.0), axis=0, keepdims=True).astype(jnp.int32)
    slot_second = jnp.sum(jnp.where(is_second, spot, 0.0), axis=0, keepdims=True).astype(jnp.int32)
    slot = lax.broadcasted_iota(jnp.int32, (slots, tokens), 0)
    at_first = slot == slot_first
    at_second = slot == slot_second
    place = jnp.where(at_first | at_second, 1.0, 0.0).astype(jnp.bfloat16)
    back_ref[...] = place.T
    scale = jnp.sum(
        jnp.where(at_first, weight_ref[0:1, :], 0.0) + jnp.where(at_second, weight_ref[1:2, :], 0.0),
        axis=1,
        keepdims=True,
    )
    width = input_ref.shape[1]
    rows_ref[:, :width] = dot(place, input_ref[...]).astype(jnp.bfloat16)
    rows_ref[:, width:] = (scale * dot(place, grad_ref[...])).astype(jnp.bfloat16)


def pick(routes, route_weight, moe_input, moe_grad, owners, depth):
    tokens, width = moe_input.shape
    slots = owners * depth
    return pl.pallas_call(
        functools.partial(pick_kernel, owners, depth),
        out_shape=(
            jax.ShapeDtypeStruct((slots, 2 * width), jnp.bfloat16),
            jax.ShapeDtypeStruct((tokens, slots), jnp.bfloat16),
        ),
        compiler_params=params(32),
        cost_estimate=pl.CostEstimate(
            flops=4 * slots * tokens * width, bytes_accessed=8 * MIB, transcendentals=0
        ),
        name="pick_rows",
    )(routes.T, route_weight.T, moe_input, moe_grad)


def weights_kernel(*refs):
    own, other, (cols_ref, down_ref, rows_ref) = refs[:3], refs[3:6], refs[6:]
    tile = own[0].shape[1]
    for place, (gate_ref, up_ref, low_ref) in enumerate((own, other)):
        for kind, ref in enumerate((gate_ref, up_ref)):
            spot = slice((2 * kind + place) * tile, (2 * kind + place + 1) * tile)
            cols_ref[0, :, spot] = ref[...]
            rows_ref[0, spot, :] = ref[...].T
        down_ref[0, :, place * tile : (place + 1) * tile] = low_ref[...].T


def prepare_weights(own, other):
    width, half = own[0].shape
    tile = 128
    steps = half // tile
    cols = pl.BlockSpec((width, tile), lambda i: (0, i))
    down = pl.BlockSpec((tile, width), lambda i: (i, 0))
    return pl.pallas_call(
        weights_kernel,
        grid=(steps,),
        in_specs=[cols, cols, down] * 2,
        out_specs=[
            pl.BlockSpec((1, width, 4 * tile), lambda i: (i, 0, 0)),
            pl.BlockSpec((1, width, 2 * tile), lambda i: (i, 0, 0)),
            pl.BlockSpec((1, 4 * tile, width), lambda i: (i, 0, 0)),
        ],
        out_shape=(
            jax.ShapeDtypeStruct((steps, width, 4 * tile), jnp.bfloat16),
            jax.ShapeDtypeStruct((steps, width, 2 * tile), jnp.bfloat16),
            jax.ShapeDtypeStruct((steps, 4 * tile, width), jnp.bfloat16),
        ),
        compiler_params=params(48),
        cost_estimate=LIGHT,
        name="prepare_weights",
    )(*own, *other)


def expert_kernel(steps, rows_ref, cols_ref, down_ref, back_ref, out_ref, hidden):
    step = pl.program_id(0)
    width = rows_ref.shape[1] // 2
    pair = down_ref.shape[2]

    @pl.when(step < steps)
    def _():
        both_pre = dot(rows_ref[:, :width], cols_ref[0])
        gate_pre = both_pre[:, :pair]
        up_pre = both_pre[:, pair:]
        down_grad = dot(rows_ref[:, width:], down_ref[0])
        sig = jax.nn.sigmoid(gate_pre)
        hidden[step, :, :pair] = (
            down_grad * up_pre * sig * (1.0 + gate_pre * (1.0 - sig))
        ).astype(jnp.bfloat16)
        hidden[step, :, pair:] = (down_grad * gate_pre * sig).astype(jnp.bfloat16)

    @pl.when(step >= steps)
    def _():
        total = dot(hidden[0], back_ref[0])
        for i in range(1, steps):
            total += dot(hidden[i], back_ref[i])
        out_ref[...] = total.astype(jnp.bfloat16)


def experts(rows, cols, down, back):
    count, twice = rows.shape
    steps, width, quad = cols.shape
    tile = 512
    last = steps - 1
    turn = lambda i: jnp.maximum(i - steps, 0)
    return pl.pallas_call(
        functools.partial(expert_kernel, steps),
        grid=(steps + width // tile,),
        in_specs=[
            pl.BlockSpec((count, twice), lambda i: (0, 0)),
            pl.BlockSpec((1, width, quad), lambda i: (jnp.minimum(i, last), 0, 0)),
            pl.BlockSpec((1, width, quad // 2), lambda i: (jnp.minimum(i, last), 0, 0)),
            pl.BlockSpec((steps, quad, tile), lambda i: (0, 0, turn(i))),
        ],
        out_specs=pl.BlockSpec((count, tile), lambda i: (0, turn(i))),
        out_shape=jax.ShapeDtypeStruct((count, width), jnp.bfloat16),
        scratch_shapes=[pltpu.VMEM((steps, count, quad), jnp.bfloat16)],
        compiler_params=params(48),
        cost_estimate=LIGHT,
        name="expert_terms",
    )(rows, cols, down, back)


def shares_kernel(
    q_ref, key_ref, value_ref, prev_key_ref, prev_value_ref, prev_seg_ref, seg_row_ref, seg_col_ref,
    low_ref, turned_ref, query_ref, key_out, value_out,
):
    tokens = q_ref.shape[0]
    seg_col = seg_col_ref[...]
    row = lax.broadcasted_iota(jnp.int32, (tokens, tokens), 0)
    col = lax.broadcasted_iota(jnp.int32, (tokens, tokens), 1)
    own_seen = jnp.where((col <= row) & (seg_row_ref[...] == seg_col), 1.0, 0.0)
    prev_seg = prev_seg_ref[tokens : tokens + 16, :].astype(jnp.float32)[0:1, :]
    prev_seen = jnp.where(prev_seg == seg_col, 1.0, 0.0)
    seen = jnp.concatenate([prev_seen, own_seen], axis=1) > 0.5
    keys = jnp.concatenate([prev_key_ref[:tokens, :], key_ref[...]], axis=0)
    values = jnp.concatenate([prev_value_ref[:tokens, :], value_ref[...]], axis=0)
    key_out[0] = keys
    value_out[0] = values.T
    for head in range(GROUP):
        rows = slice(head * tokens, (head + 1) * tokens)
        query = q_ref[:, head * HD : (head + 1) * HD]
        scores = dot(query, keys, NT) * (HD**-0.5)
        masked = jnp.where(seen, scores, FLOOR)
        raised = jnp.where(seen, jnp.exp(masked - jnp.max(masked, axis=1, keepdims=True)), 0.0)
        shares = raised / jnp.sum(raised, axis=1, keepdims=True)
        low = shares.astype(jnp.bfloat16)
        low_ref[0, rows, :] = low
        turned_ref[0, :, rows] = low.T
        query_ref[0, rows, :] = query


def attention_shares(queries, key_heads, value_heads, prev, segs):
    tokens, width = queries.shape
    span = 2 * tokens
    stack = GROUP * tokens
    high = prev.shape[0]
    own = pl.BlockSpec((tokens, HD), lambda g: (0, g))
    group = lambda shape: pl.BlockSpec((1,) + shape, lambda g: (g, 0, 0))
    made = lambda shape: jax.ShapeDtypeStruct((KVH,) + shape, jnp.bfloat16)
    shapes = ((stack, span), (span, stack), (stack, HD), (span, HD), (HD, span))
    return pl.pallas_call(
        shares_kernel,
        grid=(KVH,),
        in_specs=[
            pl.BlockSpec((tokens, GROUP * HD), lambda g: (0, g)),
            own,
            own,
            pl.BlockSpec((high, HD), lambda g: (0, g)),
            pl.BlockSpec((high, HD), lambda g: (0, KVH + g)),
            pl.BlockSpec((high, HD), lambda g: (0, 0)),
            pl.BlockSpec((1, tokens), lambda g: (0, 0)),
            pl.BlockSpec((tokens, 1), lambda g: (0, 0)),
        ],
        out_specs=[group(shape) for shape in shapes],
        out_shape=[made(shape) for shape in shapes],
        compiler_params=params(32),
        cost_estimate=LIGHT,
        name="attention_shares",
    )(queries, key_heads, value_heads, prev, prev, prev, segs[None, :], segs[:, None])


def tail_kernel(
    plan, place_info, back_ref, place_ref, grad_ref, *refs
):
    heads, tiles = plan
    own, last, twin, refs = refs[:4], refs[4:8], refs[8:12], refs[12:]
    low_ref, turned_ref, q_ref, key_ref, value_ref, *refs = refs
    moe_ref, query_out, kept_out, sent_out, by_place, stream, held, sums = refs
    step = pl.program_id(0)
    tokens = query_out.shape[0]
    part_size = by_place.shape[2]
    size = own[0].shape[1]
    mine, across = own[:2] + twin + last[:2], own[2:] + twin + last[2:]
    spread = part_size // size
    here, core = place_info[1], place_info[2]

    @pl.when(step == 0)
    def _():
        moe = dot(place_ref[...], back_ref[...]).astype(jnp.bfloat16)
        moe_ref[...] = moe
        added = (grad_ref[...].astype(jnp.float32) + moe.astype(jnp.float32)).astype(jnp.bfloat16)
        for z in range(4):
            for rest in range(spread):
                for side in range(2):
                    source = ((z * spread + rest) * 2 + side) * size
                    by_place[2 * z + side, :, rest * size : (rest + 1) * size] = added[:, source : source + size]
        for i in range(8):
            spot = slice(i * part_size, (i + 1) * part_size)
            stream[:, spot] = by_place[2 * (here ^ (i // 2)) + (core ^ (i % 2))]

    @pl.when((step > 0) & ((step - 1) % tiles == 0))
    def _():
        sums[...] = jnp.zeros_like(sums)

    def project(pieces):
        columns = jnp.concatenate([piece[...].reshape(part_size, piece.shape[-1]) for piece in pieces], axis=0)
        return dot(stream[...], columns).astype(jnp.bfloat16)

    def hold(head_grad):
        for head in range(heads):
            held[head * tokens : (head + 1) * tokens, :] = head_grad[:, head * HD : (head + 1) * HD]

    def attend():
        grads = held[...]
        low = low_ref[0].astype(jnp.float32)
        prob_grad = dot(grads, value_ref[0])
        row_dot = jnp.sum(low * prob_grad, axis=1, keepdims=True)
        score_grad = (low * (prob_grad - row_dot) * (HD**-0.5)).astype(jnp.bfloat16)
        query_grad = dot(score_grad, key_ref[0]).astype(jnp.bfloat16)
        sums[0] += dot(score_grad, q_ref[0], TN)
        sums[1] += dot(turned_ref[0], grads)
        for head in range(heads):
            query_out[:, head * HD : (head + 1) * HD] = query_grad[head * tokens : (head + 1) * tokens, :]

    @pl.when(step == 0)
    def _():
        hold(project(mine))

    @pl.when((step > 0) & (step < tiles))
    def _():
        head_grad = project(mine)
        attend()
        hold(head_grad)

    @pl.when((step >= tiles) & (step < 2 * tiles))
    def _():
        head_grad = project(across)
        attend()
        hold(head_grad)

    @pl.when(step == 2 * tiles)
    def _():
        attend()

    @pl.when((step > 0) & (step % tiles == 0))
    def _():
        kept_out[...] = sums[:, tokens:, :]
        sent_out[...] = sums[:, :tokens, :].astype(jnp.bfloat16)


def tail(place_info, back, place, moe_grad, pieces, low, turned, query, keys, values):
    tokens, width = moe_grad.shape
    spread, size, cols = pieces[0].shape
    span = keys.shape[1]
    heads = 4
    tile = heads * HD
    tiles = cols // tile
    steps = KVH * tiles
    was = lambda i: jnp.maximum(i - 1, 0)
    kv_group = lambda i, info: (was(i) // tiles) ^ info[0]
    whole = lambda shape: pl.BlockSpec(shape, lambda i, info: (0,) * len(shape))
    group = lambda shape: pl.BlockSpec((1,) + shape, lambda i, info: (kv_group(i, info), 0, 0))
    rows = lambda shape: pl.BlockSpec((1,) + shape, lambda i, info: (kv_group(i, info), was(i) % tiles, 0))
    own_tile = lambda i: jnp.minimum(i, tiles - 1)
    other_tile = lambda i: jnp.minimum(jnp.maximum(i - tiles, 0), tiles - 1)
    now = lambda i: jnp.minimum(i, steps - 1)
    twin = pl.BlockSpec((spread, 1, size, tile), lambda i, info: (0, now(i) // tiles, 0, now(i) % tiles))
    piece = lambda turn: pl.BlockSpec((spread, size, tile), lambda i, info: (0, 0, turn(i)))
    kv = pl.BlockSpec((2, tokens, HD), lambda i, info: (0, 0, kv_group(i, info)))
    return pl.pallas_call(
        functools.partial(tail_kernel, (heads, tiles)),
        grid_spec=pltpu.PrefetchScalarGridSpec(
            num_scalar_prefetch=1,
            grid=(steps + 1,),
            in_specs=[whole(back.shape), whole(place.shape), whole(moe_grad.shape)]
            + ([piece(own_tile)] * 2 + [piece(other_tile)] * 2) * 2
            + [twin] * 4
            + [
                rows((heads * tokens, span)),
                pl.BlockSpec(
                    (1, span, heads * tokens), lambda i, info: (kv_group(i, info), 0, was(i) % tiles)
                ),
                rows((heads * tokens, HD)),
                group((span, HD)),
                group((HD, span)),
            ],
            out_specs=[
                whole((tokens, width)),
                pl.BlockSpec(
                    (tokens, tile), lambda i, info: (0, kv_group(i, info) * tiles + was(i) % tiles)
                ),
                kv,
                kv,
            ],
            scratch_shapes=[
                pltpu.VMEM((8, tokens, spread * size), jnp.bfloat16),
                pltpu.VMEM((tokens, width), jnp.bfloat16),
                pltpu.VMEM((heads * tokens, HD), jnp.bfloat16),
                pltpu.VMEM((2, span, HD), jnp.float32),
            ],
        ),
        out_shape=(
            jax.ShapeDtypeStruct((tokens, width), jnp.bfloat16),
            jax.ShapeDtypeStruct((tokens, KVH * cols), jnp.bfloat16),
            jax.ShapeDtypeStruct((2, tokens, KVH * HD), jnp.float32),
            jax.ShapeDtypeStruct((2, tokens, KVH * HD), jnp.bfloat16),
        ),
        compiler_params=params(56),
        cost_estimate=pl.CostEstimate(
            flops=2 * tokens * width * KVH * cols, bytes_accessed=22 * MIB, transcendentals=0
        ),
        name="tail_attention",
    )(place_info, back, place, moe_grad, *pieces, low, turned, query, keys, values)


def finish_kernel(kept_ref, later_ref, key_ref, value_ref):
    for kind, out_ref in enumerate((key_ref, value_ref)):
        out_ref[...] = kept_ref[kind] + later_ref[kind].astype(jnp.float32)


def finish(kept, later):
    out = jax.ShapeDtypeStruct(kept.shape[1:], jnp.float32)
    return pl.pallas_call(
        finish_kernel, out_shape=(out, out), compiler_params=params(16), cost_estimate=LIGHT, name="finish"
    )(kept, later)


def local(
    moe_input,
    moe_grad,
    routes,
    route_weight,
    w_gate,
    w_up,
    w_down,
    w_out,
    queries,
    key_heads,
    value_heads,
    segments,
):
    chips = ("far", "near", "low")
    blk = chips + ("core",)
    low = lax.axis_size("low")
    owners = 4 * low
    count = 2 * owners
    parts = lax.axis_size("groups")
    tokens, width = moe_input.shape
    depth = 2 * max(1, 3 * tokens * routes.shape[1] // (2 * count))
    swap = [(0, 1), (1, 0)]
    onward = [(i, i + 1) for i in range(count - 1)]
    backward = [(i + 1, i) for i in range(count - 1)]

    share_cols = w_out.shape[1] // parts
    w_share = lax.dynamic_slice_in_dim(w_out, lax.axis_index("groups") * share_cols, share_cols, 1)
    w_near = lax.ppermute(w_share, "near", swap)
    w_far = lax.ppermute(w_share, "far", swap)

    rows, place = pick(routes, route_weight, moe_input, moe_grad, owners, depth)
    line = lambda w: lax.all_gather(w, "low", axis=0, tiled=False)
    cross = lambda w: lax.ppermute(w, "groups", swap)
    other_core = lambda w: lax.ppermute(w, "core", swap)
    own = (w_gate, w_up, w_down)
    other = tuple(other_core(w) for w in own)

    key_heads, value_heads, segments, place = lax.optimization_barrier((key_heads, value_heads, segments, place))
    kv = jnp.concatenate([key_heads, value_heads], axis=1)
    segs = (segments + 1).astype(jnp.float32)
    seg_rows = jnp.zeros((16, kv.shape[1]), jnp.bfloat16).at[0, :tokens].set(segs.astype(jnp.bfloat16))
    prev = lax.ppermute(jnp.concatenate([kv, seg_rows], axis=0), blk, onward)
    own_line = line(w_share)
    rows, w_near, w_far, own_line, prev = lax.optimization_barrier((rows, w_near, w_far, own_line, prev))

    rows_in = lax.all_to_all(rows.reshape(owners, depth, 2 * width), chips, 0, 0, tiled=True)
    near_crossed, far_crossed = cross(w_near), cross(w_far)
    near_twin = line(jnp.stack([w_near, near_crossed]))
    far_twin = line(jnp.stack([w_far, far_crossed]))
    own_line, near_crossed, far_crossed = lax.optimization_barrier((own_line, near_crossed, far_crossed))
    own_crossed = cross(own_line)
    w_last = lax.ppermute(w_far, "near", swap)
    prepared = prepare_weights(own, other)
    attention = attention_shares(queries, key_heads, value_heads, prev, segs)
    rows_in, prepared, attention, own_line, own_crossed, w_last = lax.optimization_barrier(
        (rows_in, prepared, attention, own_line, own_crossed, w_last)
    )
    if low == 2:
        moved = lax.ppermute(w_last, "low", swap)
        first = lax.axis_index("low") == 0
        last_line = jnp.where(first, jnp.stack([w_last, moved]), jnp.stack([moved, w_last]))
    else:
        last_line = line(w_last)
    terms = experts(rows_in.reshape(owners * depth, 2 * width), *prepared)
    terms, own_line, own_crossed, last_line, near_twin = lax.optimization_barrier(
        (terms, own_line, own_crossed, last_line, near_twin)
    )
    last_crossed, far_twin = lax.optimization_barrier((cross(last_line), far_twin))
    back = lax.all_to_all(terms.reshape(owners, depth, width), chips, 0, 0, tiled=True)
    both = lambda *pieces: [w for piece in pieces for w in (piece, other_core(piece))]

    z = 2 * lax.axis_index("far") + lax.axis_index("near")
    moe_input_grad, query_grad, kept, sent = tail(
        jnp.stack([lax.axis_index("groups"), z, lax.axis_index("core")]).astype(jnp.int32),
        back.reshape(owners * depth, width), place, moe_grad,
        both(own_line, own_crossed, last_line, last_crossed, near_twin, far_twin), *attention,
    )
    return (moe_input_grad, query_grad, *finish(kept, lax.ppermute(sent, blk, backward)))


def solution(mesh):
    names = ("groups", "far", "near", "low", "core")
    shape = (mesh.shape["groups"], 2, 2, mesh.shape["blk"] // 8, 2)
    fine = jax.sharding.Mesh(mesh.devices.reshape(shape), names)
    blk = names[1:]
    by_tokens = P(names, None)
    return jax.shard_map(
        local,
        mesh=fine,
        in_specs=(
            by_tokens,
            by_tokens,
            by_tokens,
            by_tokens,
            P(None, blk),
            P(None, blk),
            P(blk, None),
            P(blk, None),
            by_tokens,
            by_tokens,
            by_tokens,
            P(names),
        ),
        out_specs=(by_tokens,) * 4,
        check_vma=False,
    )
```

```python
import functools

import jax
import jax.numpy as jnp
from jax import lax
from jax.experimental import pallas as pl
from jax.experimental.pallas import tpu as pltpu
from jax.sharding import PartitionSpec as P

KVH = 2
GROUP = 16
HD = 128
FLOOR = -1e30
MIB = 1 << 20
LIGHT = pl.CostEstimate(flops=0, bytes_accessed=0, transcendentals=0)

NT = (((1,), (1,)), ((), ()))
TN = (((0,), (0,)), ((), ()))


def dot(a, b, dims=(((1,), (0,)), ((), ()))):
    return lax.dot_general(a, b, dims, preferred_element_type=jnp.float32)


def params(mib):
    return pltpu.CompilerParams(vmem_limit_bytes=mib * MIB)


def pick_kernel(owners, depth, routes_ref, weight_ref, input_ref, grad_ref, rows_ref, back_ref):
    tokens = input_ref.shape[0]
    slots = owners * depth
    first = routes_ref[0:1, :]
    second = routes_ref[1:2, :]
    expert = lax.broadcasted_iota(jnp.int32, (owners, tokens), 0)
    is_first = first == expert
    is_second = second == expert
    member = jnp.where(is_first | is_second, 1.0, 0.0)
    before = lax.broadcasted_iota(jnp.int32, (tokens, tokens), 0) < lax.broadcasted_iota(
        jnp.int32, (tokens, tokens), 1
    )
    rank = dot(member.astype(jnp.bfloat16), jnp.where(before, 1.0, 0.0).astype(jnp.bfloat16))
    spot = (expert * depth).astype(jnp.float32) + rank
    slot_first = jnp.sum(jnp.where(is_first, spot, 0.0), axis=0, keepdims=True).astype(jnp.int32)
    slot_second = jnp.sum(jnp.where(is_second, spot, 0.0), axis=0, keepdims=True).astype(jnp.int32)
    slot = lax.broadcasted_iota(jnp.int32, (slots, tokens), 0)
    at_first = slot == slot_first
    at_second = slot == slot_second
    place = jnp.where(at_first | at_second, 1.0, 0.0).astype(jnp.bfloat16)
    back_ref[...] = place.T
    scale = jnp.sum(
        jnp.where(at_first, weight_ref[0:1, :], 0.0) + jnp.where(at_second, weight_ref[1:2, :], 0.0),
        axis=1,
        keepdims=True,
    )
    width = input_ref.shape[1]
    rows_ref[:, :width] = dot(place, input_ref[...]).astype(jnp.bfloat16)
    rows_ref[:, width:] = (scale * dot(place, grad_ref[...])).astype(jnp.bfloat16)


def pick(routes, route_weight, moe_input, moe_grad, owners, depth):
    tokens, width = moe_input.shape
    slots = owners * depth
    return pl.pallas_call(
        functools.partial(pick_kernel, owners, depth),
        out_shape=(
            jax.ShapeDtypeStruct((slots, 2 * width), jnp.bfloat16),
            jax.ShapeDtypeStruct((tokens, slots), jnp.bfloat16),
        ),
        compiler_params=params(32),
        cost_estimate=pl.CostEstimate(
            flops=4 * slots * tokens * width, bytes_accessed=8 * MIB, transcendentals=0
        ),
        name="pick_rows",
    )(routes.T, route_weight.T, moe_input, moe_grad)


def weights_kernel(*refs):
    own, other, (cols_ref, down_ref, rows_ref) = refs[:3], refs[3:6], refs[6:]
    tile = own[0].shape[1]
    for place, (gate_ref, up_ref, low_ref) in enumerate((own, other)):
        for kind, ref in enumerate((gate_ref, up_ref)):
            spot = slice((2 * kind + place) * tile, (2 * kind + place + 1) * tile)
            cols_ref[0, :, spot] = ref[...]
            rows_ref[0, spot, :] = ref[...].T
        down_ref[0, :, place * tile : (place + 1) * tile] = low_ref[...].T


def prepare_weights(own, other):
    width, half = own[0].shape
    tile = 128
    steps = half // tile
    cols = pl.BlockSpec((width, tile), lambda i: (0, i))
    down = pl.BlockSpec((tile, width), lambda i: (i, 0))
    return pl.pallas_call(
        weights_kernel,
        grid=(steps,),
        in_specs=[cols, cols, down] * 2,
        out_specs=[
            pl.BlockSpec((1, width, 4 * tile), lambda i: (i, 0, 0)),
            pl.BlockSpec((1, width, 2 * tile), lambda i: (i, 0, 0)),
            pl.BlockSpec((1, 4 * tile, width), lambda i: (i, 0, 0)),
        ],
        out_shape=(
            jax.ShapeDtypeStruct((steps, width, 4 * tile), jnp.bfloat16),
            jax.ShapeDtypeStruct((steps, width, 2 * tile), jnp.bfloat16),
            jax.ShapeDtypeStruct((steps, 4 * tile, width), jnp.bfloat16),
        ),
        compiler_params=params(48),
        cost_estimate=LIGHT,
        name="prepare_weights",
    )(*own, *other)


def expert_kernel(steps, rows_ref, cols_ref, down_ref, back_ref, out_ref, hidden):
    step = pl.program_id(0)
    width = rows_ref.shape[1] // 2
    pair = down_ref.shape[2]

    @pl.when(step < steps)
    def _():
        both_pre = dot(rows_ref[:, :width], cols_ref[0])
        gate_pre = both_pre[:, :pair]
        up_pre = both_pre[:, pair:]
        down_grad = dot(rows_ref[:, width:], down_ref[0])
        sig = jax.nn.sigmoid(gate_pre)
        hidden[step, :, :pair] = (
            down_grad * up_pre * sig * (1.0 + gate_pre * (1.0 - sig))
        ).astype(jnp.bfloat16)
        hidden[step, :, pair:] = (down_grad * gate_pre * sig).astype(jnp.bfloat16)

    @pl.when(step >= steps)
    def _():
        total = dot(hidden[0], back_ref[0])
        for i in range(1, steps):
            total += dot(hidden[i], back_ref[i])
        out_ref[...] = total.astype(jnp.bfloat16)


def experts(rows, cols, down, back):
    count, twice = rows.shape
    steps, width, quad = cols.shape
    tile = 512
    last = steps - 1
    turn = lambda i: jnp.maximum(i - steps, 0)
    return pl.pallas_call(
        functools.partial(expert_kernel, steps),
        grid=(steps + width // tile,),
        in_specs=[
            pl.BlockSpec((count, twice), lambda i: (0, 0)),
            pl.BlockSpec((1, width, quad), lambda i: (jnp.minimum(i, last), 0, 0)),
            pl.BlockSpec((1, width, quad // 2), lambda i: (jnp.minimum(i, last), 0, 0)),
            pl.BlockSpec((steps, quad, tile), lambda i: (0, 0, turn(i))),
        ],
        out_specs=pl.BlockSpec((count, tile), lambda i: (0, turn(i))),
        out_shape=jax.ShapeDtypeStruct((count, width), jnp.bfloat16),
        scratch_shapes=[pltpu.VMEM((steps, count, quad), jnp.bfloat16)],
        compiler_params=params(48),
        cost_estimate=LIGHT,
        name="expert_terms",
    )(rows, cols, down, back)


def shares_kernel(
    q_ref, key_ref, value_ref, prev_key_ref, prev_value_ref, prev_seg_ref, seg_row_ref, seg_col_ref,
    low_ref, turned_ref, query_ref, key_out, value_out,
):
    tokens = q_ref.shape[0]
    seg_col = seg_col_ref[...]
    row = lax.broadcasted_iota(jnp.int32, (tokens, tokens), 0)
    col = lax.broadcasted_iota(jnp.int32, (tokens, tokens), 1)
    own_seen = jnp.where((col <= row) & (seg_row_ref[...] == seg_col), 1.0, 0.0)
    prev_seg = prev_seg_ref[tokens : tokens + 16, :].astype(jnp.float32)[0:1, :]
    prev_seen = jnp.where(prev_seg == seg_col, 1.0, 0.0)
    seen = jnp.concatenate([prev_seen, own_seen], axis=1) > 0.5
    keys = jnp.concatenate([prev_key_ref[:tokens, :], key_ref[...]], axis=0)
    values = jnp.concatenate([prev_value_ref[:tokens, :], value_ref[...]], axis=0)
    key_out[0] = keys
    value_out[0] = values.T
    for head in range(GROUP):
        rows = slice(head * tokens, (head + 1) * tokens)
        query = q_ref[:, head * HD : (head + 1) * HD]
        scores = dot(query, keys, NT) * (HD**-0.5)
        masked = jnp.where(seen, scores, FLOOR)
        raised = jnp.where(seen, jnp.exp(masked - jnp.max(masked, axis=1, keepdims=True)), 0.0)
        shares = raised / jnp.sum(raised, axis=1, keepdims=True)
        low = shares.astype(jnp.bfloat16)
        low_ref[0, rows, :] = low
        turned_ref[0, :, rows] = low.T
        query_ref[0, rows, :] = query


def attention_shares(queries, key_heads, value_heads, prev, segs):
    tokens, width = queries.shape
    span = 2 * tokens
    stack = GROUP * tokens
    high = prev.shape[0]
    own = pl.BlockSpec((tokens, HD), lambda g: (0, g))
    group = lambda shape: pl.BlockSpec((1,) + shape, lambda g: (g, 0, 0))
    made = lambda shape: jax.ShapeDtypeStruct((KVH,) + shape, jnp.bfloat16)
    shapes = ((stack, span), (span, stack), (stack, HD), (span, HD), (HD, span))
    return pl.pallas_call(
        shares_kernel,
        grid=(KVH,),
        in_specs=[
            pl.BlockSpec((tokens, GROUP * HD), lambda g: (0, g)),
            own,
            own,
            pl.BlockSpec((high, HD), lambda g: (0, g)),
            pl.BlockSpec((high, HD), lambda g: (0, KVH + g)),
            pl.BlockSpec((high, HD), lambda g: (0, 0)),
            pl.BlockSpec((1, tokens), lambda g: (0, 0)),
            pl.BlockSpec((tokens, 1), lambda g: (0, 0)),
        ],
        out_specs=[group(shape) for shape in shapes],
        out_shape=[made(shape) for shape in shapes],
        compiler_params=params(32),
        cost_estimate=LIGHT,
        name="attention_shares",
    )(queries, key_heads, value_heads, prev, prev, prev, segs[None, :], segs[:, None])


def tail_kernel(
    plan, place_info, back_ref, place_ref, grad_ref, *refs
):
    heads, tiles = plan
    own, across, twin, refs = refs[:6], refs[6:12], refs[12:14], refs[14:]
    low_ref, turned_ref, q_ref, key_ref, value_ref, *refs = refs
    moe_ref, query_out, kept_out, sent_out, by_place, stream, held, sums = refs
    step = pl.program_id(0)
    tokens = query_out.shape[0]
    part_size = by_place.shape[2]
    size = own[0].shape[1]
    mine, across = own[:4] + twin + own[4:], across[:4] + twin + across[4:]
    spread = part_size // size
    here, core = place_info[1], place_info[2]

    @pl.when(step == 0)
    def _():
        moe = dot(place_ref[...], back_ref[...]).astype(jnp.bfloat16)
        moe_ref[...] = moe
        added = (grad_ref[...].astype(jnp.float32) + moe.astype(jnp.float32)).astype(jnp.bfloat16)
        for z in range(4):
            for rest in range(spread):
                for side in range(2):
                    source = ((z * spread + rest) * 2 + side) * size
                    by_place[2 * z + side, :, rest * size : (rest + 1) * size] = added[:, source : source + size]
        for i in range(8):
            spot = slice(i * part_size, (i + 1) * part_size)
            stream[:, spot] = by_place[2 * (here ^ (i // 2)) + (core ^ (i % 2))]

    @pl.when((step > 0) & ((step - 1) % tiles == 0))
    def _():
        sums[...] = jnp.zeros_like(sums)

    def project(pieces):
        columns = jnp.concatenate([piece[...].reshape(part_size, piece.shape[-1]) for piece in pieces], axis=0)
        return dot(stream[...], columns).astype(jnp.bfloat16)

    def hold(head_grad):
        for head in range(heads):
            held[head * tokens : (head + 1) * tokens, :] = head_grad[:, head * HD : (head + 1) * HD]

    def attend():
        grads = held[...]
        low = low_ref[0].astype(jnp.float32)
        prob_grad = dot(grads, value_ref[0])
        row_dot = jnp.sum(low * prob_grad, axis=1, keepdims=True)
        score_grad = (low * (prob_grad - row_dot) * (HD**-0.5)).astype(jnp.bfloat16)
        query_grad = dot(score_grad, key_ref[0]).astype(jnp.bfloat16)
        sums[0] += dot(score_grad, q_ref[0], TN)
        sums[1] += dot(turned_ref[0], grads)
        for head in range(heads):
            query_out[:, head * HD : (head + 1) * HD] = query_grad[head * tokens : (head + 1) * tokens, :]

    @pl.when(step == 0)
    def _():
        hold(project(mine))

    @pl.when((step > 0) & (step < tiles))
    def _():
        head_grad = project(mine)
        attend()
        hold(head_grad)

    @pl.when((step >= tiles) & (step < 2 * tiles))
    def _():
        head_grad = project(across)
        attend()
        hold(head_grad)

    @pl.when(step == 2 * tiles)
    def _():
        attend()

    @pl.when((step > 0) & (step % tiles == 0))
    def _():
        kept_out[...] = sums[:, tokens:, :]
        sent_out[...] = sums[:, :tokens, :].astype(jnp.bfloat16)


def tail(place_info, back, place, moe_grad, pieces, low, turned, query, keys, values):
    tokens, width = moe_grad.shape
    spread, size, cols = pieces[0].shape
    span = keys.shape[1]
    heads = 4
    tile = heads * HD
    tiles = cols // tile
    steps = KVH * tiles
    was = lambda i: jnp.maximum(i - 1, 0)
    kv_group = lambda i, info: (was(i) // tiles) ^ info[0]
    whole = lambda shape: pl.BlockSpec(shape, lambda i, info: (0,) * len(shape))
    group = lambda shape: pl.BlockSpec((1,) + shape, lambda i, info: (kv_group(i, info), 0, 0))
    rows = lambda shape: pl.BlockSpec((1,) + shape, lambda i, info: (kv_group(i, info), was(i) % tiles, 0))
    own_tile = lambda i: jnp.minimum(i, tiles - 1)
    other_tile = lambda i: jnp.minimum(jnp.maximum(i - tiles, 0), tiles - 1)
    now = lambda i: jnp.minimum(i, steps - 1)
    twin = pl.BlockSpec((spread, 1, size, tile), lambda i, info: (0, now(i) // tiles, 0, now(i) % tiles))
    piece = lambda turn: pl.BlockSpec((spread, size, tile), lambda i, info: (0, 0, turn(i)))
    kv = pl.BlockSpec((2, tokens, HD), lambda i, info: (0, 0, kv_group(i, info)))
    return pl.pallas_call(
        functools.partial(tail_kernel, (heads, tiles)),
        grid_spec=pltpu.PrefetchScalarGridSpec(
            num_scalar_prefetch=1,
            grid=(steps + 1,),
            in_specs=[whole(back.shape), whole(place.shape), whole(moe_grad.shape)]
            + [piece(own_tile)] * 6
            + [piece(other_tile)] * 6
            + [twin] * 2
            + [
                rows((heads * tokens, span)),
                pl.BlockSpec(
                    (1, span, heads * tokens), lambda i, info: (kv_group(i, info), 0, was(i) % tiles)
                ),
                rows((heads * tokens, HD)),
                group((span, HD)),
                group((HD, span)),
            ],
            out_specs=[
                whole((tokens, width)),
                pl.BlockSpec(
                    (tokens, tile), lambda i, info: (0, kv_group(i, info) * tiles + was(i) % tiles)
                ),
                kv,
                kv,
            ],
            scratch_shapes=[
                pltpu.VMEM((8, tokens, spread * size), jnp.bfloat16),
                pltpu.VMEM((tokens, width), jnp.bfloat16),
                pltpu.VMEM((heads * tokens, HD), jnp.bfloat16),
                pltpu.VMEM((2, span, HD), jnp.float32),
            ],
        ),
        out_shape=(
            jax.ShapeDtypeStruct((tokens, width), jnp.bfloat16),
            jax.ShapeDtypeStruct((tokens, KVH * cols), jnp.bfloat16),
            jax.ShapeDtypeStruct((2, tokens, KVH * HD), jnp.float32),
            jax.ShapeDtypeStruct((2, tokens, KVH * HD), jnp.bfloat16),
        ),
        compiler_params=params(56),
        cost_estimate=pl.CostEstimate(
            flops=2 * tokens * width * KVH * cols, bytes_accessed=22 * MIB, transcendentals=0
        ),
        name="tail_attention",
    )(place_info, back, place, moe_grad, *pieces, low, turned, query, keys, values)


def finish_kernel(kept_ref, later_ref, key_ref, value_ref):
    for kind, out_ref in enumerate((key_ref, value_ref)):
        out_ref[...] = kept_ref[kind] + later_ref[kind].astype(jnp.float32)


def finish(kept, later):
    out = jax.ShapeDtypeStruct(kept.shape[1:], jnp.float32)
    return pl.pallas_call(
        finish_kernel, out_shape=(out, out), compiler_params=params(16), cost_estimate=LIGHT, name="finish"
    )(kept, later)


def local(
    moe_input,
    moe_grad,
    routes,
    route_weight,
    w_gate,
    w_up,
    w_down,
    w_out,
    queries,
    key_heads,
    value_heads,
    segments,
):
    chips = ("far", "near", "low")
    blk = chips + ("core",)
    low = lax.axis_size("low")
    owners = 4 * low
    count = 2 * owners
    parts = lax.axis_size("groups")
    tokens, width = moe_input.shape
    depth = 2 * max(1, 3 * tokens * routes.shape[1] // (2 * count))
    swap = [(0, 1), (1, 0)]
    onward = [(i, i + 1) for i in range(count - 1)]
    backward = [(i + 1, i) for i in range(count - 1)]

    share_cols = w_out.shape[1] // parts
    w_share = lax.dynamic_slice_in_dim(w_out, lax.axis_index("groups") * share_cols, share_cols, 1)
    w_near = lax.ppermute(w_share, "near", swap)
    w_far = lax.ppermute(w_share, "far", swap)

    rows, place = pick(routes, route_weight, moe_input, moe_grad, owners, depth)
    line = lambda w: lax.all_gather(w, "low", axis=0, tiled=False)
    cross = lambda w: lax.ppermute(w, "groups", swap)
    other_core = lambda w: lax.ppermute(w, "core", swap)
    own = (w_gate, w_up, w_down)
    other = tuple(other_core(w) for w in own)

    key_heads, value_heads, segments, place = lax.optimization_barrier((key_heads, value_heads, segments, place))
    kv = jnp.concatenate([key_heads, value_heads], axis=1)
    segs = (segments + 1).astype(jnp.float32)
    seg_rows = jnp.zeros((16, kv.shape[1]), jnp.bfloat16).at[0, :tokens].set(segs.astype(jnp.bfloat16))
    prev = lax.ppermute(jnp.concatenate([kv, seg_rows], axis=0), blk, onward)
    own_line = line(w_share)
    rows, w_near, w_far, own_line, prev = lax.optimization_barrier((rows, w_near, w_far, own_line, prev))

    rows_in = lax.all_to_all(rows.reshape(owners, depth, 2 * width), chips, 0, 0, tiled=True)
    near_line = line(w_near)
    far_crossed = cross(w_far)
    far_twin = line(jnp.stack([w_far, far_crossed]))
    own_line, far_crossed = lax.optimization_barrier((own_line, far_crossed))
    own_crossed = cross(own_line)
    near_crossed = cross(near_line)
    w_last = lax.ppermute(w_far, "near", swap)
    prepared = prepare_weights(own, other)
    attention = attention_shares(queries, key_heads, value_heads, prev, segs)
    rows_in, prepared, attention, own_line, near_line, own_crossed, near_crossed, w_last = (
        lax.optimization_barrier(
            (rows_in, prepared, attention, own_line, near_line, own_crossed, near_crossed, w_last)
        )
    )
    if low == 2:
        moved = lax.ppermute(w_last, "low", swap)
        first = lax.axis_index("low") == 0
        last_line = jnp.where(first, jnp.stack([w_last, moved]), jnp.stack([moved, w_last]))
    else:
        last_line = line(w_last)
    terms = experts(rows_in.reshape(owners * depth, 2 * width), *prepared)
    terms, own_line, near_line, own_crossed, near_crossed, last_line, far_twin = lax.optimization_barrier(
        (terms, own_line, near_line, own_crossed, near_crossed, last_line, far_twin)
    )
    last_crossed = cross(last_line)
    back = lax.all_to_all(terms.reshape(owners, depth, width), chips, 0, 0, tiled=True)
    both = lambda *pieces: [w for piece in pieces for w in (piece, other_core(piece))]

    z = 2 * lax.axis_index("far") + lax.axis_index("near")
    moe_input_grad, query_grad, kept, sent = tail(
        jnp.stack([lax.axis_index("groups"), z, lax.axis_index("core")]).astype(jnp.int32),
        back.reshape(owners * depth, width), place, moe_grad,
        both(own_line, near_line, last_line, own_crossed, near_crossed, last_crossed, far_twin), *attention,
    )
    return (moe_input_grad, query_grad, *finish(kept, lax.ppermute(sent, blk, backward)))


def solution(mesh):
    names = ("groups", "far", "near", "low", "core")
    shape = (mesh.shape["groups"], 2, 2, mesh.shape["blk"] // 8, 2)
    fine = jax.sharding.Mesh(mesh.devices.reshape(shape), names)
    blk = names[1:]
    by_tokens = P(names, None)
    return jax.shard_map(
        local,
        mesh=fine,
        in_specs=(
            by_tokens,
            by_tokens,
            by_tokens,
            by_tokens,
            P(None, blk),
            P(None, blk),
            P(blk, None),
            P(blk, None),
            by_tokens,
            by_tokens,
            by_tokens,
            P(names),
        ),
        out_specs=(by_tokens,) * 4,
        check_vma=False,
    )
```

```python
import functools

import jax
import jax.numpy as jnp
from jax import lax
from jax.experimental import pallas as pl
from jax.experimental.pallas import tpu as pltpu
from jax.sharding import PartitionSpec as P

KVH = 2
GROUP = 16
HD = 128
FLOOR = -1e30
MIB = 1 << 20
LIGHT = pl.CostEstimate(flops=0, bytes_accessed=0, transcendentals=0)

NT = (((1,), (1,)), ((), ()))
TN = (((0,), (0,)), ((), ()))


def dot(a, b, dims=(((1,), (0,)), ((), ()))):
    return lax.dot_general(a, b, dims, preferred_element_type=jnp.float32)


def params(mib):
    return pltpu.CompilerParams(vmem_limit_bytes=mib * MIB)


def pick_kernel(owners, depth, routes_ref, weight_ref, input_ref, grad_ref, rows_ref, back_ref):
    tokens = input_ref.shape[0]
    slots = owners * depth
    first = routes_ref[0:1, :]
    second = routes_ref[1:2, :]
    expert = lax.broadcasted_iota(jnp.int32, (owners, tokens), 0)
    is_first = first == expert
    is_second = second == expert
    member = jnp.where(is_first | is_second, 1.0, 0.0)
    before = lax.broadcasted_iota(jnp.int32, (tokens, tokens), 0) < lax.broadcasted_iota(
        jnp.int32, (tokens, tokens), 1
    )
    rank = dot(member.astype(jnp.bfloat16), jnp.where(before, 1.0, 0.0).astype(jnp.bfloat16))
    spot = (expert * depth).astype(jnp.float32) + rank
    slot_first = jnp.sum(jnp.where(is_first, spot, 0.0), axis=0, keepdims=True).astype(jnp.int32)
    slot_second = jnp.sum(jnp.where(is_second, spot, 0.0), axis=0, keepdims=True).astype(jnp.int32)
    slot = lax.broadcasted_iota(jnp.int32, (slots, tokens), 0)
    at_first = slot == slot_first
    at_second = slot == slot_second
    place = jnp.where(at_first | at_second, 1.0, 0.0).astype(jnp.bfloat16)
    back_ref[...] = place.T
    scale = jnp.sum(
        jnp.where(at_first, weight_ref[0:1, :], 0.0) + jnp.where(at_second, weight_ref[1:2, :], 0.0),
        axis=1,
        keepdims=True,
    )
    width = input_ref.shape[1]
    rows_ref[:, :width] = dot(place, input_ref[...]).astype(jnp.bfloat16)
    rows_ref[:, width:] = (scale * dot(place, grad_ref[...])).astype(jnp.bfloat16)


def pick(routes, route_weight, moe_input, moe_grad, owners, depth):
    tokens, width = moe_input.shape
    slots = owners * depth
    return pl.pallas_call(
        functools.partial(pick_kernel, owners, depth),
        out_shape=(
            jax.ShapeDtypeStruct((slots, 2 * width), jnp.bfloat16),
            jax.ShapeDtypeStruct((tokens, slots), jnp.bfloat16),
        ),
        compiler_params=params(32),
        cost_estimate=pl.CostEstimate(
            flops=4 * slots * tokens * width, bytes_accessed=8 * MIB, transcendentals=0
        ),
        name="pick_rows",
    )(routes.T, route_weight.T, moe_input, moe_grad)


def weights_kernel(*refs):
    own, other, (cols_ref, down_ref, rows_ref) = refs[:3], refs[3:6], refs[6:]
    tile = own[0].shape[1]
    for place, (gate_ref, up_ref, low_ref) in enumerate((own, other)):
        for kind, ref in enumerate((gate_ref, up_ref)):
            spot = slice((2 * kind + place) * tile, (2 * kind + place + 1) * tile)
            cols_ref[0, :, spot] = ref[...]
            rows_ref[0, spot, :] = ref[...].T
        down_ref[0, :, place * tile : (place + 1) * tile] = low_ref[...].T


def prepare_weights(own, other):
    width, half = own[0].shape
    tile = 128
    steps = half // tile
    cols = pl.BlockSpec((width, tile), lambda i: (0, i))
    down = pl.BlockSpec((tile, width), lambda i: (i, 0))
    return pl.pallas_call(
        weights_kernel,
        grid=(steps,),
        in_specs=[cols, cols, down] * 2,
        out_specs=[
            pl.BlockSpec((1, width, 4 * tile), lambda i: (i, 0, 0)),
            pl.BlockSpec((1, width, 2 * tile), lambda i: (i, 0, 0)),
            pl.BlockSpec((1, 4 * tile, width), lambda i: (i, 0, 0)),
        ],
        out_shape=(
            jax.ShapeDtypeStruct((steps, width, 4 * tile), jnp.bfloat16),
            jax.ShapeDtypeStruct((steps, width, 2 * tile), jnp.bfloat16),
            jax.ShapeDtypeStruct((steps, 4 * tile, width), jnp.bfloat16),
        ),
        compiler_params=params(48),
        cost_estimate=LIGHT,
        name="prepare_weights",
    )(*own, *other)


def expert_kernel(steps, rows_ref, cols_ref, down_ref, back_ref, out_ref, hidden):
    step = pl.program_id(0)
    width = rows_ref.shape[1] // 2
    pair = down_ref.shape[2]

    @pl.when(step < steps)
    def _():
        both_pre = dot(rows_ref[:, :width], cols_ref[0])
        gate_pre = both_pre[:, :pair]
        up_pre = both_pre[:, pair:]
        down_grad = dot(rows_ref[:, width:], down_ref[0])
        sig = jax.nn.sigmoid(gate_pre)
        hidden[step, :, :pair] = (
            down_grad * up_pre * sig * (1.0 + gate_pre * (1.0 - sig))
        ).astype(jnp.bfloat16)
        hidden[step, :, pair:] = (down_grad * gate_pre * sig).astype(jnp.bfloat16)

    @pl.when(step >= steps)
    def _():
        total = dot(hidden[0], back_ref[0])
        for i in range(1, steps):
            total += dot(hidden[i], back_ref[i])
        out_ref[...] = total.astype(jnp.bfloat16)


def experts(rows, cols, down, back):
    count, twice = rows.shape
    steps, width, quad = cols.shape
    tile = 512
    last = steps - 1
    turn = lambda i: jnp.maximum(i - steps, 0)
    return pl.pallas_call(
        functools.partial(expert_kernel, steps),
        grid=(steps + width // tile,),
        in_specs=[
            pl.BlockSpec((count, twice), lambda i: (0, 0)),
            pl.BlockSpec((1, width, quad), lambda i: (jnp.minimum(i, last), 0, 0)),
            pl.BlockSpec((1, width, quad // 2), lambda i: (jnp.minimum(i, last), 0, 0)),
            pl.BlockSpec((steps, quad, tile), lambda i: (0, 0, turn(i))),
        ],
        out_specs=pl.BlockSpec((count, tile), lambda i: (0, turn(i))),
        out_shape=jax.ShapeDtypeStruct((count, width), jnp.bfloat16),
        scratch_shapes=[pltpu.VMEM((steps, count, quad), jnp.bfloat16)],
        compiler_params=params(48),
        cost_estimate=LIGHT,
        name="expert_terms",
    )(rows, cols, down, back)


def shares_kernel(
    q_ref, key_ref, value_ref, prev_key_ref, prev_value_ref, prev_seg_ref, seg_row_ref, seg_col_ref,
    low_ref, turned_ref, query_ref, key_out, value_out,
):
    tokens = q_ref.shape[0]
    seg_col = seg_col_ref[...]
    row = lax.broadcasted_iota(jnp.int32, (tokens, tokens), 0)
    col = lax.broadcasted_iota(jnp.int32, (tokens, tokens), 1)
    own_seen = jnp.where((col <= row) & (seg_row_ref[...] == seg_col), 1.0, 0.0)
    prev_seg = prev_seg_ref[tokens : tokens + 16, :].astype(jnp.float32)[0:1, :]
    prev_seen = jnp.where(prev_seg == seg_col, 1.0, 0.0)
    seen = jnp.concatenate([prev_seen, own_seen], axis=1) > 0.5
    keys = jnp.concatenate([prev_key_ref[:tokens, :], key_ref[...]], axis=0)
    values = jnp.concatenate([prev_value_ref[:tokens, :], value_ref[...]], axis=0)
    key_out[0] = keys
    value_out[0] = values.T
    for head in range(GROUP):
        rows = slice(head * tokens, (head + 1) * tokens)
        query = q_ref[:, head * HD : (head + 1) * HD]
        scores = dot(query, keys, NT) * (HD**-0.5)
        masked = jnp.where(seen, scores, FLOOR)
        raised = jnp.where(seen, jnp.exp(masked - jnp.max(masked, axis=1, keepdims=True)), 0.0)
        shares = raised / jnp.sum(raised, axis=1, keepdims=True)
        low = shares.astype(jnp.bfloat16)
        low_ref[0, rows, :] = low
        turned_ref[0, :, rows] = low.T
        query_ref[0, rows, :] = query


def attention_shares(queries, key_heads, value_heads, prev, segs):
    tokens, width = queries.shape
    span = 2 * tokens
    stack = GROUP * tokens
    high = prev.shape[0]
    own = pl.BlockSpec((tokens, HD), lambda g: (0, g))
    group = lambda shape: pl.BlockSpec((1,) + shape, lambda g: (g, 0, 0))
    made = lambda shape: jax.ShapeDtypeStruct((KVH,) + shape, jnp.bfloat16)
    shapes = ((stack, span), (span, stack), (stack, HD), (span, HD), (HD, span))
    return pl.pallas_call(
        shares_kernel,
        grid=(KVH,),
        in_specs=[
            pl.BlockSpec((tokens, GROUP * HD), lambda g: (0, g)),
            own,
            own,
            pl.BlockSpec((high, HD), lambda g: (0, g)),
            pl.BlockSpec((high, HD), lambda g: (0, KVH + g)),
            pl.BlockSpec((high, HD), lambda g: (0, 0)),
            pl.BlockSpec((1, tokens), lambda g: (0, 0)),
            pl.BlockSpec((tokens, 1), lambda g: (0, 0)),
        ],
        out_specs=[group(shape) for shape in shapes],
        out_shape=[made(shape) for shape in shapes],
        compiler_params=params(32),
        cost_estimate=LIGHT,
        name="attention_shares",
    )(queries, key_heads, value_heads, prev, prev, prev, segs[None, :], segs[:, None])


def tail_kernel(
    plan, place_info, back_ref, place_ref, grad_ref, *refs
):
    heads, tiles = plan
    own, last, twin, refs = refs[:4], refs[4:8], refs[8:12], refs[12:]
    low_ref, turned_ref, q_ref, key_ref, value_ref, *refs = refs
    moe_ref, query_out, kept_out, sent_out, by_place, stream, held, sums = refs
    step = pl.program_id(0)
    tokens = query_out.shape[0]
    part_size = by_place.shape[2]
    size = own[0].shape[1]
    mine, across = own[:2] + twin + last[:2], own[2:] + twin + last[2:]
    spread = part_size // size
    here, core = place_info[1], place_info[2]

    @pl.when(step == 0)
    def _():
        moe = dot(place_ref[...], back_ref[...]).astype(jnp.bfloat16)
        moe_ref[...] = moe
        added = (grad_ref[...].astype(jnp.float32) + moe.astype(jnp.float32)).astype(jnp.bfloat16)
        for z in range(4):
            for rest in range(spread):
                for side in range(2):
                    source = ((z * spread + rest) * 2 + side) * size
                    by_place[2 * z + side, :, rest * size : (rest + 1) * size] = added[:, source : source + size]
        for i in range(8):
            spot = slice(i * part_size, (i + 1) * part_size)
            stream[:, spot] = by_place[2 * (here ^ (i // 2)) + (core ^ (i % 2))]

    @pl.when((step > 0) & ((step - 1) % tiles == 0))
    def _():
        sums[...] = jnp.zeros_like(sums)

    def project(pieces):
        columns = jnp.concatenate([piece[...].reshape(part_size, piece.shape[-1]) for piece in pieces], axis=0)
        return dot(stream[...], columns).astype(jnp.bfloat16)

    def hold(head_grad):
        for head in range(heads):
            held[head * tokens : (head + 1) * tokens, :] = head_grad[:, head * HD : (head + 1) * HD]

    def attend():
        grads = held[...]
        low = low_ref[0].astype(jnp.float32)
        prob_grad = dot(grads, value_ref[0])
        row_dot = jnp.sum(low * prob_grad, axis=1, keepdims=True)
        score_grad = (low * (prob_grad - row_dot) * (HD**-0.5)).astype(jnp.bfloat16)
        query_grad = dot(score_grad, key_ref[0]).astype(jnp.bfloat16)
        sums[0] += dot(score_grad, q_ref[0], TN)
        sums[1] += dot(turned_ref[0], grads)
        for head in range(heads):
            query_out[:, head * HD : (head + 1) * HD] = query_grad[head * tokens : (head + 1) * tokens, :]

    @pl.when(step == 0)
    def _():
        hold(project(mine))

    @pl.when((step > 0) & (step < tiles))
    def _():
        head_grad = project(mine)
        attend()
        hold(head_grad)

    @pl.when((step >= tiles) & (step < 2 * tiles))
    def _():
        head_grad = project(across)
        attend()
        hold(head_grad)

    @pl.when(step == 2 * tiles)
    def _():
        attend()

    @pl.when((step > 0) & (step % tiles == 0))
    def _():
        kept_out[...] = sums[:, tokens:, :]
        sent_out[...] = sums[:, :tokens, :].astype(jnp.bfloat16)


def tail(place_info, back, place, moe_grad, pieces, low, turned, query, keys, values):
    tokens, width = moe_grad.shape
    spread, size, cols = pieces[0].shape
    span = keys.shape[1]
    heads = 4
    tile = heads * HD
    tiles = cols // tile
    steps = KVH * tiles
    was = lambda i: jnp.maximum(i - 1, 0)
    kv_group = lambda i, info: (was(i) // tiles) ^ info[0]
    whole = lambda shape: pl.BlockSpec(shape, lambda i, info: (0,) * len(shape))
    group = lambda shape: pl.BlockSpec((1,) + shape, lambda i, info: (kv_group(i, info), 0, 0))
    rows = lambda shape: pl.BlockSpec((1,) + shape, lambda i, info: (kv_group(i, info), was(i) % tiles, 0))
    own_tile = lambda i: jnp.minimum(i, tiles - 1)
    other_tile = lambda i: jnp.minimum(jnp.maximum(i - tiles, 0), tiles - 1)
    now = lambda i: jnp.minimum(i, steps - 1)
    twin = pl.BlockSpec((spread, 1, size, tile), lambda i, info: (0, now(i) // tiles, 0, now(i) % tiles))
    piece = lambda turn: pl.BlockSpec((spread, size, tile), lambda i, info: (0, 0, turn(i)))
    kv = pl.BlockSpec((2, tokens, HD), lambda i, info: (0, 0, kv_group(i, info)))
    return pl.pallas_call(
        functools.partial(tail_kernel, (heads, tiles)),
        grid_spec=pltpu.PrefetchScalarGridSpec(
            num_scalar_prefetch=1,
            grid=(steps + 1,),
            in_specs=[whole(back.shape), whole(place.shape), whole(moe_grad.shape)]
            + ([piece(own_tile)] * 2 + [piece(other_tile)] * 2) * 2
            + [twin] * 4
            + [
                rows((heads * tokens, span)),
                pl.BlockSpec(
                    (1, span, heads * tokens), lambda i, info: (kv_group(i, info), 0, was(i) % tiles)
                ),
                rows((heads * tokens, HD)),
                group((span, HD)),
                group((HD, span)),
            ],
            out_specs=[
                whole((tokens, width)),
                pl.BlockSpec(
                    (tokens, tile), lambda i, info: (0, kv_group(i, info) * tiles + was(i) % tiles)
                ),
                kv,
                kv,
            ],
            scratch_shapes=[
                pltpu.VMEM((8, tokens, spread * size), jnp.bfloat16),
                pltpu.VMEM((tokens, width), jnp.bfloat16),
                pltpu.VMEM((heads * tokens, HD), jnp.bfloat16),
                pltpu.VMEM((2, span, HD), jnp.float32),
            ],
        ),
        out_shape=(
            jax.ShapeDtypeStruct((tokens, width), jnp.bfloat16),
            jax.ShapeDtypeStruct((tokens, KVH * cols), jnp.bfloat16),
            jax.ShapeDtypeStruct((2, tokens, KVH * HD), jnp.float32),
            jax.ShapeDtypeStruct((2, tokens, KVH * HD), jnp.bfloat16),
        ),
        compiler_params=params(56),
        cost_estimate=pl.CostEstimate(
            flops=2 * tokens * width * KVH * cols, bytes_accessed=22 * MIB, transcendentals=0
        ),
        name="tail_attention",
    )(place_info, back, place, moe_grad, *pieces, low, turned, query, keys, values)


def finish_kernel(kept_ref, later_ref, key_ref, value_ref):
    for kind, out_ref in enumerate((key_ref, value_ref)):
        out_ref[...] = kept_ref[kind] + later_ref[kind].astype(jnp.float32)


def finish(kept, later):
    out = jax.ShapeDtypeStruct(kept.shape[1:], jnp.float32)
    return pl.pallas_call(
        finish_kernel, out_shape=(out, out), compiler_params=params(16), cost_estimate=LIGHT, name="finish"
    )(kept, later)


def local(
    moe_input,
    moe_grad,
    routes,
    route_weight,
    w_gate,
    w_up,
    w_down,
    w_out,
    queries,
    key_heads,
    value_heads,
    segments,
):
    chips = ("far", "near", "low")
    blk = chips + ("core",)
    low = lax.axis_size("low")
    owners = 4 * low
    count = 2 * owners
    parts = lax.axis_size("groups")
    tokens, width = moe_input.shape
    depth = 2 * max(1, 3 * tokens * routes.shape[1] // (2 * count))
    swap = [(0, 1), (1, 0)]
    onward = [(i, i + 1) for i in range(count - 1)]
    backward = [(i + 1, i) for i in range(count - 1)]

    share_cols = w_out.shape[1] // parts
    w_share = lax.dynamic_slice_in_dim(w_out, lax.axis_index("groups") * share_cols, share_cols, 1)
    w_far = lax.ppermute(w_share, "far", swap)
    w_near = lax.ppermute(w_share, "near", swap)

    rows, place = pick(routes, route_weight, moe_input, moe_grad, owners, depth)
    line = lambda w: lax.all_gather(w, "low", axis=0, tiled=False)
    cross = lambda w: lax.ppermute(w, "groups", swap)
    other_core = lambda w: lax.ppermute(w, "core", swap)
    own = (w_gate, w_up, w_down)
    other = tuple(other_core(w) for w in own)

    key_heads, value_heads, segments, place = lax.optimization_barrier((key_heads, value_heads, segments, place))
    kv = jnp.concatenate([key_heads, value_heads], axis=1)
    segs = (segments + 1).astype(jnp.float32)
    seg_rows = jnp.zeros((16, kv.shape[1]), jnp.bfloat16).at[0, :tokens].set(segs.astype(jnp.bfloat16))
    prev = lax.ppermute(jnp.concatenate([kv, seg_rows], axis=0), blk, onward)
    own_line = line(w_share)
    rows, w_near, w_far, own_line, prev = lax.optimization_barrier((rows, w_near, w_far, own_line, prev))

    rows_in = lax.all_to_all(rows.reshape(owners, depth, 2 * width), chips, 0, 0, tiled=True)
    near_crossed, far_crossed = cross(w_near), cross(w_far)
    near_twin = line(jnp.stack([w_near, near_crossed]))
    far_twin = line(jnp.stack([w_far, far_crossed]))
    own_line, near_crossed, far_crossed = lax.optimization_barrier((own_line, near_crossed, far_crossed))
    own_crossed = cross(own_line)
    w_last = lax.ppermute(w_far, "near", swap)
    prepared = prepare_weights(own, other)
    attention = attention_shares(queries, key_heads, value_heads, prev, segs)
    rows_in, prepared, attention, own_line, own_crossed = lax.optimization_barrier(
        (rows_in, prepared, attention, own_line, own_crossed)
    )
    if low == 2:
        moved = lax.ppermute(w_last, "low", swap)
        first = lax.axis_index("low") == 0
        last_line = jnp.where(first, jnp.stack([w_last, moved]), jnp.stack([moved, w_last]))
    else:
        last_line = line(w_last)
    terms = experts(rows_in.reshape(owners * depth, 2 * width), *prepared)
    terms, own_line, own_crossed, last_line, near_twin = lax.optimization_barrier(
        (terms, own_line, own_crossed, last_line, near_twin)
    )
    last_crossed, far_twin = lax.optimization_barrier((cross(last_line), far_twin))
    back = lax.all_to_all(terms.reshape(owners, depth, width), chips, 0, 0, tiled=True)
    both = lambda *pieces: [w for piece in pieces for w in (piece, other_core(piece))]

    z = 2 * lax.axis_index("far") + lax.axis_index("near")
    moe_input_grad, query_grad, kept, sent = tail(
        jnp.stack([lax.axis_index("groups"), z, lax.axis_index("core")]).astype(jnp.int32),
        back.reshape(owners * depth, width), place, moe_grad,
        both(own_line, own_crossed, last_line, last_crossed, near_twin, far_twin), *attention,
    )
    return (moe_input_grad, query_grad, *finish(kept, lax.ppermute(sent, blk, backward)))


def solution(mesh):
    names = ("groups", "far", "near", "low", "core")
    shape = (mesh.shape["groups"], 2, 2, mesh.shape["blk"] // 8, 2)
    fine = jax.sharding.Mesh(mesh.devices.reshape(shape), names)
    blk = names[1:]
    by_tokens = P(names, None)
    return jax.shard_map(
        local,
        mesh=fine,
        in_specs=(
            by_tokens,
            by_tokens,
            by_tokens,
            by_tokens,
            P(None, blk),
            P(None, blk),
            P(blk, None),
            P(blk, None),
            by_tokens,
            by_tokens,
            by_tokens,
            P(names),
        ),
        out_specs=(by_tokens,) * 4,
        check_vma=False,
    )
```

```python
import functools

import jax
import jax.numpy as jnp
from jax import lax
from jax.experimental import pallas as pl
from jax.experimental.pallas import tpu as pltpu
from jax.sharding import PartitionSpec as P

KVH = 2
GROUP = 16
HD = 128
FLOOR = -1e30
MIB = 1 << 20
LIGHT = pl.CostEstimate(flops=0, bytes_accessed=0, transcendentals=0)

NT = (((1,), (1,)), ((), ()))
TN = (((0,), (0,)), ((), ()))


def dot(a, b, dims=(((1,), (0,)), ((), ()))):
    return lax.dot_general(a, b, dims, preferred_element_type=jnp.float32)


def params(mib):
    return pltpu.CompilerParams(vmem_limit_bytes=mib * MIB)


def pick_kernel(owners, depth, routes_ref, weight_ref, input_ref, grad_ref, rows_ref, back_ref):
    tokens = input_ref.shape[0]
    slots = owners * depth
    first = routes_ref[0:1, :]
    second = routes_ref[1:2, :]
    expert = lax.broadcasted_iota(jnp.int32, (owners, tokens), 0)
    is_first = first == expert
    is_second = second == expert
    member = jnp.where(is_first | is_second, 1.0, 0.0)
    before = lax.broadcasted_iota(jnp.int32, (tokens, tokens), 0) < lax.broadcasted_iota(
        jnp.int32, (tokens, tokens), 1
    )
    rank = dot(member.astype(jnp.bfloat16), jnp.where(before, 1.0, 0.0).astype(jnp.bfloat16))
    spot = (expert * depth).astype(jnp.float32) + rank
    slot_first = jnp.sum(jnp.where(is_first, spot, 0.0), axis=0, keepdims=True).astype(jnp.int32)
    slot_second = jnp.sum(jnp.where(is_second, spot, 0.0), axis=0, keepdims=True).astype(jnp.int32)
    slot = lax.broadcasted_iota(jnp.int32, (slots, tokens), 0)
    at_first = slot == slot_first
    at_second = slot == slot_second
    place = jnp.where(at_first | at_second, 1.0, 0.0).astype(jnp.bfloat16)
    back_ref[...] = place.T
    scale = jnp.sum(
        jnp.where(at_first, weight_ref[0:1, :], 0.0) + jnp.where(at_second, weight_ref[1:2, :], 0.0),
        axis=1,
        keepdims=True,
    )
    width = input_ref.shape[1]
    rows_ref[:, :width] = dot(place, input_ref[...]).astype(jnp.bfloat16)
    rows_ref[:, width:] = (scale * dot(place, grad_ref[...])).astype(jnp.bfloat16)


def pick(routes, route_weight, moe_input, moe_grad, owners, depth):
    tokens, width = moe_input.shape
    slots = owners * depth
    return pl.pallas_call(
        functools.partial(pick_kernel, owners, depth),
        out_shape=(
            jax.ShapeDtypeStruct((slots, 2 * width), jnp.bfloat16),
            jax.ShapeDtypeStruct((tokens, slots), jnp.bfloat16),
        ),
        compiler_params=params(32),
        cost_estimate=pl.CostEstimate(
            flops=4 * slots * tokens * width, bytes_accessed=8 * MIB, transcendentals=0
        ),
        name="pick_rows",
    )(routes.T, route_weight.T, moe_input, moe_grad)


def weights_kernel(*refs):
    own, other, (cols_ref, down_ref, rows_ref) = refs[:3], refs[3:6], refs[6:]
    tile = own[0].shape[1]
    for place, (gate_ref, up_ref, low_ref) in enumerate((own, other)):
        for kind, ref in enumerate((gate_ref, up_ref)):
            spot = slice((2 * kind + place) * tile, (2 * kind + place + 1) * tile)
            cols_ref[0, :, spot] = ref[...]
            rows_ref[0, spot, :] = ref[...].T
        down_ref[0, :, place * tile : (place + 1) * tile] = low_ref[...].T


def prepare_weights(own, other):
    width, half = own[0].shape
    tile = 128
    steps = half // tile
    cols = pl.BlockSpec((width, tile), lambda i: (0, i))
    down = pl.BlockSpec((tile, width), lambda i: (i, 0))
    return pl.pallas_call(
        weights_kernel,
        grid=(steps,),
        in_specs=[cols, cols, down] * 2,
        out_specs=[
            pl.BlockSpec((1, width, 4 * tile), lambda i: (i, 0, 0)),
            pl.BlockSpec((1, width, 2 * tile), lambda i: (i, 0, 0)),
            pl.BlockSpec((1, 4 * tile, width), lambda i: (i, 0, 0)),
        ],
        out_shape=(
            jax.ShapeDtypeStruct((steps, width, 4 * tile), jnp.bfloat16),
            jax.ShapeDtypeStruct((steps, width, 2 * tile), jnp.bfloat16),
            jax.ShapeDtypeStruct((steps, 4 * tile, width), jnp.bfloat16),
        ),
        compiler_params=params(48),
        cost_estimate=LIGHT,
        name="prepare_weights",
    )(*own, *other)


def expert_kernel(steps, rows_ref, cols_ref, down_ref, back_ref, out_ref, hidden):
    step = pl.program_id(0)
    width = rows_ref.shape[1] // 2
    pair = down_ref.shape[2]

    @pl.when(step < steps)
    def _():
        both_pre = dot(rows_ref[:, :width], cols_ref[0])
        gate_pre = both_pre[:, :pair]
        up_pre = both_pre[:, pair:]
        down_grad = dot(rows_ref[:, width:], down_ref[0])
        sig = jax.nn.sigmoid(gate_pre)
        hidden[step, :, :pair] = (
            down_grad * up_pre * sig * (1.0 + gate_pre * (1.0 - sig))
        ).astype(jnp.bfloat16)
        hidden[step, :, pair:] = (down_grad * gate_pre * sig).astype(jnp.bfloat16)

    @pl.when(step >= steps)
    def _():
        total = dot(hidden[0], back_ref[0])
        for i in range(1, steps):
            total += dot(hidden[i], back_ref[i])
        out_ref[...] = total.astype(jnp.bfloat16)


def experts(rows, cols, down, back):
    count, twice = rows.shape
    steps, width, quad = cols.shape
    tile = 512
    last = steps - 1
    turn = lambda i: jnp.maximum(i - steps, 0)
    return pl.pallas_call(
        functools.partial(expert_kernel, steps),
        grid=(steps + width // tile,),
        in_specs=[
            pl.BlockSpec((count, twice), lambda i: (0, 0)),
            pl.BlockSpec((1, width, quad), lambda i: (jnp.minimum(i, last), 0, 0)),
            pl.BlockSpec((1, width, quad // 2), lambda i: (jnp.minimum(i, last), 0, 0)),
            pl.BlockSpec((steps, quad, tile), lambda i: (0, 0, turn(i))),
        ],
        out_specs=pl.BlockSpec((count, tile), lambda i: (0, turn(i))),
        out_shape=jax.ShapeDtypeStruct((count, width), jnp.bfloat16),
        scratch_shapes=[pltpu.VMEM((steps, count, quad), jnp.bfloat16)],
        compiler_params=params(48),
        cost_estimate=LIGHT,
        name="expert_terms",
    )(rows, cols, down, back)


def shares_kernel(
    q_ref, key_ref, value_ref, prev_key_ref, prev_value_ref, prev_seg_ref, seg_row_ref, seg_col_ref,
    low_ref, turned_ref, query_ref, key_out, value_out,
):
    tokens = q_ref.shape[0]
    seg_col = seg_col_ref[...]
    row = lax.broadcasted_iota(jnp.int32, (tokens, tokens), 0)
    col = lax.broadcasted_iota(jnp.int32, (tokens, tokens), 1)
    own_seen = jnp.where((col <= row) & (seg_row_ref[...] == seg_col), 1.0, 0.0)
    prev_seg = prev_seg_ref[tokens : tokens + 16, :].astype(jnp.float32)[0:1, :]
    prev_seen = jnp.where(prev_seg == seg_col, 1.0, 0.0)
    seen = jnp.concatenate([prev_seen, own_seen], axis=1) > 0.5
    keys = jnp.concatenate([prev_key_ref[:tokens, :], key_ref[...]], axis=0)
    values = jnp.concatenate([prev_value_ref[:tokens, :], value_ref[...]], axis=0)
    key_out[0] = keys
    value_out[0] = values.T
    for head in range(GROUP):
        rows = slice(head * tokens, (head + 1) * tokens)
        query = q_ref[:, head * HD : (head + 1) * HD]
        scores = dot(query, keys, NT) * (HD**-0.5)
        masked = jnp.where(seen, scores, FLOOR)
        raised = jnp.where(seen, jnp.exp(masked - jnp.max(masked, axis=1, keepdims=True)), 0.0)
        shares = raised / jnp.sum(raised, axis=1, keepdims=True)
        low = shares.astype(jnp.bfloat16)
        low_ref[0, rows, :] = low
        turned_ref[0, :, rows] = low.T
        query_ref[0, rows, :] = query


def attention_shares(queries, key_heads, value_heads, prev, segs):
    tokens, width = queries.shape
    span = 2 * tokens
    stack = GROUP * tokens
    high = prev.shape[0]
    own = pl.BlockSpec((tokens, HD), lambda g: (0, g))
    group = lambda shape: pl.BlockSpec((1,) + shape, lambda g: (g, 0, 0))
    made = lambda shape: jax.ShapeDtypeStruct((KVH,) + shape, jnp.bfloat16)
    shapes = ((stack, span), (span, stack), (stack, HD), (span, HD), (HD, span))
    return pl.pallas_call(
        shares_kernel,
        grid=(KVH,),
        in_specs=[
            pl.BlockSpec((tokens, GROUP * HD), lambda g: (0, g)),
            own,
            own,
            pl.BlockSpec((high, HD), lambda g: (0, g)),
            pl.BlockSpec((high, HD), lambda g: (0, KVH + g)),
            pl.BlockSpec((high, HD), lambda g: (0, 0)),
            pl.BlockSpec((1, tokens), lambda g: (0, 0)),
            pl.BlockSpec((tokens, 1), lambda g: (0, 0)),
        ],
        out_specs=[group(shape) for shape in shapes],
        out_shape=[made(shape) for shape in shapes],
        compiler_params=params(32),
        cost_estimate=LIGHT,
        name="attention_shares",
    )(queries, key_heads, value_heads, prev, prev, prev, segs[None, :], segs[:, None])


def tail_kernel(
    plan, place_info, back_ref, place_ref, grad_ref, *refs
):
    heads, tiles = plan
    own, last, twin, refs = refs[:4], refs[4:8], refs[8:12], refs[12:]
    low_ref, turned_ref, q_ref, key_ref, value_ref, *refs = refs
    moe_ref, query_out, kept_out, sent_out, by_place, stream, held, sums = refs
    step = pl.program_id(0)
    tokens = query_out.shape[0]
    part_size = by_place.shape[2]
    size = own[0].shape[1]
    mine, across = own[:2] + twin + last[:2], own[2:] + twin + last[2:]
    spread = part_size // size
    here, core = place_info[1], place_info[2]

    @pl.when(step == 0)
    def _():
        moe = dot(place_ref[...], back_ref[...]).astype(jnp.bfloat16)
        moe_ref[...] = moe
        added = (grad_ref[...].astype(jnp.float32) + moe.astype(jnp.float32)).astype(jnp.bfloat16)
        for z in range(4):
            for rest in range(spread):
                for side in range(2):
                    source = ((z * spread + rest) * 2 + side) * size
                    by_place[2 * z + side, :, rest * size : (rest + 1) * size] = added[:, source : source + size]
        for i in range(8):
            spot = slice(i * part_size, (i + 1) * part_size)
            stream[:, spot] = by_place[2 * (here ^ (i // 2)) + (core ^ (i % 2))]

    @pl.when((step > 0) & ((step - 1) % tiles == 0))
    def _():
        sums[...] = jnp.zeros_like(sums)

    def project(pieces):
        columns = jnp.concatenate([piece[...].reshape(part_size, piece.shape[-1]) for piece in pieces], axis=0)
        return dot(stream[...], columns).astype(jnp.bfloat16)

    def hold(head_grad):
        for head in range(heads):
            held[head * tokens : (head + 1) * tokens, :] = head_grad[:, head * HD : (head + 1) * HD]

    def attend():
        grads = held[...]
        low = low_ref[0].astype(jnp.float32)
        prob_grad = dot(grads, value_ref[0])
        row_dot = jnp.sum(low * prob_grad, axis=1, keepdims=True)
        score_grad = (low * (prob_grad - row_dot) * (HD**-0.5)).astype(jnp.bfloat16)
        query_grad = dot(score_grad, key_ref[0]).astype(jnp.bfloat16)
        sums[0] += dot(score_grad, q_ref[0], TN)
        sums[1] += dot(turned_ref[0], grads)
        for head in range(heads):
            query_out[:, head * HD : (head + 1) * HD] = query_grad[head * tokens : (head + 1) * tokens, :]

    @pl.when(step == 0)
    def _():
        hold(project(mine))

    @pl.when((step > 0) & (step < tiles))
    def _():
        head_grad = project(mine)
        attend()
        hold(head_grad)

    @pl.when((step >= tiles) & (step < 2 * tiles))
    def _():
        head_grad = project(across)
        attend()
        hold(head_grad)

    @pl.when(step == 2 * tiles)
    def _():
        attend()

    @pl.when((step > 0) & (step % tiles == 0))
    def _():
        kept_out[...] = sums[:, tokens:, :]
        sent_out[...] = sums[:, :tokens, :].astype(jnp.bfloat16)


def tail(place_info, back, place, moe_grad, pieces, low, turned, query, keys, values):
    tokens, width = moe_grad.shape
    spread, size, cols = pieces[0].shape
    span = keys.shape[1]
    heads = 4
    tile = heads * HD
    tiles = cols // tile
    steps = KVH * tiles
    was = lambda i: jnp.maximum(i - 1, 0)
    kv_group = lambda i, info: (was(i) // tiles) ^ info[0]
    whole = lambda shape: pl.BlockSpec(shape, lambda i, info: (0,) * len(shape))
    group = lambda shape: pl.BlockSpec((1,) + shape, lambda i, info: (kv_group(i, info), 0, 0))
    rows = lambda shape: pl.BlockSpec((1,) + shape, lambda i, info: (kv_group(i, info), was(i) % tiles, 0))
    own_tile = lambda i: jnp.minimum(i, tiles - 1)
    other_tile = lambda i: jnp.minimum(jnp.maximum(i - tiles, 0), tiles - 1)
    now = lambda i: jnp.minimum(i, steps - 1)
    twin = pl.BlockSpec((spread, 1, size, tile), lambda i, info: (0, now(i) // tiles, 0, now(i) % tiles))
    piece = lambda turn: pl.BlockSpec((spread, size, tile), lambda i, info: (0, 0, turn(i)))
    kv = pl.BlockSpec((2, tokens, HD), lambda i, info: (0, 0, kv_group(i, info)))
    return pl.pallas_call(
        functools.partial(tail_kernel, (heads, tiles)),
        grid_spec=pltpu.PrefetchScalarGridSpec(
            num_scalar_prefetch=1,
            grid=(steps + 1,),
            in_specs=[whole(back.shape), whole(place.shape), whole(moe_grad.shape)]
            + ([piece(own_tile)] * 2 + [piece(other_tile)] * 2) * 2
            + [twin] * 4
            + [
                rows((heads * tokens, span)),
                pl.BlockSpec(
                    (1, span, heads * tokens), lambda i, info: (kv_group(i, info), 0, was(i) % tiles)
                ),
                rows((heads * tokens, HD)),
                group((span, HD)),
                group((HD, span)),
            ],
            out_specs=[
                whole((tokens, width)),
                pl.BlockSpec(
                    (tokens, tile), lambda i, info: (0, kv_group(i, info) * tiles + was(i) % tiles)
                ),
                kv,
                kv,
            ],
            scratch_shapes=[
                pltpu.VMEM((8, tokens, spread * size), jnp.bfloat16),
                pltpu.VMEM((tokens, width), jnp.bfloat16),
                pltpu.VMEM((heads * tokens, HD), jnp.bfloat16),
                pltpu.VMEM((2, span, HD), jnp.float32),
            ],
        ),
        out_shape=(
            jax.ShapeDtypeStruct((tokens, width), jnp.bfloat16),
            jax.ShapeDtypeStruct((tokens, KVH * cols), jnp.bfloat16),
            jax.ShapeDtypeStruct((2, tokens, KVH * HD), jnp.float32),
            jax.ShapeDtypeStruct((2, tokens, KVH * HD), jnp.bfloat16),
        ),
        compiler_params=params(56),
        cost_estimate=pl.CostEstimate(
            flops=2 * tokens * width * KVH * cols, bytes_accessed=22 * MIB, transcendentals=0
        ),
        name="tail_attention",
    )(place_info, back, place, moe_grad, *pieces, low, turned, query, keys, values)


def finish_kernel(kept_ref, later_ref, key_ref, value_ref):
    for kind, out_ref in enumerate((key_ref, value_ref)):
        out_ref[...] = kept_ref[kind] + later_ref[kind].astype(jnp.float32)


def finish(kept, later):
    out = jax.ShapeDtypeStruct(kept.shape[1:], jnp.float32)
    return pl.pallas_call(
        finish_kernel, out_shape=(out, out), compiler_params=params(16), cost_estimate=LIGHT, name="finish"
    )(kept, later)


def local(
    moe_input,
    moe_grad,
    routes,
    route_weight,
    w_gate,
    w_up,
    w_down,
    w_out,
    queries,
    key_heads,
    value_heads,
    segments,
):
    chips = ("far", "near", "low")
    blk = chips + ("core",)
    low = lax.axis_size("low")
    owners = 4 * low
    count = 2 * owners
    parts = lax.axis_size("groups")
    tokens, width = moe_input.shape
    depth = 2 * max(1, 3 * tokens * routes.shape[1] // (2 * count))
    swap = [(0, 1), (1, 0)]
    onward = [(i, i + 1) for i in range(count - 1)]
    backward = [(i + 1, i) for i in range(count - 1)]

    share_cols = w_out.shape[1] // parts
    w_share = lax.dynamic_slice_in_dim(w_out, lax.axis_index("groups") * share_cols, share_cols, 1)
    w_far = lax.ppermute(w_share, "far", swap)
    w_near = lax.ppermute(w_share, "near", swap)

    rows, place = pick(routes, route_weight, moe_input, moe_grad, owners, depth)
    line = lambda w: lax.all_gather(w, "low", axis=0, tiled=False)
    cross = lambda w: lax.ppermute(w, "groups", swap)
    other_core = lambda w: lax.ppermute(w, "core", swap)
    own = (w_gate, w_up, w_down)
    other = tuple(other_core(w) for w in own)

    key_heads, value_heads, segments, place = lax.optimization_barrier((key_heads, value_heads, segments, place))
    kv = jnp.concatenate([key_heads, value_heads], axis=1)
    segs = (segments + 1).astype(jnp.float32)
    seg_rows = jnp.zeros((16, kv.shape[1]), jnp.bfloat16).at[0, :tokens].set(segs.astype(jnp.bfloat16))
    prev = lax.ppermute(jnp.concatenate([kv, seg_rows], axis=0), blk, onward)
    own_line = line(w_share)
    rows, w_near, w_far, own_line, prev = lax.optimization_barrier((rows, w_near, w_far, own_line, prev))

    rows_in = lax.all_to_all(rows.reshape(owners, depth, 2 * width), chips, 0, 0, tiled=True)
    near_crossed, far_crossed = cross(w_near), cross(w_far)
    near_twin = line(jnp.stack([w_near, near_crossed]))
    far_twin = line(jnp.stack([w_far, far_crossed]))
    own_line, near_crossed, far_crossed = lax.optimization_barrier((own_line, near_crossed, far_crossed))
    own_crossed = cross(own_line)
    w_last = lax.ppermute(w_far, "near", swap)
    prepared = prepare_weights(own, other)
    attention = attention_shares(queries, key_heads, value_heads, prev, segs)
    w_last, prepared, attention = lax.optimization_barrier((w_last, prepared, attention))
    rows_in, prepared, attention, own_line, own_crossed = lax.optimization_barrier(
        (rows_in, prepared, attention, own_line, own_crossed)
    )
    if low == 2:
        moved = lax.ppermute(w_last, "low", swap)
        first = lax.axis_index("low") == 0
        last_line = jnp.where(first, jnp.stack([w_last, moved]), jnp.stack([moved, w_last]))
    else:
        last_line = line(w_last)
    terms = experts(rows_in.reshape(owners * depth, 2 * width), *prepared)
    terms, own_line, own_crossed, last_line, near_twin = lax.optimization_barrier(
        (terms, own_line, own_crossed, last_line, near_twin)
    )
    last_crossed, far_twin = lax.optimization_barrier((cross(last_line), far_twin))
    back = lax.all_to_all(terms.reshape(owners, depth, width), chips, 0, 0, tiled=True)
    both = lambda *pieces: [w for piece in pieces for w in (piece, other_core(piece))]

    z = 2 * lax.axis_index("far") + lax.axis_index("near")
    moe_input_grad, query_grad, kept, sent = tail(
        jnp.stack([lax.axis_index("groups"), z, lax.axis_index("core")]).astype(jnp.int32),
        back.reshape(owners * depth, width), place, moe_grad,
        both(own_line, own_crossed, last_line, last_crossed, near_twin, far_twin), *attention,
    )
    return (moe_input_grad, query_grad, *finish(kept, lax.ppermute(sent, blk, backward)))


def solution(mesh):
    names = ("groups", "far", "near", "low", "core")
    shape = (mesh.shape["groups"], 2, 2, mesh.shape["blk"] // 8, 2)
    fine = jax.sharding.Mesh(mesh.devices.reshape(shape), names)
    blk = names[1:]
    by_tokens = P(names, None)
    return jax.shard_map(
        local,
        mesh=fine,
        in_specs=(
            by_tokens,
            by_tokens,
            by_tokens,
            by_tokens,
            P(None, blk),
            P(None, blk),
            P(blk, None),
            P(blk, None),
            by_tokens,
            by_tokens,
            by_tokens,
            P(names),
        ),
        out_specs=(by_tokens,) * 4,
        check_vma=False,
    )
```

```python
import functools

import jax
import jax.numpy as jnp
from jax import lax
from jax.experimental import pallas as pl
from jax.experimental.pallas import tpu as pltpu
from jax.sharding import PartitionSpec as P

KVH = 2
GROUP = 16
HD = 128
FLOOR = -1e30
MIB = 1 << 20
LIGHT = pl.CostEstimate(flops=0, bytes_accessed=0, transcendentals=0)

NT = (((1,), (1,)), ((), ()))
TN = (((0,), (0,)), ((), ()))


def dot(a, b, dims=(((1,), (0,)), ((), ()))):
    return lax.dot_general(a, b, dims, preferred_element_type=jnp.float32)


def params(mib):
    return pltpu.CompilerParams(vmem_limit_bytes=mib * MIB)


def pick_kernel(owners, depth, routes_ref, weight_ref, input_ref, grad_ref, rows_ref, back_ref):
    tokens = input_ref.shape[0]
    slots = owners * depth
    first = routes_ref[0:1, :]
    second = routes_ref[1:2, :]
    expert = lax.broadcasted_iota(jnp.int32, (owners, tokens), 0)
    is_first = first == expert
    is_second = second == expert
    member = jnp.where(is_first | is_second, 1.0, 0.0)
    before = lax.broadcasted_iota(jnp.int32, (tokens, tokens), 0) < lax.broadcasted_iota(
        jnp.int32, (tokens, tokens), 1
    )
    rank = dot(member.astype(jnp.bfloat16), jnp.where(before, 1.0, 0.0).astype(jnp.bfloat16))
    spot = (expert * depth).astype(jnp.float32) + rank
    slot_first = jnp.sum(jnp.where(is_first, spot, 0.0), axis=0, keepdims=True).astype(jnp.int32)
    slot_second = jnp.sum(jnp.where(is_second, spot, 0.0), axis=0, keepdims=True).astype(jnp.int32)
    slot = lax.broadcasted_iota(jnp.int32, (slots, tokens), 0)
    at_first = slot == slot_first
    at_second = slot == slot_second
    place = jnp.where(at_first | at_second, 1.0, 0.0).astype(jnp.bfloat16)
    back_ref[...] = place.T
    scale = jnp.sum(
        jnp.where(at_first, weight_ref[0:1, :], 0.0) + jnp.where(at_second, weight_ref[1:2, :], 0.0),
        axis=1,
        keepdims=True,
    )
    width = input_ref.shape[1]
    rows_ref[:, :width] = dot(place, input_ref[...]).astype(jnp.bfloat16)
    rows_ref[:, width:] = (scale * dot(place, grad_ref[...])).astype(jnp.bfloat16)


def pick(routes, route_weight, moe_input, moe_grad, owners, depth):
    tokens, width = moe_input.shape
    slots = owners * depth
    return pl.pallas_call(
        functools.partial(pick_kernel, owners, depth),
        out_shape=(
            jax.ShapeDtypeStruct((slots, 2 * width), jnp.bfloat16),
            jax.ShapeDtypeStruct((tokens, slots), jnp.bfloat16),
        ),
        compiler_params=params(32),
        cost_estimate=pl.CostEstimate(
            flops=4 * slots * tokens * width, bytes_accessed=8 * MIB, transcendentals=0
        ),
        name="pick_rows",
    )(routes.T, route_weight.T, moe_input, moe_grad)


def weights_kernel(*refs):
    own, other, (cols_ref, down_ref, rows_ref) = refs[:3], refs[3:6], refs[6:]
    tile = own[0].shape[1]
    for place, (gate_ref, up_ref, low_ref) in enumerate((own, other)):
        for kind, ref in enumerate((gate_ref, up_ref)):
            spot = slice((2 * kind + place) * tile, (2 * kind + place + 1) * tile)
            cols_ref[0, :, spot] = ref[...]
            rows_ref[0, spot, :] = ref[...].T
        down_ref[0, :, place * tile : (place + 1) * tile] = low_ref[...].T


def prepare_weights(own, other):
    width, half = own[0].shape
    tile = 128
    steps = half // tile
    cols = pl.BlockSpec((width, tile), lambda i: (0, i))
    down = pl.BlockSpec((tile, width), lambda i: (i, 0))
    return pl.pallas_call(
        weights_kernel,
        grid=(steps,),
        in_specs=[cols, cols, down] * 2,
        out_specs=[
            pl.BlockSpec((1, width, 4 * tile), lambda i: (i, 0, 0)),
            pl.BlockSpec((1, width, 2 * tile), lambda i: (i, 0, 0)),
            pl.BlockSpec((1, 4 * tile, width), lambda i: (i, 0, 0)),
        ],
        out_shape=(
            jax.ShapeDtypeStruct((steps, width, 4 * tile), jnp.bfloat16),
            jax.ShapeDtypeStruct((steps, width, 2 * tile), jnp.bfloat16),
            jax.ShapeDtypeStruct((steps, 4 * tile, width), jnp.bfloat16),
        ),
        compiler_params=params(48),
        cost_estimate=LIGHT,
        name="prepare_weights",
    )(*own, *other)


def expert_kernel(steps, rows_ref, cols_ref, down_ref, back_ref, out_ref, hidden):
    step = pl.program_id(0)
    width = rows_ref.shape[1] // 2
    pair = down_ref.shape[2]

    @pl.when(step < steps)
    def _():
        both_pre = dot(rows_ref[:, :width], cols_ref[0])
        gate_pre = both_pre[:, :pair]
        up_pre = both_pre[:, pair:]
        down_grad = dot(rows_ref[:, width:], down_ref[0])
        sig = jax.nn.sigmoid(gate_pre)
        hidden[step, :, :pair] = (
            down_grad * up_pre * sig * (1.0 + gate_pre * (1.0 - sig))
        ).astype(jnp.bfloat16)
        hidden[step, :, pair:] = (down_grad * gate_pre * sig).astype(jnp.bfloat16)

    @pl.when(step >= steps)
    def _():
        total = dot(hidden[0], back_ref[0])
        for i in range(1, steps):
            total += dot(hidden[i], back_ref[i])
        out_ref[...] = total.astype(jnp.bfloat16)


def experts(rows, cols, down, back):
    count, twice = rows.shape
    steps, width, quad = cols.shape
    tile = 512
    last = steps - 1
    turn = lambda i: jnp.maximum(i - steps, 0)
    return pl.pallas_call(
        functools.partial(expert_kernel, steps),
        grid=(steps + width // tile,),
        in_specs=[
            pl.BlockSpec((count, twice), lambda i: (0, 0)),
            pl.BlockSpec((1, width, quad), lambda i: (jnp.minimum(i, last), 0, 0)),
            pl.BlockSpec((1, width, quad // 2), lambda i: (jnp.minimum(i, last), 0, 0)),
            pl.BlockSpec((steps, quad, tile), lambda i: (0, 0, turn(i))),
        ],
        out_specs=pl.BlockSpec((count, tile), lambda i: (0, turn(i))),
        out_shape=jax.ShapeDtypeStruct((count, width), jnp.bfloat16),
        scratch_shapes=[pltpu.VMEM((steps, count, quad), jnp.bfloat16)],
        compiler_params=params(48),
        cost_estimate=LIGHT,
        name="expert_terms",
    )(rows, cols, down, back)


def shares_kernel(
    q_ref, key_ref, value_ref, prev_key_ref, prev_value_ref, prev_seg_ref, seg_row_ref, seg_col_ref,
    low_ref, turned_ref, query_ref, key_out, value_out,
):
    tokens = q_ref.shape[0]
    seg_col = seg_col_ref[...]
    row = lax.broadcasted_iota(jnp.int32, (tokens, tokens), 0)
    col = lax.broadcasted_iota(jnp.int32, (tokens, tokens), 1)
    own_seen = jnp.where((col <= row) & (seg_row_ref[...] == seg_col), 1.0, 0.0)
    prev_seg = prev_seg_ref[tokens : tokens + 16, :].astype(jnp.float32)[0:1, :]
    prev_seen = jnp.where(prev_seg == seg_col, 1.0, 0.0)
    seen = jnp.concatenate([prev_seen, own_seen], axis=1) > 0.5
    keys = jnp.concatenate([prev_key_ref[:tokens, :], key_ref[...]], axis=0)
    values = jnp.concatenate([prev_value_ref[:tokens, :], value_ref[...]], axis=0)
    key_out[0] = keys
    value_out[0] = values.T
    for head in range(GROUP):
        rows = slice(head * tokens, (head + 1) * tokens)
        query = q_ref[:, head * HD : (head + 1) * HD]
        scores = dot(query, keys, NT) * (HD**-0.5)
        masked = jnp.where(seen, scores, FLOOR)
        raised = jnp.where(seen, jnp.exp(masked - jnp.max(masked, axis=1, keepdims=True)), 0.0)
        shares = raised / jnp.sum(raised, axis=1, keepdims=True)
        low = shares.astype(jnp.bfloat16)
        low_ref[0, rows, :] = low
        turned_ref[0, :, rows] = low.T
        query_ref[0, rows, :] = query


def attention_shares(queries, key_heads, value_heads, prev, segs):
    tokens, width = queries.shape
    span = 2 * tokens
    stack = GROUP * tokens
    high = prev.shape[0]
    own = pl.BlockSpec((tokens, HD), lambda g: (0, g))
    group = lambda shape: pl.BlockSpec((1,) + shape, lambda g: (g, 0, 0))
    made = lambda shape: jax.ShapeDtypeStruct((KVH,) + shape, jnp.bfloat16)
    shapes = ((stack, span), (span, stack), (stack, HD), (span, HD), (HD, span))
    return pl.pallas_call(
        shares_kernel,
        grid=(KVH,),
        in_specs=[
            pl.BlockSpec((tokens, GROUP * HD), lambda g: (0, g)),
            own,
            own,
            pl.BlockSpec((high, HD), lambda g: (0, g)),
            pl.BlockSpec((high, HD), lambda g: (0, KVH + g)),
            pl.BlockSpec((high, HD), lambda g: (0, 0)),
            pl.BlockSpec((1, tokens), lambda g: (0, 0)),
            pl.BlockSpec((tokens, 1), lambda g: (0, 0)),
        ],
        out_specs=[group(shape) for shape in shapes],
        out_shape=[made(shape) for shape in shapes],
        compiler_params=params(32),
        cost_estimate=LIGHT,
        name="attention_shares",
    )(queries, key_heads, value_heads, prev, prev, prev, segs[None, :], segs[:, None])


def tail_kernel(
    plan, place_info, back_ref, place_ref, grad_ref, *refs
):
    heads, tiles = plan
    own, last, twin, refs = refs[:4], refs[4:8], refs[8:12], refs[12:]
    low_ref, turned_ref, q_ref, key_ref, value_ref, *refs = refs
    moe_ref, query_out, kept_out, sent_out, by_place, stream, held, sums = refs
    step = pl.program_id(0)
    tokens = query_out.shape[0]
    part_size = by_place.shape[2]
    size = own[0].shape[1]
    mine, across = own[:2] + twin + last[:2], own[2:] + twin + last[2:]
    spread = part_size // size
    here, core = place_info[1], place_info[2]

    @pl.when(step == 0)
    def _():
        moe = dot(place_ref[...], back_ref[...]).astype(jnp.bfloat16)
        moe_ref[...] = moe
        added = (grad_ref[...].astype(jnp.float32) + moe.astype(jnp.float32)).astype(jnp.bfloat16)
        for z in range(4):
            for rest in range(spread):
                for side in range(2):
                    source = ((z * spread + rest) * 2 + side) * size
                    by_place[2 * z + side, :, rest * size : (rest + 1) * size] = added[:, source : source + size]
        for i in range(8):
            spot = slice(i * part_size, (i + 1) * part_size)
            stream[:, spot] = by_place[2 * (here ^ (i // 2)) + (core ^ (i % 2))]

    @pl.when((step > 0) & ((step - 1) % tiles == 0))
    def _():
        sums[...] = jnp.zeros_like(sums)

    def project(pieces):
        columns = jnp.concatenate([piece[...].reshape(part_size, piece.shape[-1]) for piece in pieces], axis=0)
        return dot(stream[...], columns).astype(jnp.bfloat16)

    def hold(head_grad):
        for head in range(heads):
            held[head * tokens : (head + 1) * tokens, :] = head_grad[:, head * HD : (head + 1) * HD]

    def attend():
        grads = held[...]
        low = low_ref[0].astype(jnp.float32)
        prob_grad = dot(grads, value_ref[0])
        row_dot = jnp.sum(low * prob_grad, axis=1, keepdims=True)
        score_grad = (low * (prob_grad - row_dot) * (HD**-0.5)).astype(jnp.bfloat16)
        query_grad = dot(score_grad, key_ref[0]).astype(jnp.bfloat16)
        sums[0] += dot(score_grad, q_ref[0], TN)
        sums[1] += dot(turned_ref[0], grads)
        for head in range(heads):
            query_out[:, head * HD : (head + 1) * HD] = query_grad[head * tokens : (head + 1) * tokens, :]

    @pl.when(step == 0)
    def _():
        hold(project(mine))

    @pl.when((step > 0) & (step < tiles))
    def _():
        head_grad = project(mine)
        attend()
        hold(head_grad)

    @pl.when((step >= tiles) & (step < 2 * tiles))
    def _():
        head_grad = project(across)
        attend()
        hold(head_grad)

    @pl.when(step == 2 * tiles)
    def _():
        attend()

    @pl.when((step > 0) & (step % tiles == 0))
    def _():
        kept_out[...] = sums[:, tokens:, :]
        sent_out[...] = sums[:, :tokens, :].astype(jnp.bfloat16)


def tail(place_info, back, place, moe_grad, pieces, low, turned, query, keys, values):
    tokens, width = moe_grad.shape
    spread, size, cols = pieces[0].shape
    span = keys.shape[1]
    heads = 4
    tile = heads * HD
    tiles = cols // tile
    steps = KVH * tiles
    was = lambda i: jnp.maximum(i - 1, 0)
    kv_group = lambda i, info: (was(i) // tiles) ^ info[0]
    whole = lambda shape: pl.BlockSpec(shape, lambda i, info: (0,) * len(shape))
    group = lambda shape: pl.BlockSpec((1,) + shape, lambda i, info: (kv_group(i, info), 0, 0))
    rows = lambda shape: pl.BlockSpec((1,) + shape, lambda i, info: (kv_group(i, info), was(i) % tiles, 0))
    own_tile = lambda i: jnp.minimum(i, tiles - 1)
    other_tile = lambda i: jnp.minimum(jnp.maximum(i - tiles, 0), tiles - 1)
    now = lambda i: jnp.minimum(i, steps - 1)
    twin = pl.BlockSpec((spread, 1, size, tile), lambda i, info: (0, now(i) // tiles, 0, now(i) % tiles))
    piece = lambda turn: pl.BlockSpec((spread, size, tile), lambda i, info: (0, 0, turn(i)))
    kv = pl.BlockSpec((2, tokens, HD), lambda i, info: (0, 0, kv_group(i, info)))
    return pl.pallas_call(
        functools.partial(tail_kernel, (heads, tiles)),
        grid_spec=pltpu.PrefetchScalarGridSpec(
            num_scalar_prefetch=1,
            grid=(steps + 1,),
            in_specs=[whole(back.shape), whole(place.shape), whole(moe_grad.shape)]
            + ([piece(own_tile)] * 2 + [piece(other_tile)] * 2) * 2
            + [twin] * 4
            + [
                rows((heads * tokens, span)),
                pl.BlockSpec(
                    (1, span, heads * tokens), lambda i, info: (kv_group(i, info), 0, was(i) % tiles)
                ),
                rows((heads * tokens, HD)),
                group((span, HD)),
                group((HD, span)),
            ],
            out_specs=[
                whole((tokens, width)),
                pl.BlockSpec(
                    (tokens, tile), lambda i, info: (0, kv_group(i, info) * tiles + was(i) % tiles)
                ),
                kv,
                kv,
            ],
            scratch_shapes=[
                pltpu.VMEM((8, tokens, spread * size), jnp.bfloat16),
                pltpu.VMEM((tokens, width), jnp.bfloat16),
                pltpu.VMEM((heads * tokens, HD), jnp.bfloat16),
                pltpu.VMEM((2, span, HD), jnp.float32),
            ],
        ),
        out_shape=(
            jax.ShapeDtypeStruct((tokens, width), jnp.bfloat16),
            jax.ShapeDtypeStruct((tokens, KVH * cols), jnp.bfloat16),
            jax.ShapeDtypeStruct((2, tokens, KVH * HD), jnp.float32),
            jax.ShapeDtypeStruct((2, tokens, KVH * HD), jnp.bfloat16),
        ),
        compiler_params=params(56),
        cost_estimate=pl.CostEstimate(
            flops=2 * tokens * width * KVH * cols, bytes_accessed=22 * MIB, transcendentals=0
        ),
        name="tail_attention",
    )(place_info, back, place, moe_grad, *pieces, low, turned, query, keys, values)


def finish_kernel(kept_ref, later_ref, key_ref, value_ref):
    for kind, out_ref in enumerate((key_ref, value_ref)):
        out_ref[...] = kept_ref[kind] + later_ref[kind].astype(jnp.float32)


def finish(kept, later):
    out = jax.ShapeDtypeStruct(kept.shape[1:], jnp.float32)
    return pl.pallas_call(
        finish_kernel, out_shape=(out, out), compiler_params=params(16), cost_estimate=LIGHT, name="finish"
    )(kept, later)


def local(
    moe_input,
    moe_grad,
    routes,
    route_weight,
    w_gate,
    w_up,
    w_down,
    w_out,
    queries,
    key_heads,
    value_heads,
    segments,
):
    chips = ("far", "near", "low")
    blk = chips + ("core",)
    low = lax.axis_size("low")
    owners = 4 * low
    count = 2 * owners
    parts = lax.axis_size("groups")
    tokens, width = moe_input.shape
    depth = 2 * max(1, 3 * tokens * routes.shape[1] // (2 * count))
    swap = [(0, 1), (1, 0)]
    onward = [(i, i + 1) for i in range(count - 1)]
    backward = [(i + 1, i) for i in range(count - 1)]

    share_cols = w_out.shape[1] // parts
    w_share = lax.dynamic_slice_in_dim(w_out, lax.axis_index("groups") * share_cols, share_cols, 1)
    w_far = lax.ppermute(w_share, "far", swap)
    w_near = lax.ppermute(w_share, "near", swap)

    rows, place = pick(routes, route_weight, moe_input, moe_grad, owners, depth)
    line = lambda w: lax.all_gather(w, "low", axis=0, tiled=False)
    cross = lambda w: lax.ppermute(w, "groups", swap)
    other_core = lambda w: lax.ppermute(w, "core", swap)
    own = (w_gate, w_up, w_down)
    other = tuple(other_core(w) for w in own)

    key_heads, value_heads, segments, place = lax.optimization_barrier((key_heads, value_heads, segments, place))
    kv = jnp.concatenate([key_heads, value_heads], axis=1)
    segs = (segments + 1).astype(jnp.float32)
    seg_rows = jnp.zeros((16, kv.shape[1]), jnp.bfloat16).at[0, :tokens].set(segs.astype(jnp.bfloat16))
    prev = lax.ppermute(jnp.concatenate([kv, seg_rows], axis=0), blk, onward)
    own_line = line(w_share)
    rows, w_near, w_far, own_line, prev = lax.optimization_barrier((rows, w_near, w_far, own_line, prev))

    rows_in = lax.all_to_all(rows.reshape(owners, depth, 2 * width), chips, 0, 0, tiled=True)
    near_crossed, far_crossed = cross(w_near), cross(w_far)
    near_twin = line(jnp.stack([w_near, near_crossed]))
    far_twin = line(jnp.stack([w_far, far_crossed]))
    own_line, near_crossed, far_crossed = lax.optimization_barrier((own_line, near_crossed, far_crossed))
    own_crossed = cross(own_line)
    w_last = lax.ppermute(w_far, "near", swap)
    prepared = prepare_weights(own, other)
    attention = attention_shares(queries, key_heads, value_heads, prev, segs)
    w_last, prepared, attention = lax.optimization_barrier((w_last, prepared, attention))
    rows_in, prepared, attention, own_line, own_crossed = lax.optimization_barrier(
        (rows_in, prepared, attention, own_line, own_crossed)
    )
    moved = lax.ppermute(w_last, "low", swap) if low == 2 else line(w_last)
    terms = experts(rows_in.reshape(owners * depth, 2 * width), *prepared)
    terms, own_line, own_crossed, w_last, moved, near_twin = lax.optimization_barrier(
        (terms, own_line, own_crossed, w_last, moved, near_twin)
    )
    last_line = moved
    if low == 2:
        first = lax.axis_index("low") == 0
        last_line = jnp.where(first, jnp.stack([w_last, moved]), jnp.stack([moved, w_last]))
    last_crossed, far_twin = lax.optimization_barrier((cross(last_line), far_twin))
    back = lax.all_to_all(terms.reshape(owners, depth, width), chips, 0, 0, tiled=True)
    both = lambda *pieces: [w for piece in pieces for w in (piece, other_core(piece))]

    z = 2 * lax.axis_index("far") + lax.axis_index("near")
    moe_input_grad, query_grad, kept, sent = tail(
        jnp.stack([lax.axis_index("groups"), z, lax.axis_index("core")]).astype(jnp.int32),
        back.reshape(owners * depth, width), place, moe_grad,
        both(own_line, own_crossed, last_line, last_crossed, near_twin, far_twin), *attention,
    )
    return (moe_input_grad, query_grad, *finish(kept, lax.ppermute(sent, blk, backward)))


def solution(mesh):
    names = ("groups", "far", "near", "low", "core")
    shape = (mesh.shape["groups"], 2, 2, mesh.shape["blk"] // 8, 2)
    fine = jax.sharding.Mesh(mesh.devices.reshape(shape), names)
    blk = names[1:]
    by_tokens = P(names, None)
    return jax.shard_map(
        local,
        mesh=fine,
        in_specs=(
            by_tokens,
            by_tokens,
            by_tokens,
            by_tokens,
            P(None, blk),
            P(None, blk),
            P(blk, None),
            P(blk, None),
            by_tokens,
            by_tokens,
            by_tokens,
            P(names),
        ),
        out_specs=(by_tokens,) * 4,
        check_vma=False,
    )
```

```python
import functools

import jax
import jax.numpy as jnp
from jax import lax
from jax.experimental import pallas as pl
from jax.experimental.pallas import tpu as pltpu
from jax.sharding import PartitionSpec as P

KVH = 2
GROUP = 16
HD = 128
FLOOR = -1e30
MIB = 1 << 20
LIGHT = pl.CostEstimate(flops=0, bytes_accessed=0, transcendentals=0)

NT = (((1,), (1,)), ((), ()))
TN = (((0,), (0,)), ((), ()))


def dot(a, b, dims=(((1,), (0,)), ((), ()))):
    return lax.dot_general(a, b, dims, preferred_element_type=jnp.float32)


def params(mib):
    return pltpu.CompilerParams(vmem_limit_bytes=mib * MIB)


def pick_kernel(owners, depth, routes_ref, weight_ref, input_ref, grad_ref, rows_ref, back_ref):
    tokens = input_ref.shape[0]
    slots = owners * depth
    first = routes_ref[0:1, :]
    second = routes_ref[1:2, :]
    expert = lax.broadcasted_iota(jnp.int32, (owners, tokens), 0)
    is_first = first == expert
    is_second = second == expert
    member = jnp.where(is_first | is_second, 1.0, 0.0)
    before = lax.broadcasted_iota(jnp.int32, (tokens, tokens), 0) < lax.broadcasted_iota(
        jnp.int32, (tokens, tokens), 1
    )
    rank = dot(member.astype(jnp.bfloat16), jnp.where(before, 1.0, 0.0).astype(jnp.bfloat16))
    spot = (expert * depth).astype(jnp.float32) + rank
    slot_first = jnp.sum(jnp.where(is_first, spot, 0.0), axis=0, keepdims=True).astype(jnp.int32)
    slot_second = jnp.sum(jnp.where(is_second, spot, 0.0), axis=0, keepdims=True).astype(jnp.int32)
    slot = lax.broadcasted_iota(jnp.int32, (slots, tokens), 0)
    at_first = slot == slot_first
    at_second = slot == slot_second
    place = jnp.where(at_first | at_second, 1.0, 0.0).astype(jnp.bfloat16)
    back_ref[...] = place.T
    scale = jnp.sum(
        jnp.where(at_first, weight_ref[0:1, :], 0.0) + jnp.where(at_second, weight_ref[1:2, :], 0.0),
        axis=1,
        keepdims=True,
    )
    width = input_ref.shape[1]
    rows_ref[:, :width] = dot(place, input_ref[...]).astype(jnp.bfloat16)
    rows_ref[:, width:] = (scale * dot(place, grad_ref[...])).astype(jnp.bfloat16)


def pick(routes, route_weight, moe_input, moe_grad, owners, depth):
    tokens, width = moe_input.shape
    slots = owners * depth
    return pl.pallas_call(
        functools.partial(pick_kernel, owners, depth),
        out_shape=(
            jax.ShapeDtypeStruct((slots, 2 * width), jnp.bfloat16),
            jax.ShapeDtypeStruct((tokens, slots), jnp.bfloat16),
        ),
        compiler_params=params(32),
        cost_estimate=pl.CostEstimate(
            flops=4 * slots * tokens * width, bytes_accessed=8 * MIB, transcendentals=0
        ),
        name="pick_rows",
    )(routes.T, route_weight.T, moe_input, moe_grad)


def weights_kernel(*refs):
    own, other, (cols_ref, down_ref, rows_ref) = refs[:3], refs[3:6], refs[6:]
    tile = own[0].shape[1]
    for place, (gate_ref, up_ref, low_ref) in enumerate((own, other)):
        for kind, ref in enumerate((gate_ref, up_ref)):
            spot = slice((2 * kind + place) * tile, (2 * kind + place + 1) * tile)
            cols_ref[0, :, spot] = ref[...]
            rows_ref[0, spot, :] = ref[...].T
        down_ref[0, :, place * tile : (place + 1) * tile] = low_ref[...].T


def prepare_weights(own, other):
    width, half = own[0].shape
    tile = 128
    steps = half // tile
    cols = pl.BlockSpec((width, tile), lambda i: (0, i))
    down = pl.BlockSpec((tile, width), lambda i: (i, 0))
    return pl.pallas_call(
        weights_kernel,
        grid=(steps,),
        in_specs=[cols, cols, down] * 2,
        out_specs=[
            pl.BlockSpec((1, width, 4 * tile), lambda i: (i, 0, 0)),
            pl.BlockSpec((1, width, 2 * tile), lambda i: (i, 0, 0)),
            pl.BlockSpec((1, 4 * tile, width), lambda i: (i, 0, 0)),
        ],
        out_shape=(
            jax.ShapeDtypeStruct((steps, width, 4 * tile), jnp.bfloat16),
            jax.ShapeDtypeStruct((steps, width, 2 * tile), jnp.bfloat16),
            jax.ShapeDtypeStruct((steps, 4 * tile, width), jnp.bfloat16),
        ),
        compiler_params=params(48),
        cost_estimate=LIGHT,
        name="prepare_weights",
    )(*own, *other)


def expert_kernel(steps, rows_ref, cols_ref, down_ref, back_ref, out_ref, hidden):
    step = pl.program_id(0)
    width = rows_ref.shape[1] // 2
    pair = down_ref.shape[2]

    @pl.when(step < steps)
    def _():
        both_pre = dot(rows_ref[:, :width], cols_ref[0])
        gate_pre = both_pre[:, :pair]
        up_pre = both_pre[:, pair:]
        down_grad = dot(rows_ref[:, width:], down_ref[0])
        sig = jax.nn.sigmoid(gate_pre)
        hidden[step, :, :pair] = (
            down_grad * up_pre * sig * (1.0 + gate_pre * (1.0 - sig))
        ).astype(jnp.bfloat16)
        hidden[step, :, pair:] = (down_grad * gate_pre * sig).astype(jnp.bfloat16)

    @pl.when(step >= steps)
    def _():
        total = dot(hidden[0], back_ref[0])
        for i in range(1, steps):
            total += dot(hidden[i], back_ref[i])
        out_ref[...] = total.astype(jnp.bfloat16)


def experts(rows, cols, down, back):
    count, twice = rows.shape
    steps, width, quad = cols.shape
    tile = 512
    last = steps - 1
    turn = lambda i: jnp.maximum(i - steps, 0)
    return pl.pallas_call(
        functools.partial(expert_kernel, steps),
        grid=(steps + width // tile,),
        in_specs=[
            pl.BlockSpec((count, twice), lambda i: (0, 0)),
            pl.BlockSpec((1, width, quad), lambda i: (jnp.minimum(i, last), 0, 0)),
            pl.BlockSpec((1, width, quad // 2), lambda i: (jnp.minimum(i, last), 0, 0)),
            pl.BlockSpec((steps, quad, tile), lambda i: (0, 0, turn(i))),
        ],
        out_specs=pl.BlockSpec((count, tile), lambda i: (0, turn(i))),
        out_shape=jax.ShapeDtypeStruct((count, width), jnp.bfloat16),
        scratch_shapes=[pltpu.VMEM((steps, count, quad), jnp.bfloat16)],
        compiler_params=params(48),
        cost_estimate=LIGHT,
        name="expert_terms",
    )(rows, cols, down, back)


def shares_kernel(
    q_ref, key_ref, value_ref, prev_key_ref, prev_value_ref, prev_seg_ref, seg_row_ref, seg_col_ref,
    low_ref, turned_ref, query_ref, key_out, value_out,
):
    tokens = q_ref.shape[0]
    seg_col = seg_col_ref[...]
    row = lax.broadcasted_iota(jnp.int32, (tokens, tokens), 0)
    col = lax.broadcasted_iota(jnp.int32, (tokens, tokens), 1)
    own_seen = jnp.where((col <= row) & (seg_row_ref[...] == seg_col), 1.0, 0.0)
    prev_seg = prev_seg_ref[tokens : tokens + 16, :].astype(jnp.float32)[0:1, :]
    prev_seen = jnp.where(prev_seg == seg_col, 1.0, 0.0)
    seen = jnp.concatenate([prev_seen, own_seen], axis=1) > 0.5
    keys = jnp.concatenate([prev_key_ref[:tokens, :], key_ref[...]], axis=0)
    values = jnp.concatenate([prev_value_ref[:tokens, :], value_ref[...]], axis=0)
    key_out[0] = keys
    value_out[0] = values.T
    for head in range(GROUP):
        rows = slice(head * tokens, (head + 1) * tokens)
        query = q_ref[:, head * HD : (head + 1) * HD]
        scores = dot(query, keys, NT) * (HD**-0.5)
        masked = jnp.where(seen, scores, FLOOR)
        raised = jnp.where(seen, jnp.exp(masked - jnp.max(masked, axis=1, keepdims=True)), 0.0)
        shares = raised / jnp.sum(raised, axis=1, keepdims=True)
        low = shares.astype(jnp.bfloat16)
        low_ref[0, rows, :] = low
        turned_ref[0, :, rows] = low.T
        query_ref[0, rows, :] = query


def attention_shares(queries, key_heads, value_heads, prev, segs):
    tokens, width = queries.shape
    span = 2 * tokens
    stack = GROUP * tokens
    high = prev.shape[0]
    own = pl.BlockSpec((tokens, HD), lambda g: (0, g))
    group = lambda shape: pl.BlockSpec((1,) + shape, lambda g: (g, 0, 0))
    made = lambda shape: jax.ShapeDtypeStruct((KVH,) + shape, jnp.bfloat16)
    shapes = ((stack, span), (span, stack), (stack, HD), (span, HD), (HD, span))
    return pl.pallas_call(
        shares_kernel,
        grid=(KVH,),
        in_specs=[
            pl.BlockSpec((tokens, GROUP * HD), lambda g: (0, g)),
            own,
            own,
            pl.BlockSpec((high, HD), lambda g: (0, g)),
            pl.BlockSpec((high, HD), lambda g: (0, KVH + g)),
            pl.BlockSpec((high, HD), lambda g: (0, 0)),
            pl.BlockSpec((1, tokens), lambda g: (0, 0)),
            pl.BlockSpec((tokens, 1), lambda g: (0, 0)),
        ],
        out_specs=[group(shape) for shape in shapes],
        out_shape=[made(shape) for shape in shapes],
        compiler_params=params(32),
        cost_estimate=LIGHT,
        name="attention_shares",
    )(queries, key_heads, value_heads, prev, prev, prev, segs[None, :], segs[:, None])


def tail_kernel(
    plan, place_info, back_ref, place_ref, grad_ref, *refs
):
    heads, tiles = plan
    own, last, twin, refs = refs[:4], refs[4:8], refs[8:12], refs[12:]
    low_ref, turned_ref, q_ref, key_ref, value_ref, *refs = refs
    moe_ref, query_out, kept_out, sent_out, by_place, stream, held, sums = refs
    step = pl.program_id(0)
    tokens = query_out.shape[0]
    part_size = by_place.shape[2]
    size = own[0].shape[1]
    mine, across = own[:2] + twin + last[:2], own[2:] + twin + last[2:]
    spread = part_size // size
    here, core = place_info[1], place_info[2]

    @pl.when(step == 0)
    def _():
        moe = dot(place_ref[...], back_ref[...]).astype(jnp.bfloat16)
        moe_ref[...] = moe
        added = (grad_ref[...].astype(jnp.float32) + moe.astype(jnp.float32)).astype(jnp.bfloat16)
        for z in range(4):
            for rest in range(spread):
                for side in range(2):
                    source = ((z * spread + rest) * 2 + side) * size
                    by_place[2 * z + side, :, rest * size : (rest + 1) * size] = added[:, source : source + size]
        for i in range(8):
            spot = slice(i * part_size, (i + 1) * part_size)
            stream[:, spot] = by_place[2 * (here ^ (i // 2)) + (core ^ (i % 2))]

    @pl.when((step > 0) & ((step - 1) % tiles == 0))
    def _():
        sums[...] = jnp.zeros_like(sums)

    def project(pieces):
        columns = jnp.concatenate([piece[...].reshape(part_size, piece.shape[-1]) for piece in pieces], axis=0)
        return dot(stream[...], columns).astype(jnp.bfloat16)

    def hold(head_grad):
        for head in range(heads):
            held[head * tokens : (head + 1) * tokens, :] = head_grad[:, head * HD : (head + 1) * HD]

    def attend():
        grads = held[...]
        low = low_ref[0].astype(jnp.float32)
        prob_grad = dot(grads, value_ref[0])
        row_dot = jnp.sum(low * prob_grad, axis=1, keepdims=True)
        score_grad = (low * (prob_grad - row_dot) * (HD**-0.5)).astype(jnp.bfloat16)
        query_grad = dot(score_grad, key_ref[0]).astype(jnp.bfloat16)
        sums[0] += dot(score_grad, q_ref[0], TN)
        sums[1] += dot(turned_ref[0], grads)
        for head in range(heads):
            query_out[:, head * HD : (head + 1) * HD] = query_grad[head * tokens : (head + 1) * tokens, :]

    @pl.when(step == 0)
    def _():
        hold(project(mine))

    @pl.when((step > 0) & (step < tiles))
    def _():
        head_grad = project(mine)
        attend()
        hold(head_grad)

    @pl.when((step >= tiles) & (step < 2 * tiles))
    def _():
        head_grad = project(across)
        attend()
        hold(head_grad)

    @pl.when(step == 2 * tiles)
    def _():
        attend()

    @pl.when((step > 0) & (step % tiles == 0))
    def _():
        kept_out[...] = sums[:, tokens:, :]
        sent_out[...] = sums[:, :tokens, :].astype(jnp.bfloat16)


def tail(place_info, back, place, moe_grad, pieces, low, turned, query, keys, values):
    tokens, width = moe_grad.shape
    spread, size, cols = pieces[0].shape
    span = keys.shape[1]
    heads = 4
    tile = heads * HD
    tiles = cols // tile
    steps = KVH * tiles
    was = lambda i: jnp.maximum(i - 1, 0)
    kv_group = lambda i, info: (was(i) // tiles) ^ info[0]
    whole = lambda shape: pl.BlockSpec(shape, lambda i, info: (0,) * len(shape))
    group = lambda shape: pl.BlockSpec((1,) + shape, lambda i, info: (kv_group(i, info), 0, 0))
    rows = lambda shape: pl.BlockSpec((1,) + shape, lambda i, info: (kv_group(i, info), was(i) % tiles, 0))
    own_tile = lambda i: jnp.minimum(i, tiles - 1)
    other_tile = lambda i: jnp.minimum(jnp.maximum(i - tiles, 0), tiles - 1)
    now = lambda i: jnp.minimum(i, steps - 1)
    twin = pl.BlockSpec((spread, 1, size, tile), lambda i, info: (0, now(i) // tiles, 0, now(i) % tiles))
    piece = lambda turn: pl.BlockSpec((spread, size, tile), lambda i, info: (0, 0, turn(i)))
    kv = pl.BlockSpec((2, tokens, HD), lambda i, info: (0, 0, kv_group(i, info)))
    return pl.pallas_call(
        functools.partial(tail_kernel, (heads, tiles)),
        grid_spec=pltpu.PrefetchScalarGridSpec(
            num_scalar_prefetch=1,
            grid=(steps + 1,),
            in_specs=[whole(back.shape), whole(place.shape), whole(moe_grad.shape)]
            + ([piece(own_tile)] * 2 + [piece(other_tile)] * 2) * 2
            + [twin] * 4
            + [
                rows((heads * tokens, span)),
                pl.BlockSpec(
                    (1, span, heads * tokens), lambda i, info: (kv_group(i, info), 0, was(i) % tiles)
                ),
                rows((heads * tokens, HD)),
                group((span, HD)),
                group((HD, span)),
            ],
            out_specs=[
                whole((tokens, width)),
                pl.BlockSpec(
                    (tokens, tile), lambda i, info: (0, kv_group(i, info) * tiles + was(i) % tiles)
                ),
                kv,
                kv,
            ],
            scratch_shapes=[
                pltpu.VMEM((8, tokens, spread * size), jnp.bfloat16),
                pltpu.VMEM((tokens, width), jnp.bfloat16),
                pltpu.VMEM((heads * tokens, HD), jnp.bfloat16),
                pltpu.VMEM((2, span, HD), jnp.float32),
            ],
        ),
        out_shape=(
            jax.ShapeDtypeStruct((tokens, width), jnp.bfloat16),
            jax.ShapeDtypeStruct((tokens, KVH * cols), jnp.bfloat16),
            jax.ShapeDtypeStruct((2, tokens, KVH * HD), jnp.float32),
            jax.ShapeDtypeStruct((2, tokens, KVH * HD), jnp.bfloat16),
        ),
        compiler_params=params(56),
        cost_estimate=pl.CostEstimate(
            flops=2 * tokens * width * KVH * cols, bytes_accessed=22 * MIB, transcendentals=0
        ),
        name="tail_attention",
    )(place_info, back, place, moe_grad, *pieces, low, turned, query, keys, values)


def finish_kernel(kept_ref, later_ref, key_ref, value_ref):
    for kind, out_ref in enumerate((key_ref, value_ref)):
        out_ref[...] = kept_ref[kind] + later_ref[kind].astype(jnp.float32)


def finish(kept, later):
    out = jax.ShapeDtypeStruct(kept.shape[1:], jnp.float32)
    return pl.pallas_call(
        finish_kernel, out_shape=(out, out), compiler_params=params(16), cost_estimate=LIGHT, name="finish"
    )(kept, later)


def local(
    moe_input,
    moe_grad,
    routes,
    route_weight,
    w_gate,
    w_up,
    w_down,
    w_out,
    queries,
    key_heads,
    value_heads,
    segments,
):
    chips = ("far", "near", "low")
    blk = chips + ("core",)
    low = lax.axis_size("low")
    owners = 4 * low
    count = 2 * owners
    parts = lax.axis_size("groups")
    tokens, width = moe_input.shape
    depth = 2 * max(1, 3 * tokens * routes.shape[1] // (2 * count))
    swap = [(0, 1), (1, 0)]
    onward = [(i, i + 1) for i in range(count - 1)]
    backward = [(i + 1, i) for i in range(count - 1)]

    share_cols = w_out.shape[1] // parts
    w_share = lax.dynamic_slice_in_dim(w_out, lax.axis_index("groups") * share_cols, share_cols, 1)
    w_far = lax.ppermute(w_share, "far", swap)
    w_near = lax.ppermute(w_share, "near", swap)

    rows, place = pick(routes, route_weight, moe_input, moe_grad, owners, depth)
    line = lambda w: lax.all_gather(w, "low", axis=0, tiled=False)
    cross = lambda w: lax.ppermute(w, "groups", swap)
    other_core = lambda w: lax.ppermute(w, "core", swap)
    own = (w_gate, w_up, w_down)
    other = tuple(other_core(w) for w in own)

    key_heads, value_heads, segments, place = lax.optimization_barrier((key_heads, value_heads, segments, place))
    kv = jnp.concatenate([key_heads, value_heads], axis=1)
    segs = (segments + 1).astype(jnp.float32)
    seg_rows = jnp.zeros((16, kv.shape[1]), jnp.bfloat16).at[0, :tokens].set(segs.astype(jnp.bfloat16))
    prev = lax.ppermute(jnp.concatenate([kv, seg_rows], axis=0), blk, onward)
    own_line = line(w_share)
    rows, w_far, own_line, prev = lax.optimization_barrier((rows, w_far, own_line, prev))

    rows_in = lax.all_to_all(rows.reshape(owners, depth, 2 * width), chips, 0, 0, tiled=True)
    near_crossed, far_crossed = cross(w_near), cross(w_far)
    near_twin = line(jnp.stack([w_near, near_crossed]))
    far_twin = line(jnp.stack([w_far, far_crossed]))
    own_line, near_crossed, far_crossed = lax.optimization_barrier((own_line, near_crossed, far_crossed))
    own_crossed = cross(own_line)
    w_last = lax.ppermute(w_far, "near", swap)
    prepared = prepare_weights(own, other)
    attention = attention_shares(queries, key_heads, value_heads, prev, segs)
    w_last, prepared, attention = lax.optimization_barrier((w_last, prepared, attention))
    rows_in, prepared, attention, own_line, own_crossed = lax.optimization_barrier(
        (rows_in, prepared, attention, own_line, own_crossed)
    )
    moved = lax.ppermute(w_last, "low", swap) if low == 2 else line(w_last)
    terms = experts(rows_in.reshape(owners * depth, 2 * width), *prepared)
    terms, own_line, own_crossed, w_last, moved, near_twin = lax.optimization_barrier(
        (terms, own_line, own_crossed, w_last, moved, near_twin)
    )
    last_line = moved
    if low == 2:
        first = lax.axis_index("low") == 0
        last_line = jnp.where(first, jnp.stack([w_last, moved]), jnp.stack([moved, w_last]))
    last_crossed, far_twin = lax.optimization_barrier((cross(last_line), far_twin))
    back = lax.all_to_all(terms.reshape(owners, depth, width), chips, 0, 0, tiled=True)
    both = lambda *pieces: [w for piece in pieces for w in (piece, other_core(piece))]

    z = 2 * lax.axis_index("far") + lax.axis_index("near")
    moe_input_grad, query_grad, kept, sent = tail(
        jnp.stack([lax.axis_index("groups"), z, lax.axis_index("core")]).astype(jnp.int32),
        back.reshape(owners * depth, width), place, moe_grad,
        both(own_line, own_crossed, last_line, last_crossed, near_twin, far_twin), *attention,
    )
    return (moe_input_grad, query_grad, *finish(kept, lax.ppermute(sent, blk, backward)))


def solution(mesh):
    names = ("groups", "far", "near", "low", "core")
    shape = (mesh.shape["groups"], 2, 2, mesh.shape["blk"] // 8, 2)
    fine = jax.sharding.Mesh(mesh.devices.reshape(shape), names)
    blk = names[1:]
    by_tokens = P(names, None)
    return jax.shard_map(
        local,
        mesh=fine,
        in_specs=(
            by_tokens,
            by_tokens,
            by_tokens,
            by_tokens,
            P(None, blk),
            P(None, blk),
            P(blk, None),
            P(blk, None),
            by_tokens,
            by_tokens,
            by_tokens,
            P(names),
        ),
        out_specs=(by_tokens,) * 4,
        check_vma=False,
    )
```

```python
import functools

import jax
import jax.numpy as jnp
from jax import lax
from jax.experimental import pallas as pl
from jax.experimental.pallas import tpu as pltpu
from jax.sharding import PartitionSpec as P

KVH = 2
GROUP = 16
HD = 128
FLOOR = -1e30
MIB = 1 << 20
LIGHT = pl.CostEstimate(flops=0, bytes_accessed=0, transcendentals=0)

NT = (((1,), (1,)), ((), ()))
TN = (((0,), (0,)), ((), ()))


def dot(a, b, dims=(((1,), (0,)), ((), ()))):
    return lax.dot_general(a, b, dims, preferred_element_type=jnp.float32)


def params(mib):
    return pltpu.CompilerParams(vmem_limit_bytes=mib * MIB)


def pick_kernel(owners, depth, routes_ref, weight_ref, input_ref, grad_ref, rows_ref, back_ref):
    tokens = input_ref.shape[0]
    slots = owners * depth
    first = routes_ref[0:1, :]
    second = routes_ref[1:2, :]
    expert = lax.broadcasted_iota(jnp.int32, (owners, tokens), 0)
    is_first = first == expert
    is_second = second == expert
    member = jnp.where(is_first | is_second, 1.0, 0.0)
    before = lax.broadcasted_iota(jnp.int32, (tokens, tokens), 0) < lax.broadcasted_iota(
        jnp.int32, (tokens, tokens), 1
    )
    rank = dot(member.astype(jnp.bfloat16), jnp.where(before, 1.0, 0.0).astype(jnp.bfloat16))
    spot = (expert * depth).astype(jnp.float32) + rank
    slot_first = jnp.sum(jnp.where(is_first, spot, 0.0), axis=0, keepdims=True).astype(jnp.int32)
    slot_second = jnp.sum(jnp.where(is_second, spot, 0.0), axis=0, keepdims=True).astype(jnp.int32)
    slot = lax.broadcasted_iota(jnp.int32, (slots, tokens), 0)
    at_first = slot == slot_first
    at_second = slot == slot_second
    place = jnp.where(at_first | at_second, 1.0, 0.0).astype(jnp.bfloat16)
    back_ref[...] = place.T
    scale = jnp.sum(
        jnp.where(at_first, weight_ref[0:1, :], 0.0) + jnp.where(at_second, weight_ref[1:2, :], 0.0),
        axis=1,
        keepdims=True,
    )
    width = input_ref.shape[1]
    rows_ref[:, :width] = dot(place, input_ref[...]).astype(jnp.bfloat16)
    rows_ref[:, width:] = (scale * dot(place, grad_ref[...])).astype(jnp.bfloat16)


def pick(routes, route_weight, moe_input, moe_grad, owners, depth):
    tokens, width = moe_input.shape
    slots = owners * depth
    return pl.pallas_call(
        functools.partial(pick_kernel, owners, depth),
        out_shape=(
            jax.ShapeDtypeStruct((slots, 2 * width), jnp.bfloat16),
            jax.ShapeDtypeStruct((tokens, slots), jnp.bfloat16),
        ),
        compiler_params=params(32),
        cost_estimate=pl.CostEstimate(
            flops=4 * slots * tokens * width, bytes_accessed=8 * MIB, transcendentals=0
        ),
        name="pick_rows",
    )(routes.T, route_weight.T, moe_input, moe_grad)


def weights_kernel(*refs):
    own, other, (cols_ref, down_ref, rows_ref) = refs[:3], refs[3:6], refs[6:]
    tile = own[0].shape[1]
    for place, (gate_ref, up_ref, low_ref) in enumerate((own, other)):
        for kind, ref in enumerate((gate_ref, up_ref)):
            spot = slice((2 * kind + place) * tile, (2 * kind + place + 1) * tile)
            cols_ref[0, :, spot] = ref[...]
            rows_ref[0, spot, :] = ref[...].T
        down_ref[0, :, place * tile : (place + 1) * tile] = low_ref[...].T


def prepare_weights(own, other):
    width, half = own[0].shape
    tile = 128
    steps = half // tile
    cols = pl.BlockSpec((width, tile), lambda i: (0, i))
    down = pl.BlockSpec((tile, width), lambda i: (i, 0))
    return pl.pallas_call(
        weights_kernel,
        grid=(steps,),
        in_specs=[cols, cols, down] * 2,
        out_specs=[
            pl.BlockSpec((1, width, 4 * tile), lambda i: (i, 0, 0)),
            pl.BlockSpec((1, width, 2 * tile), lambda i: (i, 0, 0)),
            pl.BlockSpec((1, 4 * tile, width), lambda i: (i, 0, 0)),
        ],
        out_shape=(
            jax.ShapeDtypeStruct((steps, width, 4 * tile), jnp.bfloat16),
            jax.ShapeDtypeStruct((steps, width, 2 * tile), jnp.bfloat16),
            jax.ShapeDtypeStruct((steps, 4 * tile, width), jnp.bfloat16),
        ),
        compiler_params=params(48),
        cost_estimate=LIGHT,
        name="prepare_weights",
    )(*own, *other)


def expert_kernel(steps, rows_ref, cols_ref, down_ref, back_ref, out_ref, hidden):
    step = pl.program_id(0)
    width = rows_ref.shape[1] // 2
    pair = down_ref.shape[2]

    @pl.when(step < steps)
    def _():
        both_pre = dot(rows_ref[:, :width], cols_ref[0])
        gate_pre = both_pre[:, :pair]
        up_pre = both_pre[:, pair:]
        down_grad = dot(rows_ref[:, width:], down_ref[0])
        sig = jax.nn.sigmoid(gate_pre)
        hidden[step, :, :pair] = (
            down_grad * up_pre * sig * (1.0 + gate_pre * (1.0 - sig))
        ).astype(jnp.bfloat16)
        hidden[step, :, pair:] = (down_grad * gate_pre * sig).astype(jnp.bfloat16)

    @pl.when(step >= steps)
    def _():
        total = dot(hidden[0], back_ref[0])
        for i in range(1, steps):
            total += dot(hidden[i], back_ref[i])
        out_ref[...] = total.astype(jnp.bfloat16)


def experts(rows, cols, down, back):
    count, twice = rows.shape
    steps, width, quad = cols.shape
    tile = 512
    last = steps - 1
    turn = lambda i: jnp.maximum(i - steps, 0)
    return pl.pallas_call(
        functools.partial(expert_kernel, steps),
        grid=(steps + width // tile,),
        in_specs=[
            pl.BlockSpec((count, twice), lambda i: (0, 0)),
            pl.BlockSpec((1, width, quad), lambda i: (jnp.minimum(i, last), 0, 0)),
            pl.BlockSpec((1, width, quad // 2), lambda i: (jnp.minimum(i, last), 0, 0)),
            pl.BlockSpec((steps, quad, tile), lambda i: (0, 0, turn(i))),
        ],
        out_specs=pl.BlockSpec((count, tile), lambda i: (0, turn(i))),
        out_shape=jax.ShapeDtypeStruct((count, width), jnp.bfloat16),
        scratch_shapes=[pltpu.VMEM((steps, count, quad), jnp.bfloat16)],
        compiler_params=params(48),
        cost_estimate=LIGHT,
        name="expert_terms",
    )(rows, cols, down, back)


def shares_kernel(
    q_ref, key_ref, value_ref, prev_key_ref, prev_value_ref, prev_seg_ref, seg_row_ref, seg_col_ref,
    low_ref, turned_ref, query_ref, key_out, value_out,
):
    tokens = q_ref.shape[0]
    seg_col = seg_col_ref[...]
    row = lax.broadcasted_iota(jnp.int32, (tokens, tokens), 0)
    col = lax.broadcasted_iota(jnp.int32, (tokens, tokens), 1)
    own_seen = jnp.where((col <= row) & (seg_row_ref[...] == seg_col), 1.0, 0.0)
    prev_seg = prev_seg_ref[tokens : tokens + 16, :].astype(jnp.float32)[0:1, :]
    prev_seen = jnp.where(prev_seg == seg_col, 1.0, 0.0)
    seen = jnp.concatenate([prev_seen, own_seen], axis=1) > 0.5
    keys = jnp.concatenate([prev_key_ref[:tokens, :], key_ref[...]], axis=0)
    values = jnp.concatenate([prev_value_ref[:tokens, :], value_ref[...]], axis=0)
    key_out[0] = keys
    value_out[0] = values.T
    for head in range(GROUP):
        rows = slice(head * tokens, (head + 1) * tokens)
        query = q_ref[:, head * HD : (head + 1) * HD]
        scores = dot(query, keys, NT) * (HD**-0.5)
        masked = jnp.where(seen, scores, FLOOR)
        raised = jnp.where(seen, jnp.exp(masked - jnp.max(masked, axis=1, keepdims=True)), 0.0)
        shares = raised / jnp.sum(raised, axis=1, keepdims=True)
        low = shares.astype(jnp.bfloat16)
        low_ref[0, rows, :] = low
        turned_ref[0, :, rows] = low.T
        query_ref[0, rows, :] = query


def attention_shares(queries, key_heads, value_heads, prev, segs):
    tokens, width = queries.shape
    span = 2 * tokens
    stack = GROUP * tokens
    high = prev.shape[0]
    own = pl.BlockSpec((tokens, HD), lambda g: (0, g))
    group = lambda shape: pl.BlockSpec((1,) + shape, lambda g: (g, 0, 0))
    made = lambda shape: jax.ShapeDtypeStruct((KVH,) + shape, jnp.bfloat16)
    shapes = ((stack, span), (span, stack), (stack, HD), (span, HD), (HD, span))
    return pl.pallas_call(
        shares_kernel,
        grid=(KVH,),
        in_specs=[
            pl.BlockSpec((tokens, GROUP * HD), lambda g: (0, g)),
            own,
            own,
            pl.BlockSpec((high, HD), lambda g: (0, g)),
            pl.BlockSpec((high, HD), lambda g: (0, KVH + g)),
            pl.BlockSpec((high, HD), lambda g: (0, 0)),
            pl.BlockSpec((1, tokens), lambda g: (0, 0)),
            pl.BlockSpec((tokens, 1), lambda g: (0, 0)),
        ],
        out_specs=[group(shape) for shape in shapes],
        out_shape=[made(shape) for shape in shapes],
        compiler_params=params(32),
        cost_estimate=LIGHT,
        name="attention_shares",
    )(queries, key_heads, value_heads, prev, prev, prev, segs[None, :], segs[:, None])


def tail_kernel(
    plan, place_info, back_ref, place_ref, grad_ref, *refs
):
    heads, tiles = plan
    own, last, twin, refs = refs[:4], refs[4:8], refs[8:12], refs[12:]
    low_ref, turned_ref, q_ref, key_ref, value_ref, *refs = refs
    moe_ref, query_out, kept_out, sent_out, by_place, stream, held, sums = refs
    step = pl.program_id(0)
    tokens = query_out.shape[0]
    part_size = by_place.shape[2]
    size = own[0].shape[1]
    mine, across = own[:2] + twin + last[:2], own[2:] + twin + last[2:]
    spread = part_size // size
    here, core = place_info[1], place_info[2]

    @pl.when(step == 0)
    def _():
        moe = dot(place_ref[...], back_ref[...]).astype(jnp.bfloat16)
        moe_ref[...] = moe
        added = (grad_ref[...].astype(jnp.float32) + moe.astype(jnp.float32)).astype(jnp.bfloat16)
        for z in range(4):
            for rest in range(spread):
                for side in range(2):
                    source = ((z * spread + rest) * 2 + side) * size
                    by_place[2 * z + side, :, rest * size : (rest + 1) * size] = added[:, source : source + size]
        for i in range(8):
            spot = slice(i * part_size, (i + 1) * part_size)
            stream[:, spot] = by_place[2 * (here ^ (i // 2)) + (core ^ (i % 2))]

    @pl.when((step > 0) & ((step - 1) % tiles == 0))
    def _():
        sums[...] = jnp.zeros_like(sums)

    def project(pieces):
        columns = jnp.concatenate([piece[...].reshape(part_size, piece.shape[-1]) for piece in pieces], axis=0)
        return dot(stream[...], columns).astype(jnp.bfloat16)

    def hold(head_grad):
        for head in range(heads):
            held[head * tokens : (head + 1) * tokens, :] = head_grad[:, head * HD : (head + 1) * HD]

    def attend():
        grads = held[...]
        low = low_ref[0].astype(jnp.float32)
        prob_grad = dot(grads, value_ref[0])
        row_dot = jnp.sum(low * prob_grad, axis=1, keepdims=True)
        score_grad = (low * (prob_grad - row_dot) * (HD**-0.5)).astype(jnp.bfloat16)
        query_grad = dot(score_grad, key_ref[0]).astype(jnp.bfloat16)
        sums[0] += dot(score_grad, q_ref[0], TN)
        sums[1] += dot(turned_ref[0], grads)
        for head in range(heads):
            query_out[:, head * HD : (head + 1) * HD] = query_grad[head * tokens : (head + 1) * tokens, :]

    @pl.when(step == 0)
    def _():
        hold(project(mine))

    @pl.when((step > 0) & (step < tiles))
    def _():
        head_grad = project(mine)
        attend()
        hold(head_grad)

    @pl.when((step >= tiles) & (step < 2 * tiles))
    def _():
        head_grad = project(across)
        attend()
        hold(head_grad)

    @pl.when(step == 2 * tiles)
    def _():
        attend()

    @pl.when((step > 0) & (step % tiles == 0))
    def _():
        kept_out[...] = sums[:, tokens:, :]
        sent_out[...] = sums[:, :tokens, :].astype(jnp.bfloat16)


def tail(place_info, back, place, moe_grad, pieces, low, turned, query, keys, values):
    tokens, width = moe_grad.shape
    spread, size, cols = pieces[0].shape
    span = keys.shape[1]
    heads = 4
    tile = heads * HD
    tiles = cols // tile
    steps = KVH * tiles
    was = lambda i: jnp.maximum(i - 1, 0)
    kv_group = lambda i, info: (was(i) // tiles) ^ info[0]
    whole = lambda shape: pl.BlockSpec(shape, lambda i, info: (0,) * len(shape))
    group = lambda shape: pl.BlockSpec((1,) + shape, lambda i, info: (kv_group(i, info), 0, 0))
    rows = lambda shape: pl.BlockSpec((1,) + shape, lambda i, info: (kv_group(i, info), was(i) % tiles, 0))
    own_tile = lambda i: jnp.minimum(i, tiles - 1)
    other_tile = lambda i: jnp.minimum(jnp.maximum(i - tiles, 0), tiles - 1)
    now = lambda i: jnp.minimum(i, steps - 1)
    twin = pl.BlockSpec((spread, 1, size, tile), lambda i, info: (0, now(i) // tiles, 0, now(i) % tiles))
    piece = lambda turn: pl.BlockSpec((spread, size, tile), lambda i, info: (0, 0, turn(i)))
    kv = pl.BlockSpec((2, tokens, HD), lambda i, info: (0, 0, kv_group(i, info)))
    return pl.pallas_call(
        functools.partial(tail_kernel, (heads, tiles)),
        grid_spec=pltpu.PrefetchScalarGridSpec(
            num_scalar_prefetch=1,
            grid=(steps + 1,),
            in_specs=[whole(back.shape), whole(place.shape), whole(moe_grad.shape)]
            + ([piece(own_tile)] * 2 + [piece(other_tile)] * 2) * 2
            + [twin] * 4
            + [
                rows((heads * tokens, span)),
                pl.BlockSpec(
                    (1, span, heads * tokens), lambda i, info: (kv_group(i, info), 0, was(i) % tiles)
                ),
                rows((heads * tokens, HD)),
                group((span, HD)),
                group((HD, span)),
            ],
            out_specs=[
                whole((tokens, width)),
                pl.BlockSpec(
                    (tokens, tile), lambda i, info: (0, kv_group(i, info) * tiles + was(i) % tiles)
                ),
                kv,
                kv,
            ],
            scratch_shapes=[
                pltpu.VMEM((8, tokens, spread * size), jnp.bfloat16),
                pltpu.VMEM((tokens, width), jnp.bfloat16),
                pltpu.VMEM((heads * tokens, HD), jnp.bfloat16),
                pltpu.VMEM((2, span, HD), jnp.float32),
            ],
        ),
        out_shape=(
            jax.ShapeDtypeStruct((tokens, width), jnp.bfloat16),
            jax.ShapeDtypeStruct((tokens, KVH * cols), jnp.bfloat16),
            jax.ShapeDtypeStruct((2, tokens, KVH * HD), jnp.float32),
            jax.ShapeDtypeStruct((2, tokens, KVH * HD), jnp.bfloat16),
        ),
        compiler_params=params(56),
        cost_estimate=pl.CostEstimate(
            flops=2 * tokens * width * KVH * cols, bytes_accessed=22 * MIB, transcendentals=0
        ),
        name="tail_attention",
    )(place_info, back, place, moe_grad, *pieces, low, turned, query, keys, values)


def finish_kernel(kept_ref, later_ref, key_ref, value_ref):
    for kind, out_ref in enumerate((key_ref, value_ref)):
        out_ref[...] = kept_ref[kind] + later_ref[kind].astype(jnp.float32)


def finish(kept, later):
    out = jax.ShapeDtypeStruct(kept.shape[1:], jnp.float32)
    return pl.pallas_call(
        finish_kernel, out_shape=(out, out), compiler_params=params(16), cost_estimate=LIGHT, name="finish"
    )(kept, later)


def local(
    moe_input,
    moe_grad,
    routes,
    route_weight,
    w_gate,
    w_up,
    w_down,
    w_out,
    queries,
    key_heads,
    value_heads,
    segments,
):
    chips = ("far", "near", "low")
    blk = chips + ("core",)
    low = lax.axis_size("low")
    owners = 4 * low
    count = 2 * owners
    parts = lax.axis_size("groups")
    tokens, width = moe_input.shape
    depth = 2 * max(1, 3 * tokens * routes.shape[1] // (2 * count))
    swap = [(0, 1), (1, 0)]
    onward = [(i, i + 1) for i in range(count - 1)]
    backward = [(i + 1, i) for i in range(count - 1)]

    share_cols = w_out.shape[1] // parts
    w_share = lax.dynamic_slice_in_dim(w_out, lax.axis_index("groups") * share_cols, share_cols, 1)
    w_far = lax.ppermute(w_share, "far", swap)
    w_near = lax.ppermute(w_share, "near", swap)

    rows, place = pick(routes, route_weight, moe_input, moe_grad, owners, depth)
    line = lambda w: lax.all_gather(w, "low", axis=0, tiled=False)
    cross = lambda w: lax.ppermute(w, "groups", swap)
    other_core = lambda w: lax.ppermute(w, "core", swap)
    own = (w_gate, w_up, w_down)
    other = tuple(other_core(w) for w in own)

    key_heads, value_heads, segments, place = lax.optimization_barrier((key_heads, value_heads, segments, place))
    kv = jnp.concatenate([key_heads, value_heads], axis=1)
    segs = (segments + 1).astype(jnp.float32)
    seg_rows = jnp.zeros((16, kv.shape[1]), jnp.bfloat16).at[0, :tokens].set(segs.astype(jnp.bfloat16))
    prev = lax.ppermute(jnp.concatenate([kv, seg_rows], axis=0), blk, onward)
    own_line = line(w_share)
    rows, w_near, w_far, own_line, prev = lax.optimization_barrier((rows, w_near, w_far, own_line, prev))

    rows_in = lax.all_to_all(rows.reshape(owners, depth, 2 * width), chips, 0, 0, tiled=True)
    near_crossed, far_crossed = cross(w_near), cross(w_far)
    near_twin = line(jnp.stack([w_near, near_crossed]))
    far_twin = line(jnp.stack([w_far, far_crossed]))
    own_line, near_crossed, far_crossed = lax.optimization_barrier((own_line, near_crossed, far_crossed))
    own_crossed = cross(own_line)
    w_last = lax.ppermute(w_far, "near", swap)
    prepared = prepare_weights(own, other)
    attention = attention_shares(queries, key_heads, value_heads, prev, segs)
    w_last, prepared, attention = lax.optimization_barrier((w_last, prepared, attention))
    own_swapped = other_core(own_line)
    rows_in, prepared, attention, own_line, own_swapped, own_crossed = lax.optimization_barrier(
        (rows_in, prepared, attention, own_line, own_swapped, own_crossed)
    )
    moved = lax.ppermute(w_last, "low", swap) if low == 2 else line(w_last)
    terms = experts(rows_in.reshape(owners * depth, 2 * width), *prepared)
    terms, own_line, own_crossed, w_last, moved, near_twin = lax.optimization_barrier(
        (terms, own_line, own_crossed, w_last, moved, near_twin)
    )
    last_line = moved
    if low == 2:
        first = lax.axis_index("low") == 0
        last_line = jnp.where(first, jnp.stack([w_last, moved]), jnp.stack([moved, w_last]))
    last_crossed, far_twin = lax.optimization_barrier((cross(last_line), far_twin))
    back = lax.all_to_all(terms.reshape(owners, depth, width), chips, 0, 0, tiled=True)
    both = lambda *pieces: [w for piece in pieces for w in (piece, other_core(piece))]

    z = 2 * lax.axis_index("far") + lax.axis_index("near")
    moe_input_grad, query_grad, kept, sent = tail(
        jnp.stack([lax.axis_index("groups"), z, lax.axis_index("core")]).astype(jnp.int32),
        back.reshape(owners * depth, width), place, moe_grad,
        [own_line, own_swapped, *both(own_crossed, last_line, last_crossed, near_twin, far_twin)], *attention,
    )
    return (moe_input_grad, query_grad, *finish(kept, lax.ppermute(sent, blk, backward)))


def solution(mesh):
    names = ("groups", "far", "near", "low", "core")
    shape = (mesh.shape["groups"], 2, 2, mesh.shape["blk"] // 8, 2)
    fine = jax.sharding.Mesh(mesh.devices.reshape(shape), names)
    blk = names[1:]
    by_tokens = P(names, None)
    return jax.shard_map(
        local,
        mesh=fine,
        in_specs=(
            by_tokens,
            by_tokens,
            by_tokens,
            by_tokens,
            P(None, blk),
            P(None, blk),
            P(blk, None),
            P(blk, None),
            by_tokens,
            by_tokens,
            by_tokens,
            P(names),
        ),
        out_specs=(by_tokens,) * 4,
        check_vma=False,
    )
```
